32 devices in a mesh: cuts: 8 (over z, y), loop: 4 (over x, core).
Axes of the slice: x: 2, y: 2, z: 4, core: 2. Of those that a mesh axis runs over, the one named last changes fastest.
Arguments:
- image_features: bfloat16 [8192, 1152], P(('cuts', 'loop')), may hold values from -0.1796875 to 0.1796875
- text_features: bfloat16 [8192, 1152], P(('cuts', 'loop')), may hold values from -0.1796875 to 0.1796875
- image_head: bfloat16 [1152, 1152], replicated, may hold values from -0.1875 to 0.1875
- text_head: bfloat16 [1152, 1152], replicated, may hold values from -0.1875 to 0.1875
Outputs:
- image_grad: float32 [8192, 1152], P(('cuts', 'loop'))
- text_grad: float32 [8192, 1152], P(('cuts', 'loop'))
- image_head_grad: float32 [1152, 1152], P('loop')
- text_head_grad: float32 [1152, 1152], P('loop')
The draws below stay inside these ranges and needn't reach their ends.
All inputs are finite; a program needn't handle non-finite values.
Results may differ from the reference program's by a relative error of at most 0.024.
Values may be sent and summed in bfloat16 or wider, within the bound.
No kernel may reach another device: no remote copies, remote signals or barrier semaphores. Data moves between devices by JAX's collectives and lax.ppermute only.
A program may use at most 128 MiB of HBM per device.

```python
import jax
import jax.numpy as jnp
from jax import lax

D = 1152
B = 256
ROWS = 8192
N_CUTS = 8
N_LOOP = 4


def steps_of(rng, extent, split, low, high):
    level, own = 1.0, jax.random.fold_in(rng, 6)
    for position, blocks in split:
        heights = jnp.exp(jax.random.uniform(jax.random.fold_in(own, position), (blocks,), jnp.float32, low / len(split), high / len(split)))
        level = level * jnp.repeat(heights, extent[position] // blocks).reshape([-1 if axis == position else 1 for axis in range(len(extent))])
    return level


def gaussian(own_key, extent, scale, bound, cuts=(), held_as=jnp.bfloat16):
    loudness = steps_of(own_key, extent, cuts, -0.22, 0.18) if cuts else 1.0
    drawn = jax.random.normal(own_key, extent, jnp.float32) * scale * loudness
    return jnp.minimum(jnp.maximum(drawn, -bound), bound).astype(held_as)


def setup_inputs(seed: int = 0) -> dict:
    seeds = jax.random.split(jax.random.key(seed), 5)
    return {
        "image_features": gaussian(seeds[0], (ROWS, D), 0.03, 0.1796875, ((0, 32),)),
        "text_features": gaussian(seeds[1], (ROWS, D), 0.03, 0.1796875, ((0, 32),)),
        "image_head": gaussian(seeds[2], (D, D), D ** -0.5, 0.1875),
        "text_head": gaussian(seeds[3], (D, D), D ** -0.5, 0.1875),
    }


SCORE_SCALE = 10.0
SCORE_BIAS = -2.5
EPSILON = 1e-06

def normalize(features, weight_matrix):
    projected = jnp.dot(features, weight_matrix, preferred_element_type=jnp.float32)
    factor = lax.rsqrt(lax.optimization_barrier(jnp.sum(projected * projected, axis=-1, keepdims=True)) + EPSILON)
    return (projected * factor, factor)

def pair_weights(image_vectors, text_vectors, image_offset, text_offset):
    pair_scores = SCORE_SCALE * lax.dot_general(image_vectors, text_vectors, (((1,), (1,)), ((), ())), preferred_element_type=jnp.float32) + SCORE_BIAS
    row_ids = image_offset + lax.broadcasted_iota(jnp.int32, pair_scores.shape, 0)
    col_ids = text_offset + lax.broadcasted_iota(jnp.int32, pair_scores.shape, 1)
    match_targets = jnp.where(row_ids == col_ids, 1.0, -1.0).astype(jnp.float32)
    return (SCORE_SCALE * -match_targets * jax.nn.sigmoid(-match_targets * pair_scores)).astype(jnp.bfloat16)

def norm_back(unit, factor, gradient):
    return (factor * (gradient - unit * lax.optimization_barrier(jnp.sum(unit * gradient, axis=-1, keepdims=True)))).astype(jnp.bfloat16)

def block_head_sum(features, back):
    feature_count = features.shape[1]

    def one_block(running, pair):
        rows, grads = pair
        term = jnp.einsum('bi,bj->ij', rows.astype(jnp.float32), grads.astype(jnp.float32))
        return (running + term.astype(jnp.bfloat16).astype(jnp.float32), None)
    stacked = (features.reshape(-1, B, feature_count), back.reshape(-1, B, feature_count))
    total, unused = lax.scan(one_block, jnp.zeros((feature_count, feature_count), jnp.float32), stacked)
    return total

def reference(image_features, text_features, image_head, text_head):
    feature_count = image_features.shape[1]
    image_groups = image_features.reshape(N_CUTS, B * N_LOOP, feature_count)
    text_groups = text_features.reshape(N_CUTS, B * N_LOOP, feature_count)

    def one_group(running, blocks):
        image_block, text_block = blocks
        image_unit, image_factor = normalize(image_block, image_head)
        text_unit, text_factor = normalize(text_block, text_head)
        image_vectors = image_unit.astype(jnp.bfloat16)
        text_vectors = text_unit.astype(jnp.bfloat16)
        weights = pair_weights(image_vectors, text_vectors, 0, 0)
        image_pull = jnp.dot(weights, text_vectors, preferred_element_type=jnp.float32)
        text_attraction = lax.dot_general(weights, image_vectors, (((0,), (0,)), ((), ())), preferred_element_type=jnp.float32)
        image_back = norm_back(image_unit, image_factor, image_pull)
        text_back = norm_back(text_unit, text_factor, text_attraction)
        image_out = lax.dot_general(image_back, image_head, (((1,), (1,)), ((), ())), preferred_element_type=jnp.float32)
        text_out = lax.dot_general(text_back, text_head, (((1,), (1,)), ((), ())), preferred_element_type=jnp.float32)
        image_wgrad = block_head_sum(image_block, image_back)
        text_wgrad = block_head_sum(text_block, text_back)
        return ((running[0] + image_wgrad, running[1] + text_wgrad), (image_out, text_out))
    zeros_head = jnp.zeros((feature_count, feature_count), jnp.float32)
    heads, outs = lax.scan(one_group, (zeros_head, zeros_head), (image_groups, text_groups))
    image_grad = outs[0].reshape(-1, feature_count)
    text_grad = outs[1].reshape(-1, feature_count)
    return (image_grad, text_grad, heads[0], heads[1])
```

```python
import functools

import jax
import jax.numpy as jnp
from jax import lax
from jax.experimental import pallas as pl
from jax.experimental.pallas import tpu as pltpu
from jax.sharding import PartitionSpec as P

SCORE_SCALE = 10.0
SCORE_BIAS = -2.5
EPSILON = 1e-06
QUAD = 4
STRIP = 32
F32 = jnp.float32
BF16 = jnp.bfloat16
VMEM_LIMIT = 56 * 1024 * 1024


def normalize(features, weight_matrix):
    projected = jnp.dot(features, weight_matrix, preferred_element_type=jnp.float32)
    factor = lax.rsqrt(jnp.sum(projected * projected, axis=-1, keepdims=True) + EPSILON)
    return (projected * factor, factor)


def pair_weights(image_vectors, text_vectors, image_offset):
    pair_scores = SCORE_SCALE * dot_nt(image_vectors, text_vectors) + SCORE_BIAS
    row_ids = image_offset + lax.broadcasted_iota(jnp.int32, pair_scores.shape, 0)
    col_ids = lax.broadcasted_iota(jnp.int32, pair_scores.shape, 1)
    match_targets = jnp.where(row_ids == col_ids, 1.0, -1.0).astype(jnp.float32)
    return (SCORE_SCALE * -match_targets * jax.nn.sigmoid(-match_targets * pair_scores)).astype(
        jnp.bfloat16
    )


def norm_back(unit, factor, gradient):
    return (factor * (gradient - unit * jnp.sum(unit * gradient, axis=-1, keepdims=True))).astype(
        jnp.bfloat16
    )


def dot_nn(left, right):
    return lax.dot_general(left, right, (((1,), (0,)), ((), ())), preferred_element_type=F32)


def dot_nt(left, right):
    return lax.dot_general(left, right, (((1,), (1,)), ((), ())), preferred_element_type=F32)


def dot_tn(left, right):
    return lax.dot_general(left, right, (((0,), (0,)), ((), ())), preferred_element_type=F32)


def plain_device(image_features, text_features, image_head, text_head):
    row_count = image_features.shape[0]
    own_start = lax.axis_index("loop") * row_count
    image_unit, image_factor = normalize(image_features, image_head)
    text_unit, text_factor = normalize(text_features, text_head)
    image_vectors = image_unit.astype(jnp.bfloat16)
    text_vectors = text_unit.astype(jnp.bfloat16)
    arrived = lax.all_gather(text_vectors, "loop", axis=0, tiled=True)
    weights = pair_weights(image_vectors, arrived, own_start)
    summed = jnp.dot(weights, arrived, preferred_element_type=jnp.float32)
    text_attraction = lax.psum_scatter(
        dot_tn(weights, image_vectors).astype(jnp.bfloat16), "loop", scatter_dimension=0, tiled=True
    ).astype(jnp.float32)
    image_back = norm_back(image_unit, image_factor, summed)
    text_back = norm_back(text_unit, text_factor, text_attraction)
    heads = []
    for features, back in ((image_features, image_back), (text_features, text_back)):
        term = dot_tn(features, back).astype(jnp.bfloat16)
        part = lax.psum_scatter(term, "loop", scatter_dimension=0, tiled=True)
        heads.append(lax.psum(part, "cuts").astype(jnp.float32))
    return (dot_nt(image_back, image_head), dot_nt(text_back, text_head), heads[0], heads[1])


def strips(rows, body):
    def step(index, carry):
        body(pl.ds(pl.multiple_of(index * STRIP, STRIP), STRIP), index * STRIP)
        return carry

    lax.fori_loop(0, rows // STRIP, step, 0, unroll=2)


def unit_rows(projected_ref, vectors_ref):
    def body(rows, first):
        p = projected_ref[rows, :]
        factor = lax.rsqrt(jnp.sum(p * p, axis=-1, keepdims=True) + EPSILON)
        vectors_ref[rows, :] = (p * factor).astype(BF16)

    strips(projected_ref.shape[0], body)


def back_rows(projected_ref, gradient_ref, back_ref):
    def body(rows, first):
        p = projected_ref[rows, :]
        factor = lax.rsqrt(jnp.sum(p * p, axis=-1, keepdims=True) + EPSILON)
        unit = p * factor
        g = gradient_ref[rows, :]
        back_ref[rows, :] = (
            factor * (g - unit * jnp.sum(unit * g, axis=-1, keepdims=True))
        ).astype(BF16)

    strips(projected_ref.shape[0], body)


def weight_rows(dots_ref, weights_ref, has_pairs):
    count = dots_ref.shape[1]

    def body(rows, first):
        score = SCORE_SCALE * dots_ref[rows, :] + SCORE_BIAS
        if has_pairs:
            same = first + lax.broadcasted_iota(jnp.int32, (STRIP, count), 0) == (
                lax.broadcasted_iota(jnp.int32, (STRIP, count), 1)
            )
            value = jax.nn.sigmoid(jnp.where(same, -score, score))
            value = jnp.where(same, -SCORE_SCALE, SCORE_SCALE) * value
        else:
            value = SCORE_SCALE * jax.nn.sigmoid(score)
        weights_ref[rows, :] = value.astype(BF16)

    strips(dots_ref.shape[0], body)


def picker(place_ref, rows, width):
    part = rows // QUAD
    pieces = []
    for k in range(QUAD):
        first = place_ref[0] * rows + (place_ref[1] ^ k) * part
        wanted = first + lax.broadcasted_iota(jnp.int32, (part, width), 0)
        column = lax.broadcasted_iota(jnp.int32, (part, width), 1)
        pieces.append(jnp.where(wanted == column, 1.0, 0.0))
    return jnp.concatenate(pieces, axis=0).astype(BF16)


def near_kernel(t0, t1, i0, i1, text_head, image_head, q_a, y_a, p_a, x_a, w_aa, dots):
    half = t0.shape[0]
    for block, (t, i) in enumerate(((t0, i0), (t1, i1))):
        rows = slice(block * half, (block + 1) * half)
        q_a[rows, :] = dot_nn(t[...], text_head[...])
        p_a[rows, :] = dot_nn(i[...], image_head[...])
    unit_rows(q_a, y_a)
    unit_rows(p_a, x_a)
    dots[...] = dot_nt(x_a[...], y_a[...])
    weight_rows(dots, w_aa, True)


def text_kernel(
    place, t0, t1, t2, t3, i0, i1, text_head, y_a, p_a, x_a, w_aa,
    q_b, y_b, dp_a, gy_a, gy_b, text_pick, image_pick, dots, gx, w_ab,
):
    half = t2.shape[0]
    rows_out = text_pick.shape[0]
    for block, t in enumerate((t2, t3)):
        q_b[block * half : (block + 1) * half, :] = dot_nn(t[...], text_head[...])
    unit_rows(q_b, y_b)
    dots[...] = dot_nt(x_a[...], y_b[...])
    weight_rows(dots, w_ab, False)
    gx[...] = dot_nn(w_aa[...], y_a[...])
    gx[...] += dot_nn(w_ab[...], y_b[...])
    back_rows(p_a, gx, dp_a)
    gy_a[...] = dot_tn(w_aa[...], x_a[...])
    gy_b[...] = dot_tn(w_ab[...], x_a[...])
    pick = picker(place, rows_out, t0.shape[1])
    for block, t in enumerate((t0, t1, t2, t3)):
        text_pick[:, block * half : (block + 1) * half] = dot_nt(pick, t[...]).astype(BF16)
    for block, i in enumerate((i0, i1)):
        image_pick[:, block * half : (block + 1) * half] = dot_nt(pick, i[...]).astype(BF16)


def last_kernel(
    place, i2, i3, image_head, y_a, y_b, q_a, q_b, gy_a_in, gy_b_in, dp_a, text_pick, image_pick,
    h0, h1, h2, h3, k0, k1, k2, k3, dq_own,
    p_b, x_b, w_ba, w_bb, dots, gx, gy, dp_b, dq_a, dq_b,
):
    half = i2.shape[0]
    rows_out = text_pick.shape[0]
    part = rows_out // QUAD
    for block, i in enumerate((i2, i3)):
        p_b[block * half : (block + 1) * half, :] = dot_nn(i[...], image_head[...])
    unit_rows(p_b, x_b)
    dots[...] = dot_nt(x_b[...], y_a[...])
    weight_rows(dots, w_ba, False)
    dots[...] = dot_nt(x_b[...], y_b[...])
    weight_rows(dots, w_bb, True)
    gx[...] = dot_nn(w_ba[...], y_a[...])
    gx[...] += dot_nn(w_bb[...], y_b[...])
    back_rows(p_b, gx, dp_b)
    pick = picker(place, rows_out, i2.shape[1])
    far = jnp.concatenate([dot_nt(pick, i2[...]), dot_nt(pick, i3[...])], axis=1).astype(BF16)
    head = dot_nn(image_pick[...], dp_a[...]) + dot_nn(far, dp_b[...])
    for k, out in enumerate((h0, h1, h2, h3)):
        out[...] = head[k * part : (k + 1) * part, :].astype(BF16)
    gy[...] = gy_a_in[...] + dot_tn(w_ba[...], x_b[...])
    back_rows(q_a, gy, dq_a)
    gy[...] = gy_b_in[...] + dot_tn(w_bb[...], x_b[...])
    back_rows(q_b, gy, dq_b)
    dq_own[...] = dq_a[:half, :]
    head = dot_nn(text_pick[:, : 2 * half], dq_a[...]) + dot_nn(text_pick[:, 2 * half :], dq_b[...])
    for k, out in enumerate((k0, k1, k2, k3)):
        out[...] = head[k * part : (k + 1) * part, :].astype(BF16)


def place_kernel(place, h0, h1, h2, h3, k0, k1, k2, k3, image_out, text_out):
    part = h0.shape[0]
    for out, pieces in ((image_out, (h0, h1, h2, h3)), (text_out, (k0, k1, k2, k3))):
        for k, piece in enumerate(pieces):
            first = pl.multiple_of((place[1] ^ k) * part, part)
            out[pl.ds(first, part), :] = piece[...].astype(F32)


def call(kernel, outs, scratch, args, flops, has_place=False):
    specs = [pl.BlockSpec(memory_space=pltpu.VMEM)] * len(args)
    if has_place:
        specs[0] = pl.BlockSpec(memory_space=pltpu.SMEM)
    moved = sum(a.size * a.dtype.itemsize for a in args)
    return pl.pallas_call(
        kernel,
        out_shape=[jax.ShapeDtypeStruct(s, t) for s, t in outs],
        in_specs=specs,
        out_specs=[pl.BlockSpec(memory_space=pltpu.VMEM)] * len(outs),
        scratch_shapes=[pltpu.VMEM(s, t) for s, t in scratch],
        compiler_params=pltpu.CompilerParams(vmem_limit_bytes=VMEM_LIMIT),
        cost_estimate=pl.CostEstimate(flops=flops, bytes_accessed=moved, transcendentals=0),
    )(*args)


def swap(array, axis, size, mask):
    return lax.ppermute(array, axis, [(i, i ^ mask) for i in range(size)])


def per_device(n_loop, n_cuts, image_features, text_features, image_head, text_head):
    half, width = image_features.shape
    near = 2 * half
    rows_out = width // n_loop
    part = rows_out // QUAD
    cut = lax.axis_index("cuts")
    place = jnp.stack([lax.axis_index("loop"), cut & (QUAD - 1)]).astype(jnp.int32)
    loop = functools.partial(swap, axis="loop", size=n_loop)
    cuts = functools.partial(swap, axis="cuts", size=n_cuts)
    macs = half * width * width

    t0, i0 = text_features, image_features
    t2 = loop(t0, mask=2)
    t1 = loop(t0, mask=1)
    i1 = loop(i0, mask=1)
    i2 = loop(i0, mask=2)
    q_a, y_a, p_a, x_a, w_aa = call(
        near_kernel,
        [((near, width), F32), ((near, width), BF16), ((near, width), F32), ((near, width), BF16),
         ((near, near), BF16)],
        [((near, near), F32)],
        (t0, t1, i0, i1, text_head, image_head),
        2 * 5 * macs,
    )
    t3 = loop(t2, mask=1)
    i3 = loop(i2, mask=1)
    q_b, y_b, dp_a, gy_a, gy_b, text_pick, image_pick = call(
        text_kernel,
        [((near, width), F32), ((near, width), BF16), ((near, width), BF16), ((near, width), F32),
         ((near, width), F32), ((rows_out, 2 * near), BF16), ((rows_out, near), BF16)],
        [((near, near), F32), ((near, width), F32), ((near, near), BF16)],
        (place, t0, t1, t2, t3, i0, i1, text_head, y_a, p_a, x_a, w_aa),
        2 * 8 * macs,
        True,
    )
    image_grad = dot_nt(dp_a[:half], image_head)
    pieces = call(
        last_kernel,
        [((part, width), BF16)] * (2 * QUAD) + [((half, width), BF16)],
        [((near, width), F32), ((near, width), BF16), ((near, near), BF16), ((near, near), BF16),
         ((near, near), F32), ((near, width), F32), ((near, width), F32), ((near, width), BF16),
         ((near, width), BF16), ((near, width), BF16)],
        (place, i2, i3, image_head, y_a, y_b, q_a, q_b, gy_a, gy_b, dp_a, text_pick, image_pick),
        2 * 9 * macs,
        True,
    )
    dq_own = pieces[-1]
    sums = []
    for own, *others in (pieces[:QUAD], pieces[QUAD : 2 * QUAD]):
        total = own.astype(F32)
        for k, other in enumerate(others):
            total = total + cuts(other, mask=k + 1).astype(F32)
        sums.append(total)
    text_grad = dot_nt(dq_own, text_head)
    upper = (cut & QUAD) != 0
    kept = jnp.where(upper, sums[1], sums[0])
    sent = jnp.where(upper, sums[0], sums[1]).astype(BF16)
    mine = (kept + cuts(sent, mask=QUAD).astype(F32)).astype(BF16)
    theirs = cuts(mine, mask=QUAD)
    mine_all = [mine] + [cuts(mine, mask=k) for k in range(1, QUAD)]
    theirs_all = [theirs] + [cuts(theirs, mask=k) for k in range(1, QUAD)]
    images = [jnp.where(upper, b, a) for a, b in zip(mine_all, theirs_all)]
    texts = [jnp.where(upper, a, b) for a, b in zip(mine_all, theirs_all)]
    image_out, text_out = call(
        place_kernel,
        [((rows_out, width), F32)] * 2,
        [],
        (place, *images, *texts),
        rows_out * width,
        True,
    )
    return (image_grad, text_grad, image_out, text_out)


def solution(mesh):
    n_loop, n_cuts = mesh.shape["loop"], mesh.shape["cuts"]
    if n_loop == 4 and n_cuts == 2 * QUAD:
        body = functools.partial(per_device, n_loop, n_cuts)
    else:
        body = plain_device
    placed = (P(("cuts", "loop"), None), P(("cuts", "loop"), None), P(), P())
    return jax.shard_map(
        body,
        mesh=mesh,
        in_specs=placed,
        out_specs=(
            P(("cuts", "loop"), None),
            P(("cuts", "loop"), None),
            P("loop", None),
            P("loop", None),
        ),
        check_vma=False,
    )
```

```python
import functools

import jax
import jax.numpy as jnp
from jax import lax
from jax.experimental import pallas as pl
from jax.experimental.pallas import tpu as pltpu
from jax.sharding import PartitionSpec as P

SCORE_SCALE = 10.0
SCORE_BIAS = -2.5
EPSILON = 1e-06
QUAD = 4
STRIP = 16
F32 = jnp.float32
BF16 = jnp.bfloat16
VMEM_LIMIT = 24 * 1024 * 1024


def normalize(features, weight_matrix):
    projected = jnp.dot(features, weight_matrix, preferred_element_type=jnp.float32)
    factor = lax.rsqrt(jnp.sum(projected * projected, axis=-1, keepdims=True) + EPSILON)
    return (projected * factor, factor)


def pair_weights(image_vectors, text_vectors, image_offset):
    pair_scores = SCORE_SCALE * dot_nt(image_vectors, text_vectors) + SCORE_BIAS
    row_ids = image_offset + lax.broadcasted_iota(jnp.int32, pair_scores.shape, 0)
    col_ids = lax.broadcasted_iota(jnp.int32, pair_scores.shape, 1)
    match_targets = jnp.where(row_ids == col_ids, 1.0, -1.0).astype(jnp.float32)
    return (SCORE_SCALE * -match_targets * jax.nn.sigmoid(-match_targets * pair_scores)).astype(
        jnp.bfloat16
    )


def norm_back(unit, factor, gradient):
    return (factor * (gradient - unit * jnp.sum(unit * gradient, axis=-1, keepdims=True))).astype(
        jnp.bfloat16
    )


def dot_nn(left, right):
    return lax.dot_general(left, right, (((1,), (0,)), ((), ())), preferred_element_type=F32)


def dot_nt(left, right):
    return lax.dot_general(left, right, (((1,), (1,)), ((), ())), preferred_element_type=F32)


def dot_tn(left, right):
    return lax.dot_general(left, right, (((0,), (0,)), ((), ())), preferred_element_type=F32)


def plain_device(image_features, text_features, image_head, text_head):
    row_count = image_features.shape[0]
    own_start = lax.axis_index("loop") * row_count
    image_unit, image_factor = normalize(image_features, image_head)
    text_unit, text_factor = normalize(text_features, text_head)
    image_vectors = image_unit.astype(jnp.bfloat16)
    text_vectors = text_unit.astype(jnp.bfloat16)
    arrived = lax.all_gather(text_vectors, "loop", axis=0, tiled=True)
    weights = pair_weights(image_vectors, arrived, own_start)
    summed = jnp.dot(weights, arrived, preferred_element_type=jnp.float32)
    text_attraction = lax.psum_scatter(
        dot_tn(weights, image_vectors).astype(jnp.bfloat16), "loop", scatter_dimension=0, tiled=True
    ).astype(jnp.float32)
    image_back = norm_back(image_unit, image_factor, summed)
    text_back = norm_back(text_unit, text_factor, text_attraction)
    heads = []
    for features, back in ((image_features, image_back), (text_features, text_back)):
        term = dot_tn(features, back).astype(jnp.bfloat16)
        part = lax.psum_scatter(term, "loop", scatter_dimension=0, tiled=True)
        heads.append(lax.psum(part, "cuts").astype(jnp.float32))
    return (dot_nt(image_back, image_head), dot_nt(text_back, text_head), heads[0], heads[1])


def factor_of(p):
    return lax.rsqrt(jnp.sum(p * p, axis=-1, keepdims=True) + EPSILON)


def unit_rows(projected_ref, vectors_ref):
    for first in range(0, projected_ref.shape[0], STRIP):
        p = projected_ref[first : first + STRIP, :]
        vectors_ref[first : first + STRIP, :] = (p * factor_of(p)).astype(BF16)


def back_rows(projected_ref, gradient_ref, back_ref):
    for first in range(0, projected_ref.shape[0], STRIP):
        p = projected_ref[first : first + STRIP, :]
        g = gradient_ref[first : first + STRIP, :]
        factor = factor_of(p)
        along = factor * factor * factor * jnp.sum(p * g, axis=-1, keepdims=True)
        back_ref[first : first + STRIP, :] = (factor * g - along * p).astype(BF16)


def weights_of(dots, pairs_from=None):
    score = SCORE_SCALE * dots + SCORE_BIAS
    if pairs_from is None:
        return (SCORE_SCALE * jax.nn.sigmoid(score)).astype(BF16)
    row = pairs_from + lax.broadcasted_iota(jnp.int32, dots.shape, 0)
    same = row == lax.broadcasted_iota(jnp.int32, dots.shape, 1)
    value = jax.nn.sigmoid(jnp.where(same, -score, score))
    return (jnp.where(same, -SCORE_SCALE, SCORE_SCALE) * value).astype(BF16)


def weight_rows(dots_ref, weights_ref, pairs_from=None):
    for first in range(0, dots_ref.shape[0], STRIP):
        pairs = None if pairs_from is None else pairs_from + first
        weights_ref[first : first + STRIP, :] = weights_of(dots_ref[first : first + STRIP, :], pairs)


def picker(place_ref, rows, width):
    part = rows // QUAD
    pieces = []
    for k in range(QUAD):
        first = place_ref[0] * rows + (place_ref[1] ^ k) * part
        wanted = first + lax.broadcasted_iota(jnp.int32, (part, width), 0)
        column = lax.broadcasted_iota(jnp.int32, (part, width), 1)
        pieces.append(jnp.where(wanted == column, 1.0, 0.0))
    return jnp.concatenate(pieces, axis=0).astype(BF16)


def near_kernel(t0, t1, i0, i1, text_head, image_head, q_a, y_a, p_a, x_a, w_aa, dots):
    half = t0.shape[0]
    q_a[:half, :] = dot_nn(t0[...], text_head[...])
    q_a[half:, :] = dot_nn(t1[...], text_head[...])
    unit_rows(q_a, y_a)
    p_a[:half, :] = dot_nn(i0[...], image_head[...])
    p_a[half:, :] = dot_nn(i1[...], image_head[...])
    unit_rows(p_a, x_a)
    dots[...] = dot_nt(x_a[...], y_a[...])
    weight_rows(dots, w_aa, 0)


def text_kernel(
    place, t0, t1, t2, t3, t4, i0, i1, text_head, y_a, p_a, x_a, w_aa,
    q_b, y_b, dp_a, gy_a, gy_b, text_pick, image_pick, dots, gx, w_ab,
):
    half = t2.shape[0]
    q_b[:half, :] = dot_nn(t2[...], text_head[...])
    t3 = jnp.concatenate([t3[...], t4[...]], axis=0)
    q_b[half:, :] = dot_nn(t3, text_head[...])
    unit_rows(q_b, y_b)
    dots[...] = dot_nt(x_a[...], y_b[...])
    weight_rows(dots, w_ab)
    gx[...] = dot_nn(w_aa[...], y_a[...]) + dot_nn(w_ab[...], y_b[...])
    back_rows(p_a, gx, dp_a)
    gy_a[...] = dot_tn(w_aa[...], x_a[...])
    gy_b[...] = dot_tn(w_ab[...], x_a[...])
    pick = picker(place, text_pick.shape[0], t0.shape[1])
    for block, t in enumerate((t0, t1, t2, t3)):
        text_pick[:, block * half : (block + 1) * half] = dot_nt(pick, t[...]).astype(BF16)
    for block, i in enumerate((i0, i1)):
        image_pick[:, block * half : (block + 1) * half] = dot_nt(pick, i[...]).astype(BF16)


def image_block(place, i, image_head, y_a, y_b, x_b, w_ba, w_bb, pick, dp_b, p_b, gx, d_a, d_b, block):
    p_b[...] = dot_nn(i[...], image_head[...])
    unit_rows(p_b, x_b)
    d_a[...] = dot_nt(x_b[...], y_a[...])
    d_b[...] = dot_nt(x_b[...], y_b[...])
    weight_rows(d_a, w_ba)
    weight_rows(d_b, w_bb, block * i.shape[0])
    gx[...] = dot_nn(w_ba[...], y_a[...]) + dot_nn(w_bb[...], y_b[...])
    back_rows(p_b, gx, dp_b)
    pick[...] = dot_nt(picker(place, pick.shape[0], i.shape[1]), i[...]).astype(BF16)


def third_kernel(place, i2, image_head, y_a, y_b, x_b, w_ba, w_bb, pick, dp_b, p_b, gx, d_a, d_b):
    image_block(place, i2, image_head, y_a, y_b, x_b, w_ba, w_bb, pick, dp_b, p_b, gx, d_a, d_b, 0)


def split_head(head, outs):
    part = head.shape[0] // QUAD
    for k, out in enumerate(outs):
        out[...] = head[k * part : (k + 1) * part, :].astype(BF16)


def fourth_kernel(
    place, i3, image_head, y_a, y_b, dp_a, dp_2, image_pick, pick_2,
    x_b, w_ba, w_bb, h0, h1, h2, h3, pick, dp_b, p_b, gx, d_a, d_b,
):
    image_block(place, i3, image_head, y_a, y_b, x_b, w_ba, w_bb, pick, dp_b, p_b, gx, d_a, d_b, 1)
    head = dot_nn(image_pick[...], dp_a[...]) + dot_nn(pick_2[...], dp_2[...])
    split_head(head + dot_nn(pick[...], dp_b[...]), (h0, h1, h2, h3))


def fifth_kernel(
    x_2, w_2a, w_2b, x_3, w_3a, w_3b, q_a, q_b, gy_a_in, gy_b_in, text_pick,
    k0, k1, k2, k3, dq_own, gy_a, gy_b, dq_a, dq_b,
):
    half = x_2.shape[0]
    gy_a[...] = gy_a_in[...] + dot_tn(w_2a[...], x_2[...]) + dot_tn(w_3a[...], x_3[...])
    gy_b[...] = gy_b_in[...] + dot_tn(w_2b[...], x_2[...]) + dot_tn(w_3b[...], x_3[...])
    back_rows(q_a, gy_a, dq_a)
    back_rows(q_b, gy_b, dq_b)
    dq_own[...] = dq_a[:half, :]
    head = dot_nn(text_pick[:, : 2 * half], dq_a[...]) + dot_nn(text_pick[:, 2 * half :], dq_b[...])
    split_head(head, (k0, k1, k2, k3))


def place_kernel(place, *refs):
    mine, theirs, outs = refs[:QUAD], refs[QUAD : 2 * QUAD], refs[2 * QUAD :]
    part = mine[0].shape[0]
    for head, out in enumerate(outs):
        for wanted, pieces in ((head, mine), (1 - head, theirs)):

            @pl.when(place[2] == wanted)
            def _(out=out, pieces=pieces):
                for k, piece in enumerate(pieces):
                    first = pl.multiple_of((place[1] ^ k) * part, part)
                    out[pl.ds(first, part), :] = piece[...].astype(F32)


def call(kernel, outs, scratch, args, macs, place=None, keep=True):
    args = [pltpu.with_memory_space_constraint(a, pltpu.VMEM) for a in args]
    specs = [pl.BlockSpec(memory_space=pltpu.VMEM)] * len(args)
    if place is not None:
        args, specs = [place, *args], [pl.BlockSpec(memory_space=pltpu.SMEM), *specs]
    shape = pltpu.VMEM if keep else jax.ShapeDtypeStruct
    return pl.pallas_call(
        kernel,
        out_shape=[shape(s, t) for s, t in outs],
        in_specs=specs,
        out_specs=[pl.BlockSpec(memory_space=pltpu.VMEM)] * len(outs),
        scratch_shapes=[pltpu.VMEM(s, t) for s, t in scratch],
        compiler_params=pltpu.CompilerParams(vmem_limit_bytes=VMEM_LIMIT),
        cost_estimate=pl.CostEstimate(flops=2 * (macs > 0), bytes_accessed=0, transcendentals=0),
    )(*args)


def swap(array, axis, size, mask):
    return lax.ppermute(array, axis, [(i, i ^ mask) for i in range(size)])


def after(value, other):
    return lax.optimization_barrier((value, other))[0]


def per_device(n_loop, n_cuts, image_features, text_features, image_head, text_head):
    half, width = image_features.shape
    near = 2 * half
    rows_out = width // n_loop
    part = rows_out // QUAD
    cut = lax.axis_index("cuts")
    upper = cut // QUAD
    place = jnp.stack([lax.axis_index("loop"), cut & (QUAD - 1), upper]).astype(jnp.int32)
    loop = functools.partial(swap, axis="loop", size=n_loop)
    cuts = functools.partial(swap, axis="cuts", size=n_cuts)
    macs = half * width * width

    t0, i0 = text_features, image_features
    t2 = loop(t0, mask=2)
    i2 = loop(i0, mask=2)
    t1 = loop(t0, mask=1)
    i1 = loop(i0, mask=1)
    wide, wide_b = ((near, width), F32), ((near, width), BF16)
    tall, tall_b = ((half, width), F32), ((half, width), BF16)
    square, block_w = ((near, near), BF16), ((half, near), BF16)
    pieces_out = [((part, width), BF16)] * QUAD
    q_a, y_a, p_a, x_a, w_aa = call(
        near_kernel,
        [wide, wide_b, wide, wide_b, square],
        [((near, near), F32)],
        (t0, t1, i0, i1, text_head, image_head),
        5 * macs,
    )
    t2 = after(t2, w_aa)
    t3 = [loop(t2[: half // 2], mask=1), loop(t2[half // 2 :], mask=1)]
    q_b, y_b, dp_a, gy_a, gy_b, text_pick, image_pick = call(
        text_kernel,
        [wide, wide_b, wide_b, wide, wide, ((rows_out, 2 * near), BF16), ((rows_out, near), BF16)],
        [((near, near), F32), wide, square],
        (t0, t1, t2, *t3, i0, i1, text_head, y_a, p_a, x_a, w_aa),
        8 * macs,
        place,
    )
    i2 = after(i2, dp_a)
    i3 = loop(i2, mask=1)
    block_scratch = [tall, tall, ((half, near), F32), ((half, near), F32)]
    x_2, w_2a, w_2b, pick_2, dp_2 = call(
        third_kernel,
        [tall_b, block_w, block_w, ((rows_out, half), BF16), tall_b],
        block_scratch,
        (i2, image_head, y_a, y_b),
        2 * macs,
        place,
    )
    x_3, w_3a, w_3b, *image_parts = call(
        fourth_kernel,
        [tall_b, block_w, block_w] + pieces_out,
        [((rows_out, half), BF16), tall_b] + block_scratch,
        (i3, image_head, y_a, y_b, dp_a, dp_2, image_pick, pick_2),
        3 * macs,
        place,
    )
    arrived = [cuts(image_parts[k], mask=k) for k in range(1, QUAD)]
    *text_parts, dq_own = call(
        fifth_kernel,
        pieces_out + [tall_b],
        [wide, wide, wide_b, wide_b],
        (x_2, w_2a, w_2b, x_3, w_3a, w_3b, q_a, q_b, gy_a, gy_b, text_pick),
        4 * macs,
    )
    image_sum = sum((a.astype(F32) for a in arrived), image_parts[0].astype(F32))
    arrived = [cuts(text_parts[k], mask=k) for k in range(1, QUAD)]
    image_grad = dot_nt(dp_a[:half], image_head)
    text_grad = dot_nt(dq_own, text_head)
    text_sum = sum((a.astype(F32) for a in arrived), text_parts[0].astype(F32))
    kept = jnp.where(upper == 1, text_sum, image_sum)
    sent = jnp.where(upper == 1, image_sum, text_sum).astype(BF16)
    mine = (kept + cuts(sent, mask=QUAD).astype(F32)).astype(BF16)
    theirs = cuts(mine, mask=QUAD)
    mine_all = [mine] + [cuts(mine, mask=k) for k in range(1, QUAD)]
    theirs_all = [theirs] + [cuts(theirs, mask=k) for k in range(1, QUAD)]
    image_out, text_out = call(
        place_kernel,
        [((rows_out, width), F32)] * 2,
        [],
        (*mine_all, *theirs_all),
        rows_out * width,
        place,
        keep=False,
    )
    return (image_grad, text_grad, image_out, text_out)


def solution(mesh):
    n_loop, n_cuts = mesh.shape["loop"], mesh.shape["cuts"]
    if n_loop == 4 and n_cuts == 2 * QUAD:
        body = functools.partial(per_device, n_loop, n_cuts)
    else:
        body = plain_device
    placed = (P(("cuts", "loop"), None), P(("cuts", "loop"), None), P(), P())
    return jax.shard_map(
        body,
        mesh=mesh,
        in_specs=placed,
        out_specs=(
            P(("cuts", "loop"), None),
            P(("cuts", "loop"), None),
            P("loop", None),
            P("loop", None),
        ),
        check_vma=False,
    )
```

```python
import functools

import jax
import jax.numpy as jnp
from jax import lax
from jax.experimental import pallas as pl
from jax.experimental.pallas import tpu as pltpu
from jax.sharding import PartitionSpec as P

SCORE_SCALE = 10.0
SCORE_BIAS = -2.5
EPSILON = 1e-06
QUAD = 4
STRIP = 16
F32 = jnp.float32
BF16 = jnp.bfloat16


def normalize(features, weight_matrix):
    projected = jnp.dot(features, weight_matrix, preferred_element_type=jnp.float32)
    factor = lax.rsqrt(jnp.sum(projected * projected, axis=-1, keepdims=True) + EPSILON)
    return (projected * factor, factor)


def pair_weights(image_vectors, text_vectors, image_offset):
    pair_scores = SCORE_SCALE * dot_nt(image_vectors, text_vectors) + SCORE_BIAS
    row_ids = image_offset + lax.broadcasted_iota(jnp.int32, pair_scores.shape, 0)
    col_ids = lax.broadcasted_iota(jnp.int32, pair_scores.shape, 1)
    match_targets = jnp.where(row_ids == col_ids, 1.0, -1.0).astype(jnp.float32)
    return (SCORE_SCALE * -match_targets * jax.nn.sigmoid(-match_targets * pair_scores)).astype(
        jnp.bfloat16
    )


def norm_back(unit, factor, gradient):
    return (factor * (gradient - unit * jnp.sum(unit * gradient, axis=-1, keepdims=True))).astype(
        jnp.bfloat16
    )


def dot_nn(left, right):
    return lax.dot_general(left, right, (((1,), (0,)), ((), ())), preferred_element_type=F32)


def dot_nt(left, right):
    return lax.dot_general(left, right, (((1,), (1,)), ((), ())), preferred_element_type=F32)


def dot_tn(left, right):
    return lax.dot_general(left, right, (((0,), (0,)), ((), ())), preferred_element_type=F32)


def plain_device(image_features, text_features, image_head, text_head):
    row_count = image_features.shape[0]
    own_start = lax.axis_index("loop") * row_count
    image_unit, image_factor = normalize(image_features, image_head)
    text_unit, text_factor = normalize(text_features, text_head)
    image_vectors = image_unit.astype(jnp.bfloat16)
    text_vectors = text_unit.astype(jnp.bfloat16)
    arrived = lax.all_gather(text_vectors, "loop", axis=0, tiled=True)
    weights = pair_weights(image_vectors, arrived, own_start)
    summed = jnp.dot(weights, arrived, preferred_element_type=jnp.float32)
    text_attraction = lax.psum_scatter(
        dot_tn(weights, image_vectors).astype(jnp.bfloat16), "loop", scatter_dimension=0, tiled=True
    ).astype(jnp.float32)
    image_back = norm_back(image_unit, image_factor, summed)
    text_back = norm_back(text_unit, text_factor, text_attraction)
    heads = []
    for features, back in ((image_features, image_back), (text_features, text_back)):
        term = dot_tn(features, back).astype(jnp.bfloat16)
        part = lax.psum_scatter(term, "loop", scatter_dimension=0, tiled=True)
        heads.append(lax.psum(part, "cuts").astype(jnp.float32))
    return (dot_nt(image_back, image_head), dot_nt(text_back, text_head), heads[0], heads[1])


def factor_of(p):
    return lax.rsqrt(jnp.sum(p * p, axis=-1, keepdims=True) + EPSILON)


def unit_rows(projected_ref, vectors_ref):
    for first in range(0, projected_ref.shape[0], STRIP):
        p = projected_ref[first : first + STRIP, :]
        vectors_ref[first : first + STRIP, :] = (p * factor_of(p)).astype(BF16)


def back_rows(projected_ref, gradient_ref, back_ref):
    for first in range(0, projected_ref.shape[0], STRIP):
        p = projected_ref[first : first + STRIP, :]
        g = gradient_ref[first : first + STRIP, :]
        factor = factor_of(p)
        along = factor * factor * factor * jnp.sum(p * g, axis=-1, keepdims=True)
        back_ref[first : first + STRIP, :] = (factor * g - along * p).astype(BF16)


def weights_of(dots, pairs_from=None):
    score = SCORE_SCALE * dots + SCORE_BIAS
    if pairs_from is None:
        return (SCORE_SCALE * jax.nn.sigmoid(score)).astype(BF16)
    row = pairs_from + lax.broadcasted_iota(jnp.int32, dots.shape, 0)
    same = row == lax.broadcasted_iota(jnp.int32, dots.shape, 1)
    value = jax.nn.sigmoid(jnp.where(same, -score, score))
    return (jnp.where(same, -SCORE_SCALE, SCORE_SCALE) * value).astype(BF16)


def weight_rows(dots_ref, weights_ref, pairs_from=None):
    for first in range(0, dots_ref.shape[0], STRIP):
        pairs = None if pairs_from is None else pairs_from + first
        weights_ref[first : first + STRIP, :] = weights_of(dots_ref[first : first + STRIP, :], pairs)


def picker(place_ref, rows, width):
    wanted = place_ref[0] * rows + lax.broadcasted_iota(jnp.int32, (rows, width), 0)
    column = lax.broadcasted_iota(jnp.int32, (rows, width), 1)
    return jnp.where(wanted == column, 1.0, 0.0).astype(BF16)


def near_kernel(t0, t1, i0, i1, text_head, image_head, q_a, y_a, p_a, x_a, w_aa, dots):
    half = t0.shape[0]
    q_a[:half, :] = dot_nn(t0[...], text_head[...])
    q_a[half:, :] = dot_nn(t1[...], text_head[...])
    unit_rows(q_a, y_a)
    p_a[:half, :] = dot_nn(i0[...], image_head[...])
    p_a[half:, :] = dot_nn(i1[...], image_head[...])
    unit_rows(p_a, x_a)
    dots[...] = dot_nt(x_a[...], y_a[...])
    weight_rows(dots, w_aa, 0)


def text_kernel(
    place, t0, t1, t2, t3, t4, i0, i1, text_head, y_a, p_a, x_a, w_aa,
    q_b, y_b, dp_a, gy_a, gy_b, text_pick, image_pick, dots, gx, w_ab,
):
    half = t2.shape[0]
    q_b[:half, :] = dot_nn(t2[...], text_head[...])
    t3 = jnp.concatenate([t3[...], t4[...]], axis=0)
    q_b[half:, :] = dot_nn(t3, text_head[...])
    unit_rows(q_b, y_b)
    dots[...] = dot_nt(x_a[...], y_b[...])
    weight_rows(dots, w_ab)
    gx[...] = dot_nn(w_aa[...], y_a[...]) + dot_nn(w_ab[...], y_b[...])
    back_rows(p_a, gx, dp_a)
    gy_a[...] = dot_tn(w_aa[...], x_a[...])
    gy_b[...] = dot_tn(w_ab[...], x_a[...])
    pick = picker(place, text_pick.shape[0], t0.shape[1])
    for block, t in enumerate((t0, t1, t2, t3)):
        text_pick[:, block * half : (block + 1) * half] = dot_nt(pick, t[...]).astype(BF16)
    for block, i in enumerate((i0, i1)):
        image_pick[:, block * half : (block + 1) * half] = dot_nt(pick, i[...]).astype(BF16)


def image_block(place, i, image_head, y_a, y_b, x_b, w_ba, w_bb, pick, dp_b, p_b, gx, d_a, d_b, block):
    p_b[...] = dot_nn(i[...], image_head[...])
    unit_rows(p_b, x_b)
    d_a[...] = dot_nt(x_b[...], y_a[...])
    d_b[...] = dot_nt(x_b[...], y_b[...])
    weight_rows(d_a, w_ba)
    weight_rows(d_b, w_bb, block * i.shape[0])
    gx[...] = dot_nn(w_ba[...], y_a[...]) + dot_nn(w_bb[...], y_b[...])
    back_rows(p_b, gx, dp_b)
    pick[...] = dot_nt(picker(place, pick.shape[0], i.shape[1]), i[...]).astype(BF16)


def third_kernel(place, i2, image_head, y_a, y_b, x_b, w_ba, w_bb, pick, dp_b, p_b, gx, d_a, d_b):
    image_block(place, i2, image_head, y_a, y_b, x_b, w_ba, w_bb, pick, dp_b, p_b, gx, d_a, d_b, 0)


def fourth_kernel(
    place, i3, image_head, y_a, y_b, dp_a, dp_2, image_pick, pick_2,
    x_b, w_ba, w_bb, head_out, pick, dp_b, p_b, gx, d_a, d_b,
):
    image_block(place, i3, image_head, y_a, y_b, x_b, w_ba, w_bb, pick, dp_b, p_b, gx, d_a, d_b, 1)
    head = dot_nn(image_pick[...], dp_a[...]) + dot_nn(pick_2[...], dp_2[...])
    head_out[...] = (head + dot_nn(pick[...], dp_b[...])).astype(BF16)


def fifth_kernel(
    x_2, w_2a, w_2b, x_3, w_3a, w_3b, q_a, q_b, gy_a_in, gy_b_in, text_pick,
    head_out, dq_own, gy_a, gy_b, dq_a, dq_b,
):
    half = x_2.shape[0]
    gy_a[...] = gy_a_in[...] + dot_tn(w_2a[...], x_2[...]) + dot_tn(w_3a[...], x_3[...])
    gy_b[...] = gy_b_in[...] + dot_tn(w_2b[...], x_2[...]) + dot_tn(w_3b[...], x_3[...])
    back_rows(q_a, gy_a, dq_a)
    back_rows(q_b, gy_b, dq_b)
    dq_own[...] = dq_a[:half, :]
    head = dot_nn(text_pick[:, : 2 * half], dq_a[...]) + dot_nn(text_pick[:, 2 * half :], dq_b[...])
    head_out[...] = head.astype(BF16)


def call(kernel, outs, scratch, args, mib, place=None, macs=1):
    args = [pltpu.with_memory_space_constraint(a, pltpu.VMEM) for a in args]
    specs = [pl.BlockSpec(memory_space=pltpu.VMEM)] * len(args)
    if place is not None:
        args, specs = [place, *args], [pl.BlockSpec(memory_space=pltpu.SMEM), *specs]
    return pl.pallas_call(
        kernel,
        out_shape=[pltpu.VMEM(s, t) for s, t in outs],
        in_specs=specs,
        out_specs=[pl.BlockSpec(memory_space=pltpu.VMEM)] * len(outs),
        scratch_shapes=[pltpu.VMEM(s, t) for s, t in scratch],
        compiler_params=pltpu.CompilerParams(vmem_limit_bytes=mib * 1024 * 1024),
        cost_estimate=pl.CostEstimate(flops=2 * macs, bytes_accessed=0, transcendentals=0),
    )(*args)


def swap(array, axis, size, mask):
    return lax.ppermute(array, axis, [(i, i ^ mask) for i in range(size)])


def after(value, other):
    return lax.optimization_barrier((value, other))[0]


def per_device(n_loop, n_cuts, image_features, text_features, image_head, text_head):
    half, width = image_features.shape
    near = 2 * half
    rows_out = width // n_loop
    part = rows_out // QUAD
    cut = lax.axis_index("cuts")
    upper = cut // QUAD
    place = lax.axis_index("loop").astype(jnp.int32).reshape(1)
    loop = functools.partial(swap, axis="loop", size=n_loop)
    cuts = functools.partial(swap, axis="cuts", size=n_cuts)
    quads = functools.partial(
        lax.all_to_all, axis_name="cuts", split_axis=0, concat_axis=0, tiled=True,
        axis_index_groups=[list(range(g, g + QUAD)) for g in range(0, n_cuts, QUAD)],
    )
    macs = half * width * width

    t0, i0 = text_features, image_features
    t2 = loop(t0, mask=2)
    i2 = loop(i0, mask=2)
    t1 = loop(t0, mask=1)
    i1 = loop(i0, mask=1)
    wide, wide_b = ((near, width), F32), ((near, width), BF16)
    tall, tall_b = ((half, width), F32), ((half, width), BF16)
    square, block_w = ((near, near), BF16), ((half, near), BF16)
    head_term = ((rows_out, width), BF16)
    q_a, y_a, p_a, x_a, w_aa = call(
        near_kernel,
        [wide, wide_b, wide, wide_b, square],
        [((near, near), F32)],
        (t0, t1, i0, i1, text_head, image_head),
        8,
    )
    t2 = after(t2, w_aa)
    t3 = [loop(t2[: half // 2], mask=1), loop(t2[half // 2 :], mask=1)]
    q_b, y_b, dp_a, gy_a, gy_b, text_pick, image_pick = call(
        text_kernel,
        [wide, wide_b, wide_b, wide, wide, ((rows_out, 2 * near), BF16), ((rows_out, near), BF16)],
        [((near, near), F32), wide, square],
        (t0, t1, t2, *t3, i0, i1, text_head, y_a, p_a, x_a, w_aa),
        8,
        place,
    )
    i2 = after(i2, dp_a)
    i3 = loop(i2, mask=1)
    block_scratch = [tall, tall, ((half, near), F32), ((half, near), F32)]
    x_2, w_2a, w_2b, pick_2, dp_2 = call(
        third_kernel,
        [tall_b, block_w, block_w, ((rows_out, half), BF16), tall_b],
        block_scratch,
        (i2, image_head, y_a, y_b),
        8,
        place,
    )
    x_3, w_3a, w_3b, image_term = call(
        fourth_kernel,
        [tall_b, block_w, block_w, head_term],
        [((rows_out, half), BF16), tall_b] + block_scratch,
        (i3, image_head, y_a, y_b, dp_a, dp_2, image_pick, pick_2),
        8,
        place,
    )
    image_terms = quads(image_term)
    text_term, dq_own = call(
        fifth_kernel,
        [head_term, tall_b],
        [wide, wide, wide_b, wide_b],
        (x_2, w_2a, w_2b, x_3, w_3a, w_3b, q_a, q_b, gy_a, gy_b, text_pick),
        14,
        macs=4 * macs,
    )
    text_terms = quads(text_term)
    image_grad = dot_nt(dp_a[:half], image_head)
    text_grad = dot_nt(dq_own, text_head)
    image_sum, text_sum = (
        jnp.sum(terms.reshape(QUAD, part, width).astype(F32), axis=0)
        for terms in (image_terms, text_terms)
    )
    kept = jnp.where(upper == 1, text_sum, image_sum)
    sent = jnp.where(upper == 1, image_sum, text_sum).astype(BF16)
    mine = (kept + cuts(sent, mask=QUAD).astype(F32)).astype(BF16)
    theirs = cuts(mine, mask=QUAD)
    mine_all = quads(jnp.tile(mine, (QUAD, 1)))
    theirs_all = quads(jnp.tile(theirs, (QUAD, 1)))
    image_out = jnp.where(upper == 1, theirs_all, mine_all).astype(F32)
    text_out = jnp.where(upper == 1, mine_all, theirs_all).astype(F32)
    return (image_grad, text_grad, image_out, text_out)


def solution(mesh):
    n_loop, n_cuts = mesh.shape["loop"], mesh.shape["cuts"]
    if n_loop == 4 and n_cuts == 2 * QUAD:
        body = functools.partial(per_device, n_loop, n_cuts)
    else:
        body = plain_device
    placed = (P(("cuts", "loop"), None), P(("cuts", "loop"), None), P(), P())
    return jax.shard_map(
        body,
        mesh=mesh,
        in_specs=placed,
        out_specs=(
            P(("cuts", "loop"), None),
            P(("cuts", "loop"), None),
            P("loop", None),
            P("loop", None),
        ),
        check_vma=False,
    )
```

```python
import functools

import jax
import jax.numpy as jnp
from jax import lax
from jax.experimental import pallas as pl
from jax.experimental.pallas import tpu as pltpu
from jax.sharding import PartitionSpec as P

SCORE_SCALE = 10.0
SCORE_BIAS = -2.5
EPSILON = 1e-06
QUAD = 4
STRIP = 16
F32 = jnp.float32
BF16 = jnp.bfloat16


def normalize(features, weight_matrix):
    projected = jnp.dot(features, weight_matrix, preferred_element_type=jnp.float32)
    factor = lax.rsqrt(jnp.sum(projected * projected, axis=-1, keepdims=True) + EPSILON)
    return (projected * factor, factor)


def pair_weights(image_vectors, text_vectors, image_offset):
    pair_scores = SCORE_SCALE * dot_nt(image_vectors, text_vectors) + SCORE_BIAS
    row_ids = image_offset + lax.broadcasted_iota(jnp.int32, pair_scores.shape, 0)
    col_ids = lax.broadcasted_iota(jnp.int32, pair_scores.shape, 1)
    match_targets = jnp.where(row_ids == col_ids, 1.0, -1.0).astype(jnp.float32)
    return (SCORE_SCALE * -match_targets * jax.nn.sigmoid(-match_targets * pair_scores)).astype(
        jnp.bfloat16
    )


def norm_back(unit, factor, gradient):
    return (factor * (gradient - unit * jnp.sum(unit * gradient, axis=-1, keepdims=True))).astype(
        jnp.bfloat16
    )


def dot_nn(left, right):
    return lax.dot_general(left, right, (((1,), (0,)), ((), ())), preferred_element_type=F32)


def dot_nt(left, right):
    return lax.dot_general(left, right, (((1,), (1,)), ((), ())), preferred_element_type=F32)


def dot_tn(left, right):
    return lax.dot_general(left, right, (((0,), (0,)), ((), ())), preferred_element_type=F32)


def plain_device(image_features, text_features, image_head, text_head):
    row_count = image_features.shape[0]
    own_start = lax.axis_index("loop") * row_count
    image_unit, image_factor = normalize(image_features, image_head)
    text_unit, text_factor = normalize(text_features, text_head)
    image_vectors = image_unit.astype(jnp.bfloat16)
    text_vectors = text_unit.astype(jnp.bfloat16)
    arrived = lax.all_gather(text_vectors, "loop", axis=0, tiled=True)
    weights = pair_weights(image_vectors, arrived, own_start)
    summed = jnp.dot(weights, arrived, preferred_element_type=jnp.float32)
    text_attraction = lax.psum_scatter(
        dot_tn(weights, image_vectors).astype(jnp.bfloat16), "loop", scatter_dimension=0, tiled=True
    ).astype(jnp.float32)
    image_back = norm_back(image_unit, image_factor, summed)
    text_back = norm_back(text_unit, text_factor, text_attraction)
    heads = []
    for features, back in ((image_features, image_back), (text_features, text_back)):
        term = dot_tn(features, back).astype(jnp.bfloat16)
        part = lax.psum_scatter(term, "loop", scatter_dimension=0, tiled=True)
        heads.append(lax.psum(part, "cuts").astype(jnp.float32))
    return (dot_nt(image_back, image_head), dot_nt(text_back, text_head), heads[0], heads[1])


def factor_of(p):
    return lax.rsqrt(jnp.sum(p * p, axis=-1, keepdims=True) + EPSILON)


def unit_rows(projected_ref, vectors_ref):
    for first in range(0, projected_ref.shape[0], STRIP):
        p = projected_ref[first : first + STRIP, :]
        vectors_ref[first : first + STRIP, :] = (p * factor_of(p)).astype(BF16)


def back_rows(projected_ref, gradient_ref, back_ref):
    for first in range(0, projected_ref.shape[0], STRIP):
        p = projected_ref[first : first + STRIP, :]
        g = gradient_ref[first : first + STRIP, :]
        factor = factor_of(p)
        along = factor * factor * factor * jnp.sum(p * g, axis=-1, keepdims=True)
        back_ref[first : first + STRIP, :] = (factor * g - along * p).astype(BF16)


def weights_of(dots, pairs_from=None):
    score = SCORE_SCALE * dots + SCORE_BIAS
    if pairs_from is None:
        return (SCORE_SCALE * jax.nn.sigmoid(score)).astype(BF16)
    row = pairs_from + lax.broadcasted_iota(jnp.int32, dots.shape, 0)
    same = row == lax.broadcasted_iota(jnp.int32, dots.shape, 1)
    value = jax.nn.sigmoid(jnp.where(same, -score, score))
    return (jnp.where(same, -SCORE_SCALE, SCORE_SCALE) * value).astype(BF16)


def weight_rows(dots_ref, weights_ref, pairs_from=None):
    for first in range(0, dots_ref.shape[0], STRIP):
        pairs = None if pairs_from is None else pairs_from + first
        weights_ref[first : first + STRIP, :] = weights_of(dots_ref[first : first + STRIP, :], pairs)


def one_hot(first, rows, width):
    wanted = first + lax.broadcasted_iota(jnp.int32, (rows, width), 0)
    column = lax.broadcasted_iota(jnp.int32, (rows, width), 1)
    return jnp.where(wanted == column, 1.0, 0.0)


def picker(place_ref, rows, width, sides):
    part = rows // QUAD
    pieces = []
    for k in range(QUAD):
        for side in sides:
            first = (place_ref[0] ^ side) * rows + (place_ref[1] ^ k) * part
            pieces.append(one_hot(first, part, width))
    return jnp.concatenate(pieces, axis=0).astype(BF16)


def split_head(head, outs):
    part = head.shape[0] // QUAD
    for k, out in enumerate(outs):
        out[...] = head[k * part : (k + 1) * part, :].astype(BF16)


def near_kernel(
    place, t0, t1, i0, i1, text_head, image_head, q_a, y_a, p_a, x_a, w_aa, pick_i, pick_t, dots
):
    half = t0.shape[0]
    q_a[:half, :] = dot_nn(t0[...], text_head[...])
    q_a[half:, :] = dot_nn(t1[...], text_head[...])
    unit_rows(q_a, y_a)
    p_a[:half, :] = dot_nn(i0[...], image_head[...])
    p_a[half:, :] = dot_nn(i1[...], image_head[...])
    unit_rows(p_a, x_a)
    dots[...] = dot_nt(x_a[...], y_a[...])
    weight_rows(dots, w_aa, 0)
    rows = pick_t.shape[0]
    pick = picker(place, rows, t0.shape[1], (0,))
    pick_t[:, :half] = dot_nt(pick, t0[...]).astype(BF16)
    pick_t[:, half:] = dot_nt(pick, t1[...]).astype(BF16)
    pick = picker(place, rows, t0.shape[1], (0, 2))
    pick_i[:, :half] = dot_nt(pick, i0[...]).astype(BF16)
    pick_i[:, half:] = dot_nt(pick, i1[...]).astype(BF16)


def image_kernel(
    t2, t3, t4, t5, t6, text_head, y_a, p_a, x_a, w_aa, pick_i,
    q_b, y_b, w_ab, dp_a, h0, h1, h2, h3, dots, gx,
):
    half = t2.shape[0]
    q_b[:half, :] = dot_nn(t2[...], text_head[...])
    q_b[half:, :] = dot_nn(jnp.concatenate([t3[...], t4[...], t5[...], t6[...]], axis=0), text_head[...])
    unit_rows(q_b, y_b)
    dots[...] = dot_nt(x_a[...], y_b[...])
    weight_rows(dots, w_ab)
    gx[...] = dot_nn(w_aa[...], y_a[...]) + dot_nn(w_ab[...], y_b[...])
    back_rows(p_a, gx, dp_a)
    split_head(dot_nn(pick_i[...], dp_a[...]), (h0, h1, h2, h3))


def pull_kernel(place, t2, t3, t4, t5, t6, x_a, w_aa, w_ab, gy_a, gy_b, pick_t):
    half = t2.shape[0]
    gy_a[...] = dot_tn(w_aa[...], x_a[...])
    gy_b[...] = dot_tn(w_ab[...], x_a[...])
    pick = picker(place, pick_t.shape[0], t2.shape[1], (0,))
    pick_t[:, :half] = dot_nt(pick, t2[...]).astype(BF16)
    far = jnp.concatenate([t3[...], t4[...], t5[...], t6[...]], axis=0)
    pick_t[:, half:] = dot_nt(pick, far).astype(BF16)


def block_kernel(block, *refs):
    *features, image_head, y_a, y_b, x_b, w_ba, w_bb, p_b, d_a, d_b = refs
    features = jnp.concatenate([i[...] for i in features], axis=0)
    p_b[...] = dot_nn(features, image_head[...])
    unit_rows(p_b, x_b)
    d_a[...] = dot_nt(x_b[...], y_a[...])
    d_b[...] = dot_nt(x_b[...], y_b[...])
    weight_rows(d_a, w_ba)
    weight_rows(d_b, w_bb, block * x_b.shape[0])


def last_kernel(
    x_2, w_2a, w_2b, x_3, w_3a, w_3b, q_a, q_b, gy_a_in, gy_b_in, pick_a, pick_b,
    h0, h1, h2, h3, dq_own, gy_a, gy_b, dq_a, dq_b,
):
    half = x_2.shape[0]
    gy_a[...] = gy_a_in[...] + dot_tn(w_2a[...], x_2[...]) + dot_tn(w_3a[...], x_3[...])
    gy_b[...] = gy_b_in[...] + dot_tn(w_2b[...], x_2[...]) + dot_tn(w_3b[...], x_3[...])
    back_rows(q_a, gy_a, dq_a)
    back_rows(q_b, gy_b, dq_b)
    dq_own[...] = dq_a[:half, :]
    split_head(dot_nn(pick_a[...], dq_a[...]) + dot_nn(pick_b[...], dq_b[...]), (h0, h1, h2, h3))


def grad_kernel(back, head, out):
    out[...] = dot_nt(back[: out.shape[0], :], head[...])


def place_kernel(place, h0, h1, h2, h3, out):
    part = h0.shape[0]
    for k, piece in enumerate((h0, h1, h2, h3)):
        first = pl.multiple_of((place[1] ^ k) * part, part)
        out[pl.ds(first, part), :] = piece[...].astype(F32)


def call(kernel, outs, scratch, args, mib, place=None, macs=1, keep=True):
    args = [pltpu.with_memory_space_constraint(a, pltpu.VMEM) for a in args]
    specs = [pl.BlockSpec(memory_space=pltpu.VMEM)] * len(args)
    if place is not None:
        args, specs = [place, *args], [pl.BlockSpec(memory_space=pltpu.SMEM), *specs]
    shape = pltpu.VMEM if keep else jax.ShapeDtypeStruct
    return pl.pallas_call(
        kernel,
        out_shape=[shape(s, t) for s, t in outs],
        in_specs=specs,
        out_specs=[pl.BlockSpec(memory_space=pltpu.VMEM)] * len(outs),
        scratch_shapes=[pltpu.VMEM(s, t) for s, t in scratch],
        compiler_params=pltpu.CompilerParams(vmem_limit_bytes=mib * 1024 * 1024),
        cost_estimate=pl.CostEstimate(flops=2 * macs, bytes_accessed=0, transcendentals=0),
    )(*args)


def swap(array, axis, size, mask):
    return lax.ppermute(array, axis, [(i, i ^ mask) for i in range(size)])


def after(value, other):
    return lax.optimization_barrier((value, other))[0]


def per_device(n_loop, n_cuts, image_features, text_features, image_head, text_head):
    half, width = image_features.shape
    near = 2 * half
    rows_out = width // n_loop
    part = rows_out // QUAD
    loop = functools.partial(swap, axis="loop", size=n_loop)
    cuts = functools.partial(swap, axis="cuts", size=n_cuts)
    macs = half * width * width

    def add(own, others):
        return sum((other.astype(F32) for other in others), own.astype(F32)).astype(BF16)

    def finish(total):
        total = add(total, [cuts(total, mask=QUAD)])
        pieces = [total] + [cuts(total, mask=k) for k in range(1, QUAD)]
        outs = [((rows_out, width), F32)]
        return call(place_kernel, outs, [], pieces, 4, place, keep=False)[0]

    t2 = loop(text_features, mask=2)
    i2 = loop(image_features, mask=2)
    place = jnp.stack([lax.axis_index("loop"), lax.axis_index("cuts") & (QUAD - 1)])
    place = place.astype(jnp.int32)
    t0, i0, place = lax.optimization_barrier((text_features, image_features, place))
    t1 = loop(t0, mask=1)
    i1 = loop(i0, mask=1)
    wide, wide_b = ((near, width), F32), ((near, width), BF16)
    tall, tall_b = ((half, width), F32), ((half, width), BF16)
    square, dots = ((near, near), BF16), ((near, near), F32)
    block_w, block_dots = ((half, near), BF16), ((half, near), F32)
    pick_one, pick_two = ((rows_out, near), BF16), ((2 * rows_out, near), BF16)
    q_a, y_a, p_a, x_a, w_aa, pick_i, pick_a = call(
        near_kernel,
        [wide, wide_b, wide, wide_b, square, pick_two, pick_one],
        [dots],
        (t0, t1, i0, i1, text_head, image_head),
        8,
        place,
    )
    t2 = after(t2, w_aa)
    t3 = [loop(rows, mask=1) for rows in jnp.split(t2, 4)]
    q_b, y_b, w_ab, dp_a, *image_parts = call(
        image_kernel,
        [wide, wide_b, square, wide_b] + [((2 * part, width), BF16)] * QUAD,
        [dots, wide],
        (t2, *t3, text_head, y_a, p_a, x_a, w_aa, pick_i),
        8,
    )
    image_others = [cuts(image_parts[k], mask=k) for k in range(1, QUAD)]
    gy_a, gy_b, pick_b = call(
        pull_kernel,
        [wide, wide, pick_one],
        [],
        (t2, *t3, x_a, w_aa, w_ab),
        8,
        place,
    )
    i2 = after(i2, gy_a)
    i3 = [loop(rows, mask=1) for rows in jnp.split(i2, 2)]
    blocks = []
    for block, i in enumerate(([i2], i3)):
        blocks += call(
            functools.partial(block_kernel, block),
            [tall_b, block_w, block_w],
            [tall, block_dots, block_dots],
            (*i, image_head, y_a, y_b),
            8,
        )
    *text_parts, dq_own = call(
        last_kernel,
        [((part, width), BF16)] * QUAD + [tall_b],
        [wide, wide, wide_b, wide_b],
        (*blocks, q_a, q_b, gy_a, gy_b, pick_a, pick_b),
        14,
    )
    text_sum = add(text_parts[0], [cuts(text_parts[k], mask=k) for k in range(1, QUAD)])
    image_others = [after(other, dq_own) for other in image_others]
    image_sum = add(image_parts[0], image_others)
    image_sum = add(image_sum[:part], [loop(image_sum[part:], mask=2)])
    image_out = finish(image_sum)
    text_out = finish(text_sum)
    grads = [
        call(grad_kernel, [tall], [], (back, head), 4, macs=macs, keep=False)[0]
        for back, head in ((after(dp_a, dq_own), image_head), (dq_own, text_head))
    ]
    return (*grads, image_out, text_out)


def solution(mesh):
    n_loop, n_cuts = mesh.shape["loop"], mesh.shape["cuts"]
    if n_loop == 4 and n_cuts == 2 * QUAD:
        body = functools.partial(per_device, n_loop, n_cuts)
    else:
        body = plain_device
    placed = (P(("cuts", "loop"), None), P(("cuts", "loop"), None), P(), P())
    return jax.shard_map(
        body,
        mesh=mesh,
        in_specs=placed,
        out_specs=(
            P(("cuts", "loop"), None),
            P(("cuts", "loop"), None),
            P("loop", None),
            P("loop", None),
        ),
        check_vma=False,
    )
```

```python
import functools

import jax
import jax.numpy as jnp
from jax import lax
from jax.experimental import pallas as pl
from jax.experimental.pallas import tpu as pltpu
from jax.sharding import PartitionSpec as P

SCORE_SCALE = 10.0
SCORE_BIAS = -2.5
EPSILON = 1e-06
QUAD = 4
STRIP = 16
F32 = jnp.float32
BF16 = jnp.bfloat16


def normalize(features, weight_matrix):
    projected = jnp.dot(features, weight_matrix, preferred_element_type=jnp.float32)
    factor = lax.rsqrt(jnp.sum(projected * projected, axis=-1, keepdims=True) + EPSILON)
    return (projected * factor, factor)


def pair_weights(image_vectors, text_vectors, image_offset):
    pair_scores = SCORE_SCALE * dot_nt(image_vectors, text_vectors) + SCORE_BIAS
    row_ids = image_offset + lax.broadcasted_iota(jnp.int32, pair_scores.shape, 0)
    col_ids = lax.broadcasted_iota(jnp.int32, pair_scores.shape, 1)
    match_targets = jnp.where(row_ids == col_ids, 1.0, -1.0).astype(jnp.float32)
    return (SCORE_SCALE * -match_targets * jax.nn.sigmoid(-match_targets * pair_scores)).astype(
        jnp.bfloat16
    )


def norm_back(unit, factor, gradient):
    return (factor * (gradient - unit * jnp.sum(unit * gradient, axis=-1, keepdims=True))).astype(
        jnp.bfloat16
    )


def dot_nn(left, right):
    return lax.dot_general(left, right, (((1,), (0,)), ((), ())), preferred_element_type=F32)


def dot_nt(left, right):
    return lax.dot_general(left, right, (((1,), (1,)), ((), ())), preferred_element_type=F32)


def dot_tn(left, right):
    return lax.dot_general(left, right, (((0,), (0,)), ((), ())), preferred_element_type=F32)


def plain_device(image_features, text_features, image_head, text_head):
    row_count = image_features.shape[0]
    own_start = lax.axis_index("loop") * row_count
    image_unit, image_factor = normalize(image_features, image_head)
    text_unit, text_factor = normalize(text_features, text_head)
    image_vectors = image_unit.astype(jnp.bfloat16)
    text_vectors = text_unit.astype(jnp.bfloat16)
    arrived = lax.all_gather(text_vectors, "loop", axis=0, tiled=True)
    weights = pair_weights(image_vectors, arrived, own_start)
    summed = jnp.dot(weights, arrived, preferred_element_type=jnp.float32)
    text_attraction = lax.psum_scatter(
        dot_tn(weights, image_vectors).astype(jnp.bfloat16), "loop", scatter_dimension=0, tiled=True
    ).astype(jnp.float32)
    image_back = norm_back(image_unit, image_factor, summed)
    text_back = norm_back(text_unit, text_factor, text_attraction)
    heads = []
    for features, back in ((image_features, image_back), (text_features, text_back)):
        term = dot_tn(features, back).astype(jnp.bfloat16)
        part = lax.psum_scatter(term, "loop", scatter_dimension=0, tiled=True)
        heads.append(lax.psum(part, "cuts").astype(jnp.float32))
    return (dot_nt(image_back, image_head), dot_nt(text_back, text_head), heads[0], heads[1])


def factor_of(p):
    return lax.rsqrt(jnp.sum(p * p, axis=-1, keepdims=True) + EPSILON)


def unit_rows(projected_ref, vectors_ref):
    for first in range(0, projected_ref.shape[0], STRIP):
        p = projected_ref[first : first + STRIP, :]
        vectors_ref[first : first + STRIP, :] = (p * factor_of(p)).astype(BF16)


def back_rows(projected_ref, gradient_ref, back_ref):
    for first in range(0, projected_ref.shape[0], STRIP):
        p = projected_ref[first : first + STRIP, :]
        g = gradient_ref[first : first + STRIP, :]
        factor = factor_of(p)
        along = factor * factor * factor * jnp.sum(p * g, axis=-1, keepdims=True)
        back_ref[first : first + STRIP, :] = (factor * g - along * p).astype(BF16)


def weights_of(dots, pairs_from=None):
    score = SCORE_SCALE * dots + SCORE_BIAS
    if pairs_from is None:
        return (SCORE_SCALE * jax.nn.sigmoid(score)).astype(BF16)
    row = pairs_from + lax.broadcasted_iota(jnp.int32, dots.shape, 0)
    same = row == lax.broadcasted_iota(jnp.int32, dots.shape, 1)
    value = jax.nn.sigmoid(jnp.where(same, -score, score))
    return (jnp.where(same, -SCORE_SCALE, SCORE_SCALE) * value).astype(BF16)


def weight_rows(dots_ref, weights_ref, pairs_from=None):
    for first in range(0, dots_ref.shape[0], STRIP):
        pairs = None if pairs_from is None else pairs_from + first
        weights_ref[first : first + STRIP, :] = weights_of(dots_ref[first : first + STRIP, :], pairs)


def one_hot(first, rows, width):
    wanted = first + lax.broadcasted_iota(jnp.int32, (rows, width), 0)
    column = lax.broadcasted_iota(jnp.int32, (rows, width), 1)
    return jnp.where(wanted == column, 1.0, 0.0)


def picker(place_ref, rows, width, sides):
    part = rows // QUAD
    pieces = []
    for k in range(QUAD):
        for side in sides:
            first = (place_ref[0] ^ side) * rows + (place_ref[1] ^ k) * part
            pieces.append(one_hot(first, part, width))
    return jnp.concatenate(pieces, axis=0).astype(BF16)


def split_head(head, outs):
    part = head.shape[0] // QUAD
    for k, out in enumerate(outs):
        out[...] = head[k * part : (k + 1) * part, :].astype(BF16)


def near_kernel(
    place, t0, t1, i0, i1, text_head, image_head, q_a, y_a, p_a, x_a, w_aa, pick_i, pick_t, dots
):
    half = t0.shape[0]
    q_a[:half, :] = dot_nn(t0[...], text_head[...])
    q_a[half:, :] = dot_nn(t1[...], text_head[...])
    unit_rows(q_a, y_a)
    p_a[:half, :] = dot_nn(i0[...], image_head[...])
    p_a[half:, :] = dot_nn(i1[...], image_head[...])
    unit_rows(p_a, x_a)
    dots[...] = dot_nt(x_a[...], y_a[...])
    weight_rows(dots, w_aa, 0)
    rows = pick_t.shape[0]
    pick = picker(place, rows, t0.shape[1], (0,))
    pick_t[:, :half] = dot_nt(pick, t0[...]).astype(BF16)
    pick_t[:, half:] = dot_nt(pick, t1[...]).astype(BF16)
    pick = picker(place, rows, t0.shape[1], (0, 2))
    pick_i[:, :half] = dot_nt(pick, i0[...]).astype(BF16)
    pick_i[:, half:] = dot_nt(pick, i1[...]).astype(BF16)


def image_kernel(t2, *refs):
    *far, text_head, y_a, p_a, x_a, w_aa, pick_i, q_b, y_b, w_ab, dp_a, h0, h1, h2, h3, dots, gx = refs
    half = t2.shape[0]
    q_b[:half, :] = dot_nn(t2[...], text_head[...])
    q_b[half:, :] = dot_nn(jnp.concatenate([t[...] for t in far], axis=0), text_head[...])
    unit_rows(q_b, y_b)
    dots[...] = dot_nt(x_a[...], y_b[...])
    weight_rows(dots, w_ab)
    gx[...] = dot_nn(w_aa[...], y_a[...]) + dot_nn(w_ab[...], y_b[...])
    back_rows(p_a, gx, dp_a)
    split_head(dot_nn(pick_i[...], dp_a[...]), (h0, h1, h2, h3))


def pull_kernel(place, t2, *refs):
    *far, x_a, w_aa, w_ab, gy_a, gy_b, pick_t = refs
    half = t2.shape[0]
    gy_a[...] = dot_tn(w_aa[...], x_a[...])
    gy_b[...] = dot_tn(w_ab[...], x_a[...])
    pick = picker(place, pick_t.shape[0], t2.shape[1], (0,))
    pick_t[:, :half] = dot_nt(pick, t2[...]).astype(BF16)
    far = jnp.concatenate([t[...] for t in far], axis=0)
    pick_t[:, half:] = dot_nt(pick, far).astype(BF16)


def block_kernel(block, *refs):
    *features, image_head, y_a, y_b, x_b, w_ba, w_bb, p_b, d_a, d_b = refs
    features = jnp.concatenate([i[...] for i in features], axis=0)
    p_b[...] = dot_nn(features, image_head[...])
    unit_rows(p_b, x_b)
    d_a[...] = dot_nt(x_b[...], y_a[...])
    d_b[...] = dot_nt(x_b[...], y_b[...])
    weight_rows(d_a, w_ba)
    weight_rows(d_b, w_bb, block * x_b.shape[0])


def last_kernel(
    x_2, w_2a, w_2b, x_3, w_3a, w_3b, q_a, q_b, gy_a_in, gy_b_in, pick_a, pick_b,
    h0, h1, h2, h3, dq_own, gy_a, gy_b, dq_a, dq_b,
):
    half = x_2.shape[0]
    gy_a[...] = gy_a_in[...] + dot_tn(w_2a[...], x_2[...]) + dot_tn(w_3a[...], x_3[...])
    gy_b[...] = gy_b_in[...] + dot_tn(w_2b[...], x_2[...]) + dot_tn(w_3b[...], x_3[...])
    back_rows(q_a, gy_a, dq_a)
    back_rows(q_b, gy_b, dq_b)
    dq_own[...] = dq_a[:half, :]
    split_head(dot_nn(pick_a[...], dq_a[...]) + dot_nn(pick_b[...], dq_b[...]), (h0, h1, h2, h3))


def grad_kernel(back, head, out):
    out[...] = dot_nt(back[: out.shape[0], :], head[...])


def place_kernel(place, h0, h1, h2, h3, out):
    part = h0.shape[0]
    for k, piece in enumerate((h0, h1, h2, h3)):
        first = pl.multiple_of((place[1] ^ k) * part, part)
        out[pl.ds(first, part), :] = piece[...].astype(F32)


def call(kernel, outs, scratch, args, mib, place=None, macs=0, keep=True):
    args = [pltpu.with_memory_space_constraint(a, pltpu.VMEM) for a in args]
    specs = [pl.BlockSpec(memory_space=pltpu.VMEM)] * len(args)
    if place is not None:
        args, specs = [place, *args], [pl.BlockSpec(memory_space=pltpu.SMEM), *specs]
    shape = pltpu.VMEM if keep else jax.ShapeDtypeStruct
    return pl.pallas_call(
        kernel,
        out_shape=[shape(s, t) for s, t in outs],
        in_specs=specs,
        out_specs=[pl.BlockSpec(memory_space=pltpu.VMEM)] * len(outs),
        scratch_shapes=[pltpu.VMEM(s, t) for s, t in scratch],
        compiler_params=pltpu.CompilerParams(vmem_limit_bytes=mib * 1024 * 1024),
        cost_estimate=pl.CostEstimate(flops=2 * macs, bytes_accessed=0, transcendentals=0),
    )(*args)


def swap(array, axis, size, mask):
    return lax.ppermute(array, axis, [(i, i ^ mask) for i in range(size)])


def after(value, other):
    return lax.optimization_barrier((value, other))[0]


def per_device(n_loop, n_cuts, image_features, text_features, image_head, text_head):
    half, width = image_features.shape
    near = 2 * half
    rows_out = width // n_loop
    part = rows_out // QUAD
    loop = functools.partial(swap, axis="loop", size=n_loop)
    cuts = functools.partial(swap, axis="cuts", size=n_cuts)
    macs = half * width * width

    def add(own, others):
        return sum((other.astype(F32) for other in others), own.astype(F32)).astype(BF16)

    def spread(total):
        return [total] + [cuts(total, mask=k) for k in range(1, QUAD)]

    def placed(pieces):
        outs = [((rows_out, width), F32)]
        return call(place_kernel, outs, [], pieces, 4, place, keep=False)[0]

    t2 = loop(text_features, mask=2)
    i2 = [loop(rows, mask=2) for rows in jnp.split(image_features, 2)]
    place = jnp.stack([lax.axis_index("loop"), lax.axis_index("cuts") & (QUAD - 1)])
    place = place.astype(jnp.int32)
    t0, i0, place = lax.optimization_barrier((text_features, image_features, place))
    t1 = loop(t0, mask=1)
    i1 = loop(i0, mask=1)
    wide, wide_b = ((near, width), F32), ((near, width), BF16)
    tall, tall_b = ((half, width), F32), ((half, width), BF16)
    square, dots = ((near, near), BF16), ((near, near), F32)
    block_w, block_dots = ((half, near), BF16), ((half, near), F32)
    pick_one, pick_two = ((rows_out, near), BF16), ((2 * rows_out, near), BF16)
    q_a, y_a, p_a, x_a, w_aa, pick_i, pick_a = call(
        near_kernel,
        [wide, wide_b, wide, wide_b, square, pick_two, pick_one],
        [dots],
        (t0, t1, i0, i1, text_head, image_head),
        8,
        place,
    )
    t2 = after(t2, w_aa)
    t3 = [loop(rows, mask=1) for rows in jnp.split(t2, 8)]
    q_b, y_b, w_ab, dp_a, *image_parts = call(
        image_kernel,
        [wide, wide_b, square, wide_b] + [((2 * part, width), BF16)] * QUAD,
        [dots, wide],
        (t2, *t3, text_head, y_a, p_a, x_a, w_aa, pick_i),
        8,
    )
    image_others = [cuts(image_parts[k], mask=k) for k in range(1, QUAD)]
    gy_a, gy_b, pick_b = call(
        pull_kernel,
        [wide, wide, pick_one],
        [],
        (t2, *t3, x_a, w_aa, w_ab),
        8,
        place,
    )
    i2 = [after(rows, gy_a) for rows in i2]
    i3 = [loop(rows, mask=1) for rows in i2]
    blocks = []
    for block, i in enumerate((i2, i3)):
        blocks += call(
            functools.partial(block_kernel, block),
            [tall_b, block_w, block_w],
            [tall, block_dots, block_dots],
            (*i, image_head, y_a, y_b),
            8,
        )
    *text_parts, dq_own = call(
        last_kernel,
        [((part, width), BF16)] * QUAD + [tall_b],
        [wide, wide, wide_b, wide_b],
        (*blocks, q_a, q_b, gy_a, gy_b, pick_a, pick_b),
        14,
    )
    text_others = [cuts(text_parts[k], mask=k) for k in range(1, QUAD)]
    image_others = [after(other, dq_own) for other in image_others]
    image_sum = add(image_parts[0], image_others)
    image_sum = add(image_sum[:part], [loop(image_sum[part:], mask=2)])
    image_sum = add(image_sum, [cuts(image_sum, mask=QUAD)])
    image_pieces = spread(image_sum)
    text_sum = add(text_parts[0], [after(other, image_sum) for other in text_others])
    text_sum = add(text_sum, [after(cuts(text_sum, mask=QUAD), image_pieces[-1])])
    image_out = placed(image_pieces)
    text_out = placed(spread(text_sum))
    grads = [
        call(grad_kernel, [tall], [], (back, head), 4, macs=macs, keep=False)[0]
        for back, head in ((after(dp_a, dq_own), image_head), (dq_own, text_head))
    ]
    return (*grads, image_out, text_out)


def solution(mesh):
    n_loop, n_cuts = mesh.shape["loop"], mesh.shape["cuts"]
    if n_loop == 4 and n_cuts == 2 * QUAD:
        body = functools.partial(per_device, n_loop, n_cuts)
    else:
        body = plain_device
    placed = (P(("cuts", "loop"), None), P(("cuts", "loop"), None), P(), P())
    return jax.shard_map(
        body,
        mesh=mesh,
        in_specs=placed,
        out_specs=(
            P(("cuts", "loop"), None),
            P(("cuts", "loop"), None),
            P("loop", None),
            P("loop", None),
        ),
        check_vma=False,
    )
```

```python
import functools

import jax
import jax.numpy as jnp
from jax import lax
from jax.experimental import pallas as pl
from jax.experimental.pallas import tpu as pltpu
from jax.sharding import PartitionSpec as P

SCORE_SCALE = 10.0
SCORE_BIAS = -2.5
EPSILON = 1e-06
QUAD = 4
STRIP = 16
F32 = jnp.float32
BF16 = jnp.bfloat16


def normalize(features, weight_matrix):
    projected = jnp.dot(features, weight_matrix, preferred_element_type=jnp.float32)
    factor = lax.rsqrt(jnp.sum(projected * projected, axis=-1, keepdims=True) + EPSILON)
    return (projected * factor, factor)


def pair_weights(image_vectors, text_vectors, image_offset):
    pair_scores = SCORE_SCALE * dot_nt(image_vectors, text_vectors) + SCORE_BIAS
    row_ids = image_offset + lax.broadcasted_iota(jnp.int32, pair_scores.shape, 0)
    col_ids = lax.broadcasted_iota(jnp.int32, pair_scores.shape, 1)
    match_targets = jnp.where(row_ids == col_ids, 1.0, -1.0).astype(jnp.float32)
    return (SCORE_SCALE * -match_targets * jax.nn.sigmoid(-match_targets * pair_scores)).astype(
        jnp.bfloat16
    )


def norm_back(unit, factor, gradient):
    return (factor * (gradient - unit * jnp.sum(unit * gradient, axis=-1, keepdims=True))).astype(
        jnp.bfloat16
    )


def dot_nn(left, right):
    return lax.dot_general(left, right, (((1,), (0,)), ((), ())), preferred_element_type=F32)


def dot_nt(left, right):
    return lax.dot_general(left, right, (((1,), (1,)), ((), ())), preferred_element_type=F32)


def dot_tn(left, right):
    return lax.dot_general(left, right, (((0,), (0,)), ((), ())), preferred_element_type=F32)


def plain_device(image_features, text_features, image_head, text_head):
    row_count = image_features.shape[0]
    own_start = lax.axis_index("loop") * row_count
    image_unit, image_factor = normalize(image_features, image_head)
    text_unit, text_factor = normalize(text_features, text_head)
    image_vectors = image_unit.astype(jnp.bfloat16)
    text_vectors = text_unit.astype(jnp.bfloat16)
    arrived = lax.all_gather(text_vectors, "loop", axis=0, tiled=True)
    weights = pair_weights(image_vectors, arrived, own_start)
    summed = jnp.dot(weights, arrived, preferred_element_type=jnp.float32)
    text_attraction = lax.psum_scatter(
        dot_tn(weights, image_vectors).astype(jnp.bfloat16), "loop", scatter_dimension=0, tiled=True
    ).astype(jnp.float32)
    image_back = norm_back(image_unit, image_factor, summed)
    text_back = norm_back(text_unit, text_factor, text_attraction)
    heads = []
    for features, back in ((image_features, image_back), (text_features, text_back)):
        term = dot_tn(features, back).astype(jnp.bfloat16)
        part = lax.psum_scatter(term, "loop", scatter_dimension=0, tiled=True)
        heads.append(lax.psum(part, "cuts").astype(jnp.float32))
    return (dot_nt(image_back, image_head), dot_nt(text_back, text_head), heads[0], heads[1])


def factor_of(p):
    return lax.rsqrt(jnp.sum(p * p, axis=-1, keepdims=True) + EPSILON)


def unit_rows(projected_ref, vectors_ref):
    for first in range(0, projected_ref.shape[0], STRIP):
        p = projected_ref[first : first + STRIP, :]
        vectors_ref[first : first + STRIP, :] = (p * factor_of(p)).astype(BF16)


def back_rows(projected_ref, gradient_ref, back_ref, at=0):
    for first in range(0, projected_ref.shape[0], STRIP):
        p = projected_ref[first : first + STRIP, :]
        g = gradient_ref[at + first : at + first + STRIP, :]
        factor = factor_of(p)
        along = factor * factor * factor * jnp.sum(p * g, axis=-1, keepdims=True)
        back_ref[at + first : at + first + STRIP, :] = (factor * g - along * p).astype(BF16)


def weights_of(dots, pairs_from=None):
    score = SCORE_SCALE * dots + SCORE_BIAS
    if pairs_from is None:
        return (SCORE_SCALE * jax.nn.sigmoid(score)).astype(BF16)
    row = pairs_from + lax.broadcasted_iota(jnp.int32, dots.shape, 0)
    same = row == lax.broadcasted_iota(jnp.int32, dots.shape, 1)
    value = jax.nn.sigmoid(jnp.where(same, -score, score))
    return (jnp.where(same, -SCORE_SCALE, SCORE_SCALE) * value).astype(BF16)


def weight_rows(dots_ref, weights_ref, pairs_from=None):
    for first in range(0, dots_ref.shape[0], STRIP):
        pairs = None if pairs_from is None else pairs_from + first
        weights_ref[first : first + STRIP, :] = weights_of(dots_ref[first : first + STRIP, :], pairs)


def one_hot(first, rows, width):
    wanted = first + lax.broadcasted_iota(jnp.int32, (rows, width), 0)
    column = lax.broadcasted_iota(jnp.int32, (rows, width), 1)
    return jnp.where(wanted == column, 1.0, 0.0)


def picker(place_ref, rows, width, sides):
    part = rows // QUAD
    pieces = []
    for k in range(QUAD):
        for side in sides:
            first = (place_ref[0] ^ side) * rows + (place_ref[1] ^ k) * part
            pieces.append(one_hot(first, part, width))
    return jnp.concatenate(pieces, axis=0).astype(BF16)


def split_head(head, outs):
    part = head.shape[0] // QUAD
    for k, out in enumerate(outs):
        out[...] = head[k * part : (k + 1) * part, :].astype(BF16)


def near_kernel(
    place, t1, i1, t0_far, i0_far, text_head_far, image_head_far,
    q_a, y_a, p_a, x_a, w_aa, gy_a, pick_i, pick_t, dots, t0, i0, text_head, image_head, sems,
):
    half = t0.shape[0]
    copies = [
        pltpu.make_async_copy(source, target, sems.at[n])
        for n, (source, target) in enumerate(
            ((t0_far, t0), (text_head_far, text_head), (i0_far, i0), (image_head_far, image_head))
        )
    ]
    for copy in copies:
        copy.start()
    copies[0].wait()
    copies[1].wait()
    q_a[:half, :] = dot_nn(t0[...], text_head[...])
    q_a[half:, :] = dot_nn(t1[...], text_head[...])
    unit_rows(q_a, y_a)
    copies[2].wait()
    copies[3].wait()
    p_a[:half, :] = dot_nn(i0[...], image_head[...])
    p_a[half:, :] = dot_nn(i1[...], image_head[...])
    unit_rows(p_a, x_a)
    dots[...] = dot_nt(x_a[...], y_a[...])
    weight_rows(dots, w_aa, 0)
    rows = pick_t.shape[0]
    pick = picker(place, rows, t0.shape[1], (0,))
    pick_t[:, :half] = dot_nt(pick, t0[...]).astype(BF16)
    pick_t[:, half:] = dot_nt(pick, t1[...]).astype(BF16)
    pick = picker(place, rows, t0.shape[1], (0, 2))
    pick_i[:, :half] = dot_nt(pick, i0[...]).astype(BF16)
    pick_i[:, half:] = dot_nt(pick, i1[...]).astype(BF16)
    gy_a[...] = dot_tn(w_aa[...], x_a[...])


def text_kernel(t2, text_head, y_a, x_a, w_aa, q_2, y_2, w_a2, gx, dots):
    q_2[...] = dot_nn(t2[...], text_head[...])
    unit_rows(q_2, y_2)
    dots[...] = dot_nt(x_a[...], y_2[...])
    weight_rows(dots, w_a2)
    gx[...] = dot_nn(w_aa[...], y_a[...]) + dot_nn(w_a2[...], y_2[...])


def image_kernel(*refs):
    *features, text_head, p_a, x_a, gx_in, pick_i, q_3, y_3, w_a3, dp_a, h0, h1, h2, h3, dots, gx = refs
    t3 = jnp.concatenate([t[...] for t in features], axis=0)
    q_3[...] = dot_nn(t3, text_head[...])
    unit_rows(q_3, y_3)
    dots[...] = dot_nt(x_a[...], y_3[...])
    weight_rows(dots, w_a3)
    gx[...] = gx_in[...] + dot_nn(w_a3[...], y_3[...])
    back_rows(p_a, gx, dp_a)
    split_head(dot_nn(pick_i[...], dp_a[...]), (h0, h1, h2, h3))


def pull_kernel(place, t2, *refs):
    *features, x_a, w_a2, w_a3, gy_2, gy_3, pick_t = refs
    half = t2.shape[0]
    gy_2[...] = dot_tn(w_a2[...], x_a[...])
    gy_3[...] = dot_tn(w_a3[...], x_a[...])
    pick = picker(place, pick_t.shape[0], t2.shape[1], (0,))
    pick_t[:, :half] = dot_nt(pick, t2[...]).astype(BF16)
    t3 = jnp.concatenate([t[...] for t in features], axis=0)
    pick_t[:, half:] = dot_nt(pick, t3).astype(BF16)


def block_kernel(block, *refs):
    *features, image_head, y_a, y_2, y_3, x_b, w_ba, w_bb, p_b, d_a, d_b = refs
    half = x_b.shape[0]
    features = jnp.concatenate([i[...] for i in features], axis=0)
    p_b[...] = dot_nn(features, image_head[...])
    unit_rows(p_b, x_b)
    d_a[...] = dot_nt(x_b[...], y_a[...])
    d_b[:, :half] = dot_nt(x_b[...], y_2[...])
    d_b[:, half:] = dot_nt(x_b[...], y_3[...])
    weight_rows(d_a, w_ba)
    weight_rows(d_b, w_bb, block * half)


def last_kernel(
    x_2, w_2a, w_2b, x_3, w_3a, w_3b, q_a, q_2, q_3, gy_a_in, gy_2, gy_3, pick_a, pick_b,
    h0, h1, h2, h3, dq_own, gy_a, gy_b, dq_a, dq_b,
):
    half = x_2.shape[0]
    gy_a[...] = gy_a_in[...] + dot_tn(w_2a[...], x_2[...]) + dot_tn(w_3a[...], x_3[...])
    back_rows(q_a, gy_a, dq_a)
    gy_b[...] = dot_tn(w_2b[...], x_2[...]) + dot_tn(w_3b[...], x_3[...])
    gy_b[:half, :] += gy_2[...]
    gy_b[half:, :] += gy_3[...]
    back_rows(q_2, gy_b, dq_b, 0)
    back_rows(q_3, gy_b, dq_b, half)
    dq_own[...] = dq_a[:half, :]
    split_head(dot_nn(pick_a[...], dq_a[...]) + dot_nn(pick_b[...], dq_b[...]), (h0, h1, h2, h3))


def grad_kernel(back, head, out):
    out[...] = dot_nt(back[: out.shape[0], :], head[...])


def place_kernel(place, h0, h1, h2, h3, out):
    part = h0.shape[0]
    for k, piece in enumerate((h0, h1, h2, h3)):
        first = pl.multiple_of((place[1] ^ k) * part, part)
        out[pl.ds(first, part), :] = piece[...].astype(F32)


def call(kernel, outs, scratch, args, mib, place=None, macs=0, keep=True, far=()):
    args = [pltpu.with_memory_space_constraint(a, pltpu.VMEM) for a in args] + list(far)
    specs = [pl.BlockSpec(memory_space=pltpu.VMEM)] * (len(args) - len(far))
    specs += [pl.BlockSpec(memory_space=pl.ANY)] * len(far)
    if place is not None:
        args, specs = [place, *args], [pl.BlockSpec(memory_space=pltpu.SMEM), *specs]
    shape = pltpu.VMEM if keep else jax.ShapeDtypeStruct
    return pl.pallas_call(
        kernel,
        out_shape=[shape(s, t) for s, t in outs],
        in_specs=specs,
        out_specs=[pl.BlockSpec(memory_space=pltpu.VMEM)] * len(outs),
        scratch_shapes=[pltpu.VMEM(s, t) for s, t in scratch]
        + [pltpu.SemaphoreType.DMA((len(far),))] * bool(far),
        compiler_params=pltpu.CompilerParams(vmem_limit_bytes=mib * 1024 * 1024),
        cost_estimate=pl.CostEstimate(flops=2 * macs, bytes_accessed=0, transcendentals=0),
    )(*args)


def swap(array, axis, size, mask):
    return lax.ppermute(array, axis, [(i, i ^ mask) for i in range(size)])


def after(value, other):
    return lax.optimization_barrier((value, other))[0]


def per_device(n_loop, n_cuts, image_features, text_features, image_head, text_head):
    half, width = image_features.shape
    near = 2 * half
    rows_out = width // n_loop
    part = rows_out // QUAD
    loop = functools.partial(swap, axis="loop", size=n_loop)
    cuts = functools.partial(swap, axis="cuts", size=n_cuts)
    macs = half * width * width

    def add(own, others):
        return sum((other.astype(F32) for other in others), own.astype(F32)).astype(BF16)

    def spread(total):
        return [total] + [cuts(total, mask=k) for k in range(1, QUAD)]

    def placed(pieces):
        outs = [((rows_out, width), F32)]
        return call(place_kernel, outs, [], pieces, 4, place, keep=False)[0]

    t2 = loop(text_features, mask=2)
    i2 = [loop(rows, mask=2) for rows in jnp.split(image_features, 2)]
    place = jnp.stack([lax.axis_index("loop"), lax.axis_index("cuts") & (QUAD - 1)])
    place = place.astype(jnp.int32)
    t0, i0, place = lax.optimization_barrier((text_features, image_features, place))
    t1 = loop(t0, mask=1)
    i1 = loop(i0, mask=1)
    wide, wide_b = ((near, width), F32), ((near, width), BF16)
    tall, tall_b = ((half, width), F32), ((half, width), BF16)
    head_b = ((width, width), BF16)
    block_w, block_dots = ((half, near), BF16), ((half, near), F32)
    side_w, side_dots = ((near, half), BF16), ((near, half), F32)
    pick_one, pick_two = ((rows_out, near), BF16), ((2 * rows_out, near), BF16)
    q_a, y_a, p_a, x_a, w_aa, gy_a, pick_i, pick_a = call(
        near_kernel,
        [wide, wide_b, wide, wide_b, ((near, near), BF16), wide, pick_two, pick_one],
        [((near, near), F32), tall_b, tall_b, head_b, head_b],
        (t1, i1),
        16,
        place,
        far=(t0, i0, text_head, image_head),
    )
    t2 = after(t2, w_aa)
    t3 = [loop(rows, mask=1) for rows in jnp.split(t2, 8)]
    q_2, y_2, w_a2, gx = call(
        text_kernel,
        [tall, tall_b, side_w, wide],
        [side_dots],
        (t2, text_head, y_a, x_a, w_aa),
        8,
    )
    t3 = [after(rows, gx) for rows in t3]
    q_3, y_3, w_a3, dp_a, *image_parts = call(
        image_kernel,
        [tall, tall_b, side_w, wide_b] + [((2 * part, width), BF16)] * QUAD,
        [side_dots, wide],
        (*t3, text_head, p_a, x_a, gx, pick_i),
        8,
    )
    image_others = [cuts(image_parts[k], mask=k) for k in range(1, QUAD)]
    gy_2, gy_3, pick_b = call(
        pull_kernel,
        [tall, tall, pick_one],
        [],
        (t2, *t3, x_a, w_a2, w_a3),
        8,
        place,
    )
    i2 = [after(rows, gy_2) for rows in i2]
    i3 = [loop(rows, mask=1) for rows in i2]
    blocks = []
    for block, i in enumerate((i2, i3)):
        blocks += call(
            functools.partial(block_kernel, block),
            [tall_b, block_w, block_w],
            [tall, block_dots, block_dots],
            (*i, image_head, y_a, y_2, y_3),
            8,
        )
    *text_parts, dq_own = call(
        last_kernel,
        [((part, width), BF16)] * QUAD + [tall_b],
        [wide, wide, wide_b, wide_b],
        (*blocks, q_a, q_2, q_3, gy_a, gy_2, gy_3, pick_a, pick_b),
        14,
    )
    text_others = [cuts(text_parts[k], mask=k) for k in range(1, QUAD)]
    image_others = [after(other, dq_own) for other in image_others]
    image_sum = add(image_parts[0], image_others)
    grads = [
        call(grad_kernel, [tall], [], (after(back, image_sum), head), 4, macs=2 * macs, keep=False)[0]
        for back, head in ((dp_a, image_head), (dq_own, text_head))
    ]
    image_sum = add(image_sum[:part], [after(loop(image_sum[part:], mask=2), grads)])
    text_sum = add(text_parts[0], [after(other, image_sum) for other in text_others])
    image_sum = add(image_sum, [cuts(image_sum, mask=QUAD)])
    image_pieces = spread(image_sum)
    text_sum = after(text_sum, image_sum)
    text_sum = add(text_sum, [after(cuts(text_sum, mask=QUAD), image_pieces[-1])])
    image_out = placed(image_pieces)
    text_out = placed(spread(text_sum))
    return (*grads, image_out, text_out)


def solution(mesh):
    n_loop, n_cuts = mesh.shape["loop"], mesh.shape["cuts"]
    if n_loop == 4 and n_cuts == 2 * QUAD:
        body = functools.partial(per_device, n_loop, n_cuts)
    else:
        body = plain_device
    placed = (P(("cuts", "loop"), None), P(("cuts", "loop"), None), P(), P())
    return jax.shard_map(
        body,
        mesh=mesh,
        in_specs=placed,
        out_specs=(
            P(("cuts", "loop"), None),
            P(("cuts", "loop"), None),
            P("loop", None),
            P("loop", None),
        ),
        check_vma=False,
    )
```

```python
import functools

import jax
import jax.numpy as jnp
from jax import lax
from jax.experimental import pallas as pl
from jax.experimental.pallas import tpu as pltpu
from jax.sharding import PartitionSpec as P

SCORE_SCALE = 10.0
SCORE_BIAS = -2.5
EPSILON = 1e-06
QUAD = 4
STRIP = 16
F32 = jnp.float32
BF16 = jnp.bfloat16


def normalize(features, weight_matrix):
    projected = jnp.dot(features, weight_matrix, preferred_element_type=jnp.float32)
    factor = lax.rsqrt(jnp.sum(projected * projected, axis=-1, keepdims=True) + EPSILON)
    return (projected * factor, factor)


def pair_weights(image_vectors, text_vectors, image_offset):
    pair_scores = SCORE_SCALE * dot_nt(image_vectors, text_vectors) + SCORE_BIAS
    row_ids = image_offset + lax.broadcasted_iota(jnp.int32, pair_scores.shape, 0)
    col_ids = lax.broadcasted_iota(jnp.int32, pair_scores.shape, 1)
    match_targets = jnp.where(row_ids == col_ids, 1.0, -1.0).astype(jnp.float32)
    return (SCORE_SCALE * -match_targets * jax.nn.sigmoid(-match_targets * pair_scores)).astype(
        jnp.bfloat16
    )


def norm_back(unit, factor, gradient):
    return (factor * (gradient - unit * jnp.sum(unit * gradient, axis=-1, keepdims=True))).astype(
        jnp.bfloat16
    )


def dot_nn(left, right):
    return lax.dot_general(left, right, (((1,), (0,)), ((), ())), preferred_element_type=F32)


def dot_nt(left, right):
    return lax.dot_general(left, right, (((1,), (1,)), ((), ())), preferred_element_type=F32)


def dot_tn(left, right):
    return lax.dot_general(left, right, (((0,), (0,)), ((), ())), preferred_element_type=F32)


def plain_device(image_features, text_features, image_head, text_head):
    row_count = image_features.shape[0]
    own_start = lax.axis_index("loop") * row_count
    image_unit, image_factor = normalize(image_features, image_head)
    text_unit, text_factor = normalize(text_features, text_head)
    image_vectors = image_unit.astype(jnp.bfloat16)
    text_vectors = text_unit.astype(jnp.bfloat16)
    arrived = lax.all_gather(text_vectors, "loop", axis=0, tiled=True)
    weights = pair_weights(image_vectors, arrived, own_start)
    summed = jnp.dot(weights, arrived, preferred_element_type=jnp.float32)
    text_attraction = lax.psum_scatter(
        dot_tn(weights, image_vectors).astype(jnp.bfloat16), "loop", scatter_dimension=0, tiled=True
    ).astype(jnp.float32)
    image_back = norm_back(image_unit, image_factor, summed)
    text_back = norm_back(text_unit, text_factor, text_attraction)
    heads = []
    for features, back in ((image_features, image_back), (text_features, text_back)):
        term = dot_tn(features, back).astype(jnp.bfloat16)
        part = lax.psum_scatter(term, "loop", scatter_dimension=0, tiled=True)
        heads.append(lax.psum(part, "cuts").astype(jnp.float32))
    return (dot_nt(image_back, image_head), dot_nt(text_back, text_head), heads[0], heads[1])


def factor_of(p):
    return lax.rsqrt(jnp.sum(p * p, axis=-1, keepdims=True) + EPSILON)


def unit_rows(projected_ref, vectors_ref):
    for first in range(0, projected_ref.shape[0], STRIP):
        p = projected_ref[first : first + STRIP, :]
        vectors_ref[first : first + STRIP, :] = (p * factor_of(p)).astype(BF16)


def back_rows(projected_ref, gradient_ref, back_ref, at=0):
    for first in range(0, projected_ref.shape[0], STRIP):
        p = projected_ref[first : first + STRIP, :]
        g = gradient_ref[at + first : at + first + STRIP, :]
        factor = factor_of(p)
        along = factor * factor * factor * jnp.sum(p * g, axis=-1, keepdims=True)
        back_ref[at + first : at + first + STRIP, :] = (factor * g - along * p).astype(BF16)


def weights_of(dots, pairs_from=None):
    score = SCORE_SCALE * dots + SCORE_BIAS
    if pairs_from is None:
        return (SCORE_SCALE * jax.nn.sigmoid(score)).astype(BF16)
    row = pairs_from + lax.broadcasted_iota(jnp.int32, dots.shape, 0)
    same = row == lax.broadcasted_iota(jnp.int32, dots.shape, 1)
    value = jax.nn.sigmoid(jnp.where(same, -score, score))
    return (jnp.where(same, -SCORE_SCALE, SCORE_SCALE) * value).astype(BF16)


def weight_rows(dots_ref, weights_ref, pairs_from=None):
    for first in range(0, dots_ref.shape[0], STRIP):
        pairs = None if pairs_from is None else pairs_from + first
        weights_ref[first : first + STRIP, :] = weights_of(dots_ref[first : first + STRIP, :], pairs)


def one_hot(first, rows, width):
    wanted = first + lax.broadcasted_iota(jnp.int32, (rows, width), 0)
    column = lax.broadcasted_iota(jnp.int32, (rows, width), 1)
    return jnp.where(wanted == column, 1.0, 0.0)


def picker(place_ref, rows, width, sides):
    part = rows // QUAD
    pieces = []
    for k in range(QUAD):
        for side in sides:
            first = (place_ref[0] ^ side) * rows + (place_ref[1] ^ k) * part
            pieces.append(one_hot(first, part, width))
    return jnp.concatenate(pieces, axis=0).astype(BF16)


def split_head(head, outs):
    part = head.shape[0] // QUAD
    for k, out in enumerate(outs):
        out[...] = head[k * part : (k + 1) * part, :].astype(BF16)


def near_kernel(
    t1, i1, t0_far, i0_far, text_head_far, image_head_far,
    q_a, y_a, p_a, x_a, w_aa, t0, i0, text_head, image_head, dots, sems,
):
    half = t0.shape[0]
    copies = [
        pltpu.make_async_copy(source, target, sems.at[n])
        for n, (source, target) in enumerate(
            ((t0_far, t0), (text_head_far, text_head), (i0_far, i0), (image_head_far, image_head))
        )
    ]
    for copy in copies:
        copy.start()
    copies[0].wait()
    copies[1].wait()
    q_a[:half, :] = dot_nn(t0[...], text_head[...])
    q_a[half:, :] = dot_nn(t1[...], text_head[...])
    unit_rows(q_a, y_a)
    copies[2].wait()
    copies[3].wait()
    p_a[:half, :] = dot_nn(i0[...], image_head[...])
    p_a[half:, :] = dot_nn(i1[...], image_head[...])
    unit_rows(p_a, x_a)
    dots[...] = dot_nt(x_a[...], y_a[...])
    weight_rows(dots, w_aa, 0)


def near_pull_kernel(place, t0, t1, i0, i1, x_a, w_aa, gy_a, pick_i, pick_t):
    half = t0.shape[0]
    rows = pick_t.shape[0]
    pick = picker(place, rows, t0.shape[1], (0, 2))
    pick_i[:, :half] = dot_nt(pick, i0[...]).astype(BF16)
    pick_i[:, half:] = dot_nt(pick, i1[...]).astype(BF16)
    pick = picker(place, rows, t0.shape[1], (0,))
    pick_t[:, :half] = dot_nt(pick, t0[...]).astype(BF16)
    pick_t[:, half:] = dot_nt(pick, t1[...]).astype(BF16)
    gy_a[...] = dot_tn(w_aa[...], x_a[...])


def rows_of(refs):
    return jnp.concatenate([ref[...] for ref in refs], axis=0)


def text_kernel(*refs):
    *features, text_head, y_a, x_a, w_aa, q_2, y_2, w_a2, gx, dots = refs
    q_2[...] = dot_nn(rows_of(features), text_head[...])
    unit_rows(q_2, y_2)
    dots[...] = dot_nt(x_a[...], y_2[...])
    weight_rows(dots, w_a2)
    gx[...] = dot_nn(w_aa[...], y_a[...]) + dot_nn(w_a2[...], y_2[...])


def image_kernel(*refs):
    *features, text_head, p_a, x_a, gx_in, pick_i, q_3, y_3, w_a3, dp_a, h0, h1, h2, h3, dots, gx = refs
    q_3[...] = dot_nn(rows_of(features), text_head[...])
    unit_rows(q_3, y_3)
    dots[...] = dot_nt(x_a[...], y_3[...])
    weight_rows(dots, w_a3)
    gx[...] = gx_in[...] + dot_nn(w_a3[...], y_3[...])
    back_rows(p_a, gx, dp_a)
    split_head(dot_nn(pick_i[...], dp_a[...]), (h0, h1, h2, h3))


def pull_kernel(place, *refs):
    *features, x_a, w_a2, w_a3, gy_2, gy_3, pick_t = refs
    gy_2[...] = dot_tn(w_a2[...], x_a[...])
    gy_3[...] = dot_tn(w_a3[...], x_a[...])
    pick = picker(place, pick_t.shape[0], x_a.shape[1], (0,))
    pick_t[...] = dot_nt(pick, rows_of(features)).astype(BF16)


def block_kernel(block, *refs):
    *features, image_head, y_a, y_2, y_3, x_b, w_ba, w_bb, p_b, d_a, d_b = refs
    half = x_b.shape[0]
    p_b[...] = dot_nn(rows_of(features), image_head[...])
    unit_rows(p_b, x_b)
    d_a[...] = dot_nt(x_b[...], y_a[...])
    d_b[:, :half] = dot_nt(x_b[...], y_2[...])
    d_b[:, half:] = dot_nt(x_b[...], y_3[...])
    weight_rows(d_a, w_ba)
    weight_rows(d_b, w_bb, block * half)


def last_kernel(
    x_2, w_2a, w_2b, x_3, w_3a, w_3b, q_a, q_2, q_3, gy_a_in, gy_2, gy_3, pick_a, pick_b,
    h0, h1, h2, h3, dq_own, gy_a, gy_b, dq_a, dq_b,
):
    half = x_2.shape[0]
    gy_a[...] = gy_a_in[...] + dot_tn(w_2a[...], x_2[...]) + dot_tn(w_3a[...], x_3[...])
    back_rows(q_a, gy_a, dq_a)
    gy_b[...] = dot_tn(w_2b[...], x_2[...]) + dot_tn(w_3b[...], x_3[...])
    gy_b[:half, :] += gy_2[...]
    gy_b[half:, :] += gy_3[...]
    back_rows(q_2, gy_b, dq_b, 0)
    back_rows(q_3, gy_b, dq_b, half)
    dq_own[...] = dq_a[:half, :]
    split_head(dot_nn(pick_a[...], dq_a[...]) + dot_nn(pick_b[...], dq_b[...]), (h0, h1, h2, h3))


def grad_kernel(back, head, out):
    out[...] = dot_nt(back[: out.shape[0], :], head[...])


def place_kernel(place, h0, h1, h2, h3, out):
    part = h0.shape[0]
    for k, piece in enumerate((h0, h1, h2, h3)):
        first = pl.multiple_of((place[1] ^ k) * part, part)
        out[pl.ds(first, part), :] = piece[...].astype(F32)


def call(kernel, outs, scratch, args, mib, place=None, macs=0, keep=True, far=()):
    far = [pltpu.with_memory_space_constraint(a, pltpu.HBM) for a in far]
    args = [pltpu.with_memory_space_constraint(a, pltpu.VMEM) for a in args] + far
    specs = [pl.BlockSpec(memory_space=pltpu.VMEM)] * (len(args) - len(far))
    specs += [pl.BlockSpec(memory_space=pltpu.HBM)] * len(far)
    if place is not None:
        args, specs = [place, *args], [pl.BlockSpec(memory_space=pltpu.SMEM), *specs]
    shape = pltpu.VMEM if keep else jax.ShapeDtypeStruct
    return pl.pallas_call(
        kernel,
        out_shape=[shape(s, t) for s, t in outs],
        in_specs=specs,
        out_specs=[pl.BlockSpec(memory_space=pltpu.VMEM)] * len(outs),
        scratch_shapes=[pltpu.VMEM(s, t) for s, t in scratch]
        + [pltpu.SemaphoreType.DMA((len(far),))] * bool(far),
        compiler_params=pltpu.CompilerParams(vmem_limit_bytes=mib * 1024 * 1024),
        cost_estimate=pl.CostEstimate(flops=2 * macs, bytes_accessed=0, transcendentals=0),
    )(*args)


def swap(array, axis, size, mask):
    return lax.ppermute(array, axis, [(i, i ^ mask) for i in range(size)])


def after(value, other):
    return lax.optimization_barrier((value, other))[0]


def per_device(n_loop, n_cuts, image_features, text_features, image_head, text_head):
    half, width = image_features.shape
    near = 2 * half
    rows_out = width // n_loop
    part = rows_out // QUAD
    loop = functools.partial(swap, axis="loop", size=n_loop)
    cuts = functools.partial(swap, axis="cuts", size=n_cuts)
    macs = half * width * width

    def both(rows, order, count):
        rows = after(rows, order)
        return [rows] + [loop(piece, mask=1) for piece in jnp.split(rows, count)]

    def add(own, others):
        return sum((other.astype(F32) for other in others), own.astype(F32)).astype(BF16)

    def spread(total):
        return [total] + [cuts(total, mask=k) for k in range(1, QUAD)]

    def placed(pieces):
        outs = [((rows_out, width), F32)]
        return call(place_kernel, outs, [], pieces, 4, place, keep=False)[0]

    t2, i2 = (
        [loop(rows, mask=2) for rows in jnp.split(features, 2)]
        for features in (text_features, image_features)
    )
    place = jnp.stack([lax.axis_index("loop"), lax.axis_index("cuts") & (QUAD - 1)])
    place = place.astype(jnp.int32)
    t0, i0, place = lax.optimization_barrier((text_features, image_features, place))
    t1 = loop(t0, mask=1)
    i1 = loop(i0, mask=1)
    wide, wide_b = ((near, width), F32), ((near, width), BF16)
    tall, tall_b = ((half, width), F32), ((half, width), BF16)
    head_b = ((width, width), BF16)
    block_w, block_dots = ((half, near), BF16), ((half, near), F32)
    side_w, side_dots = ((near, half), BF16), ((near, half), F32)
    pick_one, pick_two = ((rows_out, near), BF16), ((2 * rows_out, near), BF16)
    q_a, y_a, p_a, x_a, w_aa, t0, i0, text_head, image_head = call(
        near_kernel,
        [wide, wide_b, wide, wide_b, ((near, near), BF16), tall_b, tall_b, head_b, head_b],
        [((near, near), F32)],
        (t1, i1),
        8,
        far=(t0, i0, text_head, image_head),
    )
    first = both(t2[0], w_aa, 2)
    q_2, y_2, w_a2, gx = call(
        text_kernel,
        [tall, tall_b, side_w, wide],
        [side_dots],
        (*first, text_head, y_a, x_a, w_aa),
        8,
    )
    gy_a, pick_i, pick_a = call(
        near_pull_kernel,
        [wide, pick_two, pick_one],
        [],
        (t0, t1, i0, i1, after(x_a, gx), w_aa),
        8,
        place,
    )
    second = both(t2[1], gy_a, 2)
    q_3, y_3, w_a3, dp_a, *image_parts = call(
        image_kernel,
        [tall, tall_b, side_w, wide_b] + [((2 * part, width), BF16)] * QUAD,
        [side_dots, wide],
        (*second, text_head, p_a, x_a, gx, pick_i),
        8,
    )
    image_others = [cuts(image_parts[k], mask=k) for k in range(1, QUAD)]
    gy_2, gy_3, pick_b = call(
        pull_kernel,
        [tall, tall, pick_one],
        [],
        (*first, *second, x_a, w_a2, w_a3),
        8,
        place,
    )
    blocks = []
    for block, rows in enumerate(i2):
        blocks += call(
            functools.partial(block_kernel, block),
            [tall_b, block_w, block_w],
            [tall, block_dots, block_dots],
            (*both(rows, (blocks[-1], gy_2) if blocks else dp_a, 2), image_head, y_a, y_2, y_3),
            8,
        )
    *text_parts, dq_own = call(
        last_kernel,
        [((part, width), BF16)] * QUAD + [tall_b],
        [wide, wide, wide_b, wide_b],
        (*blocks, q_a, q_2, q_3, gy_a, gy_2, gy_3, pick_a, pick_b),
        14,
    )
    text_others = [cuts(text_parts[k], mask=k) for k in range(1, QUAD)]
    image_others = [after(other, dq_own) for other in image_others]
    image_sum = add(image_parts[0], image_others)
    grads = [
        call(grad_kernel, [tall], [], (after(back, image_sum), head), 4, macs=2 * macs, keep=False)[0]
        for back, head in ((dp_a, image_head), (dq_own, text_head))
    ]
    image_sum = add(image_sum[:part], [after(loop(image_sum[part:], mask=2), grads)])
    text_sum = add(text_parts[0], [after(other, image_sum) for other in text_others])
    image_sum = add(image_sum, [cuts(image_sum, mask=QUAD)])
    image_pieces = spread(image_sum)
    text_sum = after(text_sum, image_sum)
    text_sum = add(text_sum, [after(cuts(text_sum, mask=QUAD), image_pieces[-1])])
    image_out = placed(image_pieces)
    text_out = placed(spread(text_sum))
    return (*grads, image_out, text_out)


def solution(mesh):
    n_loop, n_cuts = mesh.shape["loop"], mesh.shape["cuts"]
    if n_loop == 4 and n_cuts == 2 * QUAD:
        body = functools.partial(per_device, n_loop, n_cuts)
    else:
        body = plain_device
    placed = (P(("cuts", "loop"), None), P(("cuts", "loop"), None), P(), P())
    return jax.shard_map(
        body,
        mesh=mesh,
        in_specs=placed,
        out_specs=(
            P(("cuts", "loop"), None),
            P(("cuts", "loop"), None),
            P("loop", None),
            P("loop", None),
        ),
        check_vma=False,
    )
```

```python
import functools

import jax
import jax.numpy as jnp
from jax import lax
from jax.experimental import pallas as pl
from jax.experimental.pallas import tpu as pltpu
from jax.sharding import PartitionSpec as P

SCORE_SCALE = 10.0
SCORE_BIAS = -2.5
EPSILON = 1e-06
QUAD = 4
STRIP = 16
LANES = 128
F32 = jnp.float32
BF16 = jnp.bfloat16


def normalize(features, weight_matrix):
    projected = jnp.dot(features, weight_matrix, preferred_element_type=jnp.float32)
    factor = lax.rsqrt(jnp.sum(projected * projected, axis=-1, keepdims=True) + EPSILON)
    return (projected * factor, factor)


def pair_weights(image_vectors, text_vectors, image_offset):
    pair_scores = SCORE_SCALE * dot_nt(image_vectors, text_vectors) + SCORE_BIAS
    row_ids = image_offset + lax.broadcasted_iota(jnp.int32, pair_scores.shape, 0)
    col_ids = lax.broadcasted_iota(jnp.int32, pair_scores.shape, 1)
    match_targets = jnp.where(row_ids == col_ids, 1.0, -1.0).astype(jnp.float32)
    return (SCORE_SCALE * -match_targets * jax.nn.sigmoid(-match_targets * pair_scores)).astype(
        jnp.bfloat16
    )


def norm_back(unit, factor, gradient):
    return (factor * (gradient - unit * jnp.sum(unit * gradient, axis=-1, keepdims=True))).astype(
        jnp.bfloat16
    )


def dot_nn(left, right):
    return lax.dot_general(left, right, (((1,), (0,)), ((), ())), preferred_element_type=F32)


def dot_nt(left, right):
    return lax.dot_general(left, right, (((1,), (1,)), ((), ())), preferred_element_type=F32)


def dot_tn(left, right):
    return lax.dot_general(left, right, (((0,), (0,)), ((), ())), preferred_element_type=F32)


def plain_device(image_features, text_features, image_head, text_head):
    row_count = image_features.shape[0]
    own_start = lax.axis_index("loop") * row_count
    image_unit, image_factor = normalize(image_features, image_head)
    text_unit, text_factor = normalize(text_features, text_head)
    image_vectors = image_unit.astype(jnp.bfloat16)
    text_vectors = text_unit.astype(jnp.bfloat16)
    arrived = lax.all_gather(text_vectors, "loop", axis=0, tiled=True)
    weights = pair_weights(image_vectors, arrived, own_start)
    summed = jnp.dot(weights, arrived, preferred_element_type=jnp.float32)
    text_attraction = lax.psum_scatter(
        dot_tn(weights, image_vectors).astype(jnp.bfloat16), "loop", scatter_dimension=0, tiled=True
    ).astype(jnp.float32)
    image_back = norm_back(image_unit, image_factor, summed)
    text_back = norm_back(text_unit, text_factor, text_attraction)
    heads = []
    for features, back in ((image_features, image_back), (text_features, text_back)):
        term = dot_tn(features, back).astype(jnp.bfloat16)
        part = lax.psum_scatter(term, "loop", scatter_dimension=0, tiled=True)
        heads.append(lax.psum(part, "cuts").astype(jnp.float32))
    return (dot_nt(image_back, image_head), dot_nt(text_back, text_head), heads[0], heads[1])


def factor_of(ref, rows):
    p = ref[rows, :]
    return lax.rsqrt(jnp.sum(p * p, axis=-1, keepdims=True) + EPSILON)


def unit_rows(projected_ref, vectors_ref):
    for first in range(0, projected_ref.shape[0], STRIP):
        rows = slice(first, first + STRIP)
        factor = factor_of(projected_ref, rows)
        vectors_ref[rows, :] = (projected_ref[rows, :] * factor).astype(BF16)


def back_rows(projected_ref, gradient_ref, back_ref, at=0):
    for first in range(0, projected_ref.shape[0], STRIP):
        rows, target = slice(first, first + STRIP), slice(at + first, at + first + STRIP)
        factor = factor_of(projected_ref, rows)
        along = jnp.sum(projected_ref[rows, :] * gradient_ref[target, :], axis=-1, keepdims=True)
        along = factor * factor * factor * along
        back = factor * gradient_ref[target, :] - along * projected_ref[rows, :]
        back_ref[target, :] = back.astype(BF16)


def weight_rows(dots_ref, weights_ref, pairs_from=None):
    half_scale = 0.5 * SCORE_SCALE
    for first in range(0, dots_ref.shape[0], STRIP):
        rows = slice(first, first + STRIP)
        score = jnp.tanh(half_scale * dots_ref[rows, :] + 0.5 * SCORE_BIAS)
        weights = half_scale + half_scale * score
        if pairs_from is None:
            weights_ref[rows, :] = weights.astype(BF16)
            continue
        pair = pairs_from + first
        left = pair // LANES * LANES
        right = min(left + LANES, weights.shape[1])
        shape = (STRIP, right - left)
        column = lax.broadcasted_iota(jnp.int32, shape, 1)
        same = column == lax.broadcasted_iota(jnp.int32, shape, 0) + (pair - left)
        middle = weights[:, left:right] - jnp.where(same, SCORE_SCALE, 0.0)
        pieces = [weights[:, :left], middle, weights[:, right:]]
        weights = jnp.concatenate([p for p in pieces if p.shape[1]], axis=1)
        weights_ref[rows, :] = weights.astype(BF16)


def one_hot(first, rows, width):
    wanted = first + lax.broadcasted_iota(jnp.int32, (rows, width), 0)
    column = lax.broadcasted_iota(jnp.int32, (rows, width), 1)
    return jnp.where(wanted == column, 1.0, 0.0)


def picker(place_ref, rows, width, sides):
    part = rows // QUAD
    pieces = []
    for k in range(QUAD):
        for side in sides:
            first = (place_ref[0] ^ side) * rows + (place_ref[1] ^ k) * part
            pieces.append(one_hot(first, part, width))
    return jnp.concatenate(pieces, axis=0).astype(BF16)


def split_head(head, outs):
    part = head.shape[0] // QUAD
    for k, out in enumerate(outs):
        out[...] = head[k * part : (k + 1) * part, :].astype(BF16)


def near_kernel(
    t1, i1, t0_far, i0_far, text_head_far, image_head_far,
    q_a, y_a, p_a, x_a, w_aa, t0, i0, text_head, image_head, dots, sems,
):
    half = t0.shape[0]
    copies = [
        pltpu.make_async_copy(source, target, sems.at[n])
        for n, (source, target) in enumerate(
            ((t0_far, t0), (text_head_far, text_head), (i0_far, i0), (image_head_far, image_head))
        )
    ]
    for copy in copies:
        copy.start()
    copies[0].wait()
    copies[1].wait()
    q_a[:half, :] = dot_nn(t0[...], text_head[...])
    q_a[half:, :] = dot_nn(t1[...], text_head[...])
    copies[2].wait()
    copies[3].wait()
    p_a[:half, :] = dot_nn(i0[...], image_head[...])
    unit_rows(q_a, y_a)
    p_a[half:, :] = dot_nn(i1[...], image_head[...])
    unit_rows(p_a, x_a)
    dots[...] = dot_nt(x_a[...], y_a[...])
    weight_rows(dots, w_aa, 0)


def rows_of(refs):
    return jnp.concatenate([ref[...] for ref in refs], axis=0)


def text_kernel(place, *refs):
    *features, t0, t1, i0, i1, text_head, y_a, x_a, w_aa = refs[:-9]
    q_2, y_2, w_a2, gx, gy_a, pick_i, pick_t, dots, near_gx = refs[-9:]
    half = t0.shape[0]
    rows = pick_t.shape[0]
    q_2[...] = dot_nn(rows_of(features), text_head[...])
    near_gx[...] = dot_nn(w_aa[...], y_a[...])
    unit_rows(q_2, y_2)
    dots[...] = dot_nt(x_a[...], y_2[...])
    pick = picker(place, rows, t0.shape[1], (0, 2))
    pick_i[:, :half] = dot_nt(pick, i0[...]).astype(BF16)
    pick_i[:, half:] = dot_nt(pick, i1[...]).astype(BF16)
    weight_rows(dots, w_a2)
    gx[...] = near_gx[...] + dot_nn(w_a2[...], y_2[...])
    pick = picker(place, rows, t0.shape[1], (0,))
    pick_t[:, :half] = dot_nt(pick, t0[...]).astype(BF16)
    pick_t[:, half:] = dot_nt(pick, t1[...]).astype(BF16)
    gy_a[...] = dot_tn(w_aa[...], x_a[...])


def image_kernel(*refs):
    *features, text_head, p_a, x_a, gx_in, pick_i, q_3, y_3, w_a3, dp_a, h0, h1, h2, h3, dots, gx = refs
    q_3[...] = dot_nn(rows_of(features), text_head[...])
    unit_rows(q_3, y_3)
    dots[...] = dot_nt(x_a[...], y_3[...])
    weight_rows(dots, w_a3)
    gx[...] = gx_in[...] + dot_nn(w_a3[...], y_3[...])
    back_rows(p_a, gx, dp_a)
    split_head(dot_nn(pick_i[...], dp_a[...]), (h0, h1, h2, h3))


def block(number, features, image_head, y_a, y_2, y_3, x_b, w_ba, w_bb, p_b, d_a, d_b):
    half = x_b.shape[0]
    p_b[...] = dot_nn(rows_of(features), image_head[...])
    unit_rows(p_b, x_b)
    d_a[...] = dot_nt(x_b[...], y_a[...])
    d_b[:, :half] = dot_nt(x_b[...], y_2[...])
    d_b[:, half:] = dot_nt(x_b[...], y_3[...])
    weight_rows(d_a, w_ba)
    weight_rows(d_b, w_bb, number * half)


def third_kernel(place, *refs):
    *features, x_a, w_a2, w_a3, image_head, y_a, y_2, y_3 = refs[:-9]
    x_b, w_ba, w_bb, gy_2, gy_3, pick_t, p_b, d_a, d_b = refs[-9:]
    texts, images = features[: len(features) // 3 * 2], features[len(features) // 3 * 2 :]
    gy_2[...] = dot_tn(w_a2[...], x_a[...])
    block(0, images, image_head, y_a, y_2, y_3, x_b, w_ba, w_bb, p_b, d_a, d_b)
    gy_3[...] = dot_tn(w_a3[...], x_a[...])
    pick = picker(place, pick_t.shape[0], x_a.shape[1], (0,))
    pick_t[...] = dot_nt(pick, rows_of(texts)).astype(BF16)


def fourth_kernel(*refs):
    block(1, refs[:-10], *refs[-10:])


def last_kernel(
    x_2, w_2a, w_2b, x_3, w_3a, w_3b, q_a, q_2, q_3, gy_a_in, gy_2, gy_3, pick_a, pick_b,
    h0, h1, h2, h3, dq_a, gy_a, gy_b, dq_b, near_head,
):
    half = x_2.shape[0]
    gy_a[...] = gy_a_in[...] + dot_tn(w_2a[...], x_2[...]) + dot_tn(w_3a[...], x_3[...])
    gy_b[...] = dot_tn(w_2b[...], x_2[...]) + dot_tn(w_3b[...], x_3[...])
    back_rows(q_a, gy_a, dq_a)
    near_head[...] = dot_nn(pick_a[...], dq_a[...])
    gy_b[:half, :] += gy_2[...]
    gy_b[half:, :] += gy_3[...]
    back_rows(q_2, gy_b, dq_b, 0)
    back_rows(q_3, gy_b, dq_b, half)
    split_head(near_head[...] + dot_nn(pick_b[...], dq_b[...]), (h0, h1, h2, h3))


def grad_kernel(back, head, out):
    out[...] = dot_nt(back[: out.shape[0], :], head[...])


def place_kernel(place, h0, h1, h2, h3, out):
    part = h0.shape[0]
    for k, piece in enumerate((h0, h1, h2, h3)):
        first = pl.multiple_of((place[1] ^ k) * part, part)
        out[pl.ds(first, part), :] = piece[...].astype(F32)


def call(kernel, outs, scratch, args, mib, place=None, macs=0, keep=True, far=()):
    far = [pltpu.with_memory_space_constraint(a, pltpu.HBM) for a in far]
    args = [pltpu.with_memory_space_constraint(a, pltpu.VMEM) for a in args] + far
    specs = [pl.BlockSpec(memory_space=pltpu.VMEM)] * (len(args) - len(far))
    specs += [pl.BlockSpec(memory_space=pltpu.HBM)] * len(far)
    if place is not None:
        args, specs = [place, *args], [pl.BlockSpec(memory_space=pltpu.SMEM), *specs]
    shape = pltpu.VMEM if keep else jax.ShapeDtypeStruct
    return pl.pallas_call(
        kernel,
        out_shape=[shape(s, t) for s, t in outs],
        in_specs=specs,
        out_specs=[pl.BlockSpec(memory_space=pltpu.VMEM)] * len(outs),
        scratch_shapes=[pltpu.VMEM(s, t) for s, t in scratch]
        + [pltpu.SemaphoreType.DMA((len(far),))] * bool(far),
        compiler_params=pltpu.CompilerParams(vmem_limit_bytes=mib * 1024 * 1024),
        cost_estimate=pl.CostEstimate(flops=2 * macs, bytes_accessed=0, transcendentals=0),
    )(*args)


def swap(array, axis, size, mask):
    return lax.ppermute(array, axis, [(i, i ^ mask) for i in range(size)])


def after(value, other):
    return lax.optimization_barrier((value, other))[0]


def per_device(n_loop, n_cuts, image_features, text_features, image_head, text_head):
    half, width = image_features.shape
    near = 2 * half
    rows_out = width // n_loop
    part = rows_out // QUAD
    loop = functools.partial(swap, axis="loop", size=n_loop)
    cuts = functools.partial(swap, axis="cuts", size=n_cuts)
    macs = half * width * width

    def both(rows, order, count):
        rows = after(rows, order)
        return [rows] + [loop(piece, mask=1) for piece in jnp.split(rows, count)]

    def add(own, others):
        return sum((other.astype(F32) for other in others), own.astype(F32)).astype(BF16)

    def spread(total):
        return [total] + [cuts(total, mask=k) for k in range(1, QUAD)]

    def placed(pieces):
        outs = [((rows_out, width), F32)]
        return call(place_kernel, outs, [], pieces, 4, place, keep=False)[0]

    t2, i2 = (
        [loop(rows, mask=2) for rows in jnp.split(features, 2)]
        for features in (text_features, image_features)
    )
    place = jnp.stack([lax.axis_index("loop"), lax.axis_index("cuts") & (QUAD - 1)])
    place = place.astype(jnp.int32)
    t0, i0, place = lax.optimization_barrier((text_features, image_features, place))
    t1 = loop(t0, mask=1)
    i1 = loop(i0, mask=1)
    wide, wide_b = ((near, width), F32), ((near, width), BF16)
    tall, tall_b = ((half, width), F32), ((half, width), BF16)
    head_b = ((width, width), BF16)
    block_w, block_dots = ((half, near), BF16), ((half, near), F32)
    side_w, side_dots = ((near, half), BF16), ((near, half), F32)
    pick_one, pick_two = ((rows_out, near), BF16), ((2 * rows_out, near), BF16)
    q_a, y_a, p_a, x_a, w_aa, t0, i0, text_head, image_head = call(
        near_kernel,
        [wide, wide_b, wide, wide_b, ((near, near), BF16), tall_b, tall_b, head_b, head_b],
        [((near, near), F32)],
        (t1, i1),
        8,
        far=(t0, i0, text_head, image_head),
    )
    first = both(t2[0], w_aa, 2)
    q_2, y_2, w_a2, gx, gy_a, pick_i, pick_a = call(
        text_kernel,
        [tall, tall_b, side_w, wide, wide, pick_two, pick_one],
        [side_dots, wide],
        (*first, t0, t1, i0, i1, text_head, y_a, x_a, w_aa),
        8,
        place,
    )
    second = both(t2[1], gy_a, 2)
    q_3, y_3, w_a3, dp_a, *image_parts = call(
        image_kernel,
        [tall, tall_b, side_w, wide_b] + [((2 * part, width), BF16)] * QUAD,
        [side_dots, wide],
        (*second, text_head, p_a, x_a, gx, pick_i),
        8,
    )
    image_others = [cuts(image_parts[k], mask=k) for k in range(1, QUAD)]
    scratch = [tall, block_dots, block_dots]
    x_2, w_2a, w_2b, gy_2, gy_3, pick_b = call(
        third_kernel,
        [tall_b, block_w, block_w, tall, tall, pick_one],
        scratch,
        (*first, *second, *both(i2[0], dp_a, 2), x_a, w_a2, w_a3, image_head, y_a, y_2, y_3),
        8,
        place,
    )
    x_3, w_3a, w_3b = call(
        fourth_kernel,
        [tall_b, block_w, block_w],
        scratch,
        (*both(i2[1], gy_2, 2), image_head, y_a, y_2, y_3),
        8,
    )
    blocks = (x_2, w_2a, w_2b, x_3, w_3a, w_3b)
    *text_parts, dq_a = call(
        last_kernel,
        [((part, width), BF16)] * QUAD + [wide_b],
        [wide, wide, wide_b, ((rows_out, width), F32)],
        (*blocks, q_a, q_2, q_3, gy_a, gy_2, gy_3, pick_a, pick_b),
        14,
    )
    text_others = [cuts(text_parts[k], mask=k) for k in range(1, QUAD)]
    image_others = [after(other, dq_a) for other in image_others]
    image_sum = add(image_parts[0], image_others)
    grads = [
        call(grad_kernel, [tall], [], (after(back, image_sum), head), 4, macs=2 * macs, keep=False)[0]
        for back, head in ((dp_a, image_head), (dq_a, text_head))
    ]
    image_sum = add(image_sum[:part], [after(loop(image_sum[part:], mask=2), grads)])
    text_sum = add(text_parts[0], [after(other, image_sum) for other in text_others])
    image_sum = add(image_sum, [cuts(image_sum, mask=QUAD)])
    image_pieces = spread(image_sum)
    text_sum = after(text_sum, image_sum)
    text_sum = add(text_sum, [after(cuts(text_sum, mask=QUAD), image_pieces[1])])
    image_out = placed(image_pieces)
    text_out = placed(spread(text_sum))
    return (*grads, image_out, text_out)


def solution(mesh):
    n_loop, n_cuts = mesh.shape["loop"], mesh.shape["cuts"]
    if n_loop == 4 and n_cuts == 2 * QUAD:
        body = functools.partial(per_device, n_loop, n_cuts)
    else:
        body = plain_device
    placed = (P(("cuts", "loop"), None), P(("cuts", "loop"), None), P(), P())
    return jax.shard_map(
        body,
        mesh=mesh,
        in_specs=placed,
        out_specs=(
            P(("cuts", "loop"), None),
            P(("cuts", "loop"), None),
            P("loop", None),
            P("loop", None),
        ),
        check_vma=False,
    )
```

```python
import functools

import jax
import jax.numpy as jnp
from jax import lax
from jax.experimental import pallas as pl
from jax.experimental.pallas import tpu as pltpu
from jax.sharding import PartitionSpec as P

SCORE_SCALE = 10.0
SCORE_BIAS = -2.5
EPSILON = 1e-06
QUAD = 4
STRIP = 16
LANES = 128
F32 = jnp.float32
BF16 = jnp.bfloat16


def normalize(features, weight_matrix):
    projected = jnp.dot(features, weight_matrix, preferred_element_type=jnp.float32)
    factor = lax.rsqrt(jnp.sum(projected * projected, axis=-1, keepdims=True) + EPSILON)
    return (projected * factor, factor)


def pair_weights(image_vectors, text_vectors, image_offset):
    pair_scores = SCORE_SCALE * dot_nt(image_vectors, text_vectors) + SCORE_BIAS
    row_ids = image_offset + lax.broadcasted_iota(jnp.int32, pair_scores.shape, 0)
    col_ids = lax.broadcasted_iota(jnp.int32, pair_scores.shape, 1)
    match_targets = jnp.where(row_ids == col_ids, 1.0, -1.0).astype(jnp.float32)
    return (SCORE_SCALE * -match_targets * jax.nn.sigmoid(-match_targets * pair_scores)).astype(
        jnp.bfloat16
    )


def norm_back(unit, factor, gradient):
    return (factor * (gradient - unit * jnp.sum(unit * gradient, axis=-1, keepdims=True))).astype(
        jnp.bfloat16
    )


def dot_nn(left, right):
    return lax.dot_general(left, right, (((1,), (0,)), ((), ())), preferred_element_type=F32)


def dot_nt(left, right):
    return lax.dot_general(left, right, (((1,), (1,)), ((), ())), preferred_element_type=F32)


def dot_tn(left, right):
    return lax.dot_general(left, right, (((0,), (0,)), ((), ())), preferred_element_type=F32)


def plain_device(image_features, text_features, image_head, text_head):
    row_count = image_features.shape[0]
    own_start = lax.axis_index("loop") * row_count
    image_unit, image_factor = normalize(image_features, image_head)
    text_unit, text_factor = normalize(text_features, text_head)
    image_vectors = image_unit.astype(jnp.bfloat16)
    text_vectors = text_unit.astype(jnp.bfloat16)
    arrived = lax.all_gather(text_vectors, "loop", axis=0, tiled=True)
    weights = pair_weights(image_vectors, arrived, own_start)
    summed = jnp.dot(weights, arrived, preferred_element_type=jnp.float32)
    text_attraction = lax.psum_scatter(
        dot_tn(weights, image_vectors).astype(jnp.bfloat16), "loop", scatter_dimension=0, tiled=True
    ).astype(jnp.float32)
    image_back = norm_back(image_unit, image_factor, summed)
    text_back = norm_back(text_unit, text_factor, text_attraction)
    heads = []
    for features, back in ((image_features, image_back), (text_features, text_back)):
        term = dot_tn(features, back).astype(jnp.bfloat16)
        part = lax.psum_scatter(term, "loop", scatter_dimension=0, tiled=True)
        heads.append(lax.psum(part, "cuts").astype(jnp.float32))
    return (dot_nt(image_back, image_head), dot_nt(text_back, text_head), heads[0], heads[1])


def factor_of(ref, rows):
    p = ref[rows, :]
    return lax.rsqrt(jnp.sum(p * p, axis=-1, keepdims=True) + EPSILON)


def unit_rows(projected_ref, vectors_ref):
    for first in range(0, projected_ref.shape[0], STRIP):
        rows = slice(first, first + STRIP)
        factor = factor_of(projected_ref, rows)
        vectors_ref[rows, :] = (projected_ref[rows, :] * factor).astype(BF16)


def back_rows(projected_ref, gradient_ref, back_ref, at=0):
    for first in range(0, projected_ref.shape[0], STRIP):
        rows = slice(first, first + STRIP)
        factor = factor_of(projected_ref, rows)
        along = jnp.sum(projected_ref[rows, :] * gradient_ref[rows, :], axis=-1, keepdims=True)
        along = factor * factor * factor * along
        back = factor * gradient_ref[rows, :] - along * projected_ref[rows, :]
        back_ref[at + first : at + first + STRIP, :] = back.astype(BF16)


def weight_rows(dots_ref, weights_ref, pairs_from=None, begin=0, end=None):
    half_scale = 0.5 * SCORE_SCALE
    for first in range(begin, dots_ref.shape[0] if end is None else end, STRIP):
        rows = slice(first, first + STRIP)
        score = jnp.tanh(half_scale * dots_ref[rows, :] + 0.5 * SCORE_BIAS)
        weights = half_scale + half_scale * score
        if pairs_from is None:
            weights_ref[rows, :] = weights.astype(BF16)
            continue
        pair = pairs_from + first - begin
        left = pair // LANES * LANES
        right = min(left + LANES, weights.shape[1])
        shape = (STRIP, right - left)
        column = lax.broadcasted_iota(jnp.int32, shape, 1)
        same = column == lax.broadcasted_iota(jnp.int32, shape, 0) + (pair - left)
        middle = weights[:, left:right] - jnp.where(same, SCORE_SCALE, 0.0)
        pieces = [weights[:, :left], middle, weights[:, right:]]
        weights = jnp.concatenate([p for p in pieces if p.shape[1]], axis=1)
        weights_ref[rows, :] = weights.astype(BF16)


def one_hot(first, rows, width):
    wanted = first + lax.broadcasted_iota(jnp.int32, (rows, width), 0)
    column = lax.broadcasted_iota(jnp.int32, (rows, width), 1)
    return jnp.where(wanted == column, 1.0, 0.0)


def picker(place_ref, rows, width, sides):
    part = rows // QUAD
    pieces = []
    for k in range(QUAD):
        for side in sides:
            first = (place_ref[0] ^ side) * rows + (place_ref[1] ^ k) * part
            pieces.append(one_hot(first, part, width))
    return jnp.concatenate(pieces, axis=0).astype(BF16)


def split_head(head, outs):
    part = head.shape[0] // QUAD
    for k, out in enumerate(outs):
        out[...] = head[k * part : (k + 1) * part, :].astype(BF16)


def near_kernel(
    t1, i1, t0_far, i0_far, text_head_far, image_head_far,
    q_a, y_a, p_a, x_a, w_aa, t0, i0, text_head, image_head, dots, sems,
):
    half = t0.shape[0]
    copies = [
        pltpu.make_async_copy(source, target, sems.at[n])
        for n, (source, target) in enumerate(
            ((t0_far, t0), (text_head_far, text_head), (i0_far, i0), (image_head_far, image_head))
        )
    ]
    for copy in copies:
        copy.start()
    copies[0].wait()
    copies[1].wait()
    q_a[:half, :] = dot_nn(t0[...], text_head[...])
    q_a[half:, :] = dot_nn(t1[...], text_head[...])
    copies[2].wait()
    copies[3].wait()
    p_a[:half, :] = dot_nn(i0[...], image_head[...])
    unit_rows(q_a, y_a)
    p_a[half:, :] = dot_nn(i1[...], image_head[...])
    unit_rows(p_a, x_a)
    dots[...] = dot_nt(x_a[...], y_a[...])
    weight_rows(dots, w_aa, 0)


def rows_of(refs):
    return jnp.concatenate([ref[...] for ref in refs], axis=0)


def text_kernel(place, *refs):
    *features, t0, t1, i0, i1, text_head, y_a, x_a, w_aa = refs[:-9]
    q_2, y_2, w_a2, gx, gy_a, pick_i, pick_t, dots, near_gx = refs[-9:]
    half = t0.shape[0]
    rows = pick_t.shape[0]
    q_2[...] = dot_nn(rows_of(features), text_head[...])
    near_gx[...] = dot_nn(w_aa[...], y_a[...])
    unit_rows(q_2, y_2)
    dots[...] = dot_nt(x_a[...], y_2[...])
    pick = picker(place, rows, t0.shape[1], (0, 2))
    pick_i[:, :half] = dot_nt(pick, i0[...]).astype(BF16)
    pick_i[:, half:] = dot_nt(pick, i1[...]).astype(BF16)
    weight_rows(dots, w_a2)
    gx[...] = near_gx[...] + dot_nn(w_a2[...], y_2[...])
    pick = picker(place, rows, t0.shape[1], (0,))
    pick_t[:, :half] = dot_nt(pick, t0[...]).astype(BF16)
    pick_t[:, half:] = dot_nt(pick, t1[...]).astype(BF16)
    gy_a[...] = dot_tn(w_aa[...], x_a[...])


def image_kernel(*refs):
    *features, text_head, p_a, x_a, gx_in, pick_i, q_3, y_3, w_a3, dp_a, h0, h1, h2, h3, dots, gx = refs
    q_3[...] = dot_nn(rows_of(features), text_head[...])
    unit_rows(q_3, y_3)
    dots[...] = dot_nt(x_a[...], y_3[...])
    weight_rows(dots, w_a3)
    gx[...] = gx_in[...] + dot_nn(w_a3[...], y_3[...])
    back_rows(p_a, gx, dp_a)
    split_head(dot_nn(pick_i[...], dp_a[...]), (h0, h1, h2, h3))


def text_pull_kernel(place, *refs):
    *features, x_a, w_a2, w_a3, gy_2, gy_3, pick_t = refs
    gy_2[...] = dot_tn(w_a2[...], x_a[...])
    gy_3[...] = dot_tn(w_a3[...], x_a[...])
    pick = picker(place, pick_t.shape[0], x_a.shape[1], (0,))
    pick_t[...] = dot_nt(pick, rows_of(features)).astype(BF16)


def far_weights(core, x, y_a, y_2, y_3, w_a, w_2, w_3, d_a, d_2, d_3):
    half = x.shape[0]
    middle = half // 2
    d_a[...] = dot_nt(x, y_a[...])
    d_2[...] = dot_nt(x, y_2[...])
    weight_rows(d_a, w_a)
    d_3[...] = dot_nt(x, y_3[...])
    weight_rows(d_2, w_2, core * middle, 0, middle)
    weight_rows(d_2, w_2, None, middle, half)
    weight_rows(d_3, w_3, None, 0, middle)
    weight_rows(d_3, w_3, core * middle, middle, half)


def block_kernel(i2, image_head, y_a, y_2, y_3, x_first, x_second, w_a, w_2, w_3, p_b, x_b, d_a, d_2, d_3):
    middle = x_first.shape[0]
    p_b[...] = dot_nn(i2[...], image_head[...])
    unit_rows(p_b, x_b)
    x_first[...] = x_b[:middle, :]
    x_second[...] = x_b[middle:, :]
    far_weights(0, x_b[...], y_a, y_2, y_3, w_a, w_2, w_3, d_a, d_2, d_3)


def own_pull_kernel(x_first, x_second, w_a, w_2, w_3, gy_a_in, gy_2_in, gy_3_in, gy_a, gy_2, gy_3):
    x = rows_of((x_first, x_second))
    gy_a[...] = gy_a_in[...] + dot_tn(w_a[...], x)
    gy_2[...] = gy_2_in[...] + dot_tn(w_2[...], x)
    gy_3[...] = gy_3_in[...] + dot_tn(w_3[...], x)


def last_kernel(
    x_first, x_second, y_a, y_2, y_3, q_a, q_2, q_3, gy_a_in, gy_2_in, gy_3_in, pick_a, pick_b,
    h0, h1, h2, h3, dq_a, gy_a, gy_2, gy_3, dq_b, near_head, w_a, w_2, w_3, d_a, d_2, d_3,
):
    half = q_2.shape[0]
    x = rows_of((x_first, x_second))
    far_weights(1, x, y_a, y_2, y_3, w_a, w_2, w_3, d_a, d_2, d_3)
    gy_a[...] = gy_a_in[...] + dot_tn(w_a[...], x)
    gy_2[...] = gy_2_in[...] + dot_tn(w_2[...], x)
    back_rows(q_a, gy_a, dq_a)
    gy_3[...] = gy_3_in[...] + dot_tn(w_3[...], x)
    near_head[...] = dot_nn(pick_a[...], dq_a[...])
    back_rows(q_2, gy_2, dq_b, 0)
    back_rows(q_3, gy_3, dq_b, half)
    split_head(near_head[...] + dot_nn(pick_b[...], dq_b[...]), (h0, h1, h2, h3))


def grad_kernel(back, head, out):
    out[...] = dot_nt(back[: out.shape[0], :], head[...])


def place_kernel(place, ks, *refs):
    out, buffer, sems = refs[-3:]
    part = refs[0].shape[0]
    copies = []
    for n, k in enumerate(ks):
        buffer[n] = refs[n][...].astype(F32)
        first = pl.multiple_of((place[1] ^ k) * part, part)
        copies.append(pltpu.make_async_copy(buffer.at[n], out.at[pl.ds(first, part), :], sems.at[n]))
        copies[-1].start()
    for copy in copies:
        copy.wait()


def place_pieces(place, pieces, ks, out=None):
    rows, width = pieces[0].shape
    args = [pltpu.with_memory_space_constraint(a, pltpu.VMEM) for a in pieces]
    specs = [pl.BlockSpec(memory_space=pltpu.SMEM)]
    specs += [pl.BlockSpec(memory_space=pltpu.VMEM)] * len(pieces)
    if out is not None:
        args, specs = args + [out], specs + [pl.BlockSpec(memory_space=pltpu.HBM)]
    return pl.pallas_call(
        lambda place_ref, *refs: place_kernel(place_ref, ks, *refs),
        out_shape=pltpu.HBM((QUAD * rows, width), F32),
        in_specs=specs,
        out_specs=pl.BlockSpec(memory_space=pltpu.HBM),
        scratch_shapes=[
            pltpu.VMEM((len(ks), rows, width), F32), pltpu.SemaphoreType.DMA((len(ks),))
        ],
        input_output_aliases={} if out is None else {len(pieces) + 1: 0},
        compiler_params=pltpu.CompilerParams(vmem_limit_bytes=4 * 1024 * 1024),
        cost_estimate=pl.CostEstimate(flops=0, bytes_accessed=0, transcendentals=0),
    )(place, *args)


def call(kernel, outs, scratch, args, mib, place=None, macs=0, keep=True, far=()):
    far = [pltpu.with_memory_space_constraint(a, pltpu.HBM) for a in far]
    args = [pltpu.with_memory_space_constraint(a, pltpu.VMEM) for a in args] + far
    specs = [pl.BlockSpec(memory_space=pltpu.VMEM)] * (len(args) - len(far))
    specs += [pl.BlockSpec(memory_space=pltpu.HBM)] * len(far)
    if place is not None:
        args, specs = [place, *args], [pl.BlockSpec(memory_space=pltpu.SMEM), *specs]
    shape = pltpu.VMEM if keep else jax.ShapeDtypeStruct
    return pl.pallas_call(
        kernel,
        out_shape=[shape(s, t) for s, t in outs],
        in_specs=specs,
        out_specs=[pl.BlockSpec(memory_space=pltpu.VMEM)] * len(outs),
        scratch_shapes=[pltpu.VMEM(s, t) for s, t in scratch]
        + [pltpu.SemaphoreType.DMA((len(far),))] * bool(far),
        compiler_params=pltpu.CompilerParams(vmem_limit_bytes=mib * 1024 * 1024),
        cost_estimate=pl.CostEstimate(flops=2 * macs, bytes_accessed=0, transcendentals=0),
    )(*args)


def swap(array, axis, size, mask):
    return lax.ppermute(array, axis, [(i, i ^ mask) for i in range(size)])


def after(value, other):
    return lax.optimization_barrier((value, other))[0]


def per_device(n_loop, n_cuts, image_features, text_features, image_head, text_head):
    half, width = image_features.shape
    near = 2 * half
    rows_out = width // n_loop
    part = rows_out // QUAD
    loop = functools.partial(swap, axis="loop", size=n_loop)
    cuts = functools.partial(swap, axis="cuts", size=n_cuts)
    macs = half * width * width

    def both(rows, order, count):
        rows = after(rows, order)
        return [rows] + [loop(piece, mask=1) for piece in jnp.split(rows, count)]

    def add(own, others):
        return sum((other.astype(F32) for other in others), own.astype(F32)).astype(BF16)

    def spread(total):
        return [total] + [cuts(total, mask=k) for k in range(1, QUAD)]

    def placed(pieces):
        out = place_pieces(place, pieces[:-1], tuple(range(QUAD - 1)))
        return place_pieces(place, pieces[-1:], (QUAD - 1,), out)

    t2 = [loop(rows, mask=2) for rows in jnp.split(text_features, 2)]
    i2 = loop(image_features, mask=2)
    place = jnp.stack([lax.axis_index("loop"), lax.axis_index("cuts") & (QUAD - 1)])
    place = place.astype(jnp.int32)
    t0, i0, place = lax.optimization_barrier((text_features, image_features, place))
    t1 = loop(t0, mask=1)
    i1 = loop(i0, mask=1)
    wide, wide_b = ((near, width), F32), ((near, width), BF16)
    tall, tall_b = ((half, width), F32), ((half, width), BF16)
    head_b = ((width, width), BF16)
    block_w, block_dots = ((half, near), BF16), ((half, near), F32)
    side_w, side_dots = ((near, half), BF16), ((near, half), F32)
    pick_one, pick_two = ((rows_out, near), BF16), ((2 * rows_out, near), BF16)
    q_a, y_a, p_a, x_a, w_aa, t0, i0, text_head, image_head = call(
        near_kernel,
        [wide, wide_b, wide, wide_b, ((near, near), BF16), tall_b, tall_b, head_b, head_b],
        [((near, near), F32)],
        (t1, i1),
        8,
        far=(t0, i0, text_head, image_head),
    )
    first = both(t2[0], w_aa, 2)
    q_2, y_2, w_a2, gx, gy_a, pick_i, pick_a = call(
        text_kernel,
        [tall, tall_b, side_w, wide, wide, pick_two, pick_one],
        [side_dots, wide],
        (*first, t0, t1, i0, i1, text_head, y_a, x_a, w_aa),
        8,
        place,
    )
    second = both(t2[1], gy_a, 2)
    q_3, y_3, w_a3, dp_a, *image_parts = call(
        image_kernel,
        [tall, tall_b, side_w, wide_b] + [((2 * part, width), BF16)] * QUAD,
        [side_dots, wide],
        (*second, text_head, p_a, x_a, gx, pick_i),
        8,
    )
    image_others = [cuts(image_parts[k], mask=k) for k in range(1, QUAD)]
    gy_2, gy_3, pick_b = call(
        text_pull_kernel,
        [tall, tall, pick_one],
        [],
        (*first, *second, after(x_a, dp_a), w_a2, w_a3),
        8,
        place,
    )
    middle_b, corner, corner_dots = ((half // 2, width), BF16), ((half, half), BF16), ((half, half), F32)
    *x_2, w_2a, w_22, w_23 = call(
        block_kernel,
        [middle_b, middle_b, block_w, corner, corner],
        [tall, tall_b, block_dots, corner_dots, corner_dots],
        (after(i2, gy_2), image_head, y_a, y_2, y_3),
        8,
    )
    x_3 = [loop(rows, mask=1) for rows in x_2]
    gy_a, gy_2, gy_3 = call(
        own_pull_kernel,
        [wide, tall, tall],
        [],
        (*x_2, w_2a, w_22, w_23, gy_a, gy_2, gy_3),
        8,
    )
    x_3 = [after(rows, gy_a) for rows in x_3]
    *text_parts, dq_a = call(
        last_kernel,
        [((part, width), BF16)] * QUAD + [wide_b],
        [wide, tall, tall, wide_b, ((rows_out, width), F32), block_w, corner, corner]
        + [block_dots, corner_dots, corner_dots],
        (*x_3, y_a, y_2, y_3, q_a, q_2, q_3, gy_a, gy_2, gy_3, pick_a, pick_b),
        16,
    )
    text_others = [cuts(text_parts[k], mask=k) for k in range(1, QUAD)]
    image_others = [after(other, dq_a) for other in image_others]
    image_sum = add(image_parts[0], image_others)
    grads = [
        call(grad_kernel, [tall], [], (after(back, image_sum), head), 4, macs=2 * macs, keep=False)[0]
        for back, head in ((dp_a, image_head), (dq_a, text_head))
    ]
    image_sum = add(image_sum[:part], [after(loop(image_sum[part:], mask=2), grads)])
    text_sum = add(text_parts[0], [after(other, image_sum) for other in text_others])
    image_sum = add(image_sum, [cuts(image_sum, mask=QUAD)])
    image_pieces = spread(image_sum)
    text_sum = after(text_sum, image_sum)
    text_sum = add(text_sum, [after(cuts(text_sum, mask=QUAD), image_pieces[1])])
    image_out = placed(image_pieces)
    text_out = placed(spread(text_sum))
    return (*grads, image_out, text_out)


def solution(mesh):
    n_loop, n_cuts = mesh.shape["loop"], mesh.shape["cuts"]
    if n_loop == 4 and n_cuts == 2 * QUAD:
        body = functools.partial(per_device, n_loop, n_cuts)
    else:
        body = plain_device
    placed = (P(("cuts", "loop"), None), P(("cuts", "loop"), None), P(), P())
    return jax.shard_map(
        body,
        mesh=mesh,
        in_specs=placed,
        out_specs=(
            P(("cuts", "loop"), None),
            P(("cuts", "loop"), None),
            P("loop", None),
            P("loop", None),
        ),
        check_vma=False,
    )
```

```python
import functools

import jax
import jax.numpy as jnp
from jax import lax
from jax.experimental import pallas as pl
from jax.experimental.pallas import tpu as pltpu
from jax.sharding import PartitionSpec as P

SCORE_SCALE = 10.0
SCORE_BIAS = -2.5
EPSILON = 1e-06
QUAD = 4
STRIP = 16
LANES = 128
F32 = jnp.float32
BF16 = jnp.bfloat16


def normalize(features, weight_matrix):
    projected = jnp.dot(features, weight_matrix, preferred_element_type=jnp.float32)
    factor = lax.rsqrt(jnp.sum(projected * projected, axis=-1, keepdims=True) + EPSILON)
    return (projected * factor, factor)


def pair_weights(image_vectors, text_vectors, image_offset):
    pair_scores = SCORE_SCALE * dot_nt(image_vectors, text_vectors) + SCORE_BIAS
    row_ids = image_offset + lax.broadcasted_iota(jnp.int32, pair_scores.shape, 0)
    col_ids = lax.broadcasted_iota(jnp.int32, pair_scores.shape, 1)
    match_targets = jnp.where(row_ids == col_ids, 1.0, -1.0).astype(jnp.float32)
    return (SCORE_SCALE * -match_targets * jax.nn.sigmoid(-match_targets * pair_scores)).astype(
        jnp.bfloat16
    )


def norm_back(unit, factor, gradient):
    return (factor * (gradient - unit * jnp.sum(unit * gradient, axis=-1, keepdims=True))).astype(
        jnp.bfloat16
    )


def dot_nn(left, right):
    return lax.dot_general(left, right, (((1,), (0,)), ((), ())), preferred_element_type=F32)


def dot_nt(left, right):
    return lax.dot_general(left, right, (((1,), (1,)), ((), ())), preferred_element_type=F32)


def dot_tn(left, right):
    return lax.dot_general(left, right, (((0,), (0,)), ((), ())), preferred_element_type=F32)


def plain_device(image_features, text_features, image_head, text_head):
    row_count = image_features.shape[0]
    own_start = lax.axis_index("loop") * row_count
    image_unit, image_factor = normalize(image_features, image_head)
    text_unit, text_factor = normalize(text_features, text_head)
    image_vectors = image_unit.astype(jnp.bfloat16)
    text_vectors = text_unit.astype(jnp.bfloat16)
    arrived = lax.all_gather(text_vectors, "loop", axis=0, tiled=True)
    weights = pair_weights(image_vectors, arrived, own_start)
    summed = jnp.dot(weights, arrived, preferred_element_type=jnp.float32)
    text_attraction = lax.psum_scatter(
        dot_tn(weights, image_vectors).astype(jnp.bfloat16), "loop", scatter_dimension=0, tiled=True
    ).astype(jnp.float32)
    image_back = norm_back(image_unit, image_factor, summed)
    text_back = norm_back(text_unit, text_factor, text_attraction)
    heads = []
    for features, back in ((image_features, image_back), (text_features, text_back)):
        term = dot_tn(features, back).astype(jnp.bfloat16)
        part = lax.psum_scatter(term, "loop", scatter_dimension=0, tiled=True)
        heads.append(lax.psum(part, "cuts").astype(jnp.float32))
    return (dot_nt(image_back, image_head), dot_nt(text_back, text_head), heads[0], heads[1])


def factor_of(ref, rows):
    p = ref[rows, :]
    return lax.rsqrt(jnp.sum(p * p, axis=-1, keepdims=True) + EPSILON)


def unit_rows(projected_ref, vectors_ref):
    for first in range(0, projected_ref.shape[0], STRIP):
        rows = slice(first, first + STRIP)
        factor = factor_of(projected_ref, rows)
        vectors_ref[rows, :] = (projected_ref[rows, :] * factor).astype(BF16)


def back_rows(projected_ref, gradient_ref, back_ref, at=0):
    for first in range(0, projected_ref.shape[0], STRIP):
        rows = slice(first, first + STRIP)
        factor = factor_of(projected_ref, rows)
        along = jnp.sum(projected_ref[rows, :] * gradient_ref[rows, :], axis=-1, keepdims=True)
        along = factor * factor * factor * along
        back = factor * gradient_ref[rows, :] - along * projected_ref[rows, :]
        back_ref[at + first : at + first + STRIP, :] = back.astype(BF16)


def weight_rows(dots_ref, weights_ref, pairs_from=None, begin=0, end=None):
    half_scale = 0.5 * SCORE_SCALE
    for first in range(begin, dots_ref.shape[0] if end is None else end, STRIP):
        rows = slice(first, first + STRIP)
        score = jnp.tanh(half_scale * dots_ref[rows, :] + 0.5 * SCORE_BIAS)
        weights = half_scale + half_scale * score
        if pairs_from is None:
            weights_ref[rows, :] = weights.astype(BF16)
            continue
        pair = pairs_from + first - begin
        left = pair // LANES * LANES
        right = min(left + LANES, weights.shape[1])
        shape = (STRIP, right - left)
        column = lax.broadcasted_iota(jnp.int32, shape, 1)
        same = column == lax.broadcasted_iota(jnp.int32, shape, 0) + (pair - left)
        middle = weights[:, left:right] - jnp.where(same, SCORE_SCALE, 0.0)
        pieces = [weights[:, :left], middle, weights[:, right:]]
        weights = jnp.concatenate([p for p in pieces if p.shape[1]], axis=1)
        weights_ref[rows, :] = weights.astype(BF16)


def one_hot(first, rows, width):
    wanted = first + lax.broadcasted_iota(jnp.int32, (rows, width), 0)
    column = lax.broadcasted_iota(jnp.int32, (rows, width), 1)
    return jnp.where(wanted == column, 1.0, 0.0)


def picker(place_ref, rows, width, sides):
    part = rows // QUAD
    pieces = []
    for k in range(QUAD):
        for side in sides:
            first = (place_ref[0] ^ side) * rows + (place_ref[1] ^ k) * part
            pieces.append(one_hot(first, part, width))
    return jnp.concatenate(pieces, axis=0).astype(BF16)


def split_head(head, outs):
    part = head.shape[0] // QUAD
    for k, out in enumerate(outs):
        out[...] = head[k * part : (k + 1) * part, :].astype(BF16)


def near_kernel(
    t1, i1, t0_far, i0_far, text_head_far, image_head_far,
    q_a, y_a, p_a, x_a, w_aa, t0, i0, text_head, image_head, dots, sems,
):
    half = t0.shape[0]
    copies = [
        pltpu.make_async_copy(source, target, sems.at[n])
        for n, (source, target) in enumerate(
            ((t0_far, t0), (text_head_far, text_head), (i0_far, i0), (image_head_far, image_head))
        )
    ]
    for copy in copies:
        copy.start()
    copies[0].wait()
    copies[1].wait()
    q_a[:half, :] = dot_nn(t0[...], text_head[...])
    q_a[half:, :] = dot_nn(t1[...], text_head[...])
    copies[2].wait()
    copies[3].wait()
    p_a[:half, :] = dot_nn(i0[...], image_head[...])
    unit_rows(q_a, y_a)
    p_a[half:, :] = dot_nn(i1[...], image_head[...])
    unit_rows(p_a, x_a)
    dots[...] = dot_nt(x_a[...], y_a[...])
    weight_rows(dots, w_aa, 0)


def rows_of(refs):
    return jnp.concatenate([ref[...] for ref in refs], axis=0)


def text_kernel(place, *refs):
    *features, t0, t1, i0, i1, text_head, y_a, x_a, w_aa = refs[:-9]
    q_2, y_2, w_a2, gx, gy_a, pick_i, pick_t, dots, near_gx = refs[-9:]
    half = t0.shape[0]
    rows = pick_t.shape[0]
    q_2[...] = dot_nn(rows_of(features), text_head[...])
    near_gx[...] = dot_nn(w_aa[...], y_a[...])
    unit_rows(q_2, y_2)
    dots[...] = dot_nt(x_a[...], y_2[...])
    pick = picker(place, rows, t0.shape[1], (0, 2))
    pick_i[:, :half] = dot_nt(pick, i0[...]).astype(BF16)
    pick_i[:, half:] = dot_nt(pick, i1[...]).astype(BF16)
    weight_rows(dots, w_a2)
    gx[...] = near_gx[...] + dot_nn(w_a2[...], y_2[...])
    pick = picker(place, rows, t0.shape[1], (0,))
    pick_t[:, :half] = dot_nt(pick, t0[...]).astype(BF16)
    pick_t[:, half:] = dot_nt(pick, t1[...]).astype(BF16)
    gy_a[...] = dot_tn(w_aa[...], x_a[...])


def image_kernel(*refs):
    *features, text_head, p_a, x_a, gx_in, pick_i, q_3, y_3, w_a3, dp_a = refs[:-8]
    near_0, near_2, near_sent, far_0, far_1, far_sent, dots, gx = refs[-8:]
    q_3[...] = dot_nn(rows_of(features), text_head[...])
    unit_rows(q_3, y_3)
    dots[...] = dot_nt(x_a[...], y_3[...])
    weight_rows(dots, w_a3)
    gx[...] = gx_in[...] + dot_nn(w_a3[...], y_3[...])
    back_rows(p_a, gx, dp_a)
    head = dot_nn(pick_i[...], dp_a[...]).astype(BF16)
    part = near_0.shape[0]
    near_side, far_side = (
        [head[first : first + part, :] for first in range(side * part, 2 * QUAD * part, 2 * part)]
        for side in range(2)
    )
    near_0[...] = near_side[0]
    near_2[...] = near_side[2]
    near_sent[:part, :] = near_side[1]
    near_sent[part:, :] = near_side[3]
    far_0[...] = far_side[0]
    far_1[...] = far_side[1]
    far_sent[:part, :] = far_side[2]
    far_sent[part:, :] = far_side[3]


def text_pull_kernel(place, *refs):
    *features, x_a, w_a2, w_a3, gy_2, gy_3, pick_t = refs
    gy_2[...] = dot_tn(w_a2[...], x_a[...])
    gy_3[...] = dot_tn(w_a3[...], x_a[...])
    pick = picker(place, pick_t.shape[0], x_a.shape[1], (0,))
    pick_t[...] = dot_nt(pick, rows_of(features)).astype(BF16)


def far_weights(core, x, y_a, y_2, y_3, w_a, w_2, w_3, d_a, d_2, d_3):
    half = x.shape[0]
    middle = half // 2
    d_a[...] = dot_nt(x, y_a[...])
    d_2[...] = dot_nt(x, y_2[...])
    weight_rows(d_a, w_a)
    d_3[...] = dot_nt(x, y_3[...])
    weight_rows(d_2, w_2, core * middle, 0, middle)
    weight_rows(d_2, w_2, None, middle, half)
    weight_rows(d_3, w_3, None, 0, middle)
    weight_rows(d_3, w_3, core * middle, middle, half)


def block_kernel(i2, image_head, y_a, y_2, y_3, x_first, x_second, w_a, w_2, w_3, p_b, x_b, d_a, d_2, d_3):
    middle = x_first.shape[0]
    p_b[...] = dot_nn(i2[...], image_head[...])
    unit_rows(p_b, x_b)
    x_first[...] = x_b[:middle, :]
    x_second[...] = x_b[middle:, :]
    far_weights(0, x_b[...], y_a, y_2, y_3, w_a, w_2, w_3, d_a, d_2, d_3)


def own_pull_kernel(x_first, x_second, w_a, w_2, w_3, gy_a_in, gy_2_in, gy_3_in, gy_a, gy_2, gy_3):
    x = rows_of((x_first, x_second))
    gy_a[...] = gy_a_in[...] + dot_tn(w_a[...], x)
    gy_2[...] = gy_2_in[...] + dot_tn(w_2[...], x)
    gy_3[...] = gy_3_in[...] + dot_tn(w_3[...], x)


def last_kernel(
    x_first, x_second, y_a, y_2, y_3, q_a, q_2, q_3, gy_a_in, gy_2_in, gy_3_in, pick_a, pick_b,
    h0, h1, h2, h3, dq_a, gy_a, gy_2, gy_3, dq_b, near_head, w_a, w_2, w_3, d_a, d_2, d_3,
):
    half = q_2.shape[0]
    x = rows_of((x_first, x_second))
    far_weights(1, x, y_a, y_2, y_3, w_a, w_2, w_3, d_a, d_2, d_3)
    gy_a[...] = gy_a_in[...] + dot_tn(w_a[...], x)
    gy_2[...] = gy_2_in[...] + dot_tn(w_2[...], x)
    back_rows(q_a, gy_a, dq_a)
    gy_3[...] = gy_3_in[...] + dot_tn(w_3[...], x)
    near_head[...] = dot_nn(pick_a[...], dq_a[...])
    back_rows(q_2, gy_2, dq_b, 0)
    back_rows(q_3, gy_3, dq_b, half)
    split_head(near_head[...] + dot_nn(pick_b[...], dq_b[...]), (h0, h1, h2, h3))


def grad_kernel(back, head, out):
    out[...] = dot_nt(back[: out.shape[0], :], head[...])


def place_kernel(place, ks, *refs):
    out, buffer, sems = refs[-3:]
    part = refs[0].shape[0]
    copies = []
    for n, k in enumerate(ks):
        buffer[n] = refs[n][...].astype(F32)
        first = pl.multiple_of((place[1] ^ k) * part, part)
        copies.append(pltpu.make_async_copy(buffer.at[n], out.at[pl.ds(first, part), :], sems.at[n]))
        copies[-1].start()
    for copy in copies:
        copy.wait()


def place_pieces(place, pieces, ks, out=None):
    rows, width = pieces[0].shape
    args = [pltpu.with_memory_space_constraint(a, pltpu.VMEM) for a in pieces]
    specs = [pl.BlockSpec(memory_space=pltpu.SMEM)]
    specs += [pl.BlockSpec(memory_space=pltpu.VMEM)] * len(pieces)
    if out is not None:
        args, specs = args + [out], specs + [pl.BlockSpec(memory_space=pltpu.HBM)]
    return pl.pallas_call(
        lambda place_ref, *refs: place_kernel(place_ref, ks, *refs),
        out_shape=pltpu.HBM((QUAD * rows, width), F32),
        in_specs=specs,
        out_specs=pl.BlockSpec(memory_space=pltpu.HBM),
        scratch_shapes=[
            pltpu.VMEM((len(ks), rows, width), F32), pltpu.SemaphoreType.DMA((len(ks),))
        ],
        input_output_aliases={} if out is None else {len(pieces) + 1: 0},
        compiler_params=pltpu.CompilerParams(vmem_limit_bytes=4 * 1024 * 1024),
        cost_estimate=pl.CostEstimate(flops=0, bytes_accessed=0, transcendentals=0),
    )(place, *args)


def call(kernel, outs, scratch, args, mib, place=None, macs=0, keep=True, far=()):
    far = [pltpu.with_memory_space_constraint(a, pltpu.HBM) for a in far]
    args = [pltpu.with_memory_space_constraint(a, pltpu.VMEM) for a in args] + far
    specs = [pl.BlockSpec(memory_space=pltpu.VMEM)] * (len(args) - len(far))
    specs += [pl.BlockSpec(memory_space=pltpu.HBM)] * len(far)
    if place is not None:
        args, specs = [place, *args], [pl.BlockSpec(memory_space=pltpu.SMEM), *specs]
    shape = pltpu.VMEM if keep else jax.ShapeDtypeStruct
    return pl.pallas_call(
        kernel,
        out_shape=[shape(s, t) for s, t in outs],
        in_specs=specs,
        out_specs=[pl.BlockSpec(memory_space=pltpu.VMEM)] * len(outs),
        scratch_shapes=[pltpu.VMEM(s, t) for s, t in scratch]
        + [pltpu.SemaphoreType.DMA((len(far),))] * bool(far),
        compiler_params=pltpu.CompilerParams(vmem_limit_bytes=mib * 1024 * 1024),
        cost_estimate=pl.CostEstimate(flops=2 * macs, bytes_accessed=0, transcendentals=0),
    )(*args)


def swap(array, axis, size, mask):
    return lax.ppermute(array, axis, [(i, i ^ mask) for i in range(size)])


def after(value, other):
    return lax.optimization_barrier((value, other))[0]


def per_device(n_loop, n_cuts, image_features, text_features, image_head, text_head):
    half, width = image_features.shape
    near = 2 * half
    rows_out = width // n_loop
    part = rows_out // QUAD
    loop = functools.partial(swap, axis="loop", size=n_loop)
    cuts = functools.partial(swap, axis="cuts", size=n_cuts)
    macs = half * width * width

    def both(rows, order, count):
        rows = after(rows, order)
        return [rows] + [loop(piece, mask=1) for piece in jnp.split(rows, count)]

    def add(own, others):
        return sum((other.astype(F32) for other in others), own.astype(F32)).astype(BF16)

    def spread(total):
        return [total] + [cuts(total, mask=k) for k in range(1, QUAD)]

    def placed(pieces):
        out = place_pieces(place, pieces[:-1], tuple(range(QUAD - 1)))
        return place_pieces(place, pieces[-1:], (QUAD - 1,), out)

    t2 = [loop(rows, mask=2) for rows in jnp.split(text_features, 2)]
    i2 = loop(image_features, mask=2)
    place = jnp.stack([lax.axis_index("loop"), lax.axis_index("cuts") & (QUAD - 1)])
    place = place.astype(jnp.int32)
    t0, i0, place = lax.optimization_barrier((text_features, image_features, place))
    t1 = loop(t0, mask=1)
    i1 = loop(i0, mask=1)
    wide, wide_b = ((near, width), F32), ((near, width), BF16)
    tall, tall_b = ((half, width), F32), ((half, width), BF16)
    head_b = ((width, width), BF16)
    block_w, block_dots = ((half, near), BF16), ((half, near), F32)
    side_w, side_dots = ((near, half), BF16), ((near, half), F32)
    pick_one, pick_two = ((rows_out, near), BF16), ((2 * rows_out, near), BF16)
    q_a, y_a, p_a, x_a, w_aa, t0, i0, text_head, image_head = call(
        near_kernel,
        [wide, wide_b, wide, wide_b, ((near, near), BF16), tall_b, tall_b, head_b, head_b],
        [((near, near), F32)],
        (t1, i1),
        8,
        far=(t0, i0, text_head, image_head),
    )
    first = both(t2[0], w_aa, 2)
    q_2, y_2, w_a2, gx, gy_a, pick_i, pick_a = call(
        text_kernel,
        [tall, tall_b, side_w, wide, wide, pick_two, pick_one],
        [side_dots, wide],
        (*first, t0, t1, i0, i1, text_head, y_a, x_a, w_aa),
        8,
        place,
    )
    second = both(t2[1], gy_a, 2)
    part_b, parts_b = ((part, width), BF16), ((2 * part, width), BF16)
    q_3, y_3, w_a3, dp_a, near_0, near_2, near_sent, far_0, far_1, far_sent = call(
        image_kernel,
        [tall, tall_b, side_w, wide_b] + [part_b, part_b, parts_b] * 2,
        [side_dots, wide],
        (*second, text_head, p_a, x_a, gx, pick_i),
        8,
    )
    near_came, far_came = cuts(near_sent, mask=1), cuts(far_sent, mask=2)
    gy_2, gy_3, pick_b = call(
        text_pull_kernel,
        [tall, tall, pick_one],
        [],
        (*first, *second, after(x_a, dp_a), w_a2, w_a3),
        8,
        place,
    )
    middle_b, corner, corner_dots = ((half // 2, width), BF16), ((half, half), BF16), ((half, half), F32)
    *x_2, w_2a, w_22, w_23 = call(
        block_kernel,
        [middle_b, middle_b, block_w, corner, corner],
        [tall, tall_b, block_dots, corner_dots, corner_dots],
        (after(i2, gy_2), image_head, y_a, y_2, y_3),
        8,
    )
    x_3 = [loop(rows, mask=1) for rows in x_2]
    gy_a, gy_2, gy_3 = call(
        own_pull_kernel,
        [wide, tall, tall],
        [],
        (*x_2, w_2a, w_22, w_23, gy_a, gy_2, gy_3),
        8,
    )
    near_came, far_came = after(near_came, gy_a), after(far_came, gy_a)
    near_sent, far_sent = add(near_2, [near_came[part:]]), add(far_1, [far_came[part:]])
    near_last, far_last = cuts(near_sent, mask=2), cuts(far_sent, mask=1)
    x_3 = [after(rows, (gy_a, near_sent, far_sent)) for rows in x_3]
    *text_parts, dq_a = call(
        last_kernel,
        [((part, width), BF16)] * QUAD + [wide_b],
        [wide, tall, tall, wide_b, ((rows_out, width), F32), block_w, corner, corner]
        + [block_dots, corner_dots, corner_dots],
        (*x_3, y_a, y_2, y_3, q_a, q_2, q_3, gy_a, gy_2, gy_3, pick_a, pick_b),
        16,
    )
    text_others = [cuts(text_parts[k], mask=k) for k in range(1, QUAD)]
    far_sum = add(far_0, [far_came[:part], after(far_last, dq_a)])
    near_sum = add(near_0, [near_came[:part], after(near_last, dq_a)])
    image_sum = add(near_sum, [loop(far_sum, mask=2)])
    grads = [
        call(grad_kernel, [tall], [], (after(back, image_sum), head), 4, macs=2 * macs, keep=False)[0]
        for back, head in ((dp_a, image_head), (dq_a, text_head))
    ]
    text_sum = add(text_parts[0], [after(other, image_sum) for other in text_others])
    image_sum = add(image_sum, [after(cuts(image_sum, mask=QUAD), grads)])
    image_pieces = spread(image_sum)
    text_sum = add(text_sum, [after(cuts(text_sum, mask=QUAD), image_pieces[1])])
    image_out = placed(image_pieces)
    text_out = placed(spread(text_sum))
    return (*grads, image_out, text_out)


def solution(mesh):
    n_loop, n_cuts = mesh.shape["loop"], mesh.shape["cuts"]
    if n_loop == 4 and n_cuts == 2 * QUAD:
        body = functools.partial(per_device, n_loop, n_cuts)
    else:
        body = plain_device
    placed = (P(("cuts", "loop"), None), P(("cuts", "loop"), None), P(), P())
    return jax.shard_map(
        body,
        mesh=mesh,
        in_specs=placed,
        out_specs=(
            P(("cuts", "loop"), None),
            P(("cuts", "loop"), None),
            P("loop", None),
            P("loop", None),
        ),
        check_vma=False,
    )
```

```python
import functools

import jax
import jax.numpy as jnp
from jax import lax
from jax.experimental import pallas as pl
from jax.experimental.pallas import tpu as pltpu
from jax.sharding import PartitionSpec as P

SCORE_SCALE = 10.0
SCORE_BIAS = -2.5
EPSILON = 1e-06
QUAD = 4
STRIP = 16
LANES = 128
F32 = jnp.float32
BF16 = jnp.bfloat16


def normalize(features, weight_matrix):
    projected = jnp.dot(features, weight_matrix, preferred_element_type=jnp.float32)
    factor = lax.rsqrt(jnp.sum(projected * projected, axis=-1, keepdims=True) + EPSILON)
    return (projected * factor, factor)


def pair_weights(image_vectors, text_vectors, image_offset):
    pair_scores = SCORE_SCALE * dot_nt(image_vectors, text_vectors) + SCORE_BIAS
    row_ids = image_offset + lax.broadcasted_iota(jnp.int32, pair_scores.shape, 0)
    col_ids = lax.broadcasted_iota(jnp.int32, pair_scores.shape, 1)
    match_targets = jnp.where(row_ids == col_ids, 1.0, -1.0).astype(jnp.float32)
    return (SCORE_SCALE * -match_targets * jax.nn.sigmoid(-match_targets * pair_scores)).astype(
        jnp.bfloat16
    )


def norm_back(unit, factor, gradient):
    return (factor * (gradient - unit * jnp.sum(unit * gradient, axis=-1, keepdims=True))).astype(
        jnp.bfloat16
    )


def dot_nn(left, right):
    return lax.dot_general(left, right, (((1,), (0,)), ((), ())), preferred_element_type=F32)


def dot_nt(left, right):
    return lax.dot_general(left, right, (((1,), (1,)), ((), ())), preferred_element_type=F32)


def dot_tn(left, right):
    return lax.dot_general(left, right, (((0,), (0,)), ((), ())), preferred_element_type=F32)


def plain_device(image_features, text_features, image_head, text_head):
    row_count = image_features.shape[0]
    own_start = lax.axis_index("loop") * row_count
    image_unit, image_factor = normalize(image_features, image_head)
    text_unit, text_factor = normalize(text_features, text_head)
    image_vectors = image_unit.astype(jnp.bfloat16)
    text_vectors = text_unit.astype(jnp.bfloat16)
    arrived = lax.all_gather(text_vectors, "loop", axis=0, tiled=True)
    weights = pair_weights(image_vectors, arrived, own_start)
    summed = jnp.dot(weights, arrived, preferred_element_type=jnp.float32)
    text_attraction = lax.psum_scatter(
        dot_tn(weights, image_vectors).astype(jnp.bfloat16), "loop", scatter_dimension=0, tiled=True
    ).astype(jnp.float32)
    image_back = norm_back(image_unit, image_factor, summed)
    text_back = norm_back(text_unit, text_factor, text_attraction)
    heads = []
    for features, back in ((image_features, image_back), (text_features, text_back)):
        term = dot_tn(features, back).astype(jnp.bfloat16)
        part = lax.psum_scatter(term, "loop", scatter_dimension=0, tiled=True)
        heads.append(lax.psum(part, "cuts").astype(jnp.float32))
    return (dot_nt(image_back, image_head), dot_nt(text_back, text_head), heads[0], heads[1])


def factor_of(ref, rows):
    p = ref[rows, :]
    return lax.rsqrt(jnp.sum(p * p, axis=-1, keepdims=True) + EPSILON)


def unit_rows(projected_ref, vectors_ref):
    for first in range(0, projected_ref.shape[0], STRIP):
        rows = slice(first, first + STRIP)
        factor = factor_of(projected_ref, rows)
        vectors_ref[rows, :] = (projected_ref[rows, :] * factor).astype(BF16)


def back_rows(projected_ref, gradient_ref, back_ref, at=0):
    for first in range(0, projected_ref.shape[0], STRIP):
        rows = slice(first, first + STRIP)
        factor = factor_of(projected_ref, rows)
        along = jnp.sum(projected_ref[rows, :] * gradient_ref[rows, :], axis=-1, keepdims=True)
        along = factor * factor * factor * along
        back = factor * gradient_ref[rows, :] - along * projected_ref[rows, :]
        back_ref[at + first : at + first + STRIP, :] = back.astype(BF16)


def weight_rows(dots_ref, weights_ref, pairs_from=None, begin=0, end=None):
    half_scale = 0.5 * SCORE_SCALE
    for first in range(begin, dots_ref.shape[0] if end is None else end, STRIP):
        rows = slice(first, first + STRIP)
        score = jnp.tanh(half_scale * dots_ref[rows, :] + 0.5 * SCORE_BIAS)
        weights = half_scale + half_scale * score
        if pairs_from is None:
            weights_ref[rows, :] = weights.astype(BF16)
            continue
        pair = pairs_from + first - begin
        left = pair // LANES * LANES
        right = min(left + LANES, weights.shape[1])
        shape = (STRIP, right - left)
        column = lax.broadcasted_iota(jnp.int32, shape, 1)
        same = column == lax.broadcasted_iota(jnp.int32, shape, 0) + (pair - left)
        middle = weights[:, left:right] - jnp.where(same, SCORE_SCALE, 0.0)
        pieces = [weights[:, :left], middle, weights[:, right:]]
        weights = jnp.concatenate([p for p in pieces if p.shape[1]], axis=1)
        weights_ref[rows, :] = weights.astype(BF16)


def one_hot(first, rows, width):
    wanted = first + lax.broadcasted_iota(jnp.int32, (rows, width), 0)
    column = lax.broadcasted_iota(jnp.int32, (rows, width), 1)
    return jnp.where(wanted == column, 1.0, 0.0)


def picker(place_ref, rows, width, sides):
    part = rows // QUAD
    pieces = []
    for k in range(QUAD):
        for side in sides:
            first = (place_ref[0] ^ side) * rows + (place_ref[1] ^ k) * part
            pieces.append(one_hot(first, part, width))
    return jnp.concatenate(pieces, axis=0).astype(BF16)


def split_head(head, outs):
    part = head.shape[0] // QUAD
    for k, out in enumerate(outs):
        out[...] = head[k * part : (k + 1) * part, :].astype(BF16)


def near_kernel(
    t1, i1, t0_far, i0_far, text_head_far, image_head_far,
    q_a, y_a, p_a, x_a, w_aa, gx, t0, i0, text_head, image_head, dots, sems,
):
    half = t0.shape[0]
    copies = [
        pltpu.make_async_copy(source, target, sems.at[n])
        for n, (source, target) in enumerate(
            ((t0_far, t0), (text_head_far, text_head), (i0_far, i0), (image_head_far, image_head))
        )
    ]
    for copy in copies:
        copy.start()
    copies[0].wait()
    copies[1].wait()
    q_a[:half, :] = dot_nn(t0[...], text_head[...])
    q_a[half:, :] = dot_nn(t1[...], text_head[...])
    copies[2].wait()
    copies[3].wait()
    p_a[:half, :] = dot_nn(i0[...], image_head[...])
    unit_rows(q_a, y_a)
    p_a[half:, :] = dot_nn(i1[...], image_head[...])
    unit_rows(p_a, x_a)
    dots[...] = dot_nt(x_a[...], y_a[...])
    weight_rows(dots, w_aa, 0)
    gx[...] = dot_nn(w_aa[...], y_a[...])


def rows_of(refs):
    return jnp.concatenate([ref[...] for ref in refs], axis=0)


def text_kernel(place, *refs):
    *features, i0, i1, text_head, gx_in, x_a, w_aa = refs[:-7]
    q_2, y_2, w_a2, gx, gy_a, pick_i, dots = refs[-7:]
    half, width = i0.shape
    q_2[...] = dot_nn(rows_of(features), text_head[...])
    pick = picker(place, pick_i.shape[0] // 2, width, (0, 2))
    unit_rows(q_2, y_2)
    dots[...] = dot_nt(x_a[...], y_2[...])
    pick_i[:, :half] = dot_nt(pick, i0[...]).astype(BF16)
    pick_i[:, half:] = dot_nt(pick, i1[...]).astype(BF16)
    weight_rows(dots, w_a2)
    gx[...] = gx_in[...] + dot_nn(w_a2[...], y_2[...])
    gy_a[...] = dot_tn(w_aa[...], x_a[...])


def image_kernel(*refs):
    *features, text_head, p_a, x_a, gx_in, pick_i, q_3, y_3, w_a3, dp_a = refs[:-8]
    near_0, near_2, near_sent, far_0, far_1, far_sent, dots, gx = refs[-8:]
    q_3[...] = dot_nn(rows_of(features), text_head[...])
    unit_rows(q_3, y_3)
    dots[...] = dot_nt(x_a[...], y_3[...])
    weight_rows(dots, w_a3)
    gx[...] = gx_in[...] + dot_nn(w_a3[...], y_3[...])
    back_rows(p_a, gx, dp_a)
    head = dot_nn(pick_i[...], dp_a[...]).astype(BF16)
    part = near_0.shape[0]
    near_side, far_side = (
        [head[first : first + part, :] for first in range(side * part, 2 * QUAD * part, 2 * part)]
        for side in range(2)
    )
    near_0[...] = near_side[0]
    near_2[...] = near_side[2]
    near_sent[:part, :] = near_side[1]
    near_sent[part:, :] = near_side[3]
    far_0[...] = far_side[0]
    far_1[...] = far_side[1]
    far_sent[:part, :] = far_side[2]
    far_sent[part:, :] = far_side[3]


def text_pull_kernel(place, *refs):
    *features, t0, t1, x_a, w_a2, w_a3, gy_2, gy_3, pick_a, pick_b = refs
    half = t0.shape[0]
    gy_2[...] = dot_tn(w_a2[...], x_a[...])
    gy_3[...] = dot_tn(w_a3[...], x_a[...])
    pick = picker(place, pick_a.shape[0], t0.shape[1], (0,))
    pick_a[:, :half] = dot_nt(pick, t0[...]).astype(BF16)
    pick_a[:, half:] = dot_nt(pick, t1[...]).astype(BF16)
    pick_b[...] = dot_nt(pick, rows_of(features)).astype(BF16)


def far_weights(core, x, y_a, y_2, y_3, w_a, w_2, w_3, d_a, d_2, d_3):
    half = x.shape[0]
    middle = half // 2
    d_a[...] = dot_nt(x, y_a[...])
    d_2[...] = dot_nt(x, y_2[...])
    weight_rows(d_a, w_a)
    d_3[...] = dot_nt(x, y_3[...])
    weight_rows(d_2, w_2, core * middle, 0, middle)
    weight_rows(d_2, w_2, None, middle, half)
    weight_rows(d_3, w_3, None, 0, middle)
    weight_rows(d_3, w_3, core * middle, middle, half)


def block_kernel(i2, image_head, y_a, y_2, y_3, x_first, x_second, w_a, w_2, w_3, p_b, x_b, d_a, d_2, d_3):
    middle = x_first.shape[0]
    p_b[...] = dot_nn(i2[...], image_head[...])
    unit_rows(p_b, x_b)
    x_first[...] = x_b[:middle, :]
    x_second[...] = x_b[middle:, :]
    far_weights(0, x_b[...], y_a, y_2, y_3, w_a, w_2, w_3, d_a, d_2, d_3)


def own_pull_kernel(x_first, x_second, w_a, w_2, w_3, gy_a_in, gy_2_in, gy_3_in, gy_a, gy_2, gy_3):
    x = rows_of((x_first, x_second))
    gy_a[...] = gy_a_in[...] + dot_tn(w_a[...], x)
    gy_2[...] = gy_2_in[...] + dot_tn(w_2[...], x)
    gy_3[...] = gy_3_in[...] + dot_tn(w_3[...], x)


def last_kernel(
    x_first, x_second, y_a, y_2, y_3, q_a, q_2, q_3, gy_a_in, gy_2_in, gy_3_in, pick_a, pick_b,
    h0, h1, h2, h3, dq_a, gy_a, gy_2, gy_3, dq_b, near_head, w_a, w_2, w_3, d_a, d_2, d_3,
):
    half = q_2.shape[0]
    x = rows_of((x_first, x_second))
    far_weights(1, x, y_a, y_2, y_3, w_a, w_2, w_3, d_a, d_2, d_3)
    gy_a[...] = gy_a_in[...] + dot_tn(w_a[...], x)
    gy_2[...] = gy_2_in[...] + dot_tn(w_2[...], x)
    back_rows(q_a, gy_a, dq_a)
    gy_3[...] = gy_3_in[...] + dot_tn(w_3[...], x)
    near_head[...] = dot_nn(pick_a[...], dq_a[...])
    back_rows(q_2, gy_2, dq_b, 0)
    back_rows(q_3, gy_3, dq_b, half)
    split_head(near_head[...] + dot_nn(pick_b[...], dq_b[...]), (h0, h1, h2, h3))


def grad_kernel(back, head, out):
    out[...] = dot_nt(back[: out.shape[0], :], head[...])


def place_kernel(place, *refs):
    *pieces, out, buffer, sems = refs
    part = pieces[0].shape[0]
    copies = []
    for k, piece in enumerate(pieces):
        buffer[k] = piece[...].astype(F32)
        first = pl.multiple_of((place[1] ^ k) * part, part)
        copies.append(pltpu.make_async_copy(buffer.at[k], out.at[pl.ds(first, part), :], sems.at[k]))
        copies[-1].start()
    for copy in copies:
        copy.wait()


def placed(place, last_row, pieces):
    rows, width = pieces[0].shape
    *early, last = pieces
    out = pl.pallas_call(
        place_kernel,
        out_shape=pltpu.HBM((QUAD * rows, width), F32),
        in_specs=[pl.BlockSpec(memory_space=pltpu.SMEM)]
        + [pl.BlockSpec(memory_space=pltpu.VMEM)] * len(early),
        out_specs=pl.BlockSpec(memory_space=pltpu.HBM),
        scratch_shapes=[
            pltpu.VMEM((len(early), rows, width), F32), pltpu.SemaphoreType.DMA((len(early),))
        ],
        compiler_params=pltpu.CompilerParams(vmem_limit_bytes=4 * 1024 * 1024),
        cost_estimate=pl.CostEstimate(flops=0, bytes_accessed=0, transcendentals=0),
    )(place, *(pltpu.with_memory_space_constraint(a, pltpu.VMEM) for a in early))
    last = after(last, out)
    return lax.dynamic_update_slice(out, last.astype(F32), (last_row, 0), allow_negative_indices=False)


def call(kernel, outs, scratch, args, mib, place=None, macs=0, keep=True, far=()):
    far = [pltpu.with_memory_space_constraint(a, pltpu.HBM) for a in far]
    args = [pltpu.with_memory_space_constraint(a, pltpu.VMEM) for a in args] + far
    specs = [pl.BlockSpec(memory_space=pltpu.VMEM)] * (len(args) - len(far))
    specs += [pl.BlockSpec(memory_space=pltpu.HBM)] * len(far)
    if place is not None:
        args, specs = [place, *args], [pl.BlockSpec(memory_space=pltpu.SMEM), *specs]
    shape = pltpu.VMEM if keep else jax.ShapeDtypeStruct
    return pl.pallas_call(
        kernel,
        out_shape=[shape(s, t) for s, t in outs],
        in_specs=specs,
        out_specs=[pl.BlockSpec(memory_space=pltpu.VMEM)] * len(outs),
        scratch_shapes=[pltpu.VMEM(s, t) for s, t in scratch]
        + [pltpu.SemaphoreType.DMA((len(far),))] * bool(far),
        compiler_params=pltpu.CompilerParams(vmem_limit_bytes=mib * 1024 * 1024),
        cost_estimate=pl.CostEstimate(flops=2 * macs, bytes_accessed=0, transcendentals=0),
    )(*args)


def swap(array, axis, size, mask):
    return lax.ppermute(array, axis, [(i, i ^ mask) for i in range(size)])


def after(value, other):
    return lax.optimization_barrier((value, other))[0]


def per_device(n_loop, n_cuts, image_features, text_features, image_head, text_head):
    half, width = image_features.shape
    near = 2 * half
    rows_out = width // n_loop
    part = rows_out // QUAD
    loop = functools.partial(swap, axis="loop", size=n_loop)
    cuts = functools.partial(swap, axis="cuts", size=n_cuts)
    macs = half * width * width

    def both(rows, order, count):
        rows = after(rows, order)
        return [rows] + [loop(piece, mask=1) for piece in jnp.split(rows, count)]

    def add(own, others):
        return sum((other.astype(F32) for other in others), own.astype(F32)).astype(BF16)

    def spread(total):
        return [total] + [cuts(total, mask=k) for k in range(1, QUAD)]

    t2 = [loop(rows, mask=2) for rows in jnp.split(text_features, 2)]
    i2 = loop(image_features, mask=2)
    place = jnp.stack([lax.axis_index("loop"), lax.axis_index("cuts") & (QUAD - 1)])
    last_row = ((place[1] ^ (QUAD - 1)) * part).astype(jnp.int32)
    place = place.astype(jnp.int32)
    t0, i0, place, last_row = lax.optimization_barrier(
        (text_features, image_features, place, last_row)
    )
    t1 = loop(t0, mask=1)
    i1 = loop(i0, mask=1)
    wide, wide_b = ((near, width), F32), ((near, width), BF16)
    tall, tall_b = ((half, width), F32), ((half, width), BF16)
    head_b = ((width, width), BF16)
    block_w, block_dots = ((half, near), BF16), ((half, near), F32)
    side_w, side_dots = ((near, half), BF16), ((near, half), F32)
    pick_one, pick_two = ((rows_out, near), BF16), ((2 * rows_out, near), BF16)
    q_a, y_a, p_a, x_a, w_aa, gx, t0, i0, text_head, image_head = call(
        near_kernel,
        [wide, wide_b, wide, wide_b, ((near, near), BF16), wide, tall_b, tall_b, head_b, head_b],
        [((near, near), F32)],
        (t1, i1),
        8,
        far=(t0, i0, text_head, image_head),
    )
    first = both(t2[0], w_aa, 2)
    q_2, y_2, w_a2, gx, gy_a, pick_i = call(
        text_kernel,
        [tall, tall_b, side_w, wide, wide, pick_two],
        [side_dots],
        (*first, i0, i1, text_head, gx, x_a, w_aa),
        8,
        place,
    )
    second = both(t2[1], gy_a, 2)
    part_b, parts_b = ((part, width), BF16), ((2 * part, width), BF16)
    q_3, y_3, w_a3, dp_a, near_0, near_2, near_sent, far_0, far_1, far_sent = call(
        image_kernel,
        [tall, tall_b, side_w, wide_b] + [part_b, part_b, parts_b] * 2,
        [side_dots, wide],
        (*second, text_head, p_a, x_a, gx, pick_i),
        8,
    )
    near_came, far_came = cuts(near_sent, mask=1), cuts(far_sent, mask=2)
    gy_2, gy_3, pick_a, pick_b = call(
        text_pull_kernel,
        [tall, tall, pick_one, pick_one],
        [],
        (*first, *second, t0, t1, after(x_a, dp_a), w_a2, w_a3),
        8,
        place,
    )
    middle_b, corner, corner_dots = ((half // 2, width), BF16), ((half, half), BF16), ((half, half), F32)
    *x_2, w_2a, w_22, w_23 = call(
        block_kernel,
        [middle_b, middle_b, block_w, corner, corner],
        [tall, tall_b, block_dots, corner_dots, corner_dots],
        (after(i2, gy_2), image_head, y_a, y_2, y_3),
        8,
    )
    x_3 = [loop(rows, mask=1) for rows in x_2]
    gy_a, gy_2, gy_3 = call(
        own_pull_kernel,
        [wide, tall, tall],
        [],
        (*x_2, w_2a, w_22, w_23, gy_a, gy_2, gy_3),
        8,
    )
    near_came, far_came = after(near_came, gy_a), after(far_came, gy_a)
    near_sent, far_sent = add(near_2, [near_came[part:]]), add(far_1, [far_came[part:]])
    near_last, far_last = cuts(near_sent, mask=2), cuts(far_sent, mask=1)
    x_3 = [after(rows, (gy_a, near_sent, far_sent)) for rows in x_3]
    *text_parts, dq_a = call(
        last_kernel,
        [((part, width), BF16)] * QUAD + [wide_b],
        [wide, tall, tall, wide_b, ((rows_out, width), F32), block_w, corner, corner]
        + [block_dots, corner_dots, corner_dots],
        (*x_3, y_a, y_2, y_3, q_a, q_2, q_3, gy_a, gy_2, gy_3, pick_a, pick_b),
        16,
    )
    text_others = [cuts(text_parts[k], mask=k) for k in range(1, QUAD)]
    far_sum = add(far_0, [far_came[:part], after(far_last, dq_a)])
    near_sum = add(near_0, [near_came[:part], after(near_last, dq_a)])
    image_sum = add(near_sum, [loop(far_sum, mask=2)])
    grads = [
        call(grad_kernel, [tall], [], (after(back, image_sum), head), 4, macs=2 * macs, keep=False)[0]
        for back, head in ((dp_a, image_head), (dq_a, text_head))
    ]
    text_sum = add(text_parts[0], [after(other, (image_sum, grads)) for other in text_others])
    image_sum = add(image_sum, [cuts(image_sum, mask=QUAD)])
    image_pieces = spread(image_sum)
    text_sum = add(text_sum, [after(cuts(text_sum, mask=QUAD), image_pieces[1])])
    image_out = placed(place, last_row, image_pieces)
    text_out = placed(place, last_row, spread(text_sum))
    return (*grads, image_out, text_out)


def solution(mesh):
    n_loop, n_cuts = mesh.shape["loop"], mesh.shape["cuts"]
    if n_loop == 4 and n_cuts == 2 * QUAD:
        body = functools.partial(per_device, n_loop, n_cuts)
    else:
        body = plain_device
    placed = (P(("cuts", "loop"), None), P(("cuts", "loop"), None), P(), P())
    return jax.shard_map(
        body,
        mesh=mesh,
        in_specs=placed,
        out_specs=(
            P(("cuts", "loop"), None),
            P(("cuts", "loop"), None),
            P("loop", None),
            P("loop", None),
        ),
        check_vma=False,
    )
```

```python
import functools

import jax
import jax.numpy as jnp
from jax import lax
from jax.experimental import pallas as pl
from jax.experimental.pallas import tpu as pltpu
from jax.sharding import PartitionSpec as P

SCORE_SCALE = 10.0
SCORE_BIAS = -2.5
EPSILON = 1e-06
QUAD = 4
STRIP = 16
LANES = 128
F32 = jnp.float32
BF16 = jnp.bfloat16


def normalize(features, weight_matrix):
    projected = jnp.dot(features, weight_matrix, preferred_element_type=jnp.float32)
    factor = lax.rsqrt(jnp.sum(projected * projected, axis=-1, keepdims=True) + EPSILON)
    return (projected * factor, factor)


def pair_weights(image_vectors, text_vectors, image_offset):
    pair_scores = SCORE_SCALE * dot_nt(image_vectors, text_vectors) + SCORE_BIAS
    row_ids = image_offset + lax.broadcasted_iota(jnp.int32, pair_scores.shape, 0)
    col_ids = lax.broadcasted_iota(jnp.int32, pair_scores.shape, 1)
    match_targets = jnp.where(row_ids == col_ids, 1.0, -1.0).astype(jnp.float32)
    return (SCORE_SCALE * -match_targets * jax.nn.sigmoid(-match_targets * pair_scores)).astype(
        jnp.bfloat16
    )


def norm_back(unit, factor, gradient):
    return (factor * (gradient - unit * jnp.sum(unit * gradient, axis=-1, keepdims=True))).astype(
        jnp.bfloat16
    )


def dot_nn(left, right):
    return lax.dot_general(left, right, (((1,), (0,)), ((), ())), preferred_element_type=F32)


def dot_nt(left, right):
    return lax.dot_general(left, right, (((1,), (1,)), ((), ())), preferred_element_type=F32)


def dot_tn(left, right):
    return lax.dot_general(left, right, (((0,), (0,)), ((), ())), preferred_element_type=F32)


def plain_device(image_features, text_features, image_head, text_head):
    row_count = image_features.shape[0]
    own_start = lax.axis_index("loop") * row_count
    image_unit, image_factor = normalize(image_features, image_head)
    text_unit, text_factor = normalize(text_features, text_head)
    image_vectors = image_unit.astype(jnp.bfloat16)
    text_vectors = text_unit.astype(jnp.bfloat16)
    arrived = lax.all_gather(text_vectors, "loop", axis=0, tiled=True)
    weights = pair_weights(image_vectors, arrived, own_start)
    summed = jnp.dot(weights, arrived, preferred_element_type=jnp.float32)
    text_attraction = lax.psum_scatter(
        dot_tn(weights, image_vectors).astype(jnp.bfloat16), "loop", scatter_dimension=0, tiled=True
    ).astype(jnp.float32)
    image_back = norm_back(image_unit, image_factor, summed)
    text_back = norm_back(text_unit, text_factor, text_attraction)
    heads = []
    for features, back in ((image_features, image_back), (text_features, text_back)):
        term = dot_tn(features, back).astype(jnp.bfloat16)
        part = lax.psum_scatter(term, "loop", scatter_dimension=0, tiled=True)
        heads.append(lax.psum(part, "cuts").astype(jnp.float32))
    return (dot_nt(image_back, image_head), dot_nt(text_back, text_head), heads[0], heads[1])


def factor_of(ref, rows):
    p = ref[rows, :]
    return lax.rsqrt(jnp.sum(p * p, axis=-1, keepdims=True) + EPSILON)


def unit_rows(projected_ref, vectors_ref):
    for first in range(0, projected_ref.shape[0], STRIP):
        rows = slice(first, first + STRIP)
        factor = factor_of(projected_ref, rows)
        vectors_ref[rows, :] = (projected_ref[rows, :] * factor).astype(BF16)


def back_rows(projected_ref, gradient_ref, back_ref, at=0):
    for first in range(0, projected_ref.shape[0], STRIP):
        rows = slice(first, first + STRIP)
        factor = factor_of(projected_ref, rows)
        along = jnp.sum(projected_ref[rows, :] * gradient_ref[rows, :], axis=-1, keepdims=True)
        along = factor * factor * factor * along
        back = factor * gradient_ref[rows, :] - along * projected_ref[rows, :]
        back_ref[at + first : at + first + STRIP, :] = back.astype(BF16)


def weight_rows(dots_ref, weights_ref, pairs_from=None, begin=0, end=None):
    half_scale = 0.5 * SCORE_SCALE
    for first in range(begin, dots_ref.shape[0] if end is None else end, STRIP):
        rows = slice(first, first + STRIP)
        score = jnp.tanh(half_scale * dots_ref[rows, :] + 0.5 * SCORE_BIAS)
        weights = half_scale + half_scale * score
        if pairs_from is None:
            weights_ref[rows, :] = weights.astype(BF16)
            continue
        pair = pairs_from + first - begin
        left = pair // LANES * LANES
        right = min(left + LANES, weights.shape[1])
        shape = (STRIP, right - left)
        column = lax.broadcasted_iota(jnp.int32, shape, 1)
        same = column == lax.broadcasted_iota(jnp.int32, shape, 0) + (pair - left)
        middle = weights[:, left:right] - jnp.where(same, SCORE_SCALE, 0.0)
        pieces = [weights[:, :left], middle, weights[:, right:]]
        weights = jnp.concatenate([p for p in pieces if p.shape[1]], axis=1)
        weights_ref[rows, :] = weights.astype(BF16)


def one_hot(first, rows, width):
    wanted = first + lax.broadcasted_iota(jnp.int32, (rows, width), 0)
    column = lax.broadcasted_iota(jnp.int32, (rows, width), 1)
    return jnp.where(wanted == column, 1.0, 0.0)


def picker(place_ref, rows, width, sides):
    part = rows // QUAD
    pieces = []
    for k in range(QUAD):
        for side in sides:
            first = (place_ref[0] ^ side) * rows + (place_ref[1] ^ k) * part
            pieces.append(one_hot(first, part, width))
    return jnp.concatenate(pieces, axis=0).astype(BF16)


def split_head(head, outs):
    part = head.shape[0] // QUAD
    for k, out in enumerate(outs):
        out[...] = head[k * part : (k + 1) * part, :].astype(BF16)


def near_kernel(
    t1, i1, t0_far, i0_far, text_head_far, image_head_far,
    q_a, y_a, p_a, x_a, w_aa, gx, t0, i0, text_head, image_head, dots, sems,
):
    copies = [
        pltpu.make_async_copy(source, target, sems.at[n])
        for n, (source, target) in enumerate(
            ((t0_far, t0), (text_head_far, text_head), (i0_far, i0), (image_head_far, image_head))
        )
    ]
    for copy in copies:
        copy.start()
    copies[0].wait()
    copies[1].wait()
    q_a[...] = dot_nn(rows_of((t0, t1)), text_head[...])
    copies[2].wait()
    copies[3].wait()
    p_a[...] = dot_nn(rows_of((i0, i1)), image_head[...])
    unit_rows(q_a, y_a)
    unit_rows(p_a, x_a)
    dots[...] = dot_nt(x_a[...], y_a[...])
    weight_rows(dots, w_aa, 0)
    gx[...] = dot_nn(w_aa[...], y_a[...])


def rows_of(refs):
    return jnp.concatenate([ref[...] for ref in refs], axis=0)


def text_kernel(place, *refs):
    *features, i0, i1, text_head, gx_in, x_a, w_aa = refs[:-7]
    q_2, y_2, w_a2, gx, gy_a, pick_i, dots = refs[-7:]
    half, width = i0.shape
    q_2[...] = dot_nn(rows_of(features), text_head[...])
    pick = picker(place, pick_i.shape[0] // 2, width, (0, 2))
    unit_rows(q_2, y_2)
    dots[...] = dot_nt(x_a[...], y_2[...])
    pick_i[:, :half] = dot_nt(pick, i0[...]).astype(BF16)
    pick_i[:, half:] = dot_nt(pick, i1[...]).astype(BF16)
    weight_rows(dots, w_a2)
    gx[...] = gx_in[...] + dot_nn(w_a2[...], y_2[...])
    gy_a[...] = dot_tn(w_aa[...], x_a[...])


def image_kernel(*refs):
    *features, text_head, p_a, x_a, gx_in, pick_i, q_3, y_3, w_a3, dp_a = refs[:-8]
    near_0, near_2, near_sent, far_0, far_1, far_sent, dots, gx = refs[-8:]
    q_3[...] = dot_nn(rows_of(features), text_head[...])
    unit_rows(q_3, y_3)
    dots[...] = dot_nt(x_a[...], y_3[...])
    weight_rows(dots, w_a3)
    gx[...] = gx_in[...] + dot_nn(w_a3[...], y_3[...])
    back_rows(p_a, gx, dp_a)
    head = dot_nn(pick_i[...], dp_a[...]).astype(BF16)
    part = near_0.shape[0]
    near_side, far_side = (
        [head[first : first + part, :] for first in range(side * part, 2 * QUAD * part, 2 * part)]
        for side in range(2)
    )
    near_0[...] = near_side[0]
    near_2[...] = near_side[2]
    near_sent[:part, :] = near_side[1]
    near_sent[part:, :] = near_side[3]
    far_0[...] = far_side[0]
    far_1[...] = far_side[1]
    far_sent[:part, :] = far_side[2]
    far_sent[part:, :] = far_side[3]


def text_pull_kernel(place, *refs):
    *features, t0, t1, x_a, w_a2, w_a3, gy_2, gy_3, pick_a, pick_b = refs
    half = t0.shape[0]
    gy_2[...] = dot_tn(w_a2[...], x_a[...])
    gy_3[...] = dot_tn(w_a3[...], x_a[...])
    pick = picker(place, pick_a.shape[0], t0.shape[1], (0,))
    pick_a[:, :half] = dot_nt(pick, t0[...]).astype(BF16)
    pick_a[:, half:] = dot_nt(pick, t1[...]).astype(BF16)
    pick_b[...] = dot_nt(pick, rows_of(features)).astype(BF16)


def far_weights(core, x, y_a, y_2, y_3, w_a, w_2, w_3, d_a, d_2, d_3):
    half = x.shape[0]
    middle = half // 2
    d_a[...] = dot_nt(x, y_a[...])
    d_2[...] = dot_nt(x, y_2[...])
    weight_rows(d_a, w_a)
    d_3[...] = dot_nt(x, y_3[...])
    weight_rows(d_2, w_2, core * middle, 0, middle)
    weight_rows(d_2, w_2, None, middle, half)
    weight_rows(d_3, w_3, None, 0, middle)
    weight_rows(d_3, w_3, core * middle, middle, half)


def block_kernel(i2, image_head, y_a, y_2, y_3, x_first, x_second, w_a, w_2, w_3, p_b, x_b, d_a, d_2, d_3):
    middle = x_first.shape[0]
    p_b[...] = dot_nn(i2[...], image_head[...])
    unit_rows(p_b, x_b)
    x_first[...] = x_b[:middle, :]
    x_second[...] = x_b[middle:, :]
    far_weights(0, x_b[...], y_a, y_2, y_3, w_a, w_2, w_3, d_a, d_2, d_3)


def own_pull_kernel(x_first, x_second, w_a, w_2, w_3, gy_a_in, gy_2_in, gy_3_in, gy_a, gy_2, gy_3):
    x = rows_of((x_first, x_second))
    gy_a[...] = gy_a_in[...] + dot_tn(w_a[...], x)
    gy_2[...] = gy_2_in[...] + dot_tn(w_2[...], x)
    gy_3[...] = gy_3_in[...] + dot_tn(w_3[...], x)


def last_kernel(
    x_first, x_second, y_a, y_2, y_3, q_a, q_2, q_3, gy_a_in, gy_2_in, gy_3_in, pick_a, pick_b,
    h0, h1, h2, h3, dq_a, gy_a, gy_2, gy_3, dq_b, near_head, w_a, w_2, w_3, d_a, d_2, d_3,
):
    half = q_2.shape[0]
    x = rows_of((x_first, x_second))
    far_weights(1, x, y_a, y_2, y_3, w_a, w_2, w_3, d_a, d_2, d_3)
    gy_a[...] = gy_a_in[...] + dot_tn(w_a[...], x)
    gy_2[...] = gy_2_in[...] + dot_tn(w_2[...], x)
    back_rows(q_a, gy_a, dq_a)
    gy_3[...] = gy_3_in[...] + dot_tn(w_3[...], x)
    near_head[...] = dot_nn(pick_a[...], dq_a[...])
    back_rows(q_2, gy_2, dq_b, 0)
    back_rows(q_3, gy_3, dq_b, half)
    split_head(near_head[...] + dot_nn(pick_b[...], dq_b[...]), (h0, h1, h2, h3))


def grad_kernel(back, head, out):
    out[...] = dot_nt(back[: out.shape[0], :], head[...])


def place_kernel(place, *refs):
    *pieces, out = refs
    part = pieces[0].shape[0]
    for k, piece in enumerate(pieces):
        first = pl.multiple_of((place[1] ^ k) * part, part)
        out[pl.ds(first, part), :] = piece[...].astype(F32)


def call(kernel, outs, scratch, args, mib, place=None, macs=0, keep=True, far=()):
    far = [pltpu.with_memory_space_constraint(a, pltpu.HBM) for a in far]
    args = [pltpu.with_memory_space_constraint(a, pltpu.VMEM) for a in args] + far
    specs = [pl.BlockSpec(memory_space=pltpu.VMEM)] * (len(args) - len(far))
    specs += [pl.BlockSpec(memory_space=pltpu.HBM)] * len(far)
    if place is not None:
        args, specs = [place, *args], [pl.BlockSpec(memory_space=pltpu.SMEM), *specs]
    shape = pltpu.VMEM if keep else jax.ShapeDtypeStruct
    return pl.pallas_call(
        kernel,
        out_shape=[shape(s, t) for s, t in outs],
        in_specs=specs,
        out_specs=[pl.BlockSpec(memory_space=pltpu.VMEM)] * len(outs),
        scratch_shapes=[pltpu.VMEM(s, t) for s, t in scratch]
        + [pltpu.SemaphoreType.DMA((len(far),))] * bool(far),
        compiler_params=pltpu.CompilerParams(vmem_limit_bytes=mib * 1024 * 1024),
        cost_estimate=pl.CostEstimate(flops=2 * macs, bytes_accessed=0, transcendentals=0),
    )(*args)


def swap(array, axis, size, mask):
    return lax.ppermute(array, axis, [(i, i ^ mask) for i in range(size)])


def after(value, other):
    return lax.optimization_barrier((value, other))[0]


def per_device(n_loop, n_cuts, image_features, text_features, image_head, text_head):
    half, width = image_features.shape
    near = 2 * half
    rows_out = width // n_loop
    part = rows_out // QUAD
    loop = functools.partial(swap, axis="loop", size=n_loop)
    cuts = functools.partial(swap, axis="cuts", size=n_cuts)
    macs = half * width * width

    def both(rows, order, count):
        rows = after(rows, order)
        return [rows] + [loop(piece, mask=1) for piece in jnp.split(rows, count)]

    def add(own, others):
        return sum((other.astype(F32) for other in others), own.astype(F32)).astype(BF16)

    def spread(total):
        return [total] + [cuts(total, mask=k) for k in range(1, QUAD)]

    t2 = loop(text_features[: half // 2], mask=2)
    i2 = loop(image_features, mask=2)
    place = jnp.stack([lax.axis_index("loop"), lax.axis_index("cuts") & (QUAD - 1)])
    place = place.astype(jnp.int32)
    t0, i0, place = lax.optimization_barrier((text_features, image_features, place))
    t2 = [t2, loop(t0[half // 2 :], mask=2)]
    t1 = loop(t0, mask=1)
    i1 = loop(i0, mask=1)
    wide, wide_b = ((near, width), F32), ((near, width), BF16)
    tall, tall_b = ((half, width), F32), ((half, width), BF16)
    head_b = ((width, width), BF16)
    block_w, block_dots = ((half, near), BF16), ((half, near), F32)
    side_w, side_dots = ((near, half), BF16), ((near, half), F32)
    pick_one, pick_two = ((rows_out, near), BF16), ((2 * rows_out, near), BF16)
    q_a, y_a, p_a, x_a, w_aa, gx, t0, i0, text_head, image_head = call(
        near_kernel,
        [wide, wide_b, wide, wide_b, ((near, near), BF16), wide, tall_b, tall_b, head_b, head_b],
        [((near, near), F32)],
        (t1, i1),
        8,
        far=(t0, i0, text_head, image_head),
    )
    first = both(t2[0], w_aa, 2)
    q_2, y_2, w_a2, gx, gy_a, pick_i = call(
        text_kernel,
        [tall, tall_b, side_w, wide, wide, pick_two],
        [side_dots],
        (*first, i0, i1, text_head, gx, x_a, w_aa),
        8,
        place,
    )
    second = both(t2[1], gy_a, 2)
    part_b, parts_b = ((part, width), BF16), ((2 * part, width), BF16)
    q_3, y_3, w_a3, dp_a, near_0, near_2, near_sent, far_0, far_1, far_sent = call(
        image_kernel,
        [tall, tall_b, side_w, wide_b] + [part_b, part_b, parts_b] * 2,
        [side_dots, wide],
        (*second, text_head, p_a, x_a, gx, pick_i),
        8,
    )
    near_came, far_came = cuts(near_sent, mask=1), cuts(far_sent, mask=2)
    gy_2, gy_3, pick_a, pick_b = call(
        text_pull_kernel,
        [tall, tall, pick_one, pick_one],
        [],
        (*first, *second, t0, t1, after(x_a, dp_a), w_a2, w_a3),
        8,
        place,
    )
    middle_b, corner, corner_dots = ((half // 2, width), BF16), ((half, half), BF16), ((half, half), F32)
    *x_2, w_2a, w_22, w_23 = call(
        block_kernel,
        [middle_b, middle_b, block_w, corner, corner],
        [tall, tall_b, block_dots, corner_dots, corner_dots],
        (after(i2, gy_2), image_head, y_a, y_2, y_3),
        8,
    )
    x_3 = [loop(rows, mask=1) for rows in x_2]
    gy_a, gy_2, gy_3 = call(
        own_pull_kernel,
        [wide, tall, tall],
        [],
        (*x_2, w_2a, w_22, w_23, gy_a, gy_2, gy_3),
        8,
    )
    near_came, far_came = after(near_came, gy_a), after(far_came, gy_a)
    near_sent, far_sent = add(near_2, [near_came[part:]]), add(far_1, [far_came[part:]])
    near_last, far_last = cuts(near_sent, mask=2), cuts(far_sent, mask=1)
    x_3 = [after(rows, (gy_a, near_sent, far_sent)) for rows in x_3]
    *text_parts, dq_a = call(
        last_kernel,
        [((part, width), BF16)] * QUAD + [wide_b],
        [wide, tall, tall, wide_b, ((rows_out, width), F32), block_w, corner, corner]
        + [block_dots, corner_dots, corner_dots],
        (*x_3, y_a, y_2, y_3, q_a, q_2, q_3, gy_a, gy_2, gy_3, pick_a, pick_b),
        16,
    )
    text_others = [cuts(text_parts[k], mask=k) for k in range(1, QUAD)]
    far_sum = add(far_0, [far_came[:part], after(far_last, dq_a)])
    near_sum = add(near_0, [near_came[:part], after(near_last, dq_a)])
    image_sum = add(near_sum, [loop(far_sum, mask=2)])
    grads = [
        call(grad_kernel, [tall], [], (after(back, image_sum), head), 4, macs=2 * macs, keep=False)[0]
        for back, head in ((dp_a, image_head), (dq_a, text_head))
    ]
    text_sum = add(text_parts[0], [after(other, (image_sum, grads)) for other in text_others])
    image_sum = add(image_sum, [cuts(image_sum, mask=QUAD)])
    image_pieces = spread(image_sum)
    text_sum = add(text_sum, [after(cuts(text_sum, mask=QUAD), image_pieces[1])])
    image_out, text_out = (
        call(place_kernel, [((rows_out, width), F32)], [], pieces, 4, place, keep=False)[0]
        for pieces in (image_pieces, spread(text_sum))
    )
    return (*grads, image_out, text_out)


def solution(mesh):
    n_loop, n_cuts = mesh.shape["loop"], mesh.shape["cuts"]
    if n_loop == 4 and n_cuts == 2 * QUAD:
        body = functools.partial(per_device, n_loop, n_cuts)
    else:
        body = plain_device
    placed = (P(("cuts", "loop"), None), P(("cuts", "loop"), None), P(), P())
    return jax.shard_map(
        body,
        mesh=mesh,
        in_specs=placed,
        out_specs=(
            P(("cuts", "loop"), None),
            P(("cuts", "loop"), None),
            P("loop", None),
            P("loop", None),
        ),
        check_vma=False,
    )
```

```python
import functools

import jax
import jax.numpy as jnp
from jax import lax
from jax.experimental import pallas as pl
from jax.experimental.pallas import tpu as pltpu
from jax.sharding import PartitionSpec as P

SCORE_SCALE = 10.0
SCORE_BIAS = -2.5
EPSILON = 1e-06
QUAD = 4
STRIP = 16
LANES = 128
F32 = jnp.float32
BF16 = jnp.bfloat16


def normalize(features, weight_matrix):
    projected = jnp.dot(features, weight_matrix, preferred_element_type=jnp.float32)
    factor = lax.rsqrt(jnp.sum(projected * projected, axis=-1, keepdims=True) + EPSILON)
    return (projected * factor, factor)


def pair_weights(image_vectors, text_vectors, image_offset):
    pair_scores = SCORE_SCALE * dot_nt(image_vectors, text_vectors) + SCORE_BIAS
    row_ids = image_offset + lax.broadcasted_iota(jnp.int32, pair_scores.shape, 0)
    col_ids = lax.broadcasted_iota(jnp.int32, pair_scores.shape, 1)
    match_targets = jnp.where(row_ids == col_ids, 1.0, -1.0).astype(jnp.float32)
    return (SCORE_SCALE * -match_targets * jax.nn.sigmoid(-match_targets * pair_scores)).astype(
        jnp.bfloat16
    )


def norm_back(unit, factor, gradient):
    return (factor * (gradient - unit * jnp.sum(unit * gradient, axis=-1, keepdims=True))).astype(
        jnp.bfloat16
    )


def dot_nn(left, right):
    return lax.dot_general(left, right, (((1,), (0,)), ((), ())), preferred_element_type=F32)


def dot_nt(left, right):
    return lax.dot_general(left, right, (((1,), (1,)), ((), ())), preferred_element_type=F32)


def dot_tn(left, right):
    return lax.dot_general(left, right, (((0,), (0,)), ((), ())), preferred_element_type=F32)


def plain_device(image_features, text_features, image_head, text_head):
    row_count = image_features.shape[0]
    own_start = lax.axis_index("loop") * row_count
    image_unit, image_factor = normalize(image_features, image_head)
    text_unit, text_factor = normalize(text_features, text_head)
    image_vectors = image_unit.astype(jnp.bfloat16)
    text_vectors = text_unit.astype(jnp.bfloat16)
    arrived = lax.all_gather(text_vectors, "loop", axis=0, tiled=True)
    weights = pair_weights(image_vectors, arrived, own_start)
    summed = jnp.dot(weights, arrived, preferred_element_type=jnp.float32)
    text_attraction = lax.psum_scatter(
        dot_tn(weights, image_vectors).astype(jnp.bfloat16), "loop", scatter_dimension=0, tiled=True
    ).astype(jnp.float32)
    image_back = norm_back(image_unit, image_factor, summed)
    text_back = norm_back(text_unit, text_factor, text_attraction)
    heads = []
    for features, back in ((image_features, image_back), (text_features, text_back)):
        term = dot_tn(features, back).astype(jnp.bfloat16)
        part = lax.psum_scatter(term, "loop", scatter_dimension=0, tiled=True)
        heads.append(lax.psum(part, "cuts").astype(jnp.float32))
    return (dot_nt(image_back, image_head), dot_nt(text_back, text_head), heads[0], heads[1])


def factor_of(ref, rows):
    p = ref[rows, :]
    return lax.rsqrt(jnp.sum(p * p, axis=-1, keepdims=True) + EPSILON)


def unit_rows(projected_ref, vectors_ref):
    for first in range(0, projected_ref.shape[0], STRIP):
        rows = slice(first, first + STRIP)
        factor = factor_of(projected_ref, rows)
        vectors_ref[rows, :] = (projected_ref[rows, :] * factor).astype(BF16)


def back_rows(projected_ref, gradient_ref, back_ref, at=0):
    for first in range(0, projected_ref.shape[0], STRIP):
        rows = slice(first, first + STRIP)
        factor = factor_of(projected_ref, rows)
        along = jnp.sum(projected_ref[rows, :] * gradient_ref[rows, :], axis=-1, keepdims=True)
        along = factor * factor * factor * along
        back = factor * gradient_ref[rows, :] - along * projected_ref[rows, :]
        back_ref[at + first : at + first + STRIP, :] = back.astype(BF16)


def weight_rows(dots_ref, weights_ref, pairs_from=None, begin=0, end=None):
    half_scale = 0.5 * SCORE_SCALE
    for first in range(begin, dots_ref.shape[0] if end is None else end, STRIP):
        rows = slice(first, first + STRIP)
        score = jnp.tanh(half_scale * dots_ref[rows, :] + 0.5 * SCORE_BIAS)
        weights = half_scale + half_scale * score
        if pairs_from is None:
            weights_ref[rows, :] = weights.astype(BF16)
            continue
        pair = pairs_from + first - begin
        left = pair // LANES * LANES
        right = min(left + LANES, weights.shape[1])
        shape = (STRIP, right - left)
        column = lax.broadcasted_iota(jnp.int32, shape, 1)
        same = column == lax.broadcasted_iota(jnp.int32, shape, 0) + (pair - left)
        middle = weights[:, left:right] - jnp.where(same, SCORE_SCALE, 0.0)
        pieces = [weights[:, :left], middle, weights[:, right:]]
        weights = jnp.concatenate([p for p in pieces if p.shape[1]], axis=1)
        weights_ref[rows, :] = weights.astype(BF16)


def one_hot(first, rows, width):
    wanted = first + lax.broadcasted_iota(jnp.int32, (rows, width), 0)
    column = lax.broadcasted_iota(jnp.int32, (rows, width), 1)
    return jnp.where(wanted == column, 1.0, 0.0)


def picker(place_ref, rows, width, sides):
    part = rows // QUAD
    pieces = []
    for k in range(QUAD):
        for side in sides:
            first = (place_ref[0] ^ side) * rows + (place_ref[1] ^ k) * part
            pieces.append(one_hot(first, part, width))
    return jnp.concatenate(pieces, axis=0).astype(BF16)


def near_kernel(
    t1, i1, t0_far, i0_far, text_head_far, image_head_far,
    q_a, y_a, p_a, x_a, w_aa, gx, t0, i0, text_head, image_head, dots, sems,
):
    half = t0.shape[0]
    copies = [
        pltpu.make_async_copy(source, target, sems.at[n])
        for n, (source, target) in enumerate(
            ((t0_far, t0), (text_head_far, text_head), (i0_far, i0), (image_head_far, image_head))
        )
    ]
    for copy in copies:
        copy.start()
    copies[0].wait()
    copies[1].wait()
    q_a[:half, :] = dot_nn(t0[...], text_head[...])
    q_a[half:, :] = dot_nn(t1[...], text_head[...])
    copies[2].wait()
    copies[3].wait()
    p_a[:half, :] = dot_nn(i0[...], image_head[...])
    unit_rows(q_a, y_a)
    p_a[half:, :] = dot_nn(i1[...], image_head[...])
    unit_rows(p_a, x_a)
    dots[...] = dot_nt(x_a[...], y_a[...])
    weight_rows(dots, w_aa, 0)
    gx[...] = dot_nn(w_aa[...], y_a[...])


def rows_of(refs):
    return jnp.concatenate([ref[...] for ref in refs], axis=0)


def text_kernel(place, *refs):
    *features, i0, i1, text_head, gx_in, x_a = refs[:-6]
    q_2, y_2, w_a2, gx, pick_i, dots = refs[-6:]
    half, width = i0.shape
    q_2[...] = dot_nn(rows_of(features), text_head[...])
    pick = picker(place, pick_i.shape[0] // 2, width, (0, 2))
    unit_rows(q_2, y_2)
    dots[...] = dot_nt(x_a[...], y_2[...])
    pick_i[:, :half] = dot_nt(pick, i0[...]).astype(BF16)
    pick_i[:, half:] = dot_nt(pick, i1[...]).astype(BF16)
    weight_rows(dots, w_a2)
    gx[...] = gx_in[...] + dot_nn(w_a2[...], y_2[...])


def image_kernel(*refs):
    *features, text_head, p_a, x_a, gx_in, pick_i, q_3, y_3, w_a3, dp_a = refs[:-8]
    near_0, near_2, near_sent, far_0, far_1, far_sent, dots, gx = refs[-8:]
    q_3[...] = dot_nn(rows_of(features), text_head[...])
    unit_rows(q_3, y_3)
    dots[...] = dot_nt(x_a[...], y_3[...])
    weight_rows(dots, w_a3)
    gx[...] = gx_in[...] + dot_nn(w_a3[...], y_3[...])
    back_rows(p_a, gx, dp_a)
    head = dot_nn(pick_i[...], dp_a[...]).astype(BF16)
    part = near_0.shape[0]
    near_side, far_side = (
        [head[first : first + part, :] for first in range(side * part, 2 * QUAD * part, 2 * part)]
        for side in range(2)
    )
    near_0[...] = near_side[0]
    near_2[...] = near_side[2]
    near_sent[:part, :] = near_side[1]
    near_sent[part:, :] = near_side[3]
    far_0[...] = far_side[0]
    far_1[...] = far_side[1]
    far_sent[:part, :] = far_side[2]
    far_sent[part:, :] = far_side[3]


def text_pull_kernel(place, *refs):
    *features, t0, t1, x_a, w_aa, w_a2, w_a3, gy_a, gy_2, gy_3, pick_a, pick_b = refs
    half = t0.shape[0]
    gy_a[...] = dot_tn(w_aa[...], x_a[...])
    gy_2[...] = dot_tn(w_a2[...], x_a[...])
    gy_3[...] = dot_tn(w_a3[...], x_a[...])
    pick = picker(place, pick_a.shape[0], t0.shape[1], (0,))
    pick_a[:, :half] = dot_nt(pick, t0[...]).astype(BF16)
    pick_a[:, half:] = dot_nt(pick, t1[...]).astype(BF16)
    pick_b[...] = dot_nt(pick, rows_of(features)).astype(BF16)


def far_weights(core, x, y_a, y_2, y_3, w_a, w_2, w_3, d_a, d_2, d_3):
    half = x.shape[0]
    middle = half // 2
    d_a[...] = dot_nt(x, y_a[...])
    d_2[...] = dot_nt(x, y_2[...])
    weight_rows(d_a, w_a)
    d_3[...] = dot_nt(x, y_3[...])
    weight_rows(d_2, w_2, core * middle, 0, middle)
    weight_rows(d_2, w_2, None, middle, half)
    weight_rows(d_3, w_3, None, 0, middle)
    weight_rows(d_3, w_3, core * middle, middle, half)


def block_kernel(i2, image_head, y_a, y_2, y_3, x_first, x_second, w_a, w_2, w_3, p_b, x_b, d_a, d_2, d_3):
    middle = x_first.shape[0]
    p_b[...] = dot_nn(i2[...], image_head[...])
    unit_rows(p_b, x_b)
    x_first[...] = x_b[:middle, :]
    x_second[...] = x_b[middle:, :]
    far_weights(0, x_b[...], y_a, y_2, y_3, w_a, w_2, w_3, d_a, d_2, d_3)


def own_pull_kernel(x_first, x_second, w_a, w_2, w_3, gy_a_in, gy_2_in, gy_3_in, gy_a, gy_2, gy_3):
    x = rows_of((x_first, x_second))
    gy_a[...] = gy_a_in[...] + dot_tn(w_a[...], x)
    gy_2[...] = gy_2_in[...] + dot_tn(w_2[...], x)
    gy_3[...] = gy_3_in[...] + dot_tn(w_3[...], x)


def last_kernel(
    x_first, x_second, y_a, y_2, y_3, q_a, q_2, q_3, gy_a_in, gy_2_in, gy_3_in, pick_a, pick_b,
    kept_0, kept_2, sent, dq_a, gy_a, gy_2, gy_3, dq_b, near_head, w_a, w_2, w_3, d_a, d_2, d_3,
):
    half = q_2.shape[0]
    x = rows_of((x_first, x_second))
    far_weights(1, x, y_a, y_2, y_3, w_a, w_2, w_3, d_a, d_2, d_3)
    gy_a[...] = gy_a_in[...] + dot_tn(w_a[...], x)
    gy_2[...] = gy_2_in[...] + dot_tn(w_2[...], x)
    back_rows(q_a, gy_a, dq_a)
    gy_3[...] = gy_3_in[...] + dot_tn(w_3[...], x)
    near_head[...] = dot_nn(pick_a[...], dq_a[...])
    back_rows(q_2, gy_2, dq_b, 0)
    back_rows(q_3, gy_3, dq_b, half)
    head = (near_head[...] + dot_nn(pick_b[...], dq_b[...])).astype(BF16)
    part = kept_0.shape[0]
    kept_0[...] = head[:part, :]
    kept_2[...] = head[2 * part : 3 * part, :]
    sent[:part, :] = head[part : 2 * part, :]
    sent[part:, :] = head[3 * part :, :]


def add_kernel(left, right, out):
    out[...] = (left[...].astype(F32) + right[...].astype(F32)).astype(BF16)


def grad_kernel(back, head, out):
    out[...] = dot_nt(back[: out.shape[0], :], head[...])


def place_kernel(place, *refs):
    *pieces, out = refs
    part = pieces[0].shape[0]
    for k, piece in enumerate(pieces):
        first = pl.multiple_of((place[1] ^ k) * part, part)
        out[pl.ds(first, part), :] = piece[...].astype(F32)


def call(kernel, outs, scratch, args, mib, place=None, macs=0, keep=True, far=()):
    far = [pltpu.with_memory_space_constraint(a, pltpu.HBM) for a in far]
    args = [pltpu.with_memory_space_constraint(a, pltpu.VMEM) for a in args] + far
    specs = [pl.BlockSpec(memory_space=pltpu.VMEM)] * (len(args) - len(far))
    specs += [pl.BlockSpec(memory_space=pltpu.HBM)] * len(far)
    if place is not None:
        args, specs = [place, *args], [pl.BlockSpec(memory_space=pltpu.SMEM), *specs]
    shape = pltpu.VMEM if keep else jax.ShapeDtypeStruct
    return pl.pallas_call(
        kernel,
        out_shape=[shape(s, t) for s, t in outs],
        in_specs=specs,
        out_specs=[pl.BlockSpec(memory_space=pltpu.VMEM)] * len(outs),
        scratch_shapes=[pltpu.VMEM(s, t) for s, t in scratch]
        + [pltpu.SemaphoreType.DMA((len(far),))] * bool(far),
        compiler_params=pltpu.CompilerParams(vmem_limit_bytes=mib * 1024 * 1024),
        cost_estimate=pl.CostEstimate(flops=2 * macs, bytes_accessed=0, transcendentals=0),
    )(*args)


def swap(array, axis, size, mask):
    return lax.ppermute(array, axis, [(i, i ^ mask) for i in range(size)])


def after(value, other):
    return lax.optimization_barrier((value, other))[0]


def per_device(n_loop, n_cuts, image_features, text_features, image_head, text_head):
    half, width = image_features.shape
    near = 2 * half
    rows_out = width // n_loop
    part = rows_out // QUAD
    loop = functools.partial(swap, axis="loop", size=n_loop)
    cuts = functools.partial(swap, axis="cuts", size=n_cuts)
    macs = half * width * width

    def both(rows, order, count):
        rows = after(rows, order)
        return [rows] + [loop(piece, mask=1) for piece in jnp.split(rows, count)]

    def add(own, others):
        return sum((other.astype(F32) for other in others), own.astype(F32)).astype(BF16)

    def spread(total):
        return [total] + [cuts(total, mask=k) for k in range(1, QUAD)]

    t2 = [loop(rows, mask=2) for rows in jnp.split(text_features, 2)]
    i2 = loop(image_features, mask=2)
    place = jnp.stack([lax.axis_index("loop"), lax.axis_index("cuts") & (QUAD - 1)])
    place = place.astype(jnp.int32)
    t0, i0, place = lax.optimization_barrier((text_features, image_features, place))
    t1 = loop(t0, mask=1)
    i1 = loop(i0, mask=1)
    wide, wide_b = ((near, width), F32), ((near, width), BF16)
    tall, tall_b = ((half, width), F32), ((half, width), BF16)
    head_b = ((width, width), BF16)
    block_w, block_dots = ((half, near), BF16), ((half, near), F32)
    side_w, side_dots = ((near, half), BF16), ((near, half), F32)
    pick_one, pick_two = ((rows_out, near), BF16), ((2 * rows_out, near), BF16)
    q_a, y_a, p_a, x_a, w_aa, gx, t0, i0, text_head, image_head = call(
        near_kernel,
        [wide, wide_b, wide, wide_b, ((near, near), BF16), wide, tall_b, tall_b, head_b, head_b],
        [((near, near), F32)],
        (t1, i1),
        8,
        far=(t0, i0, text_head, image_head),
    )
    first = both(t2[0], w_aa, 2)
    q_2, y_2, w_a2, gx, pick_i = call(
        text_kernel,
        [tall, tall_b, side_w, wide, pick_two],
        [side_dots],
        (*first, i0, i1, text_head, gx, x_a),
        8,
        place,
    )
    second = both(t2[1], gx, 2)
    part_b, parts_b = ((part, width), BF16), ((2 * part, width), BF16)
    q_3, y_3, w_a3, dp_a, near_0, near_2, near_sent, far_0, far_1, far_sent = call(
        image_kernel,
        [tall, tall_b, side_w, wide_b] + [part_b, part_b, parts_b] * 2,
        [side_dots, wide],
        (*second, text_head, p_a, x_a, gx, pick_i),
        8,
    )
    near_came, far_came = cuts(near_sent, mask=1), cuts(far_sent, mask=2)
    gy_a, gy_2, gy_3, pick_a, pick_b = call(
        text_pull_kernel,
        [wide, tall, tall, pick_one, pick_one],
        [],
        (*first, *second, t0, t1, after(x_a, dp_a), w_aa, w_a2, w_a3),
        8,
        place,
    )
    middle_b, corner, corner_dots = ((half // 2, width), BF16), ((half, half), BF16), ((half, half), F32)
    *x_2, w_2a, w_22, w_23 = call(
        block_kernel,
        [middle_b, middle_b, block_w, corner, corner],
        [tall, tall_b, block_dots, corner_dots, corner_dots],
        (after(i2, gy_2), image_head, y_a, y_2, y_3),
        8,
    )
    x_3 = [loop(rows, mask=1) for rows in x_2]
    gy_a, gy_2, gy_3 = call(
        own_pull_kernel,
        [wide, tall, tall],
        [],
        (*x_2, w_2a, w_22, w_23, gy_a, gy_2, gy_3),
        8,
    )
    near_came, far_came = after(near_came, gy_a), after(far_came, gy_a)
    near_sent, far_sent = add(near_2, [near_came[part:]]), add(far_1, [far_came[part:]])
    near_last, far_last = cuts(near_sent, mask=2), cuts(far_sent, mask=1)
    x_3 = [after(rows, (gy_a, near_sent, far_sent)) for rows in x_3]
    text_0, text_2, text_sent, dq_a = call(
        last_kernel,
        [part_b, part_b, parts_b, wide_b],
        [wide, tall, tall, wide_b, ((rows_out, width), F32), block_w, corner, corner]
        + [block_dots, corner_dots, corner_dots],
        (*x_3, y_a, y_2, y_3, q_a, q_2, q_3, gy_a, gy_2, gy_3, pick_a, pick_b),
        16,
    )
    text_came = cuts(text_sent, mask=1)
    far_sum = add(far_0, [far_came[:part], after(far_last, dq_a)])
    near_sum = add(near_0, [near_came[:part], after(near_last, dq_a)])
    image_sum = add(near_sum, [loop(far_sum, mask=2)])
    grads = [
        call(grad_kernel, [tall], [], (after(back, image_sum), head), 4, macs=2 * macs, keep=False)[0]
        for back, head in ((dp_a, image_head), (dq_a, text_head))
    ]
    text_came = after(text_came, (image_sum, grads))
    text_last = cuts(add(text_2, [text_came[part:]]), mask=2)
    text_sum = add(text_0, [text_came[:part], text_last])
    image_sum = call(
        add_kernel, [part_b], [], (image_sum, cuts(image_sum, mask=QUAD)), 4, macs=4 * macs
    )[0]
    image_pieces = spread(image_sum)
    text_sum = add(text_sum, [after(cuts(text_sum, mask=QUAD), image_pieces[1])])
    image_out, text_out = (
        call(place_kernel, [((rows_out, width), F32)], [], pieces, 4, place, keep=False)[0]
        for pieces in (image_pieces, spread(text_sum))
    )
    return (*grads, image_out, text_out)


def solution(mesh):
    n_loop, n_cuts = mesh.shape["loop"], mesh.shape["cuts"]
    if n_loop == 4 and n_cuts == 2 * QUAD:
        body = functools.partial(per_device, n_loop, n_cuts)
    else:
        body = plain_device
    placed = (P(("cuts", "loop"), None), P(("cuts", "loop"), None), P(), P())
    return jax.shard_map(
        body,
        mesh=mesh,
        in_specs=placed,
        out_specs=(
            P(("cuts", "loop"), None),
            P(("cuts", "loop"), None),
            P("loop", None),
            P("loop", None),
        ),
        check_vma=False,
    )
```

```python
import functools

import jax
import jax.numpy as jnp
from jax import lax
from jax.experimental import pallas as pl
from jax.experimental.pallas import tpu as pltpu
from jax.sharding import PartitionSpec as P

SCORE_SCALE = 10.0
SCORE_BIAS = -2.5
EPSILON = 1e-06
QUAD = 4
STRIP = 16
LANES = 128
F32 = jnp.float32
BF16 = jnp.bfloat16


def normalize(features, weight_matrix):
    projected = jnp.dot(features, weight_matrix, preferred_element_type=jnp.float32)
    factor = lax.rsqrt(jnp.sum(projected * projected, axis=-1, keepdims=True) + EPSILON)
    return (projected * factor, factor)


def pair_weights(image_vectors, text_vectors, image_offset):
    pair_scores = SCORE_SCALE * dot_nt(image_vectors, text_vectors) + SCORE_BIAS
    row_ids = image_offset + lax.broadcasted_iota(jnp.int32, pair_scores.shape, 0)
    col_ids = lax.broadcasted_iota(jnp.int32, pair_scores.shape, 1)
    match_targets = jnp.where(row_ids == col_ids, 1.0, -1.0).astype(jnp.float32)
    return (SCORE_SCALE * -match_targets * jax.nn.sigmoid(-match_targets * pair_scores)).astype(
        jnp.bfloat16
    )


def norm_back(unit, factor, gradient):
    return (factor * (gradient - unit * jnp.sum(unit * gradient, axis=-1, keepdims=True))).astype(
        jnp.bfloat16
    )


def dot_nn(left, right):
    return lax.dot_general(left, right, (((1,), (0,)), ((), ())), preferred_element_type=F32)


def dot_nt(left, right):
    return lax.dot_general(left, right, (((1,), (1,)), ((), ())), preferred_element_type=F32)


def dot_tn(left, right):
    return lax.dot_general(left, right, (((0,), (0,)), ((), ())), preferred_element_type=F32)


def plain_device(image_features, text_features, image_head, text_head):
    row_count = image_features.shape[0]
    own_start = lax.axis_index("loop") * row_count
    image_unit, image_factor = normalize(image_features, image_head)
    text_unit, text_factor = normalize(text_features, text_head)
    image_vectors = image_unit.astype(jnp.bfloat16)
    text_vectors = text_unit.astype(jnp.bfloat16)
    arrived = lax.all_gather(text_vectors, "loop", axis=0, tiled=True)
    weights = pair_weights(image_vectors, arrived, own_start)
    summed = jnp.dot(weights, arrived, preferred_element_type=jnp.float32)
    text_attraction = lax.psum_scatter(
        dot_tn(weights, image_vectors).astype(jnp.bfloat16), "loop", scatter_dimension=0, tiled=True
    ).astype(jnp.float32)
    image_back = norm_back(image_unit, image_factor, summed)
    text_back = norm_back(text_unit, text_factor, text_attraction)
    heads = []
    for features, back in ((image_features, image_back), (text_features, text_back)):
        term = dot_tn(features, back).astype(jnp.bfloat16)
        part = lax.psum_scatter(term, "loop", scatter_dimension=0, tiled=True)
        heads.append(lax.psum(part, "cuts").astype(jnp.float32))
    return (dot_nt(image_back, image_head), dot_nt(text_back, text_head), heads[0], heads[1])


def factor_of(ref, rows):
    p = ref[rows, :]
    return lax.rsqrt(jnp.sum(p * p, axis=-1, keepdims=True) + EPSILON)


def unit_rows(projected_ref, vectors_ref):
    for first in range(0, projected_ref.shape[0], STRIP):
        rows = slice(first, first + STRIP)
        factor = factor_of(projected_ref, rows)
        vectors_ref[rows, :] = (projected_ref[rows, :] * factor).astype(BF16)


def back_rows(projected_ref, gradient_ref, back_ref):
    for first in range(0, projected_ref.shape[0], STRIP):
        rows = slice(first, first + STRIP)
        factor = factor_of(projected_ref, rows)
        along = jnp.sum(projected_ref[rows, :] * gradient_ref[rows, :], axis=-1, keepdims=True)
        along = factor * factor * factor * along
        back = factor * gradient_ref[rows, :] - along * projected_ref[rows, :]
        back_ref[rows, :] = back.astype(BF16)


def weight_rows(dots_ref, weights_ref, pairs_from=None):
    half_scale = 0.5 * SCORE_SCALE
    for first in range(0, dots_ref.shape[0], STRIP):
        rows = slice(first, first + STRIP)
        score = jnp.tanh(half_scale * dots_ref[rows, :] + 0.5 * SCORE_BIAS)
        weights = half_scale + half_scale * score
        if pairs_from is None:
            weights_ref[rows, :] = weights.astype(BF16)
            continue
        pair = pairs_from + first
        left = pair // LANES * LANES
        right = min(left + LANES, weights.shape[1])
        shape = (STRIP, right - left)
        column = lax.broadcasted_iota(jnp.int32, shape, 1)
        same = column == lax.broadcasted_iota(jnp.int32, shape, 0) + (pair - left)
        middle = weights[:, left:right] - jnp.where(same, SCORE_SCALE, 0.0)
        pieces = [weights[:, :left], middle, weights[:, right:]]
        weights = jnp.concatenate([p for p in pieces if p.shape[1]], axis=1)
        weights_ref[rows, :] = weights.astype(BF16)


def one_hot(first, rows, width):
    wanted = first + lax.broadcasted_iota(jnp.int32, (rows, width), 0)
    column = lax.broadcasted_iota(jnp.int32, (rows, width), 1)
    return jnp.where(wanted == column, 1.0, 0.0)


def picker(place_ref, rows, width, sides):
    part = rows // QUAD
    pieces = []
    for k in range(QUAD):
        for side in sides:
            first = (place_ref[0] ^ side) * rows + (place_ref[1] ^ k) * part
            pieces.append(one_hot(first, part, width))
    return jnp.concatenate(pieces, axis=0).astype(BF16)


def split_head(head, outs):
    part = head.shape[0] // QUAD
    for k, out in enumerate(outs):
        out[...] = head[k * part : (k + 1) * part, :].astype(BF16)


def near_kernel(
    t1, i1, t0_far, i0_far, text_head_far, image_head_far,
    q_a, y_a, p_a, x_a, w_aa, gx, t0, i0, text_head, image_head, dots, sems,
):
    half = t0.shape[0]
    copies = [
        pltpu.make_async_copy(source, target, sems.at[n])
        for n, (source, target) in enumerate(
            ((t0_far, t0), (text_head_far, text_head), (i0_far, i0), (image_head_far, image_head))
        )
    ]
    for copy in copies:
        copy.start()
    copies[0].wait()
    copies[1].wait()
    q_a[:half, :] = dot_nn(t0[...], text_head[...])
    q_a[half:, :] = dot_nn(t1[...], text_head[...])
    copies[2].wait()
    copies[3].wait()
    p_a[:half, :] = dot_nn(i0[...], image_head[...])
    unit_rows(q_a, y_a)
    p_a[half:, :] = dot_nn(i1[...], image_head[...])
    unit_rows(p_a, x_a)
    dots[...] = dot_nt(x_a[...], y_a[...])
    weight_rows(dots, w_aa, 0)
    gx[...] = dot_nn(w_aa[...], y_a[...])


def rows_of(refs):
    return jnp.concatenate([ref[...] for ref in refs], axis=0)


def near_pull_kernel(place, t0, t1, i0, i1, x_a, w_aa, gy_a, pick_i, pick_t):
    half, width = t0.shape
    rows = pick_t.shape[0]
    pick = picker(place, rows, width, (0, 2))
    pick_i[:, :half] = dot_nt(pick, i0[...]).astype(BF16)
    pick_i[:, half:] = dot_nt(pick, i1[...]).astype(BF16)
    pick = picker(place, rows, width, (0,))
    pick_t[:, :half] = dot_nt(pick, t0[...]).astype(BF16)
    pick_t[:, half:] = dot_nt(pick, t1[...]).astype(BF16)
    gy_a[...] = dot_tn(w_aa[...], x_a[...])


def image_kernel(*refs):
    *features, text_head, p_a, x_a, gx_in, pick_i, q_b, y_b, w_ab, dp_a = refs[:-8]
    near_0, near_2, near_sent, far_0, far_1, far_sent, dots, gx = refs[-8:]
    q_b[...] = dot_nn(rows_of(features), text_head[...])
    unit_rows(q_b, y_b)
    dots[...] = dot_nt(x_a[...], y_b[...])
    weight_rows(dots, w_ab)
    gx[...] = gx_in[...] + dot_nn(w_ab[...], y_b[...])
    back_rows(p_a, gx, dp_a)
    head = dot_nn(pick_i[...], dp_a[...]).astype(BF16)
    part = near_0.shape[0]
    near_side, far_side = (
        [head[first : first + part, :] for first in range(side * part, 2 * QUAD * part, 2 * part)]
        for side in range(2)
    )
    near_0[...] = near_side[0]
    near_2[...] = near_side[2]
    near_sent[:part, :] = near_side[1]
    near_sent[part:, :] = near_side[3]
    far_0[...] = far_side[0]
    far_1[...] = far_side[1]
    far_sent[:part, :] = far_side[2]
    far_sent[part:, :] = far_side[3]


def text_pull_kernel(place, *refs):
    *features, x_a, w_ab, gy_b, pick_b = refs
    gy_b[...] = dot_tn(w_ab[...], x_a[...])
    pick = picker(place, pick_b.shape[0], x_a.shape[1], (0,))
    pick_b[...] = dot_nt(pick, rows_of(features)).astype(BF16)


def far_weights(core, x, y_a, y_b, w_a, w_b, d_a, d_b):
    d_a[...] = dot_nt(x, y_a[...])
    d_b[...] = dot_nt(x, y_b[...])
    weight_rows(d_a, w_a)
    weight_rows(d_b, w_b, core * x.shape[0])


def block_kernel(i2, image_head, y_a, y_b, x_first, x_second, w_a, w_b, p_b, x_b, d_a, d_b):
    middle = x_first.shape[0]
    p_b[...] = dot_nn(i2[...], image_head[...])
    unit_rows(p_b, x_b)
    x_first[...] = x_b[:middle, :]
    x_second[...] = x_b[middle:, :]
    far_weights(0, x_b[...], y_a, y_b, w_a, w_b, d_a, d_b)


def own_pull_kernel(x_first, x_second, w_a, w_b, gy_a_in, gy_b_in, gy_a, gy_b):
    x = rows_of((x_first, x_second))
    gy_a[...] = gy_a_in[...] + dot_tn(w_a[...], x)
    gy_b[...] = gy_b_in[...] + dot_tn(w_b[...], x)


def last_kernel(
    x_first, x_second, y_a, y_b, q_a, q_b, gy_a_in, gy_b_in, pick_a, pick_b,
    h0, h1, h2, h3, dq_a, gy_a, gy_b, dq_b, near_head, w_a, w_b, d_a, d_b,
):
    x = rows_of((x_first, x_second))
    far_weights(1, x, y_a, y_b, w_a, w_b, d_a, d_b)
    gy_a[...] = gy_a_in[...] + dot_tn(w_a[...], x)
    back_rows(q_a, gy_a, dq_a)
    gy_b[...] = gy_b_in[...] + dot_tn(w_b[...], x)
    near_head[...] = dot_nn(pick_a[...], dq_a[...])
    back_rows(q_b, gy_b, dq_b)
    split_head(near_head[...] + dot_nn(pick_b[...], dq_b[...]), (h0, h1, h2, h3))


def grad_kernel(back, head, out):
    out[...] = dot_nt(back[: out.shape[0], :], head[...])


def place_kernel(place, *refs):
    *pieces, out = refs
    part = pieces[0].shape[0]
    for k, piece in enumerate(pieces):
        first = pl.multiple_of((place[1] ^ k) * part, part)
        out[pl.ds(first, part), :] = piece[...].astype(F32)


def call(kernel, outs, scratch, args, mib, place=None, macs=0, keep=True, far=()):
    far = [pltpu.with_memory_space_constraint(a, pltpu.HBM) for a in far]
    args = [pltpu.with_memory_space_constraint(a, pltpu.VMEM) for a in args] + far
    specs = [pl.BlockSpec(memory_space=pltpu.VMEM)] * (len(args) - len(far))
    specs += [pl.BlockSpec(memory_space=pltpu.HBM)] * len(far)
    if place is not None:
        args, specs = [place, *args], [pl.BlockSpec(memory_space=pltpu.SMEM), *specs]
    shape = pltpu.VMEM if keep else jax.ShapeDtypeStruct
    return pl.pallas_call(
        kernel,
        out_shape=[shape(s, t) for s, t in outs],
        in_specs=specs,
        out_specs=[pl.BlockSpec(memory_space=pltpu.VMEM)] * len(outs),
        scratch_shapes=[pltpu.VMEM(s, t) for s, t in scratch]
        + [pltpu.SemaphoreType.DMA((len(far),))] * bool(far),
        compiler_params=pltpu.CompilerParams(vmem_limit_bytes=mib * 1024 * 1024),
        cost_estimate=pl.CostEstimate(flops=2 * macs, bytes_accessed=0, transcendentals=0),
    )(*args)


def swap(array, axis, size, mask):
    return lax.ppermute(array, axis, [(i, i ^ mask) for i in range(size)])


def after(value, other):
    return lax.optimization_barrier((value, other))[0]


def per_device(n_loop, n_cuts, image_features, text_features, image_head, text_head):
    half, width = image_features.shape
    near = 2 * half
    rows_out = width // n_loop
    part = rows_out // QUAD
    loop = functools.partial(swap, axis="loop", size=n_loop)
    cuts = functools.partial(swap, axis="cuts", size=n_cuts)
    macs = half * width * width

    def both(rows, order, count):
        rows = after(rows, order)
        return [rows] + [loop(piece, mask=1) for piece in jnp.split(rows, count)]

    def add(own, others):
        return sum((other.astype(F32) for other in others), own.astype(F32)).astype(BF16)

    def spread(total):
        return [total] + [cuts(total, mask=k) for k in range(1, QUAD)]

    t2 = loop(text_features, mask=2)
    i2 = loop(image_features, mask=2)
    place = jnp.stack([lax.axis_index("loop"), lax.axis_index("cuts") & (QUAD - 1)])
    place = place.astype(jnp.int32)
    t0, i0, place = lax.optimization_barrier((text_features, image_features, place))
    t1 = loop(t0, mask=1)
    i1 = loop(i0, mask=1)
    wide, wide_b = ((near, width), F32), ((near, width), BF16)
    tall, tall_b = ((half, width), F32), ((half, width), BF16)
    head_b = ((width, width), BF16)
    block_w, block_dots = ((half, near), BF16), ((half, near), F32)
    pick_one, pick_two = ((rows_out, near), BF16), ((2 * rows_out, near), BF16)
    q_a, y_a, p_a, x_a, w_aa, gx, t0, i0, text_head, image_head = call(
        near_kernel,
        [wide, wide_b, wide, wide_b, ((near, near), BF16), wide, tall_b, tall_b, head_b, head_b],
        [((near, near), F32)],
        (t1, i1),
        8,
        far=(t0, i0, text_head, image_head),
    )
    gy_a, pick_i, pick_a = call(
        near_pull_kernel,
        [wide, pick_two, pick_one],
        [],
        (t0, t1, i0, i1, x_a, w_aa),
        8,
        place,
    )
    far_text = both(t2, gy_a, 4)
    part_b, parts_b = ((part, width), BF16), ((2 * part, width), BF16)
    square_b, square = ((near, near), BF16), ((near, near), F32)
    q_b, y_b, w_ab, dp_a, near_0, near_2, near_sent, far_0, far_1, far_sent = call(
        image_kernel,
        [wide, wide_b, square_b, wide_b] + [part_b, part_b, parts_b] * 2,
        [square, wide],
        (*far_text, text_head, p_a, x_a, gx, pick_i),
        8,
    )
    near_came, far_came = cuts(near_sent, mask=1), cuts(far_sent, mask=2)
    gy_b, pick_b = call(
        text_pull_kernel,
        [wide, pick_one],
        [],
        (*far_text, after(x_a, dp_a), w_ab),
        8,
        place,
    )
    middle_b = ((half // 2, width), BF16)
    *x_2, w_2a, w_2b = call(
        block_kernel,
        [middle_b, middle_b, block_w, block_w],
        [tall, tall_b, block_dots, block_dots],
        (after(i2, gy_b), image_head, y_a, y_b),
        8,
    )
    x_3 = [loop(rows, mask=1) for rows in x_2]
    gy_a, gy_b = call(
        own_pull_kernel,
        [wide, wide],
        [],
        (*x_2, w_2a, w_2b, gy_a, gy_b),
        8,
    )
    near_came, far_came = after(near_came, gy_a), after(far_came, gy_a)
    near_sent, far_sent = add(near_2, [near_came[part:]]), add(far_1, [far_came[part:]])
    near_last, far_last = cuts(near_sent, mask=2), cuts(far_sent, mask=1)
    x_3 = [after(rows, (gy_a, near_sent, far_sent)) for rows in x_3]
    *text_parts, dq_a = call(
        last_kernel,
        [part_b] * QUAD + [wide_b],
        [wide, wide, wide_b, ((rows_out, width), F32), block_w, block_w, block_dots, block_dots],
        (*x_3, y_a, y_b, q_a, q_b, gy_a, gy_b, pick_a, pick_b),
        16,
    )
    text_others = [cuts(text_parts[k], mask=k) for k in range(1, QUAD)]
    far_sum = add(far_0, [far_came[:part], after(far_last, dq_a)])
    near_sum = add(near_0, [near_came[:part], after(near_last, dq_a)])
    image_sum = add(near_sum, [loop(far_sum, mask=2)])
    grads = [
        call(grad_kernel, [tall], [], (after(back, image_sum), head), 4, macs=2 * macs, keep=False)[0]
        for back, head in ((dp_a, image_head), (dq_a, text_head))
    ]
    text_sum = add(text_parts[0], [after(other, (image_sum, grads)) for other in text_others])
    image_sum = add(image_sum, [cuts(image_sum, mask=QUAD)])
    image_pieces = spread(image_sum)
    text_sum = add(text_sum, [after(cuts(text_sum, mask=QUAD), image_pieces[1])])
    image_out, text_out = (
        call(place_kernel, [((rows_out, width), F32)], [], pieces, 4, place, keep=False)[0]
        for pieces in (image_pieces, spread(text_sum))
    )
    return (*grads, image_out, text_out)


def solution(mesh):
    n_loop, n_cuts = mesh.shape["loop"], mesh.shape["cuts"]
    if n_loop == 4 and n_cuts == 2 * QUAD:
        body = functools.partial(per_device, n_loop, n_cuts)
    else:
        body = plain_device
    placed = (P(("cuts", "loop"), None), P(("cuts", "loop"), None), P(), P())
    return jax.shard_map(
        body,
        mesh=mesh,
        in_specs=placed,
        out_specs=(
            P(("cuts", "loop"), None),
            P(("cuts", "loop"), None),
            P("loop", None),
            P("loop", None),
        ),
        check_vma=False,
    )
```

```python
import functools

import jax
import jax.numpy as jnp
from jax import lax
from jax.experimental import pallas as pl
from jax.experimental.pallas import tpu as pltpu
from jax.sharding import PartitionSpec as P

SCORE_SCALE = 10.0
SCORE_BIAS = -2.5
EPSILON = 1e-06
QUAD = 4
STRIP = 16
LANES = 128
F32 = jnp.float32
BF16 = jnp.bfloat16


def normalize(features, weight_matrix):
    projected = jnp.dot(features, weight_matrix, preferred_element_type=jnp.float32)
    factor = lax.rsqrt(jnp.sum(projected * projected, axis=-1, keepdims=True) + EPSILON)
    return (projected * factor, factor)


def pair_weights(image_vectors, text_vectors, image_offset):
    pair_scores = SCORE_SCALE * dot_nt(image_vectors, text_vectors) + SCORE_BIAS
    row_ids = image_offset + lax.broadcasted_iota(jnp.int32, pair_scores.shape, 0)
    col_ids = lax.broadcasted_iota(jnp.int32, pair_scores.shape, 1)
    match_targets = jnp.where(row_ids == col_ids, 1.0, -1.0).astype(jnp.float32)
    return (SCORE_SCALE * -match_targets * jax.nn.sigmoid(-match_targets * pair_scores)).astype(
        jnp.bfloat16
    )


def norm_back(unit, factor, gradient):
    return (factor * (gradient - unit * jnp.sum(unit * gradient, axis=-1, keepdims=True))).astype(
        jnp.bfloat16
    )


def dot_nn(left, right):
    return lax.dot_general(left, right, (((1,), (0,)), ((), ())), preferred_element_type=F32)


def dot_nt(left, right):
    return lax.dot_general(left, right, (((1,), (1,)), ((), ())), preferred_element_type=F32)


def dot_tn(left, right):
    return lax.dot_general(left, right, (((0,), (0,)), ((), ())), preferred_element_type=F32)


def plain_device(image_features, text_features, image_head, text_head):
    row_count = image_features.shape[0]
    own_start = lax.axis_index("loop") * row_count
    image_unit, image_factor = normalize(image_features, image_head)
    text_unit, text_factor = normalize(text_features, text_head)
    image_vectors = image_unit.astype(jnp.bfloat16)
    text_vectors = text_unit.astype(jnp.bfloat16)
    arrived = lax.all_gather(text_vectors, "loop", axis=0, tiled=True)
    weights = pair_weights(image_vectors, arrived, own_start)
    summed = jnp.dot(weights, arrived, preferred_element_type=jnp.float32)
    text_attraction = lax.psum_scatter(
        dot_tn(weights, image_vectors).astype(jnp.bfloat16), "loop", scatter_dimension=0, tiled=True
    ).astype(jnp.float32)
    image_back = norm_back(image_unit, image_factor, summed)
    text_back = norm_back(text_unit, text_factor, text_attraction)
    heads = []
    for features, back in ((image_features, image_back), (text_features, text_back)):
        term = dot_tn(features, back).astype(jnp.bfloat16)
        part = lax.psum_scatter(term, "loop", scatter_dimension=0, tiled=True)
        heads.append(lax.psum(part, "cuts").astype(jnp.float32))
    return (dot_nt(image_back, image_head), dot_nt(text_back, text_head), heads[0], heads[1])


def factor_of(ref, rows):
    p = ref[rows, :]
    return lax.rsqrt(jnp.sum(p * p, axis=-1, keepdims=True) + EPSILON)


def unit_rows(projected_ref, vectors_ref):
    for first in range(0, projected_ref.shape[0], STRIP):
        rows = slice(first, first + STRIP)
        factor = factor_of(projected_ref, rows)
        vectors_ref[rows, :] = (projected_ref[rows, :] * factor).astype(BF16)


def back_rows(projected_ref, gradient_ref, back_ref):
    for first in range(0, projected_ref.shape[0], STRIP):
        rows = slice(first, first + STRIP)
        factor = factor_of(projected_ref, rows)
        along = jnp.sum(projected_ref[rows, :] * gradient_ref[rows, :], axis=-1, keepdims=True)
        along = factor * factor * factor * along
        back = factor * gradient_ref[rows, :] - along * projected_ref[rows, :]
        back_ref[rows, :] = back.astype(BF16)


def weight_rows(dots_ref, weights_ref, pairs_from=None):
    half_scale = 0.5 * SCORE_SCALE
    for first in range(0, dots_ref.shape[0], STRIP):
        rows = slice(first, first + STRIP)
        score = jnp.tanh(half_scale * dots_ref[rows, :] + 0.5 * SCORE_BIAS)
        weights = half_scale + half_scale * score
        if pairs_from is None:
            weights_ref[rows, :] = weights.astype(BF16)
            continue
        pair = pairs_from + first
        left = pair // LANES * LANES
        right = min(left + LANES, weights.shape[1])
        shape = (STRIP, right - left)
        column = lax.broadcasted_iota(jnp.int32, shape, 1)
        same = column == lax.broadcasted_iota(jnp.int32, shape, 0) + (pair - left)
        middle = weights[:, left:right] - jnp.where(same, SCORE_SCALE, 0.0)
        pieces = [weights[:, :left], middle, weights[:, right:]]
        weights = jnp.concatenate([p for p in pieces if p.shape[1]], axis=1)
        weights_ref[rows, :] = weights.astype(BF16)


def one_hot(first, rows, width):
    wanted = first + lax.broadcasted_iota(jnp.int32, (rows, width), 0)
    column = lax.broadcasted_iota(jnp.int32, (rows, width), 1)
    return jnp.where(wanted == column, 1.0, 0.0)


def picker(place_ref, rows, width, sides):
    part = rows // QUAD
    pieces = []
    for k in range(QUAD):
        for side in sides:
            first = (place_ref[0] ^ side) * rows + (place_ref[1] ^ k) * part
            pieces.append(one_hot(first, part, width))
    return jnp.concatenate(pieces, axis=0).astype(BF16)


def split_head(head, outs):
    part = head.shape[0] // QUAD
    for k, out in enumerate(outs):
        out[...] = head[k * part : (k + 1) * part, :].astype(BF16)


def near_kernel(
    t1, i1, t0_far, i0_far, text_head_far, image_head_far,
    q_a, y_a, p_a, x_a, w_aa, gx, t0, i0, text_head, image_head, dots, sems,
):
    half = t0.shape[0]
    copies = [
        pltpu.make_async_copy(source, target, sems.at[n])
        for n, (source, target) in enumerate(
            ((t0_far, t0), (text_head_far, text_head), (i0_far, i0), (image_head_far, image_head))
        )
    ]
    for copy in copies:
        copy.start()
    copies[0].wait()
    copies[1].wait()
    q_a[:half, :] = dot_nn(t0[...], text_head[...])
    q_a[half:, :] = dot_nn(t1[...], text_head[...])
    copies[2].wait()
    copies[3].wait()
    p_a[:half, :] = dot_nn(i0[...], image_head[...])
    unit_rows(q_a, y_a)
    p_a[half:, :] = dot_nn(i1[...], image_head[...])
    unit_rows(p_a, x_a)
    dots[...] = dot_nt(x_a[...], y_a[...])
    weight_rows(dots, w_aa, 0)
    gx[...] = dot_nn(w_aa[...], y_a[...])


def rows_of(refs):
    return jnp.concatenate([ref[...] for ref in refs], axis=0)


def near_pull_kernel(place, t0, t1, i0, i1, x_a, w_aa, gy_a, pick_i, pick_t):
    half, width = t0.shape
    rows = pick_t.shape[0]
    pick = picker(place, rows, width, (0, 2))
    pick_i[:, :half] = dot_nt(pick, i0[...]).astype(BF16)
    pick_i[:, half:] = dot_nt(pick, i1[...]).astype(BF16)
    pick = picker(place, rows, width, (0,))
    pick_t[:, :half] = dot_nt(pick, t0[...]).astype(BF16)
    pick_t[:, half:] = dot_nt(pick, t1[...]).astype(BF16)
    gy_a[...] = dot_tn(w_aa[...], x_a[...])


def image_kernel(*refs):
    *features, text_head, p_a, x_a, gx_in, pick_i, q_b, y_b, w_ab, dp_a = refs[:-8]
    near_0, near_2, near_sent, far_0, far_1, far_sent, dots, gx = refs[-8:]
    q_b[...] = dot_nn(rows_of(features), text_head[...])
    unit_rows(q_b, y_b)
    dots[...] = dot_nt(x_a[...], y_b[...])
    weight_rows(dots, w_ab)
    gx[...] = gx_in[...] + dot_nn(w_ab[...], y_b[...])
    back_rows(p_a, gx, dp_a)
    head = dot_nn(pick_i[...], dp_a[...]).astype(BF16)
    part = near_0.shape[0]
    near_side, far_side = (
        [head[first : first + part, :] for first in range(side * part, 2 * QUAD * part, 2 * part)]
        for side in range(2)
    )
    near_0[...] = near_side[0]
    near_2[...] = near_side[2]
    near_sent[:part, :] = near_side[1]
    near_sent[part:, :] = near_side[3]
    far_0[...] = far_side[0]
    far_1[...] = far_side[1]
    far_sent[:part, :] = far_side[2]
    far_sent[part:, :] = far_side[3]


def text_pull_kernel(place, *refs):
    *features, x_a, w_ab, gy_b, pick_b = refs
    gy_b[...] = dot_tn(w_ab[...], x_a[...])
    pick = picker(place, pick_b.shape[0], x_a.shape[1], (0,))
    pick_b[...] = dot_nt(pick, rows_of(features)).astype(BF16)


def far_weights(core, x, y_a, y_b, w_a, w_b, d_a, d_b):
    d_a[...] = dot_nt(x, y_a[...])
    d_b[...] = dot_nt(x, y_b[...])
    weight_rows(d_a, w_a)
    weight_rows(d_b, w_b, core * x.shape[0])


def block_kernel(i2, image_head, y_a, y_b, x_first, x_second, w_a, w_b, p_b, x_b, d_a, d_b):
    middle = x_first.shape[0]
    p_b[...] = dot_nn(i2[...], image_head[...])
    unit_rows(p_b, x_b)
    x_first[...] = x_b[:middle, :]
    x_second[...] = x_b[middle:, :]
    far_weights(0, x_b[...], y_a, y_b, w_a, w_b, d_a, d_b)


def own_pull_kernel(x_first, x_second, w_a, w_b, gy_a_in, gy_b_in, gy_a, gy_b):
    x = rows_of((x_first, x_second))
    gy_a[...] = gy_a_in[...] + dot_tn(w_a[...], x)
    gy_b[...] = gy_b_in[...] + dot_tn(w_b[...], x)


def last_kernel(
    x_first, x_second, y_a, y_b, q_a, q_b, gy_a_in, gy_b_in, pick_a, pick_b,
    h0, h1, h2, h3, dq_a, gy_a, gy_b, dq_b, near_head, w_a, w_b, d_a, d_b,
):
    x = rows_of((x_first, x_second))
    far_weights(1, x, y_a, y_b, w_a, w_b, d_a, d_b)
    gy_a[...] = gy_a_in[...] + dot_tn(w_a[...], x)
    back_rows(q_a, gy_a, dq_a)
    gy_b[...] = gy_b_in[...] + dot_tn(w_b[...], x)
    near_head[...] = dot_nn(pick_a[...], dq_a[...])
    back_rows(q_b, gy_b, dq_b)
    split_head(near_head[...] + dot_nn(pick_b[...], dq_b[...]), (h0, h1, h2, h3))


def grad_kernel(back, head, out):
    out[...] = dot_nt(back[: out.shape[0], :], head[...])


def place_kernel(place, *refs):
    *pieces, out = refs
    part = pieces[0].shape[0]
    for k, piece in enumerate(pieces):
        first = pl.multiple_of((place[1] ^ k) * part, part)
        out[pl.ds(first, part), :] = piece[...].astype(F32)


def call(kernel, outs, scratch, args, mib, place=None, macs=0, keep=True, far=()):
    far = [pltpu.with_memory_space_constraint(a, pltpu.HBM) for a in far]
    args = [pltpu.with_memory_space_constraint(a, pltpu.VMEM) for a in args] + far
    specs = [pl.BlockSpec(memory_space=pltpu.VMEM)] * (len(args) - len(far))
    specs += [pl.BlockSpec(memory_space=pltpu.HBM)] * len(far)
    if place is not None:
        args, specs = [place, *args], [pl.BlockSpec(memory_space=pltpu.SMEM), *specs]
    shape = pltpu.VMEM if keep else jax.ShapeDtypeStruct
    return pl.pallas_call(
        kernel,
        out_shape=[shape(s, t) for s, t in outs],
        in_specs=specs,
        out_specs=[pl.BlockSpec(memory_space=pltpu.VMEM)] * len(outs),
        scratch_shapes=[pltpu.VMEM(s, t) for s, t in scratch]
        + [pltpu.SemaphoreType.DMA((len(far),))] * bool(far),
        compiler_params=pltpu.CompilerParams(vmem_limit_bytes=mib * 1024 * 1024),
        cost_estimate=pl.CostEstimate(flops=2 * macs, bytes_accessed=0, transcendentals=0),
    )(*args)


def swap(array, axis, size, mask):
    return lax.ppermute(array, axis, [(i, i ^ mask) for i in range(size)])


def after(value, other):
    return lax.optimization_barrier((value, other))[0]


def per_device(n_loop, n_cuts, image_features, text_features, image_head, text_head):
    half, width = image_features.shape
    near = 2 * half
    rows_out = width // n_loop
    part = rows_out // QUAD
    loop = functools.partial(swap, axis="loop", size=n_loop)
    cuts = functools.partial(swap, axis="cuts", size=n_cuts)
    macs = half * width * width

    def both(rows, order, count):
        rows = after(rows, order)
        return [rows] + [loop(piece, mask=1) for piece in jnp.split(rows, count)]

    def add(own, others):
        return sum((other.astype(F32) for other in others), own.astype(F32)).astype(BF16)

    def spread(total):
        return [total] + [cuts(total, mask=k) for k in range(1, QUAD)]

    t2 = loop(text_features, mask=2)
    i2 = loop(image_features, mask=2)
    place = jnp.stack([lax.axis_index("loop"), lax.axis_index("cuts") & (QUAD - 1)])
    place = place.astype(jnp.int32)
    t0, i0, place = lax.optimization_barrier((text_features, image_features, place))
    t1 = loop(t0, mask=1)
    i1 = loop(i0, mask=1)
    wide, wide_b = ((near, width), F32), ((near, width), BF16)
    tall, tall_b = ((half, width), F32), ((half, width), BF16)
    head_b = ((width, width), BF16)
    block_w, block_dots = ((half, near), BF16), ((half, near), F32)
    pick_one, pick_two = ((rows_out, near), BF16), ((2 * rows_out, near), BF16)
    q_a, y_a, p_a, x_a, w_aa, gx, t0, i0, text_head, image_head = call(
        near_kernel,
        [wide, wide_b, wide, wide_b, ((near, near), BF16), wide, tall_b, tall_b, head_b, head_b],
        [((near, near), F32)],
        (t1, i1),
        8,
        far=(t0, i0, text_head, image_head),
    )
    gy_a, pick_i, pick_a = call(
        near_pull_kernel,
        [wide, pick_two, pick_one],
        [],
        (t0, t1, i0, i1, x_a, w_aa),
        8,
        place,
    )
    far_text = both(t2, gy_a, 4)
    part_b, parts_b = ((part, width), BF16), ((2 * part, width), BF16)
    square_b, square = ((near, near), BF16), ((near, near), F32)
    q_b, y_b, w_ab, dp_a, near_0, near_2, near_sent, far_0, far_1, far_sent = call(
        image_kernel,
        [wide, wide_b, square_b, wide_b] + [part_b, part_b, parts_b] * 2,
        [square, wide],
        (*far_text, text_head, p_a, x_a, gx, pick_i),
        8,
    )
    near_came, far_came = cuts(near_sent, mask=1), cuts(far_sent, mask=2)
    gy_b, pick_b = call(
        text_pull_kernel,
        [wide, pick_one],
        [],
        (*far_text, after(x_a, dp_a), w_ab),
        8,
        place,
    )
    middle_b = ((half // 2, width), BF16)
    *x_2, w_2a, w_2b = call(
        block_kernel,
        [middle_b, middle_b, block_w, block_w],
        [tall, tall_b, block_dots, block_dots],
        (after(i2, gy_b), image_head, y_a, y_b),
        8,
    )
    x_3 = [loop(rows, mask=1) for rows in x_2]
    gy_a, gy_b = call(
        own_pull_kernel,
        [wide, wide],
        [],
        (*x_2, w_2a, w_2b, gy_a, gy_b),
        8,
    )
    near_came, far_came = after(near_came, gy_a), after(far_came, gy_a)
    near_sent, far_sent = add(near_2, [near_came[part:]]), add(far_1, [far_came[part:]])
    near_last, far_last = cuts(near_sent, mask=2), cuts(far_sent, mask=1)
    x_3 = [after(rows, (gy_a, near_sent, far_sent)) for rows in x_3]
    *text_parts, dq_a = call(
        last_kernel,
        [part_b] * QUAD + [wide_b],
        [wide, wide, wide_b, ((rows_out, width), F32), block_w, block_w, block_dots, block_dots],
        (*x_3, y_a, y_b, q_a, q_b, gy_a, gy_b, pick_a, pick_b),
        16,
    )
    text_others = [cuts(text_parts[k], mask=k) for k in range(1, QUAD)]
    far_sum = add(far_0, [far_came[:part], after(far_last, dq_a)])
    near_sum = add(near_0, [near_came[:part], after(near_last, dq_a)])
    image_sum = add(near_sum, [loop(far_sum, mask=2)])
    grads = [
        call(grad_kernel, [tall], [], (after(back, image_sum), head), 4, macs=2 * macs, keep=False)[0]
        for back, head in ((dp_a, image_head), (dq_a, text_head))
    ]
    text_sum = add(text_parts[0], [after(other, (image_sum, grads)) for other in text_others])
    image_sum = add(image_sum, [cuts(image_sum, mask=QUAD)])
    image_pieces = [image_sum, cuts(image_sum, mask=1), cuts(image_sum, mask=2)]
    image_pieces.append(cuts(image_pieces[2], mask=1))
    text_sum = add(text_sum, [after(cuts(text_sum, mask=QUAD), image_pieces[1])])
    image_out, text_out = (
        call(place_kernel, [((rows_out, width), F32)], [], pieces, 4, place, keep=False)[0]
        for pieces in (image_pieces, spread(text_sum))
    )
    return (*grads, image_out, text_out)


def solution(mesh):
    n_loop, n_cuts = mesh.shape["loop"], mesh.shape["cuts"]
    if n_loop == 4 and n_cuts == 2 * QUAD:
        body = functools.partial(per_device, n_loop, n_cuts)
    else:
        body = plain_device
    placed = (P(("cuts", "loop"), None), P(("cuts", "loop"), None), P(), P())
    return jax.shard_map(
        body,
        mesh=mesh,
        in_specs=placed,
        out_specs=(
            P(("cuts", "loop"), None),
            P(("cuts", "loop"), None),
            P("loop", None),
            P("loop", None),
        ),
        check_vma=False,
    )
```

```python
import functools

import jax
import jax.numpy as jnp
from jax import lax
from jax.experimental import pallas as pl
from jax.experimental.pallas import tpu as pltpu
from jax.sharding import PartitionSpec as P

SCORE_SCALE = 10.0
SCORE_BIAS = -2.5
EPSILON = 1e-06
QUAD = 4
STRIP = 16
LANES = 128
F32 = jnp.float32
BF16 = jnp.bfloat16


def normalize(features, weight_matrix):
    projected = jnp.dot(features, weight_matrix, preferred_element_type=jnp.float32)
    factor = lax.rsqrt(jnp.sum(projected * projected, axis=-1, keepdims=True) + EPSILON)
    return (projected * factor, factor)


def pair_weights(image_vectors, text_vectors, image_offset):
    pair_scores = SCORE_SCALE * dot_nt(image_vectors, text_vectors) + SCORE_BIAS
    row_ids = image_offset + lax.broadcasted_iota(jnp.int32, pair_scores.shape, 0)
    col_ids = lax.broadcasted_iota(jnp.int32, pair_scores.shape, 1)
    match_targets = jnp.where(row_ids == col_ids, 1.0, -1.0).astype(jnp.float32)
    return (SCORE_SCALE * -match_targets * jax.nn.sigmoid(-match_targets * pair_scores)).astype(
        jnp.bfloat16
    )


def norm_back(unit, factor, gradient):
    return (factor * (gradient - unit * jnp.sum(unit * gradient, axis=-1, keepdims=True))).astype(
        jnp.bfloat16
    )


def dot_nn(left, right):
    return lax.dot_general(left, right, (((1,), (0,)), ((), ())), preferred_element_type=F32)


def dot_nt(left, right):
    return lax.dot_general(left, right, (((1,), (1,)), ((), ())), preferred_element_type=F32)


def dot_tn(left, right):
    return lax.dot_general(left, right, (((0,), (0,)), ((), ())), preferred_element_type=F32)


def plain_device(image_features, text_features, image_head, text_head):
    row_count = image_features.shape[0]
    own_start = lax.axis_index("loop") * row_count
    image_unit, image_factor = normalize(image_features, image_head)
    text_unit, text_factor = normalize(text_features, text_head)
    image_vectors = image_unit.astype(jnp.bfloat16)
    text_vectors = text_unit.astype(jnp.bfloat16)
    arrived = lax.all_gather(text_vectors, "loop", axis=0, tiled=True)
    weights = pair_weights(image_vectors, arrived, own_start)
    summed = jnp.dot(weights, arrived, preferred_element_type=jnp.float32)
    text_attraction = lax.psum_scatter(
        dot_tn(weights, image_vectors).astype(jnp.bfloat16), "loop", scatter_dimension=0, tiled=True
    ).astype(jnp.float32)
    image_back = norm_back(image_unit, image_factor, summed)
    text_back = norm_back(text_unit, text_factor, text_attraction)
    heads = []
    for features, back in ((image_features, image_back), (text_features, text_back)):
        term = dot_tn(features, back).astype(jnp.bfloat16)
        part = lax.psum_scatter(term, "loop", scatter_dimension=0, tiled=True)
        heads.append(lax.psum(part, "cuts").astype(jnp.float32))
    return (dot_nt(image_back, image_head), dot_nt(text_back, text_head), heads[0], heads[1])


def factor_of(ref, rows):
    p = ref[rows, :]
    return lax.rsqrt(jnp.sum(p * p, axis=-1, keepdims=True) + EPSILON)


def unit_rows(projected_ref, vectors_ref):
    for first in range(0, projected_ref.shape[0], STRIP):
        rows = slice(first, first + STRIP)
        factor = factor_of(projected_ref, rows)
        vectors_ref[rows, :] = (projected_ref[rows, :] * factor).astype(BF16)


def back_rows(projected_ref, gradient_ref, back_ref):
    for first in range(0, projected_ref.shape[0], STRIP):
        rows = slice(first, first + STRIP)
        factor = factor_of(projected_ref, rows)
        along = jnp.sum(projected_ref[rows, :] * gradient_ref[rows, :], axis=-1, keepdims=True)
        along = factor * factor * factor * along
        back = factor * gradient_ref[rows, :] - along * projected_ref[rows, :]
        back_ref[rows, :] = back.astype(BF16)


def weight_rows(dots_ref, weights_ref, pairs_from=None):
    half_scale = 0.5 * SCORE_SCALE
    for first in range(0, dots_ref.shape[0], STRIP):
        rows = slice(first, first + STRIP)
        score = jnp.tanh(half_scale * dots_ref[rows, :] + 0.5 * SCORE_BIAS)
        weights = half_scale + half_scale * score
        if pairs_from is None:
            weights_ref[rows, :] = weights.astype(BF16)
            continue
        pair = pairs_from + first
        left = pair // LANES * LANES
        right = min(left + LANES, weights.shape[1])
        shape = (STRIP, right - left)
        column = lax.broadcasted_iota(jnp.int32, shape, 1)
        same = column == lax.broadcasted_iota(jnp.int32, shape, 0) + (pair - left)
        middle = weights[:, left:right] - jnp.where(same, SCORE_SCALE, 0.0)
        pieces = [weights[:, :left], middle, weights[:, right:]]
        weights = jnp.concatenate([p for p in pieces if p.shape[1]], axis=1)
        weights_ref[rows, :] = weights.astype(BF16)


def one_hot(first, rows, width):
    wanted = first + lax.broadcasted_iota(jnp.int32, (rows, width), 0)
    column = lax.broadcasted_iota(jnp.int32, (rows, width), 1)
    return jnp.where(wanted == column, 1.0, 0.0)


def picker(place_ref, rows, width, sides):
    part = rows // QUAD
    pieces = []
    for k in range(QUAD):
        for side in sides:
            first = (place_ref[0] ^ side) * rows + (place_ref[1] ^ k) * part
            pieces.append(one_hot(first, part, width))
    return jnp.concatenate(pieces, axis=0).astype(BF16)


def split_head(head, outs):
    part = head.shape[0] // QUAD
    for k, out in enumerate(outs):
        out[...] = head[k * part : (k + 1) * part, :].astype(BF16)


def near_kernel(
    t1, i1, t0_far, i0_far, text_head_far, image_head_far,
    q_a, y_a, p_a, x_a, w_aa, gx, t0, i0, text_head, image_head, dots, sems,
):
    half = t0.shape[0]
    copies = [
        pltpu.make_async_copy(source, target, sems.at[n])
        for n, (source, target) in enumerate(
            ((t0_far, t0), (text_head_far, text_head), (i0_far, i0), (image_head_far, image_head))
        )
    ]
    for copy in copies:
        copy.start()
    copies[0].wait()
    copies[1].wait()
    q_a[:half, :] = dot_nn(t0[...], text_head[...])
    q_a[half:, :] = dot_nn(t1[...], text_head[...])
    copies[2].wait()
    copies[3].wait()
    p_a[:half, :] = dot_nn(i0[...], image_head[...])
    unit_rows(q_a, y_a)
    p_a[half:, :] = dot_nn(i1[...], image_head[...])
    unit_rows(p_a, x_a)
    dots[...] = dot_nt(x_a[...], y_a[...])
    weight_rows(dots, w_aa, 0)
    gx[...] = dot_nn(w_aa[...], y_a[...])


def rows_of(refs):
    return jnp.concatenate([ref[...] for ref in refs], axis=0)


def near_pull_kernel(place, t0, t1, i0, i1, x_a, w_aa, gy_a, pick_i, pick_t):
    half, width = t0.shape
    rows = pick_t.shape[0]
    pick = picker(place, rows, width, (0, 2))
    pick_i[:, :half] = dot_nt(pick, i0[...]).astype(BF16)
    pick_i[:, half:] = dot_nt(pick, i1[...]).astype(BF16)
    pick = picker(place, rows, width, (0,))
    pick_t[:, :half] = dot_nt(pick, t0[...]).astype(BF16)
    pick_t[:, half:] = dot_nt(pick, t1[...]).astype(BF16)
    gy_a[...] = dot_tn(w_aa[...], x_a[...])


def image_kernel(*refs):
    *features, text_head, p_a, x_a, gx_in, pick_i, q_b, y_b, w_ab, dp_a = refs[:-8]
    near_0, near_2, near_sent, far_0, far_1, far_sent, dots, gx = refs[-8:]
    q_b[...] = dot_nn(rows_of(features), text_head[...])
    unit_rows(q_b, y_b)
    dots[...] = dot_nt(x_a[...], y_b[...])
    weight_rows(dots, w_ab)
    gx[...] = gx_in[...] + dot_nn(w_ab[...], y_b[...])
    back_rows(p_a, gx, dp_a)
    head = dot_nn(pick_i[...], dp_a[...]).astype(BF16)
    part = near_0.shape[0]
    near_side, far_side = (
        [head[first : first + part, :] for first in range(side * part, 2 * QUAD * part, 2 * part)]
        for side in range(2)
    )
    near_0[...] = near_side[0]
    near_2[...] = near_side[2]
    near_sent[:part, :] = near_side[1]
    near_sent[part:, :] = near_side[3]
    far_0[...] = far_side[0]
    far_1[...] = far_side[1]
    far_sent[:part, :] = far_side[2]
    far_sent[part:, :] = far_side[3]


def text_pull_kernel(place, *refs):
    *features, x_a, w_ab, gy_b, pick_b = refs
    gy_b[...] = dot_tn(w_ab[...], x_a[...])
    pick = picker(place, pick_b.shape[0], x_a.shape[1], (0,))
    pick_b[...] = dot_nt(pick, rows_of(features)).astype(BF16)


def far_weights(core, x, y_a, y_b, w_a, w_b, d_a, d_b):
    d_a[...] = dot_nt(x, y_a[...])
    d_b[...] = dot_nt(x, y_b[...])
    weight_rows(d_a, w_a)
    weight_rows(d_b, w_b, core * x.shape[0])


def block_kernel(i2, image_head, y_a, y_b, x_first, x_second, w_a, w_b, p_b, x_b, d_a, d_b):
    middle = x_first.shape[0]
    p_b[...] = dot_nn(i2[...], image_head[...])
    unit_rows(p_b, x_b)
    x_first[...] = x_b[:middle, :]
    x_second[...] = x_b[middle:, :]
    far_weights(0, x_b[...], y_a, y_b, w_a, w_b, d_a, d_b)


def own_pull_kernel(x_first, x_second, w_a, w_b, gy_a_in, gy_b_in, gy_a, gy_b):
    x = rows_of((x_first, x_second))
    gy_a[...] = gy_a_in[...] + dot_tn(w_a[...], x)
    gy_b[...] = gy_b_in[...] + dot_tn(w_b[...], x)


def last_kernel(
    x_first, x_second, y_a, y_b, q_a, q_b, gy_a_in, gy_b_in, pick_a, pick_b,
    h0, h1, h2, h3, dq_a, gy_a, gy_b, dq_b, near_head, w_a, w_b, d_a, d_b,
):
    x = rows_of((x_first, x_second))
    far_weights(1, x, y_a, y_b, w_a, w_b, d_a, d_b)
    gy_a[...] = gy_a_in[...] + dot_tn(w_a[...], x)
    back_rows(q_a, gy_a, dq_a)
    gy_b[...] = gy_b_in[...] + dot_tn(w_b[...], x)
    near_head[...] = dot_nn(pick_a[...], dq_a[...])
    back_rows(q_b, gy_b, dq_b)
    split_head(near_head[...] + dot_nn(pick_b[...], dq_b[...]), (h0, h1, h2, h3))


def grad_kernel(back, head, out):
    out[...] = dot_nt(back[: out.shape[0], :], head[...])


def place_kernel(place, *refs):
    *pieces, out = refs
    part = pieces[0].shape[0]
    for k, piece in enumerate(pieces):
        first = pl.multiple_of((place[1] ^ k) * part, part)
        out[pl.ds(first, part), :] = piece[...].astype(F32)


def call(kernel, outs, scratch, args, mib, place=None, macs=0, keep=True, far=()):
    far = [pltpu.with_memory_space_constraint(a, pltpu.HBM) for a in far]
    args = [pltpu.with_memory_space_constraint(a, pltpu.VMEM) for a in args] + far
    specs = [pl.BlockSpec(memory_space=pltpu.VMEM)] * (len(args) - len(far))
    specs += [pl.BlockSpec(memory_space=pltpu.HBM)] * len(far)
    if place is not None:
        args, specs = [place, *args], [pl.BlockSpec(memory_space=pltpu.SMEM), *specs]
    shape = pltpu.VMEM if keep else jax.ShapeDtypeStruct
    return pl.pallas_call(
        kernel,
        out_shape=[shape(s, t) for s, t in outs],
        in_specs=specs,
        out_specs=[pl.BlockSpec(memory_space=pltpu.VMEM)] * len(outs),
        scratch_shapes=[pltpu.VMEM(s, t) for s, t in scratch]
        + [pltpu.SemaphoreType.DMA((len(far),))] * bool(far),
        compiler_params=pltpu.CompilerParams(vmem_limit_bytes=mib * 1024 * 1024),
        cost_estimate=pl.CostEstimate(flops=2 * macs, bytes_accessed=0, transcendentals=0),
    )(*args)


def swap(array, axis, size, mask):
    return lax.ppermute(array, axis, [(i, i ^ mask) for i in range(size)])


def after(value, other):
    return lax.optimization_barrier((value, other))[0]


def per_device(n_loop, n_cuts, image_features, text_features, image_head, text_head):
    half, width = image_features.shape
    near = 2 * half
    rows_out = width // n_loop
    part = rows_out // QUAD
    loop = functools.partial(swap, axis="loop", size=n_loop)
    cuts = functools.partial(swap, axis="cuts", size=n_cuts)
    macs = half * width * width

    def both(rows, order, count):
        rows = after(rows, order)
        return [rows] + [loop(piece, mask=1) for piece in jnp.split(rows, count)]

    def add(own, others):
        return sum((other.astype(F32) for other in others), own.astype(F32)).astype(BF16)

    def placed(pieces):
        outs = [((rows_out, width), F32)]
        return call(place_kernel, outs, [], pieces, 4, place, keep=False)[0]

    def spread(total):
        return [total] + [cuts(total, mask=k) for k in range(1, QUAD)]

    t2 = loop(text_features, mask=2)
    i2 = loop(image_features, mask=2)
    place = jnp.stack([lax.axis_index("loop"), lax.axis_index("cuts") & (QUAD - 1)])
    place = place.astype(jnp.int32)
    t0, i0, place = lax.optimization_barrier((text_features, image_features, place))
    t1 = loop(t0, mask=1)
    i1 = loop(i0, mask=1)
    wide, wide_b = ((near, width), F32), ((near, width), BF16)
    tall, tall_b = ((half, width), F32), ((half, width), BF16)
    head_b = ((width, width), BF16)
    block_w, block_dots = ((half, near), BF16), ((half, near), F32)
    pick_one, pick_two = ((rows_out, near), BF16), ((2 * rows_out, near), BF16)
    q_a, y_a, p_a, x_a, w_aa, gx, t0, i0, text_head, image_head = call(
        near_kernel,
        [wide, wide_b, wide, wide_b, ((near, near), BF16), wide, tall_b, tall_b, head_b, head_b],
        [((near, near), F32)],
        (t1, i1),
        8,
        far=(t0, i0, text_head, image_head),
    )
    gy_a, pick_i, pick_a = call(
        near_pull_kernel,
        [wide, pick_two, pick_one],
        [],
        (t0, t1, i0, i1, x_a, w_aa),
        8,
        place,
    )
    far_text = both(t2, gy_a, 4)
    part_b, parts_b = ((part, width), BF16), ((2 * part, width), BF16)
    square_b, square = ((near, near), BF16), ((near, near), F32)
    q_b, y_b, w_ab, dp_a, near_0, near_2, near_sent, far_0, far_1, far_sent = call(
        image_kernel,
        [wide, wide_b, square_b, wide_b] + [part_b, part_b, parts_b] * 2,
        [square, wide],
        (*far_text, text_head, p_a, x_a, gx, pick_i),
        8,
    )
    near_came, far_came = cuts(near_sent, mask=1), cuts(far_sent, mask=2)
    gy_b, pick_b = call(
        text_pull_kernel,
        [wide, pick_one],
        [],
        (*far_text, after(x_a, dp_a), w_ab),
        8,
        place,
    )
    middle_b = ((half // 2, width), BF16)
    *x_2, w_2a, w_2b = call(
        block_kernel,
        [middle_b, middle_b, block_w, block_w],
        [tall, tall_b, block_dots, block_dots],
        (after(i2, gy_b), image_head, y_a, y_b),
        8,
    )
    x_3 = [loop(rows, mask=1) for rows in x_2]
    gy_a, gy_b = call(
        own_pull_kernel,
        [wide, wide],
        [],
        (*x_2, w_2a, w_2b, gy_a, gy_b),
        8,
    )
    near_came, far_came = after(near_came, gy_a), after(far_came, gy_a)
    near_sent, far_sent = add(near_2, [near_came[part:]]), add(far_1, [far_came[part:]])
    near_last, far_last = cuts(near_sent, mask=2), cuts(far_sent, mask=1)
    x_3 = [after(rows, (gy_a, near_sent, far_sent)) for rows in x_3]
    *text_parts, dq_a = call(
        last_kernel,
        [part_b] * QUAD + [wide_b],
        [wide, wide, wide_b, ((rows_out, width), F32), block_w, block_w, block_dots, block_dots],
        (*x_3, y_a, y_b, q_a, q_b, gy_a, gy_b, pick_a, pick_b),
        16,
    )
    text_others = [cuts(text_parts[k], mask=k) for k in range(1, QUAD)]
    far_sum = add(far_0, [far_came[:part], after(far_last, dq_a)])
    near_sum = add(near_0, [near_came[:part], after(near_last, dq_a)])
    image_sum = add(near_sum, [loop(far_sum, mask=2)])
    grads = [
        call(grad_kernel, [tall], [], (after(back, image_sum), head), 4, macs=2 * macs, keep=False)[0]
        for back, head in ((dp_a, image_head), (dq_a, text_head))
    ]
    text_sum = add(text_parts[0], [after(other, (image_sum, grads)) for other in text_others])
    image_sum = add(image_sum, [cuts(image_sum, mask=QUAD)])
    image_pieces = [image_sum, cuts(image_sum, mask=1), cuts(image_sum, mask=2)]
    text_sum = add(text_sum, [after(cuts(text_sum, mask=QUAD), image_pieces[1])])
    text_out = placed(spread(text_sum))
    image_pieces.append(after(cuts(image_pieces[2], mask=1), text_out))
    image_out = placed(image_pieces)
    return (*grads, image_out, text_out)


def solution(mesh):
    n_loop, n_cuts = mesh.shape["loop"], mesh.shape["cuts"]
    if n_loop == 4 and n_cuts == 2 * QUAD:
        body = functools.partial(per_device, n_loop, n_cuts)
    else:
        body = plain_device
    placed = (P(("cuts", "loop"), None), P(("cuts", "loop"), None), P(), P())
    return jax.shard_map(
        body,
        mesh=mesh,
        in_specs=placed,
        out_specs=(
            P(("cuts", "loop"), None),
            P(("cuts", "loop"), None),
            P("loop", None),
            P("loop", None),
        ),
        check_vma=False,
    )
```

```python
import functools

import jax
import jax.numpy as jnp
from jax import lax
from jax.experimental import pallas as pl
from jax.experimental.pallas import tpu as pltpu
from jax.sharding import PartitionSpec as P

SCORE_SCALE = 10.0
SCORE_BIAS = -2.5
EPSILON = 1e-06
QUAD = 4
STRIP = 16
LANES = 128
F32 = jnp.float32
BF16 = jnp.bfloat16


def normalize(features, weight_matrix):
    projected = jnp.dot(features, weight_matrix, preferred_element_type=jnp.float32)
    factor = lax.rsqrt(jnp.sum(projected * projected, axis=-1, keepdims=True) + EPSILON)
    return (projected * factor, factor)


def pair_weights(image_vectors, text_vectors, image_offset):
    pair_scores = SCORE_SCALE * dot_nt(image_vectors, text_vectors) + SCORE_BIAS
    row_ids = image_offset + lax.broadcasted_iota(jnp.int32, pair_scores.shape, 0)
    col_ids = lax.broadcasted_iota(jnp.int32, pair_scores.shape, 1)
    match_targets = jnp.where(row_ids == col_ids, 1.0, -1.0).astype(jnp.float32)
    return (SCORE_SCALE * -match_targets * jax.nn.sigmoid(-match_targets * pair_scores)).astype(
        jnp.bfloat16
    )


def norm_back(unit, factor, gradient):
    return (factor * (gradient - unit * jnp.sum(unit * gradient, axis=-1, keepdims=True))).astype(
        jnp.bfloat16
    )


def dot_nn(left, right):
    return lax.dot_general(left, right, (((1,), (0,)), ((), ())), preferred_element_type=F32)


def dot_nt(left, right):
    return lax.dot_general(left, right, (((1,), (1,)), ((), ())), preferred_element_type=F32)


def dot_tn(left, right):
    return lax.dot_general(left, right, (((0,), (0,)), ((), ())), preferred_element_type=F32)


def plain_device(image_features, text_features, image_head, text_head):
    row_count = image_features.shape[0]
    own_start = lax.axis_index("loop") * row_count
    image_unit, image_factor = normalize(image_features, image_head)
    text_unit, text_factor = normalize(text_features, text_head)
    image_vectors = image_unit.astype(jnp.bfloat16)
    text_vectors = text_unit.astype(jnp.bfloat16)
    arrived = lax.all_gather(text_vectors, "loop", axis=0, tiled=True)
    weights = pair_weights(image_vectors, arrived, own_start)
    summed = jnp.dot(weights, arrived, preferred_element_type=jnp.float32)
    text_attraction = lax.psum_scatter(
        dot_tn(weights, image_vectors).astype(jnp.bfloat16), "loop", scatter_dimension=0, tiled=True
    ).astype(jnp.float32)
    image_back = norm_back(image_unit, image_factor, summed)
    text_back = norm_back(text_unit, text_factor, text_attraction)
    heads = []
    for features, back in ((image_features, image_back), (text_features, text_back)):
        term = dot_tn(features, back).astype(jnp.bfloat16)
        part = lax.psum_scatter(term, "loop", scatter_dimension=0, tiled=True)
        heads.append(lax.psum(part, "cuts").astype(jnp.float32))
    return (dot_nt(image_back, image_head), dot_nt(text_back, text_head), heads[0], heads[1])


def factor_of(ref, rows):
    p = ref[rows, :]
    return lax.rsqrt(jnp.sum(p * p, axis=-1, keepdims=True) + EPSILON)


def unit_rows(projected_ref, vectors_ref):
    for first in range(0, projected_ref.shape[0], STRIP):
        rows = slice(first, first + STRIP)
        factor = factor_of(projected_ref, rows)
        vectors_ref[rows, :] = (projected_ref[rows, :] * factor).astype(BF16)


def back_rows(projected_ref, gradient_ref, back_ref):
    for first in range(0, projected_ref.shape[0], STRIP):
        rows = slice(first, first + STRIP)
        factor = factor_of(projected_ref, rows)
        along = jnp.sum(projected_ref[rows, :] * gradient_ref[rows, :], axis=-1, keepdims=True)
        along = factor * factor * factor * along
        back = factor * gradient_ref[rows, :] - along * projected_ref[rows, :]
        back_ref[rows, :] = back.astype(BF16)


def weight_rows(dots_ref, weights_ref, pairs_from=None):
    half_scale = 0.5 * SCORE_SCALE
    for first in range(0, dots_ref.shape[0], STRIP):
        rows = slice(first, first + STRIP)
        score = jnp.tanh(half_scale * dots_ref[rows, :] + 0.5 * SCORE_BIAS)
        weights = half_scale + half_scale * score
        if pairs_from is None:
            weights_ref[rows, :] = weights.astype(BF16)
            continue
        pair = pairs_from + first
        left = pair // LANES * LANES
        right = min(left + LANES, weights.shape[1])
        shape = (STRIP, right - left)
        column = lax.broadcasted_iota(jnp.int32, shape, 1)
        same = column == lax.broadcasted_iota(jnp.int32, shape, 0) + (pair - left)
        middle = weights[:, left:right] - jnp.where(same, SCORE_SCALE, 0.0)
        pieces = [weights[:, :left], middle, weights[:, right:]]
        weights = jnp.concatenate([p for p in pieces if p.shape[1]], axis=1)
        weights_ref[rows, :] = weights.astype(BF16)


def one_hot(first, rows, width):
    wanted = first + lax.broadcasted_iota(jnp.int32, (rows, width), 0)
    column = lax.broadcasted_iota(jnp.int32, (rows, width), 1)
    return jnp.where(wanted == column, 1.0, 0.0)


def slot_masks(place_ref):
    core = place_ref[0] & 1
    return (0, 1 + core, 2 - core, 3)


def picker(place_ref, rows, width, sides):
    part = rows // QUAD
    pieces = []
    for mask in slot_masks(place_ref):
        for side in sides:
            first = (place_ref[0] ^ side) * rows + (place_ref[1] ^ mask) * part
            pieces.append(one_hot(first, part, width))
    return jnp.concatenate(pieces, axis=0).astype(BF16)


def split_head(head, outs):
    part = head.shape[0] // QUAD
    for k, out in enumerate(outs):
        out[...] = head[k * part : (k + 1) * part, :].astype(BF16)


def near_kernel(
    t1, i1, t0_far, i0_far, text_head_far, image_head_far,
    q_a, y_a, p_a, x_a, w_aa, gx, t0, i0, text_head, image_head, dots, sems,
):
    half = t0.shape[0]
    copies = [
        pltpu.make_async_copy(source, target, sems.at[n])
        for n, (source, target) in enumerate(
            ((t0_far, t0), (text_head_far, text_head), (i0_far, i0), (image_head_far, image_head))
        )
    ]
    for copy in copies:
        copy.start()
    copies[0].wait()
    copies[1].wait()
    q_a[:half, :] = dot_nn(t0[...], text_head[...])
    q_a[half:, :] = dot_nn(t1[...], text_head[...])
    copies[2].wait()
    copies[3].wait()
    p_a[:half, :] = dot_nn(i0[...], image_head[...])
    unit_rows(q_a, y_a)
    p_a[half:, :] = dot_nn(i1[...], image_head[...])
    unit_rows(p_a, x_a)
    dots[...] = dot_nt(x_a[...], y_a[...])
    weight_rows(dots, w_aa, 0)
    gx[...] = dot_nn(w_aa[...], y_a[...])


def rows_of(refs):
    return jnp.concatenate([ref[...] for ref in refs], axis=0)


def near_pull_kernel(place, t0, t1, i0, i1, x_a, w_aa, gy_a, pick_i, pick_t):
    half, width = t0.shape
    rows = pick_t.shape[0]
    pick = picker(place, rows, width, (0, 2))
    pick_i[:, :half] = dot_nt(pick, i0[...]).astype(BF16)
    pick_i[:, half:] = dot_nt(pick, i1[...]).astype(BF16)
    pick = picker(place, rows, width, (0,))
    pick_t[:, :half] = dot_nt(pick, t0[...]).astype(BF16)
    pick_t[:, half:] = dot_nt(pick, t1[...]).astype(BF16)
    gy_a[...] = dot_tn(w_aa[...], x_a[...])


def image_kernel(*refs):
    *features, text_head, p_a, x_a, gx_in, pick_i, q_b, y_b, w_ab, dp_a = refs[:-8]
    near_0, near_2, near_sent, far_0, far_1, far_sent, dots, gx = refs[-8:]
    q_b[...] = dot_nn(rows_of(features), text_head[...])
    unit_rows(q_b, y_b)
    dots[...] = dot_nt(x_a[...], y_b[...])
    weight_rows(dots, w_ab)
    gx[...] = gx_in[...] + dot_nn(w_ab[...], y_b[...])
    back_rows(p_a, gx, dp_a)
    head = dot_nn(pick_i[...], dp_a[...]).astype(BF16)
    part = near_0.shape[0]
    near_side, far_side = (
        [head[first : first + part, :] for first in range(side * part, 2 * QUAD * part, 2 * part)]
        for side in range(2)
    )
    near_0[...] = near_side[0]
    near_2[...] = near_side[2]
    near_sent[:part, :] = near_side[1]
    near_sent[part:, :] = near_side[3]
    far_0[...] = far_side[0]
    far_1[...] = far_side[1]
    far_sent[:part, :] = far_side[2]
    far_sent[part:, :] = far_side[3]


def text_pull_kernel(place, *refs):
    *features, x_a, w_ab, gy_b, pick_b = refs
    gy_b[...] = dot_tn(w_ab[...], x_a[...])
    pick = picker(place, pick_b.shape[0], x_a.shape[1], (0,))
    pick_b[...] = dot_nt(pick, rows_of(features)).astype(BF16)


def far_weights(core, x, y_a, y_b, w_a, w_b, d_a, d_b):
    d_a[...] = dot_nt(x, y_a[...])
    d_b[...] = dot_nt(x, y_b[...])
    weight_rows(d_a, w_a)
    weight_rows(d_b, w_b, core * x.shape[0])


def block_kernel(i2, image_head, y_a, y_b, x_first, x_second, w_a, w_b, p_b, x_b, d_a, d_b):
    middle = x_first.shape[0]
    p_b[...] = dot_nn(i2[...], image_head[...])
    unit_rows(p_b, x_b)
    x_first[...] = x_b[:middle, :]
    x_second[...] = x_b[middle:, :]
    far_weights(0, x_b[...], y_a, y_b, w_a, w_b, d_a, d_b)


def own_pull_kernel(x_first, x_second, w_a, w_b, gy_a_in, gy_b_in, gy_a, gy_b):
    x = rows_of((x_first, x_second))
    gy_a[...] = gy_a_in[...] + dot_tn(w_a[...], x)
    gy_b[...] = gy_b_in[...] + dot_tn(w_b[...], x)


def last_kernel(
    x_first, x_second, y_a, y_b, q_a, q_b, gy_a_in, gy_b_in, pick_a, pick_b,
    h0, h1, h2, h3, dq_a, gy_a, gy_b, dq_b, near_head, w_a, w_b, d_a, d_b,
):
    x = rows_of((x_first, x_second))
    far_weights(1, x, y_a, y_b, w_a, w_b, d_a, d_b)
    gy_a[...] = gy_a_in[...] + dot_tn(w_a[...], x)
    back_rows(q_a, gy_a, dq_a)
    gy_b[...] = gy_b_in[...] + dot_tn(w_b[...], x)
    near_head[...] = dot_nn(pick_a[...], dq_a[...])
    back_rows(q_b, gy_b, dq_b)
    split_head(near_head[...] + dot_nn(pick_b[...], dq_b[...]), (h0, h1, h2, h3))


def grad_kernel(back, head, out):
    out[...] = dot_nt(back[: out.shape[0], :], head[...])


def place_kernel(place, *refs):
    *pieces, out = refs
    part = pieces[0].shape[0]
    for mask, piece in zip(slot_masks(place), pieces):
        first = pl.multiple_of((place[1] ^ mask) * part, part)
        out[pl.ds(first, part), :] = piece[...].astype(F32)


def call(kernel, outs, scratch, args, mib, place=None, macs=0, keep=True, far=()):
    far = [pltpu.with_memory_space_constraint(a, pltpu.HBM) for a in far]
    args = [pltpu.with_memory_space_constraint(a, pltpu.VMEM) for a in args] + far
    specs = [pl.BlockSpec(memory_space=pltpu.VMEM)] * (len(args) - len(far))
    specs += [pl.BlockSpec(memory_space=pltpu.HBM)] * len(far)
    if place is not None:
        args, specs = [place, *args], [pl.BlockSpec(memory_space=pltpu.SMEM), *specs]
    shape = pltpu.VMEM if keep else jax.ShapeDtypeStruct
    return pl.pallas_call(
        kernel,
        out_shape=[shape(s, t) for s, t in outs],
        in_specs=specs,
        out_specs=[pl.BlockSpec(memory_space=pltpu.VMEM)] * len(outs),
        scratch_shapes=[pltpu.VMEM(s, t) for s, t in scratch]
        + [pltpu.SemaphoreType.DMA((len(far),))] * bool(far),
        compiler_params=pltpu.CompilerParams(vmem_limit_bytes=mib * 1024 * 1024),
        cost_estimate=pl.CostEstimate(flops=2 * macs, bytes_accessed=0, transcendentals=0),
    )(*args)


def swap(array, axis, size, mask):
    return lax.ppermute(array, axis, [(i, i ^ mask) for i in range(size)])


def swap_slot(array, slot, n_cuts, n_loop):
    masks = ((1, 2), (2, 1), (3, 3))[slot - 1]
    pairs = [
        (c * n_loop + l, (c ^ masks[l % 2]) * n_loop + l) for c in range(n_cuts) for l in range(n_loop)
    ]
    return lax.ppermute(array, ("cuts", "loop"), pairs)


def after(value, other):
    return lax.optimization_barrier((value, other))[0]


def per_device(n_loop, n_cuts, image_features, text_features, image_head, text_head):
    half, width = image_features.shape
    near = 2 * half
    rows_out = width // n_loop
    part = rows_out // QUAD
    loop = functools.partial(swap, axis="loop", size=n_loop)
    cuts = functools.partial(swap, axis="cuts", size=n_cuts)
    quad = functools.partial(swap_slot, n_cuts=n_cuts, n_loop=n_loop)
    macs = half * width * width

    def both(rows, order, count):
        rows = after(rows, order)
        return [rows] + [loop(piece, mask=1) for piece in jnp.split(rows, count)]

    def add(own, others):
        return sum((other.astype(F32) for other in others), own.astype(F32)).astype(BF16)

    def spread(total):
        return [total] + [quad(total, slot=slot) for slot in range(1, QUAD)]

    t2 = loop(text_features, mask=2)
    i2 = loop(image_features, mask=2)
    place = jnp.stack([lax.axis_index("loop"), lax.axis_index("cuts") & (QUAD - 1)])
    place = place.astype(jnp.int32)
    t0, i0, place = lax.optimization_barrier((text_features, image_features, place))
    t1 = loop(t0, mask=1)
    i1 = loop(i0, mask=1)
    wide, wide_b = ((near, width), F32), ((near, width), BF16)
    tall, tall_b = ((half, width), F32), ((half, width), BF16)
    head_b = ((width, width), BF16)
    block_w, block_dots = ((half, near), BF16), ((half, near), F32)
    pick_one, pick_two = ((rows_out, near), BF16), ((2 * rows_out, near), BF16)
    q_a, y_a, p_a, x_a, w_aa, gx, t0, i0, text_head, image_head = call(
        near_kernel,
        [wide, wide_b, wide, wide_b, ((near, near), BF16), wide, tall_b, tall_b, head_b, head_b],
        [((near, near), F32)],
        (t1, i1),
        8,
        far=(t0, i0, text_head, image_head),
    )
    gy_a, pick_i, pick_a = call(
        near_pull_kernel,
        [wide, pick_two, pick_one],
        [],
        (t0, t1, i0, i1, x_a, w_aa),
        8,
        place,
    )
    far_text = both(t2, gy_a, 4)
    part_b, parts_b = ((part, width), BF16), ((2 * part, width), BF16)
    square_b, square = ((near, near), BF16), ((near, near), F32)
    q_b, y_b, w_ab, dp_a, near_0, near_2, near_sent, far_0, far_1, far_sent = call(
        image_kernel,
        [wide, wide_b, square_b, wide_b] + [part_b, part_b, parts_b] * 2,
        [square, wide],
        (*far_text, text_head, p_a, x_a, gx, pick_i),
        8,
    )
    near_came, far_came = quad(near_sent, slot=1), quad(far_sent, slot=2)
    gy_b, pick_b = call(
        text_pull_kernel,
        [wide, pick_one],
        [],
        (*far_text, after(x_a, dp_a), w_ab),
        8,
        place,
    )
    middle_b = ((half // 2, width), BF16)
    *x_2, w_2a, w_2b = call(
        block_kernel,
        [middle_b, middle_b, block_w, block_w],
        [tall, tall_b, block_dots, block_dots],
        (after(i2, gy_b), image_head, y_a, y_b),
        8,
    )
    x_3 = [loop(rows, mask=1) for rows in x_2]
    gy_a, gy_b = call(
        own_pull_kernel,
        [wide, wide],
        [],
        (*x_2, w_2a, w_2b, gy_a, gy_b),
        8,
    )
    near_came, far_came = after(near_came, gy_a), after(far_came, gy_a)
    near_sent, far_sent = add(near_2, [near_came[part:]]), add(far_1, [far_came[part:]])
    near_last, far_last = quad(near_sent, slot=2), quad(far_sent, slot=1)
    x_3 = [after(rows, (gy_a, near_sent, far_sent)) for rows in x_3]
    *text_parts, dq_a = call(
        last_kernel,
        [part_b] * QUAD + [wide_b],
        [wide, wide, wide_b, ((rows_out, width), F32), block_w, block_w, block_dots, block_dots],
        (*x_3, y_a, y_b, q_a, q_b, gy_a, gy_b, pick_a, pick_b),
        16,
    )
    text_others = [quad(text_parts[slot], slot=slot) for slot in range(1, QUAD)]
    far_sum = add(far_0, [far_came[:part], after(far_last, dq_a)])
    near_sum = add(near_0, [near_came[:part], after(near_last, dq_a)])
    image_sum = add(near_sum, [loop(far_sum, mask=2)])
    grads = [
        call(grad_kernel, [tall], [], (after(back, image_sum), head), 4, macs=2 * macs, keep=False)[0]
        for back, head in ((dp_a, image_head), (dq_a, text_head))
    ]
    text_sum = add(text_parts[0], [after(other, (image_sum, grads)) for other in text_others])
    image_sum = add(image_sum, [cuts(image_sum, mask=QUAD)])
    image_pieces = spread(image_sum)
    text_sum = add(text_sum, [after(cuts(text_sum, mask=QUAD), image_pieces[1])])
    image_out, text_out = (
        call(place_kernel, [((rows_out, width), F32)], [], pieces, 4, place, keep=False)[0]
        for pieces in (image_pieces, spread(text_sum))
    )
    return (*grads, image_out, text_out)


def solution(mesh):
    n_loop, n_cuts = mesh.shape["loop"], mesh.shape["cuts"]
    if n_loop == 4 and n_cuts == 2 * QUAD:
        body = functools.partial(per_device, n_loop, n_cuts)
    else:
        body = plain_device
    placed = (P(("cuts", "loop"), None), P(("cuts", "loop"), None), P(), P())
    return jax.shard_map(
        body,
        mesh=mesh,
        in_specs=placed,
        out_specs=(
            P(("cuts", "loop"), None),
            P(("cuts", "loop"), None),
            P("loop", None),
            P("loop", None),
        ),
        check_vma=False,
    )
```

```python
import functools

import jax
import jax.numpy as jnp
from jax import lax
from jax.experimental import pallas as pl
from jax.experimental.pallas import tpu as pltpu
from jax.sharding import PartitionSpec as P

SCORE_SCALE = 10.0
SCORE_BIAS = -2.5
EPSILON = 1e-06
QUAD = 4
STRIP = 16
LANES = 128
F32 = jnp.float32
BF16 = jnp.bfloat16


def normalize(features, weight_matrix):
    projected = jnp.dot(features, weight_matrix, preferred_element_type=jnp.float32)
    factor = lax.rsqrt(jnp.sum(projected * projected, axis=-1, keepdims=True) + EPSILON)
    return (projected * factor, factor)


def pair_weights(image_vectors, text_vectors, image_offset):
    pair_scores = SCORE_SCALE * dot_nt(image_vectors, text_vectors) + SCORE_BIAS
    row_ids = image_offset + lax.broadcasted_iota(jnp.int32, pair_scores.shape, 0)
    col_ids = lax.broadcasted_iota(jnp.int32, pair_scores.shape, 1)
    match_targets = jnp.where(row_ids == col_ids, 1.0, -1.0).astype(jnp.float32)
    return (SCORE_SCALE * -match_targets * jax.nn.sigmoid(-match_targets * pair_scores)).astype(
        jnp.bfloat16
    )


def norm_back(unit, factor, gradient):
    return (factor * (gradient - unit * jnp.sum(unit * gradient, axis=-1, keepdims=True))).astype(
        jnp.bfloat16
    )


def dot_nn(left, right):
    return lax.dot_general(left, right, (((1,), (0,)), ((), ())), preferred_element_type=F32)


def dot_nt(left, right):
    return lax.dot_general(left, right, (((1,), (1,)), ((), ())), preferred_element_type=F32)


def dot_tn(left, right):
    return lax.dot_general(left, right, (((0,), (0,)), ((), ())), preferred_element_type=F32)


def plain_device(image_features, text_features, image_head, text_head):
    row_count = image_features.shape[0]
    own_start = lax.axis_index("loop") * row_count
    image_unit, image_factor = normalize(image_features, image_head)
    text_unit, text_factor = normalize(text_features, text_head)
    image_vectors = image_unit.astype(jnp.bfloat16)
    text_vectors = text_unit.astype(jnp.bfloat16)
    arrived = lax.all_gather(text_vectors, "loop", axis=0, tiled=True)
    weights = pair_weights(image_vectors, arrived, own_start)
    summed = jnp.dot(weights, arrived, preferred_element_type=jnp.float32)
    text_attraction = lax.psum_scatter(
        dot_tn(weights, image_vectors).astype(jnp.bfloat16), "loop", scatter_dimension=0, tiled=True
    ).astype(jnp.float32)
    image_back = norm_back(image_unit, image_factor, summed)
    text_back = norm_back(text_unit, text_factor, text_attraction)
    heads = []
    for features, back in ((image_features, image_back), (text_features, text_back)):
        term = dot_tn(features, back).astype(jnp.bfloat16)
        part = lax.psum_scatter(term, "loop", scatter_dimension=0, tiled=True)
        heads.append(lax.psum(part, "cuts").astype(jnp.float32))
    return (dot_nt(image_back, image_head), dot_nt(text_back, text_head), heads[0], heads[1])


def factor_of(ref, rows):
    p = ref[rows, :]
    return lax.rsqrt(jnp.sum(p * p, axis=-1, keepdims=True) + EPSILON)


def unit_rows(projected_ref, vectors_ref):
    for first in range(0, projected_ref.shape[0], STRIP):
        rows = slice(first, first + STRIP)
        factor = factor_of(projected_ref, rows)
        vectors_ref[rows, :] = (projected_ref[rows, :] * factor).astype(BF16)


def back_rows(projected_ref, gradient_ref, back_ref):
    for first in range(0, projected_ref.shape[0], STRIP):
        rows = slice(first, first + STRIP)
        factor = factor_of(projected_ref, rows)
        along = jnp.sum(projected_ref[rows, :] * gradient_ref[rows, :], axis=-1, keepdims=True)
        along = factor * factor * factor * along
        back = factor * gradient_ref[rows, :] - along * projected_ref[rows, :]
        back_ref[rows, :] = back.astype(BF16)


def weight_rows(dots_ref, weights_ref, pairs_from=None):
    half_scale = 0.5 * SCORE_SCALE
    for first in range(0, dots_ref.shape[0], STRIP):
        rows = slice(first, first + STRIP)
        score = jnp.tanh(half_scale * dots_ref[rows, :] + 0.5 * SCORE_BIAS)
        weights = half_scale + half_scale * score
        if pairs_from is None:
            weights_ref[rows, :] = weights.astype(BF16)
            continue
        pair = pairs_from + first
        left = pair // LANES * LANES
        right = min(left + LANES, weights.shape[1])
        shape = (STRIP, right - left)
        column = lax.broadcasted_iota(jnp.int32, shape, 1)
        same = column == lax.broadcasted_iota(jnp.int32, shape, 0) + (pair - left)
        middle = weights[:, left:right] - jnp.where(same, SCORE_SCALE, 0.0)
        pieces = [weights[:, :left], middle, weights[:, right:]]
        weights = jnp.concatenate([p for p in pieces if p.shape[1]], axis=1)
        weights_ref[rows, :] = weights.astype(BF16)


def one_hot(first, rows, width):
    wanted = first + lax.broadcasted_iota(jnp.int32, (rows, width), 0)
    column = lax.broadcasted_iota(jnp.int32, (rows, width), 1)
    return jnp.where(wanted == column, 1.0, 0.0)


def picker(place_ref, rows, width, sides):
    part = rows // QUAD
    pieces = []
    for k in range(QUAD):
        for side in sides:
            first = (place_ref[0] ^ side) * rows + (place_ref[1] ^ k) * part
            pieces.append(one_hot(first, part, width))
    return jnp.concatenate(pieces, axis=0).astype(BF16)


def split_head(head, outs):
    part = head.shape[0] // QUAD
    for k, out in enumerate(outs):
        out[...] = head[k * part : (k + 1) * part, :].astype(BF16)


def near_kernel(
    t1, i1, t0_far, i0_far, text_head_far, image_head_far,
    q_a, y_a, p_a, x_a, w_aa, gx, t0, i0, text_head, image_head, dots, sems,
):
    half = t0.shape[0]
    copies = [
        pltpu.make_async_copy(source, target, sems.at[n])
        for n, (source, target) in enumerate(
            ((t0_far, t0), (text_head_far, text_head), (i0_far, i0), (image_head_far, image_head))
        )
    ]
    for copy in copies:
        copy.start()
    copies[0].wait()
    copies[1].wait()
    q_a[:half, :] = dot_nn(t0[...], text_head[...])
    q_a[half:, :] = dot_nn(t1[...], text_head[...])
    copies[2].wait()
    copies[3].wait()
    p_a[:half, :] = dot_nn(i0[...], image_head[...])
    unit_rows(q_a, y_a)
    p_a[half:, :] = dot_nn(i1[...], image_head[...])
    unit_rows(p_a, x_a)
    dots[...] = dot_nt(x_a[...], y_a[...])
    weight_rows(dots, w_aa, 0)
    gx[...] = dot_nn(w_aa[...], y_a[...])


def rows_of(refs):
    return jnp.concatenate([ref[...] for ref in refs], axis=0)


def near_pull_kernel(place, t0, t1, i0, i1, x_a, w_aa, gy_a, pick_i, pick_t):
    half, width = t0.shape
    rows = pick_t.shape[0]
    pick = picker(place, rows, width, (0, 2))
    pick_i[:, :half] = dot_nt(pick, i0[...]).astype(BF16)
    pick_i[:, half:] = dot_nt(pick, i1[...]).astype(BF16)
    pick = picker(place, rows, width, (0,))
    pick_t[:, :half] = dot_nt(pick, t0[...]).astype(BF16)
    pick_t[:, half:] = dot_nt(pick, t1[...]).astype(BF16)
    gy_a[...] = dot_tn(w_aa[...], x_a[...])


def image_kernel(*refs):
    *features, text_head, p_a, x_a, gx_in, pick_i, q_b, y_b, w_ab, dp_a = refs[:-8]
    near_0, near_2, near_sent, far_0, far_1, far_sent, dots, gx = refs[-8:]
    q_b[...] = dot_nn(rows_of(features), text_head[...])
    unit_rows(q_b, y_b)
    dots[...] = dot_nt(x_a[...], y_b[...])
    weight_rows(dots, w_ab)
    gx[...] = gx_in[...] + dot_nn(w_ab[...], y_b[...])
    back_rows(p_a, gx, dp_a)
    head = dot_nn(pick_i[...], dp_a[...]).astype(BF16)
    part = near_0.shape[0]
    near_side, far_side = (
        [head[first : first + part, :] for first in range(side * part, 2 * QUAD * part, 2 * part)]
        for side in range(2)
    )
    near_0[...] = near_side[0]
    near_2[...] = near_side[2]
    near_sent[:part, :] = near_side[1]
    near_sent[part:, :] = near_side[3]
    far_0[...] = far_side[0]
    far_1[...] = far_side[1]
    far_sent[:part, :] = far_side[2]
    far_sent[part:, :] = far_side[3]


def text_pull_kernel(place, *refs):
    *features, x_a, w_ab, gy_b, pick_b = refs
    gy_b[...] = dot_tn(w_ab[...], x_a[...])
    pick = picker(place, pick_b.shape[0], x_a.shape[1], (0,))
    pick_b[...] = dot_nt(pick, rows_of(features)).astype(BF16)


def far_weights(core, x, y_a, y_b, w_a, w_b, d_a, d_b):
    d_a[...] = dot_nt(x, y_a[...])
    d_b[...] = dot_nt(x, y_b[...])
    weight_rows(d_a, w_a)
    weight_rows(d_b, w_b, core * x.shape[0])


def block_kernel(i2, image_head, y_a, y_b, x_first, x_second, w_a, w_b, p_b, x_b, d_a, d_b):
    middle = x_first.shape[0]
    p_b[...] = dot_nn(i2[...], image_head[...])
    unit_rows(p_b, x_b)
    x_first[...] = x_b[:middle, :]
    x_second[...] = x_b[middle:, :]
    far_weights(0, x_b[...], y_a, y_b, w_a, w_b, d_a, d_b)


def own_pull_kernel(x_first, x_second, w_a, w_b, gy_a_in, gy_b_in, gy_a, gy_b):
    x = rows_of((x_first, x_second))
    gy_a[...] = gy_a_in[...] + dot_tn(w_a[...], x)
    gy_b[...] = gy_b_in[...] + dot_tn(w_b[...], x)


def other_pull_kernel(
    x_first, x_second, y_a, y_b, gy_a_in, gy_b_in, gy_a, gy_b, w_a, w_b, d_a, d_b
):
    x = rows_of((x_first, x_second))
    far_weights(1, x, y_a, y_b, w_a, w_b, d_a, d_b)
    gy_a[...] = gy_a_in[...] + dot_tn(w_a[...], x)
    gy_b[...] = gy_b_in[...] + dot_tn(w_b[...], x)


def last_kernel(q_a, q_b, gy_a, gy_b, pick_a, pick_b, h0, h1, h2, h3, dq_a, dq_b, near_head):
    back_rows(q_a, gy_a, dq_a)
    near_head[...] = dot_nn(pick_a[...], dq_a[...])
    back_rows(q_b, gy_b, dq_b)
    split_head(near_head[...] + dot_nn(pick_b[...], dq_b[...]), (h0, h1, h2, h3))


def grad_kernel(back, head, out):
    out[...] = dot_nt(back[: out.shape[0], :], head[...])


def place_kernel(place, *refs):
    *pieces, out = refs
    part = pieces[0].shape[0]
    for k, piece in enumerate(pieces):
        first = pl.multiple_of((place[1] ^ k) * part, part)
        out[pl.ds(first, part), :] = piece[...].astype(F32)


def call(kernel, outs, scratch, args, mib, place=None, macs=0, keep=True, far=()):
    far = [pltpu.with_memory_space_constraint(a, pltpu.HBM) for a in far]
    args = [pltpu.with_memory_space_constraint(a, pltpu.VMEM) for a in args] + far
    specs = [pl.BlockSpec(memory_space=pltpu.VMEM)] * (len(args) - len(far))
    specs += [pl.BlockSpec(memory_space=pltpu.HBM)] * len(far)
    if place is not None:
        args, specs = [place, *args], [pl.BlockSpec(memory_space=pltpu.SMEM), *specs]
    shape = pltpu.VMEM if keep else jax.ShapeDtypeStruct
    return pl.pallas_call(
        kernel,
        out_shape=[shape(s, t) for s, t in outs],
        in_specs=specs,
        out_specs=[pl.BlockSpec(memory_space=pltpu.VMEM)] * len(outs),
        scratch_shapes=[pltpu.VMEM(s, t) for s, t in scratch]
        + [pltpu.SemaphoreType.DMA((len(far),))] * bool(far),
        compiler_params=pltpu.CompilerParams(vmem_limit_bytes=mib * 1024 * 1024),
        cost_estimate=pl.CostEstimate(flops=2 * macs, bytes_accessed=0, transcendentals=0),
    )(*args)


def swap(array, axis, size, mask):
    return lax.ppermute(array, axis, [(i, i ^ mask) for i in range(size)])


def after(value, other):
    return lax.optimization_barrier((value, other))[0]


def per_device(n_loop, n_cuts, image_features, text_features, image_head, text_head):
    half, width = image_features.shape
    near = 2 * half
    rows_out = width // n_loop
    part = rows_out // QUAD
    loop = functools.partial(swap, axis="loop", size=n_loop)
    cuts = functools.partial(swap, axis="cuts", size=n_cuts)
    macs = half * width * width

    def both(rows, order, count):
        rows = after(rows, order)
        return [rows] + [loop(piece, mask=1) for piece in jnp.split(rows, count)]

    def add(own, others):
        return sum((other.astype(F32) for other in others), own.astype(F32)).astype(BF16)

    def spread(total):
        return [total] + [cuts(total, mask=k) for k in range(1, QUAD)]

    t2 = loop(text_features, mask=2)
    i2 = loop(image_features, mask=2)
    place = jnp.stack([lax.axis_index("loop"), lax.axis_index("cuts") & (QUAD - 1)])
    place = place.astype(jnp.int32)
    t0, i0, place = lax.optimization_barrier((text_features, image_features, place))
    t1 = loop(t0, mask=1)
    i1 = loop(i0, mask=1)
    wide, wide_b = ((near, width), F32), ((near, width), BF16)
    tall, tall_b = ((half, width), F32), ((half, width), BF16)
    head_b = ((width, width), BF16)
    block_w, block_dots = ((half, near), BF16), ((half, near), F32)
    pick_one, pick_two = ((rows_out, near), BF16), ((2 * rows_out, near), BF16)
    q_a, y_a, p_a, x_a, w_aa, gx, t0, i0, text_head, image_head = call(
        near_kernel,
        [wide, wide_b, wide, wide_b, ((near, near), BF16), wide, tall_b, tall_b, head_b, head_b],
        [((near, near), F32)],
        (t1, i1),
        8,
        far=(t0, i0, text_head, image_head),
    )
    gy_a, pick_i, pick_a = call(
        near_pull_kernel,
        [wide, pick_two, pick_one],
        [],
        (t0, t1, i0, i1, x_a, w_aa),
        8,
        place,
    )
    far_text = both(t2, gy_a, 4)
    part_b, parts_b = ((part, width), BF16), ((2 * part, width), BF16)
    square_b, square = ((near, near), BF16), ((near, near), F32)
    q_b, y_b, w_ab, dp_a, near_0, near_2, near_sent, far_0, far_1, far_sent = call(
        image_kernel,
        [wide, wide_b, square_b, wide_b] + [part_b, part_b, parts_b] * 2,
        [square, wide],
        (*far_text, text_head, p_a, x_a, gx, pick_i),
        8,
    )
    near_came, far_came = cuts(near_sent, mask=1), cuts(far_sent, mask=2)
    gy_b, pick_b = call(
        text_pull_kernel,
        [wide, pick_one],
        [],
        (*far_text, after(x_a, dp_a), w_ab),
        8,
        place,
    )
    middle_b = ((half // 2, width), BF16)
    *x_2, w_2a, w_2b = call(
        block_kernel,
        [middle_b, middle_b, block_w, block_w],
        [tall, tall_b, block_dots, block_dots],
        (after(i2, gy_b), image_head, y_a, y_b),
        8,
    )
    x_3 = [loop(rows, mask=1) for rows in x_2]
    gy_a, gy_b = call(
        own_pull_kernel,
        [wide, wide],
        [],
        (*x_2, w_2a, w_2b, gy_a, gy_b),
        8,
    )
    x_3 = [after(rows, gy_a) for rows in x_3]
    gy_a, gy_b = call(
        other_pull_kernel,
        [wide, wide],
        [block_w, block_w, block_dots, block_dots],
        (*x_3, y_a, y_b, gy_a, gy_b),
        8,
    )
    near_came, far_came = after(near_came, gy_a), after(far_came, gy_a)
    near_sent, far_sent = add(near_2, [near_came[part:]]), add(far_1, [far_came[part:]])
    near_last, far_last = cuts(near_sent, mask=2), cuts(far_sent, mask=1)
    *text_parts, dq_a = call(
        last_kernel,
        [part_b] * QUAD + [wide_b],
        [wide_b, ((rows_out, width), F32)],
        (q_a, q_b, after(gy_a, (near_sent, far_sent)), gy_b, pick_a, pick_b),
        12,
    )
    text_others = [cuts(text_parts[k], mask=k) for k in range(1, QUAD)]
    far_sum = add(far_0, [far_came[:part], after(far_last, dq_a)])
    near_sum = add(near_0, [near_came[:part], after(near_last, dq_a)])
    image_sum = add(near_sum, [loop(far_sum, mask=2)])
    grads = [
        call(grad_kernel, [tall], [], (after(back, image_sum), head), 4, macs=2 * macs, keep=False)[0]
        for back, head in ((dp_a, image_head), (dq_a, text_head))
    ]
    text_sum = add(text_parts[0], [after(other, (image_sum, grads)) for other in text_others])
    image_sum = add(image_sum, [cuts(image_sum, mask=QUAD)])
    image_pieces = spread(image_sum)
    text_sum = add(text_sum, [after(cuts(text_sum, mask=QUAD), image_pieces[1])])
    image_out, text_out = (
        call(place_kernel, [((rows_out, width), F32)], [], pieces, 4, place, keep=False)[0]
        for pieces in (image_pieces, spread(text_sum))
    )
    return (*grads, image_out, text_out)


def solution(mesh):
    n_loop, n_cuts = mesh.shape["loop"], mesh.shape["cuts"]
    if n_loop == 4 and n_cuts == 2 * QUAD:
        body = functools.partial(per_device, n_loop, n_cuts)
    else:
        body = plain_device
    placed = (P(("cuts", "loop"), None), P(("cuts", "loop"), None), P(), P())
    return jax.shard_map(
        body,
        mesh=mesh,
        in_specs=placed,
        out_specs=(
            P(("cuts", "loop"), None),
            P(("cuts", "loop"), None),
            P("loop", None),
            P("loop", None),
        ),
        check_vma=False,
    )
```

```python
import functools

import jax
import jax.numpy as jnp
from jax import lax
from jax.experimental import pallas as pl
from jax.experimental.pallas import tpu as pltpu
from jax.sharding import PartitionSpec as P

SCORE_SCALE = 10.0
SCORE_BIAS = -2.5
EPSILON = 1e-06
QUAD = 4
STRIP = 16
LANES = 128
F32 = jnp.float32
BF16 = jnp.bfloat16


def normalize(features, weight_matrix):
    projected = jnp.dot(features, weight_matrix, preferred_element_type=jnp.float32)
    factor = lax.rsqrt(jnp.sum(projected * projected, axis=-1, keepdims=True) + EPSILON)
    return (projected * factor, factor)


def pair_weights(image_vectors, text_vectors, image_offset):
    pair_scores = SCORE_SCALE * dot_nt(image_vectors, text_vectors) + SCORE_BIAS
    row_ids = image_offset + lax.broadcasted_iota(jnp.int32, pair_scores.shape, 0)
    col_ids = lax.broadcasted_iota(jnp.int32, pair_scores.shape, 1)
    match_targets = jnp.where(row_ids == col_ids, 1.0, -1.0).astype(jnp.float32)
    return (SCORE_SCALE * -match_targets * jax.nn.sigmoid(-match_targets * pair_scores)).astype(
        jnp.bfloat16
    )


def norm_back(unit, factor, gradient):
    return (factor * (gradient - unit * jnp.sum(unit * gradient, axis=-1, keepdims=True))).astype(
        jnp.bfloat16
    )


def dot_nn(left, right):
    return lax.dot_general(left, right, (((1,), (0,)), ((), ())), preferred_element_type=F32)


def dot_nt(left, right):
    return lax.dot_general(left, right, (((1,), (1,)), ((), ())), preferred_element_type=F32)


def dot_tn(left, right):
    return lax.dot_general(left, right, (((0,), (0,)), ((), ())), preferred_element_type=F32)


def plain_device(image_features, text_features, image_head, text_head):
    row_count = image_features.shape[0]
    own_start = lax.axis_index("loop") * row_count
    image_unit, image_factor = normalize(image_features, image_head)
    text_unit, text_factor = normalize(text_features, text_head)
    image_vectors = image_unit.astype(jnp.bfloat16)
    text_vectors = text_unit.astype(jnp.bfloat16)
    arrived = lax.all_gather(text_vectors, "loop", axis=0, tiled=True)
    weights = pair_weights(image_vectors, arrived, own_start)
    summed = jnp.dot(weights, arrived, preferred_element_type=jnp.float32)
    text_attraction = lax.psum_scatter(
        dot_tn(weights, image_vectors).astype(jnp.bfloat16), "loop", scatter_dimension=0, tiled=True
    ).astype(jnp.float32)
    image_back = norm_back(image_unit, image_factor, summed)
    text_back = norm_back(text_unit, text_factor, text_attraction)
    heads = []
    for features, back in ((image_features, image_back), (text_features, text_back)):
        term = dot_tn(features, back).astype(jnp.bfloat16)
        part = lax.psum_scatter(term, "loop", scatter_dimension=0, tiled=True)
        heads.append(lax.psum(part, "cuts").astype(jnp.float32))
    return (dot_nt(image_back, image_head), dot_nt(text_back, text_head), heads[0], heads[1])


def factor_of(ref, rows):
    p = ref[rows, :]
    return lax.rsqrt(jnp.sum(p * p, axis=-1, keepdims=True) + EPSILON)


def unit_rows(projected_ref, vectors_ref):
    for first in range(0, projected_ref.shape[0], STRIP):
        rows = slice(first, first + STRIP)
        factor = factor_of(projected_ref, rows)
        vectors_ref[rows, :] = (projected_ref[rows, :] * factor).astype(BF16)


def back_rows(projected_ref, gradient_ref, back_ref):
    for first in range(0, projected_ref.shape[0], STRIP):
        rows = slice(first, first + STRIP)
        factor = factor_of(projected_ref, rows)
        along = jnp.sum(projected_ref[rows, :] * gradient_ref[rows, :], axis=-1, keepdims=True)
        along = factor * factor * factor * along
        back = factor * gradient_ref[rows, :] - along * projected_ref[rows, :]
        back_ref[rows, :] = back.astype(BF16)


def weight_rows(dots_ref, weights_ref, pairs_from=None):
    half_scale = 0.5 * SCORE_SCALE
    for first in range(0, dots_ref.shape[0], STRIP):
        rows = slice(first, first + STRIP)
        score = jnp.tanh(half_scale * dots_ref[rows, :] + 0.5 * SCORE_BIAS)
        weights = half_scale + half_scale * score
        if pairs_from is None:
            weights_ref[rows, :] = weights.astype(BF16)
            continue
        pair = pairs_from + first
        left = pair // LANES * LANES
        right = min(left + LANES, weights.shape[1])
        shape = (STRIP, right - left)
        column = lax.broadcasted_iota(jnp.int32, shape, 1)
        same = column == lax.broadcasted_iota(jnp.int32, shape, 0) + (pair - left)
        middle = weights[:, left:right] - jnp.where(same, SCORE_SCALE, 0.0)
        pieces = [weights[:, :left], middle, weights[:, right:]]
        weights = jnp.concatenate([p for p in pieces if p.shape[1]], axis=1)
        weights_ref[rows, :] = weights.astype(BF16)


def one_hot(first, rows, width):
    wanted = first + lax.broadcasted_iota(jnp.int32, (rows, width), 0)
    column = lax.broadcasted_iota(jnp.int32, (rows, width), 1)
    return jnp.where(wanted == column, 1.0, 0.0)


def picker(place_ref, rows, width, sides):
    part = rows // QUAD
    pieces = []
    for k in range(QUAD):
        for side in sides:
            first = (place_ref[0] ^ side) * rows + (place_ref[1] ^ k) * part
            pieces.append(one_hot(first, part, width))
    return jnp.concatenate(pieces, axis=0).astype(BF16)


def split_head(head, outs):
    part = head.shape[0] // QUAD
    for k, out in enumerate(outs):
        out[...] = head[k * part : (k + 1) * part, :].astype(BF16)


def near_kernel(
    t1, i1, t0_far, i0_far, text_head_far, image_head_far,
    q_a, y_a, p_a, x_a, w_aa, gx, t0, i0, text_head, image_head, dots, sems,
):
    half = t0.shape[0]
    copies = [
        pltpu.make_async_copy(source, target, sems.at[n])
        for n, (source, target) in enumerate(
            ((t0_far, t0), (text_head_far, text_head), (i0_far, i0), (image_head_far, image_head))
        )
    ]
    for copy in copies:
        copy.start()
    copies[0].wait()
    copies[1].wait()
    q_a[:half, :] = dot_nn(t0[...], text_head[...])
    q_a[half:, :] = dot_nn(t1[...], text_head[...])
    copies[2].wait()
    copies[3].wait()
    p_a[:half, :] = dot_nn(i0[...], image_head[...])
    unit_rows(q_a, y_a)
    p_a[half:, :] = dot_nn(i1[...], image_head[...])
    unit_rows(p_a, x_a)
    dots[...] = dot_nt(x_a[...], y_a[...])
    weight_rows(dots, w_aa, 0)
    gx[...] = dot_nn(w_aa[...], y_a[...])


def rows_of(refs):
    return jnp.concatenate([ref[...] for ref in refs], axis=0)


def near_pull_kernel(place, t0, t1, i0, i1, x_a, w_aa, gy_a, pick_i, pick_t):
    half, width = t0.shape
    rows = pick_t.shape[0]
    pick = picker(place, rows, width, (0, 2))
    pick_i[:, :half] = dot_nt(pick, i0[...]).astype(BF16)
    pick_i[:, half:] = dot_nt(pick, i1[...]).astype(BF16)
    pick = picker(place, rows, width, (0,))
    pick_t[:, :half] = dot_nt(pick, t0[...]).astype(BF16)
    pick_t[:, half:] = dot_nt(pick, t1[...]).astype(BF16)
    gy_a[...] = dot_tn(w_aa[...], x_a[...])


def image_kernel(*refs):
    *features, text_head, p_a, x_a, gx_in, pick_i, q_b, y_b, w_ab, dp_a = refs[:-6]
    *parts, dots, gx = refs[-6:]
    q_b[...] = dot_nn(rows_of(features), text_head[...])
    unit_rows(q_b, y_b)
    dots[...] = dot_nt(x_a[...], y_b[...])
    weight_rows(dots, w_ab)
    gx[...] = gx_in[...] + dot_nn(w_ab[...], y_b[...])
    back_rows(p_a, gx, dp_a)
    split_head(dot_nn(pick_i[...], dp_a[...]), parts)


def text_pull_kernel(place, *refs):
    *features, x_a, w_ab, gy_b, pick_b = refs
    gy_b[...] = dot_tn(w_ab[...], x_a[...])
    pick = picker(place, pick_b.shape[0], x_a.shape[1], (0,))
    pick_b[...] = dot_nt(pick, rows_of(features)).astype(BF16)


def far_weights(core, x, y_a, y_b, w_a, w_b, d_a, d_b):
    d_a[...] = dot_nt(x, y_a[...])
    d_b[...] = dot_nt(x, y_b[...])
    weight_rows(d_a, w_a)
    weight_rows(d_b, w_b, core * x.shape[0])


def block_kernel(i2, image_head, y_a, y_b, x_first, x_second, w_a, w_b, p_b, x_b, d_a, d_b):
    middle = x_first.shape[0]
    p_b[...] = dot_nn(i2[...], image_head[...])
    unit_rows(p_b, x_b)
    x_first[...] = x_b[:middle, :]
    x_second[...] = x_b[middle:, :]
    far_weights(0, x_b[...], y_a, y_b, w_a, w_b, d_a, d_b)


def own_pull_kernel(x_first, x_second, w_a, w_b, gy_a_in, gy_b_in, gy_a, gy_b):
    x = rows_of((x_first, x_second))
    gy_a[...] = gy_a_in[...] + dot_tn(w_a[...], x)
    gy_b[...] = gy_b_in[...] + dot_tn(w_b[...], x)


def last_kernel(
    x_first, x_second, y_a, y_b, q_a, q_b, gy_a_in, gy_b_in, pick_a, pick_b,
    h0, h1, h2, h3, dq_a, gy_a, gy_b, dq_b, near_head, w_a, w_b, d_a, d_b,
):
    x = rows_of((x_first, x_second))
    far_weights(1, x, y_a, y_b, w_a, w_b, d_a, d_b)
    gy_a[...] = gy_a_in[...] + dot_tn(w_a[...], x)
    back_rows(q_a, gy_a, dq_a)
    gy_b[...] = gy_b_in[...] + dot_tn(w_b[...], x)
    near_head[...] = dot_nn(pick_a[...], dq_a[...])
    back_rows(q_b, gy_b, dq_b)
    split_head(near_head[...] + dot_nn(pick_b[...], dq_b[...]), (h0, h1, h2, h3))


def grad_kernel(back, head, out):
    out[...] = dot_nt(back[: out.shape[0], :], head[...])


def place_kernel(place, *refs):
    *pieces, out = refs
    part = pieces[0].shape[0]
    for k, piece in enumerate(pieces):
        first = pl.multiple_of((place[1] ^ k) * part, part)
        out[pl.ds(first, part), :] = piece[...].astype(F32)


def call(kernel, outs, scratch, args, mib, place=None, macs=0, keep=True, far=()):
    far = [pltpu.with_memory_space_constraint(a, pltpu.HBM) for a in far]
    args = [pltpu.with_memory_space_constraint(a, pltpu.VMEM) for a in args] + far
    specs = [pl.BlockSpec(memory_space=pltpu.VMEM)] * (len(args) - len(far))
    specs += [pl.BlockSpec(memory_space=pltpu.HBM)] * len(far)
    if place is not None:
        args, specs = [place, *args], [pl.BlockSpec(memory_space=pltpu.SMEM), *specs]
    shape = pltpu.VMEM if keep else jax.ShapeDtypeStruct
    return pl.pallas_call(
        kernel,
        out_shape=[shape(s, t) for s, t in outs],
        in_specs=specs,
        out_specs=[pl.BlockSpec(memory_space=pltpu.VMEM)] * len(outs),
        scratch_shapes=[pltpu.VMEM(s, t) for s, t in scratch]
        + [pltpu.SemaphoreType.DMA((len(far),))] * bool(far),
        compiler_params=pltpu.CompilerParams(vmem_limit_bytes=mib * 1024 * 1024),
        cost_estimate=pl.CostEstimate(flops=2 * macs, bytes_accessed=0, transcendentals=0),
    )(*args)


def swap(array, axis, size, mask):
    return lax.ppermute(array, axis, [(i, i ^ mask) for i in range(size)])


def after(value, other):
    return lax.optimization_barrier((value, other))[0]


def per_device(n_loop, n_cuts, image_features, text_features, image_head, text_head):
    half, width = image_features.shape
    near = 2 * half
    rows_out = width // n_loop
    part = rows_out // QUAD
    loop = functools.partial(swap, axis="loop", size=n_loop)
    cuts = functools.partial(swap, axis="cuts", size=n_cuts)
    macs = half * width * width

    def both(rows, order, count):
        rows = after(rows, order)
        return [rows] + [loop(piece, mask=1) for piece in jnp.split(rows, count)]

    def add(own, others):
        return sum((other.astype(F32) for other in others), own.astype(F32)).astype(BF16)

    def spread(total):
        return [total] + [cuts(total, mask=k) for k in range(1, QUAD)]

    t2 = loop(text_features, mask=2)
    i2 = loop(image_features, mask=2)
    place = jnp.stack([lax.axis_index("loop"), lax.axis_index("cuts") & (QUAD - 1)])
    place = place.astype(jnp.int32)
    t0, i0, place = lax.optimization_barrier((text_features, image_features, place))
    t1 = loop(t0, mask=1)
    i1 = loop(i0, mask=1)
    wide, wide_b = ((near, width), F32), ((near, width), BF16)
    tall, tall_b = ((half, width), F32), ((half, width), BF16)
    head_b = ((width, width), BF16)
    block_w, block_dots = ((half, near), BF16), ((half, near), F32)
    pick_one, pick_two = ((rows_out, near), BF16), ((2 * rows_out, near), BF16)
    q_a, y_a, p_a, x_a, w_aa, gx, t0, i0, text_head, image_head = call(
        near_kernel,
        [wide, wide_b, wide, wide_b, ((near, near), BF16), wide, tall_b, tall_b, head_b, head_b],
        [((near, near), F32)],
        (t1, i1),
        8,
        far=(t0, i0, text_head, image_head),
    )
    gy_a, pick_i, pick_a = call(
        near_pull_kernel,
        [wide, pick_two, pick_one],
        [],
        (t0, t1, i0, i1, x_a, w_aa),
        8,
        place,
    )
    far_text = both(t2, gy_a, 4)
    part_b, parts_b = ((part, width), BF16), ((2 * part, width), BF16)
    square_b, square = ((near, near), BF16), ((near, near), F32)
    q_b, y_b, w_ab, dp_a, *image_parts = call(
        image_kernel,
        [wide, wide_b, square_b, wide_b] + [parts_b] * QUAD,
        [square, wide],
        (*far_text, text_head, p_a, x_a, gx, pick_i),
        8,
    )
    image_others = [cuts(image_parts[k], mask=k) for k in range(1, QUAD)]
    gy_b, pick_b = call(
        text_pull_kernel,
        [wide, pick_one],
        [],
        (*far_text, after(x_a, dp_a), w_ab),
        8,
        place,
    )
    middle_b = ((half // 2, width), BF16)
    *x_2, w_2a, w_2b = call(
        block_kernel,
        [middle_b, middle_b, block_w, block_w],
        [tall, tall_b, block_dots, block_dots],
        (after(i2, gy_b), image_head, y_a, y_b),
        8,
    )
    x_3 = [loop(rows, mask=1) for rows in x_2]
    gy_a, gy_b = call(
        own_pull_kernel,
        [wide, wide],
        [],
        (*x_2, w_2a, w_2b, gy_a, gy_b),
        8,
    )
    x_3 = [after(rows, gy_a) for rows in x_3]
    *text_parts, dq_a = call(
        last_kernel,
        [part_b] * QUAD + [wide_b],
        [wide, wide, wide_b, ((rows_out, width), F32), block_w, block_w, block_dots, block_dots],
        (*x_3, y_a, y_b, q_a, q_b, gy_a, gy_b, pick_a, pick_b),
        16,
    )
    text_others = [cuts(text_parts[k], mask=k) for k in range(1, QUAD)]
    both_sides = add(image_parts[0], [after(other, dq_a) for other in image_others])
    came = loop(both_sides[part:], mask=2)
    text_sum = add(text_parts[0], [after(other, both_sides) for other in text_others])
    text_other = cuts(text_sum, mask=QUAD)
    image_sum = add(both_sides[:part], [after(came, text_sum)])
    image_other = cuts(image_sum, mask=QUAD)
    grads = [
        call(grad_kernel, [tall], [], (after(back, image_sum), head), 4, macs=2 * macs, keep=False)[0]
        for back, head in ((dp_a, image_head), (dq_a, text_head))
    ]
    text_pieces = spread(add(text_sum, [after(text_other, grads)]))
    image_pieces = spread(add(image_sum, [after(image_other, text_pieces[1])]))
    text_out, image_out = (
        call(place_kernel, [((rows_out, width), F32)], [], pieces, 4, place, keep=False)[0]
        for pieces in (text_pieces, image_pieces)
    )
    return (*grads, image_out, text_out)


def solution(mesh):
    n_loop, n_cuts = mesh.shape["loop"], mesh.shape["cuts"]
    if n_loop == 4 and n_cuts == 2 * QUAD:
        body = functools.partial(per_device, n_loop, n_cuts)
    else:
        body = plain_device
    placed = (P(("cuts", "loop"), None), P(("cuts", "loop"), None), P(), P())
    return jax.shard_map(
        body,
        mesh=mesh,
        in_specs=placed,
        out_specs=(
            P(("cuts", "loop"), None),
            P(("cuts", "loop"), None),
            P("loop", None),
            P("loop", None),
        ),
        check_vma=False,
    )
```

```python
import functools

import jax
import jax.numpy as jnp
from jax import lax
from jax.experimental import pallas as pl
from jax.experimental.pallas import tpu as pltpu
from jax.sharding import PartitionSpec as P

SCORE_SCALE = 10.0
SCORE_BIAS = -2.5
EPSILON = 1e-06
QUAD = 4
STRIP = 16
LANES = 128
F32 = jnp.float32
BF16 = jnp.bfloat16


def normalize(features, weight_matrix):
    projected = jnp.dot(features, weight_matrix, preferred_element_type=jnp.float32)
    factor = lax.rsqrt(jnp.sum(projected * projected, axis=-1, keepdims=True) + EPSILON)
    return (projected * factor, factor)


def pair_weights(image_vectors, text_vectors, image_offset):
    pair_scores = SCORE_SCALE * dot_nt(image_vectors, text_vectors) + SCORE_BIAS
    row_ids = image_offset + lax.broadcasted_iota(jnp.int32, pair_scores.shape, 0)
    col_ids = lax.broadcasted_iota(jnp.int32, pair_scores.shape, 1)
    match_targets = jnp.where(row_ids == col_ids, 1.0, -1.0).astype(jnp.float32)
    return (SCORE_SCALE * -match_targets * jax.nn.sigmoid(-match_targets * pair_scores)).astype(
        jnp.bfloat16
    )


def norm_back(unit, factor, gradient):
    return (factor * (gradient - unit * jnp.sum(unit * gradient, axis=-1, keepdims=True))).astype(
        jnp.bfloat16
    )


def dot_nn(left, right):
    return lax.dot_general(left, right, (((1,), (0,)), ((), ())), preferred_element_type=F32)


def dot_nt(left, right):
    return lax.dot_general(left, right, (((1,), (1,)), ((), ())), preferred_element_type=F32)


def dot_tn(left, right):
    return lax.dot_general(left, right, (((0,), (0,)), ((), ())), preferred_element_type=F32)


def plain_device(image_features, text_features, image_head, text_head):
    row_count = image_features.shape[0]
    own_start = lax.axis_index("loop") * row_count
    image_unit, image_factor = normalize(image_features, image_head)
    text_unit, text_factor = normalize(text_features, text_head)
    image_vectors = image_unit.astype(jnp.bfloat16)
    text_vectors = text_unit.astype(jnp.bfloat16)
    arrived = lax.all_gather(text_vectors, "loop", axis=0, tiled=True)
    weights = pair_weights(image_vectors, arrived, own_start)
    summed = jnp.dot(weights, arrived, preferred_element_type=jnp.float32)
    text_attraction = lax.psum_scatter(
        dot_tn(weights, image_vectors).astype(jnp.bfloat16), "loop", scatter_dimension=0, tiled=True
    ).astype(jnp.float32)
    image_back = norm_back(image_unit, image_factor, summed)
    text_back = norm_back(text_unit, text_factor, text_attraction)
    heads = []
    for features, back in ((image_features, image_back), (text_features, text_back)):
        term = dot_tn(features, back).astype(jnp.bfloat16)
        part = lax.psum_scatter(term, "loop", scatter_dimension=0, tiled=True)
        heads.append(lax.psum(part, "cuts").astype(jnp.float32))
    return (dot_nt(image_back, image_head), dot_nt(text_back, text_head), heads[0], heads[1])


def factor_of(ref, rows):
    p = ref[rows, :]
    return lax.rsqrt(jnp.sum(p * p, axis=-1, keepdims=True) + EPSILON)


def unit_rows(projected_ref, vectors_ref):
    for first in range(0, projected_ref.shape[0], STRIP):
        rows = slice(first, first + STRIP)
        factor = factor_of(projected_ref, rows)
        vectors_ref[rows, :] = (projected_ref[rows, :] * factor).astype(BF16)


def back_rows(projected_ref, gradient_ref, back_ref, at=0):
    for first in range(0, projected_ref.shape[0], STRIP):
        rows = slice(first, first + STRIP)
        factor = factor_of(projected_ref, rows)
        along = jnp.sum(projected_ref[rows, :] * gradient_ref[rows, :], axis=-1, keepdims=True)
        along = factor * factor * factor * along
        back = factor * gradient_ref[rows, :] - along * projected_ref[rows, :]
        back_ref[at + first : at + first + STRIP, :] = back.astype(BF16)


def weight_rows(dots_ref, weights_ref, pairs_from=None, begin=0, end=None):
    half_scale = 0.5 * SCORE_SCALE
    for first in range(begin, dots_ref.shape[0] if end is None else end, STRIP):
        rows = slice(first, first + STRIP)
        score = jnp.tanh(half_scale * dots_ref[rows, :] + 0.5 * SCORE_BIAS)
        weights = half_scale + half_scale * score
        if pairs_from is None:
            weights_ref[rows, :] = weights.astype(BF16)
            continue
        pair = pairs_from + first - begin
        left = pair // LANES * LANES
        right = min(left + LANES, weights.shape[1])
        shape = (STRIP, right - left)
        column = lax.broadcasted_iota(jnp.int32, shape, 1)
        same = column == lax.broadcasted_iota(jnp.int32, shape, 0) + (pair - left)
        middle = weights[:, left:right] - jnp.where(same, SCORE_SCALE, 0.0)
        pieces = [weights[:, :left], middle, weights[:, right:]]
        weights = jnp.concatenate([p for p in pieces if p.shape[1]], axis=1)
        weights_ref[rows, :] = weights.astype(BF16)


def one_hot(first, rows, width):
    wanted = first + lax.broadcasted_iota(jnp.int32, (rows, width), 0)
    column = lax.broadcasted_iota(jnp.int32, (rows, width), 1)
    return jnp.where(wanted == column, 1.0, 0.0)


def picker(place_ref, rows, width, sides):
    part = rows // QUAD
    pieces = []
    for k in range(QUAD):
        for side in sides:
            first = (place_ref[0] ^ side) * rows + (place_ref[1] ^ k) * part
            pieces.append(one_hot(first, part, width))
    return jnp.concatenate(pieces, axis=0).astype(BF16)


def near_kernel(
    t1, i1, t0_far, i0_far, text_head_far, image_head_far,
    q_a, y_a, p_a, x_a, w_aa, gx, t0, i0, text_head, image_head, dots, sems,
):
    half = t0.shape[0]
    copies = [
        pltpu.make_async_copy(source, target, sems.at[n])
        for n, (source, target) in enumerate(
            ((t0_far, t0), (text_head_far, text_head), (i0_far, i0), (image_head_far, image_head))
        )
    ]
    for copy in copies:
        copy.start()
    copies[0].wait()
    copies[1].wait()
    q_a[:half, :] = dot_nn(t0[...], text_head[...])
    q_a[half:, :] = dot_nn(t1[...], text_head[...])
    copies[2].wait()
    copies[3].wait()
    p_a[:half, :] = dot_nn(i0[...], image_head[...])
    unit_rows(q_a, y_a)
    p_a[half:, :] = dot_nn(i1[...], image_head[...])
    unit_rows(p_a, x_a)
    dots[...] = dot_nt(x_a[...], y_a[...])
    weight_rows(dots, w_aa, 0)
    gx[...] = dot_nn(w_aa[...], y_a[...])


def rows_of(refs):
    return jnp.concatenate([ref[...] for ref in refs], axis=0)


def text_kernel(place, *refs):
    *features, i0, i1, text_head, gx_in, x_a = refs[:-6]
    q_2, y_2, w_a2, gx, pick_i, dots = refs[-6:]
    half, width = i0.shape
    q_2[...] = dot_nn(rows_of(features), text_head[...])
    pick = picker(place, pick_i.shape[0] // 2, width, (0, 2))
    unit_rows(q_2, y_2)
    dots[...] = dot_nt(x_a[...], y_2[...])
    pick_i[:, :half] = dot_nt(pick, i0[...]).astype(BF16)
    pick_i[:, half:] = dot_nt(pick, i1[...]).astype(BF16)
    weight_rows(dots, w_a2)
    gx[...] = gx_in[...] + dot_nn(w_a2[...], y_2[...])


def image_kernel(*refs):
    *features, text_head, p_a, x_a, gx_in, pick_i, q_3, y_3, w_a3, dp_a = refs[:-8]
    near_0, near_2, near_sent, far_0, far_1, far_sent, dots, gx = refs[-8:]
    q_3[...] = dot_nn(rows_of(features), text_head[...])
    unit_rows(q_3, y_3)
    dots[...] = dot_nt(x_a[...], y_3[...])
    weight_rows(dots, w_a3)
    gx[...] = gx_in[...] + dot_nn(w_a3[...], y_3[...])
    back_rows(p_a, gx, dp_a)
    head = dot_nn(pick_i[...], dp_a[...]).astype(BF16)
    part = near_0.shape[0]
    near_side, far_side = (
        [head[first : first + part, :] for first in range(side * part, 2 * QUAD * part, 2 * part)]
        for side in range(2)
    )
    near_0[...] = near_side[0]
    near_2[...] = near_side[2]
    near_sent[:part, :] = near_side[1]
    near_sent[part:, :] = near_side[3]
    far_0[...] = far_side[0]
    far_1[...] = far_side[1]
    far_sent[:part, :] = far_side[2]
    far_sent[part:, :] = far_side[3]


def text_pull_kernel(place, *refs):
    *features, t0, t1, x_a, w_aa, w_a2, w_a3, gy_a, gy_2, gy_3, pick_a, pick_b = refs
    half = t0.shape[0]
    gy_a[...] = dot_tn(w_aa[...], x_a[...])
    gy_2[...] = dot_tn(w_a2[...], x_a[...])
    gy_3[...] = dot_tn(w_a3[...], x_a[...])
    pick = picker(place, pick_a.shape[0], t0.shape[1], (0,))
    pick_a[:, :half] = dot_nt(pick, t0[...]).astype(BF16)
    pick_a[:, half:] = dot_nt(pick, t1[...]).astype(BF16)
    pick_b[...] = dot_nt(pick, rows_of(features)).astype(BF16)


def far_weights(core, x, y_a, y_2, y_3, w_a, w_2, w_3, d_a, d_2, d_3):
    half = x.shape[0]
    middle = half // 2
    d_a[...] = dot_nt(x, y_a[...])
    d_2[...] = dot_nt(x, y_2[...])
    weight_rows(d_a, w_a)
    d_3[...] = dot_nt(x, y_3[...])
    weight_rows(d_2, w_2, core * middle, 0, middle)
    weight_rows(d_2, w_2, None, middle, half)
    weight_rows(d_3, w_3, None, 0, middle)
    weight_rows(d_3, w_3, core * middle, middle, half)


def block_kernel(i2, image_head, y_a, y_2, y_3, x_first, x_second, w_a, w_2, w_3, p_b, x_b, d_a, d_2, d_3):
    middle = x_first.shape[0]
    p_b[...] = dot_nn(i2[...], image_head[...])
    unit_rows(p_b, x_b)
    x_first[...] = x_b[:middle, :]
    x_second[...] = x_b[middle:, :]
    far_weights(0, x_b[...], y_a, y_2, y_3, w_a, w_2, w_3, d_a, d_2, d_3)


def own_pull_kernel(x_first, x_second, w_a, w_2, w_3, gy_a_in, gy_2_in, gy_3_in, gy_a, gy_2, gy_3):
    x = rows_of((x_first, x_second))
    gy_a[...] = gy_a_in[...] + dot_tn(w_a[...], x)
    gy_2[...] = gy_2_in[...] + dot_tn(w_2[...], x)
    gy_3[...] = gy_3_in[...] + dot_tn(w_3[...], x)


def last_kernel(
    x_first, x_second, y_a, y_2, y_3, q_a, q_2, q_3, gy_a_in, gy_2_in, gy_3_in, pick_a, pick_b,
    kept_0, kept_2, sent, dq_a, gy_a, gy_2, gy_3, dq_b, near_head, w_a, w_2, w_3, d_a, d_2, d_3,
):
    half = q_2.shape[0]
    x = rows_of((x_first, x_second))
    far_weights(1, x, y_a, y_2, y_3, w_a, w_2, w_3, d_a, d_2, d_3)
    gy_a[...] = gy_a_in[...] + dot_tn(w_a[...], x)
    gy_2[...] = gy_2_in[...] + dot_tn(w_2[...], x)
    back_rows(q_a, gy_a, dq_a)
    gy_3[...] = gy_3_in[...] + dot_tn(w_3[...], x)
    near_head[...] = dot_nn(pick_a[...], dq_a[...])
    back_rows(q_2, gy_2, dq_b, 0)
    back_rows(q_3, gy_3, dq_b, half)
    head = (near_head[...] + dot_nn(pick_b[...], dq_b[...])).astype(BF16)
    part = kept_0.shape[0]
    kept_0[...] = head[:part, :]
    kept_2[...] = head[2 * part : 3 * part, :]
    sent[:part, :] = head[part : 2 * part, :]
    sent[part:, :] = head[3 * part :, :]


def add_kernel(left, right, out):
    out[...] = (left[...].astype(F32) + right[...].astype(F32)).astype(BF16)


def grad_kernel(back, head, out):
    out[...] = dot_nt(back[: out.shape[0], :], head[...])


def place_kernel(place, *refs):
    *pieces, out = refs
    part = pieces[0].shape[0]
    for k, piece in enumerate(pieces):
        first = pl.multiple_of((place[1] ^ k) * part, part)
        out[pl.ds(first, part), :] = piece[...].astype(F32)


def call(kernel, outs, scratch, args, mib, place=None, macs=0, keep=True, far=()):
    far = [pltpu.with_memory_space_constraint(a, pltpu.HBM) for a in far]
    args = [pltpu.with_memory_space_constraint(a, pltpu.VMEM) for a in args] + far
    specs = [pl.BlockSpec(memory_space=pltpu.VMEM)] * (len(args) - len(far))
    specs += [pl.BlockSpec(memory_space=pltpu.HBM)] * len(far)
    if place is not None:
        args, specs = [place, *args], [pl.BlockSpec(memory_space=pltpu.SMEM), *specs]
    shape = pltpu.VMEM if keep else jax.ShapeDtypeStruct
    return pl.pallas_call(
        kernel,
        out_shape=[shape(s, t) for s, t in outs],
        in_specs=specs,
        out_specs=[pl.BlockSpec(memory_space=pltpu.VMEM)] * len(outs),
        scratch_shapes=[pltpu.VMEM(s, t) for s, t in scratch]
        + [pltpu.SemaphoreType.DMA((len(far),))] * bool(far),
        compiler_params=pltpu.CompilerParams(vmem_limit_bytes=mib * 1024 * 1024),
        cost_estimate=pl.CostEstimate(flops=2 * macs, bytes_accessed=0, transcendentals=0),
    )(*args)


def swap(array, axis, size, mask):
    return lax.ppermute(array, axis, [(i, i ^ mask) for i in range(size)])


def after(value, other):
    return lax.optimization_barrier((value, other))[0]


def per_device(n_loop, n_cuts, image_features, text_features, image_head, text_head):
    half, width = image_features.shape
    near = 2 * half
    rows_out = width // n_loop
    part = rows_out // QUAD
    loop = functools.partial(swap, axis="loop", size=n_loop)
    cuts = functools.partial(swap, axis="cuts", size=n_cuts)
    macs = half * width * width

    def both(rows, order, count):
        rows = after(rows, order)
        return [rows] + [loop(piece, mask=1) for piece in jnp.split(rows, count)]

    def add(own, others):
        return sum((other.astype(F32) for other in others), own.astype(F32)).astype(BF16)

    def spread(total):
        return [total] + [cuts(total, mask=k) for k in range(1, QUAD)]

    t2 = [loop(rows, mask=2) for rows in jnp.split(text_features, 2)]
    i2 = loop(image_features, mask=2)
    place = jnp.stack([lax.axis_index("loop"), lax.axis_index("cuts") & (QUAD - 1)])
    place = place.astype(jnp.int32)
    t0, i0, place = lax.optimization_barrier((text_features, image_features, place))
    t1 = loop(t0, mask=1)
    i1 = loop(i0, mask=1)
    wide, wide_b = ((near, width), F32), ((near, width), BF16)
    tall, tall_b = ((half, width), F32), ((half, width), BF16)
    head_b = ((width, width), BF16)
    block_w, block_dots = ((half, near), BF16), ((half, near), F32)
    side_w, side_dots = ((near, half), BF16), ((near, half), F32)
    pick_one, pick_two = ((rows_out, near), BF16), ((2 * rows_out, near), BF16)
    q_a, y_a, p_a, x_a, w_aa, gx, t0, i0, text_head, image_head = call(
        near_kernel,
        [wide, wide_b, wide, wide_b, ((near, near), BF16), wide, tall_b, tall_b, head_b, head_b],
        [((near, near), F32)],
        (t1, i1),
        8,
        far=(t0, i0, text_head, image_head),
    )
    first = both(t2[0], w_aa, 2)
    q_2, y_2, w_a2, gx, pick_i = call(
        text_kernel,
        [tall, tall_b, side_w, wide, pick_two],
        [side_dots],
        (*first, i0, i1, text_head, gx, x_a),
        8,
        place,
    )
    second = both(t2[1], gx, 2)
    part_b, parts_b = ((part, width), BF16), ((2 * part, width), BF16)
    q_3, y_3, w_a3, dp_a, near_0, near_2, near_sent, far_0, far_1, far_sent = call(
        image_kernel,
        [tall, tall_b, side_w, wide_b] + [part_b, part_b, parts_b] * 2,
        [side_dots, wide],
        (*second, text_head, p_a, x_a, gx, pick_i),
        8,
    )
    near_came, far_came = cuts(near_sent, mask=1), cuts(far_sent, mask=2)
    gy_a, gy_2, gy_3, pick_a, pick_b = call(
        text_pull_kernel,
        [wide, tall, tall, pick_one, pick_one],
        [],
        (*first, *second, t0, t1, after(x_a, dp_a), w_aa, w_a2, w_a3),
        8,
        place,
    )
    middle_b, corner, corner_dots = ((half // 2, width), BF16), ((half, half), BF16), ((half, half), F32)
    *x_2, w_2a, w_22, w_23 = call(
        block_kernel,
        [middle_b, middle_b, block_w, corner, corner],
        [tall, tall_b, block_dots, corner_dots, corner_dots],
        (after(i2, gy_2), image_head, y_a, y_2, y_3),
        8,
    )
    x_3 = [loop(rows, mask=1) for rows in x_2]
    gy_a, gy_2, gy_3 = call(
        own_pull_kernel,
        [wide, tall, tall],
        [],
        (*x_2, w_2a, w_22, w_23, gy_a, gy_2, gy_3),
        8,
    )
    near_came, far_came = after(near_came, gy_a), after(far_came, gy_a)
    near_sent, far_sent = add(near_2, [near_came[part:]]), add(far_1, [far_came[part:]])
    near_last, far_last = cuts(near_sent, mask=2), cuts(far_sent, mask=1)
    x_3 = [after(rows, (gy_a, near_sent, far_sent)) for rows in x_3]
    text_0, text_2, text_sent, dq_a = call(
        last_kernel,
        [part_b, part_b, parts_b, wide_b],
        [wide, tall, tall, wide_b, ((rows_out, width), F32), block_w, corner, corner]
        + [block_dots, corner_dots, corner_dots],
        (*x_3, y_a, y_2, y_3, q_a, q_2, q_3, gy_a, gy_2, gy_3, pick_a, pick_b),
        16,
    )
    text_came = cuts(text_sent, mask=1)
    far_sum = add(far_0, [far_came[:part], after(far_last, dq_a)])
    near_sum = add(near_0, [near_came[:part], after(near_last, dq_a)])
    image_sum = add(near_sum, [loop(far_sum, mask=2)])
    text_came = after(text_came, image_sum)
    text_middle = add(text_2, [text_came[part:]])
    text_last = cuts(text_middle, mask=2)
    grads = [
        call(grad_kernel, [tall], [], (after(back, text_middle), head), 4, keep=False)[0]
        for back, head in ((dp_a, image_head), (dq_a, text_head))
    ]
    text_sum = add(text_0, [text_came[:part], text_last])
    image_sum = call(
        add_kernel, [part_b], [], (image_sum, after(cuts(image_sum, mask=QUAD), grads)), 4, macs=4 * macs
    )[0]
    image_pieces = spread(image_sum)
    text_sum = add(text_sum, [after(cuts(text_sum, mask=QUAD), image_pieces[1])])
    image_out, text_out = (
        call(place_kernel, [((rows_out, width), F32)], [], pieces, 4, place, keep=False)[0]
        for pieces in (image_pieces, spread(text_sum))
    )
    return (*grads, image_out, text_out)


def solution(mesh):
    n_loop, n_cuts = mesh.shape["loop"], mesh.shape["cuts"]
    if n_loop == 4 and n_cuts == 2 * QUAD:
        body = functools.partial(per_device, n_loop, n_cuts)
    else:
        body = plain_device
    placed = (P(("cuts", "loop"), None), P(("cuts", "loop"), None), P(), P())
    return jax.shard_map(
        body,
        mesh=mesh,
        in_specs=placed,
        out_specs=(
            P(("cuts", "loop"), None),
            P(("cuts", "loop"), None),
            P("loop", None),
            P("loop", None),
        ),
        check_vma=False,
    )
```

```python
import functools

import jax
import jax.numpy as jnp
from jax import lax
from jax.experimental import pallas as pl
from jax.experimental.pallas import tpu as pltpu
from jax.sharding import PartitionSpec as P

SCORE_SCALE = 10.0
SCORE_BIAS = -2.5
EPSILON = 1e-06
QUAD = 4
STRIP = 16
LANES = 128
F32 = jnp.float32
BF16 = jnp.bfloat16


def normalize(features, weight_matrix):
    projected = jnp.dot(features, weight_matrix, preferred_element_type=jnp.float32)
    factor = lax.rsqrt(jnp.sum(projected * projected, axis=-1, keepdims=True) + EPSILON)
    return (projected * factor, factor)


def pair_weights(image_vectors, text_vectors, image_offset):
    pair_scores = SCORE_SCALE * dot_nt(image_vectors, text_vectors) + SCORE_BIAS
    row_ids = image_offset + lax.broadcasted_iota(jnp.int32, pair_scores.shape, 0)
    col_ids = lax.broadcasted_iota(jnp.int32, pair_scores.shape, 1)
    match_targets = jnp.where(row_ids == col_ids, 1.0, -1.0).astype(jnp.float32)
    return (SCORE_SCALE * -match_targets * jax.nn.sigmoid(-match_targets * pair_scores)).astype(
        jnp.bfloat16
    )


def norm_back(unit, factor, gradient):
    return (factor * (gradient - unit * jnp.sum(unit * gradient, axis=-1, keepdims=True))).astype(
        jnp.bfloat16
    )


def dot_nn(left, right):
    return lax.dot_general(left, right, (((1,), (0,)), ((), ())), preferred_element_type=F32)


def dot_nt(left, right):
    return lax.dot_general(left, right, (((1,), (1,)), ((), ())), preferred_element_type=F32)


def dot_tn(left, right):
    return lax.dot_general(left, right, (((0,), (0,)), ((), ())), preferred_element_type=F32)


def plain_device(image_features, text_features, image_head, text_head):
    row_count = image_features.shape[0]
    own_start = lax.axis_index("loop") * row_count
    image_unit, image_factor = normalize(image_features, image_head)
    text_unit, text_factor = normalize(text_features, text_head)
    image_vectors = image_unit.astype(jnp.bfloat16)
    text_vectors = text_unit.astype(jnp.bfloat16)
    arrived = lax.all_gather(text_vectors, "loop", axis=0, tiled=True)
    weights = pair_weights(image_vectors, arrived, own_start)
    summed = jnp.dot(weights, arrived, preferred_element_type=jnp.float32)
    text_attraction = lax.psum_scatter(
        dot_tn(weights, image_vectors).astype(jnp.bfloat16), "loop", scatter_dimension=0, tiled=True
    ).astype(jnp.float32)
    image_back = norm_back(image_unit, image_factor, summed)
    text_back = norm_back(text_unit, text_factor, text_attraction)
    heads = []
    for features, back in ((image_features, image_back), (text_features, text_back)):
        term = dot_tn(features, back).astype(jnp.bfloat16)
        part = lax.psum_scatter(term, "loop", scatter_dimension=0, tiled=True)
        heads.append(lax.psum(part, "cuts").astype(jnp.float32))
    return (dot_nt(image_back, image_head), dot_nt(text_back, text_head), heads[0], heads[1])


def factor_of(ref, rows):
    p = ref[rows, :]
    return lax.rsqrt(jnp.sum(p * p, axis=-1, keepdims=True) + EPSILON)


def unit_rows(projected_ref, vectors_ref):
    for first in range(0, projected_ref.shape[0], STRIP):
        rows = slice(first, first + STRIP)
        factor = factor_of(projected_ref, rows)
        vectors_ref[rows, :] = (projected_ref[rows, :] * factor).astype(BF16)


def back_rows(projected_ref, gradient_ref, back_ref, at=0):
    for first in range(0, projected_ref.shape[0], STRIP):
        rows = slice(first, first + STRIP)
        factor = factor_of(projected_ref, rows)
        along = jnp.sum(projected_ref[rows, :] * gradient_ref[rows, :], axis=-1, keepdims=True)
        along = factor * factor * factor * along
        back = factor * gradient_ref[rows, :] - along * projected_ref[rows, :]
        back_ref[at + first : at + first + STRIP, :] = back.astype(BF16)


def weight_rows(dots_ref, weights_ref, pairs_from=None, begin=0, end=None):
    half_scale = 0.5 * SCORE_SCALE
    for first in range(begin, dots_ref.shape[0] if end is None else end, STRIP):
        rows = slice(first, first + STRIP)
        score = jnp.tanh(half_scale * dots_ref[rows, :] + 0.5 * SCORE_BIAS)
        weights = half_scale + half_scale * score
        if pairs_from is None:
            weights_ref[rows, :] = weights.astype(BF16)
            continue
        pair = pairs_from + first - begin
        left = pair // LANES * LANES
        right = min(left + LANES, weights.shape[1])
        shape = (STRIP, right - left)
        column = lax.broadcasted_iota(jnp.int32, shape, 1)
        same = column == lax.broadcasted_iota(jnp.int32, shape, 0) + (pair - left)
        middle = weights[:, left:right] - jnp.where(same, SCORE_SCALE, 0.0)
        pieces = [weights[:, :left], middle, weights[:, right:]]
        weights = jnp.concatenate([p for p in pieces if p.shape[1]], axis=1)
        weights_ref[rows, :] = weights.astype(BF16)


def one_hot(first, rows, width):
    wanted = first + lax.broadcasted_iota(jnp.int32, (rows, width), 0)
    column = lax.broadcasted_iota(jnp.int32, (rows, width), 1)
    return jnp.where(wanted == column, 1.0, 0.0)


def picker(place_ref, rows, width, sides):
    part = rows // QUAD
    pieces = []
    for k in range(QUAD):
        for side in sides:
            first = (place_ref[0] ^ side) * rows + (place_ref[1] ^ k) * part
            pieces.append(one_hot(first, part, width))
    return jnp.concatenate(pieces, axis=0).astype(BF16)


def split_head(head, outs):
    part = head.shape[0] // QUAD
    for k, out in enumerate(outs):
        out[...] = head[k * part : (k + 1) * part, :].astype(BF16)


def near_kernel(
    t1, i1, t0_far, i0_far, text_head_far, image_head_far,
    q_a, y_a, p_a, x_a, w_aa, gx, t0, i0, text_head, image_head, dots, sems,
):
    half = t0.shape[0]
    copies = [
        pltpu.make_async_copy(source, target, sems.at[n])
        for n, (source, target) in enumerate(
            ((t0_far, t0), (text_head_far, text_head), (i0_far, i0), (image_head_far, image_head))
        )
    ]
    for copy in copies:
        copy.start()
    copies[0].wait()
    copies[1].wait()
    q_a[:half, :] = dot_nn(t0[...], text_head[...])
    q_a[half:, :] = dot_nn(t1[...], text_head[...])
    copies[2].wait()
    copies[3].wait()
    p_a[:half, :] = dot_nn(i0[...], image_head[...])
    unit_rows(q_a, y_a)
    p_a[half:, :] = dot_nn(i1[...], image_head[...])
    unit_rows(p_a, x_a)
    dots[...] = dot_nt(x_a[...], y_a[...])
    weight_rows(dots, w_aa, 0)
    gx[...] = dot_nn(w_aa[...], y_a[...])


def rows_of(refs):
    return jnp.concatenate([ref[...] for ref in refs], axis=0)


def text_kernel(place, *refs):
    *features, i0, i1, text_head, gx_in, x_a, w_aa = refs[:-7]
    q_2, y_2, w_a2, gx, gy_a, pick_i, dots = refs[-7:]
    half, width = i0.shape
    q_2[...] = dot_nn(rows_of(features), text_head[...])
    pick = picker(place, pick_i.shape[0] // 2, width, (0, 2))
    unit_rows(q_2, y_2)
    dots[...] = dot_nt(x_a[...], y_2[...])
    pick_i[:, :half] = dot_nt(pick, i0[...]).astype(BF16)
    pick_i[:, half:] = dot_nt(pick, i1[...]).astype(BF16)
    weight_rows(dots, w_a2)
    gx[...] = gx_in[...] + dot_nn(w_a2[...], y_2[...])
    gy_a[...] = dot_tn(w_aa[...], x_a[...])


def image_kernel(*refs):
    *features, text_head, p_a, x_a, gx_in, pick_i, q_3, y_3, w_a3, dp_a = refs[:-8]
    near_0, near_2, near_sent, far_0, far_1, far_sent, dots, gx = refs[-8:]
    q_3[...] = dot_nn(rows_of(features), text_head[...])
    unit_rows(q_3, y_3)
    dots[...] = dot_nt(x_a[...], y_3[...])
    weight_rows(dots, w_a3)
    gx[...] = gx_in[...] + dot_nn(w_a3[...], y_3[...])
    back_rows(p_a, gx, dp_a)
    head = dot_nn(pick_i[...], dp_a[...]).astype(BF16)
    part = near_0.shape[0]
    near_side, far_side = (
        [head[first : first + part, :] for first in range(side * part, 2 * QUAD * part, 2 * part)]
        for side in range(2)
    )
    near_0[...] = near_side[0]
    near_2[...] = near_side[2]
    near_sent[:part, :] = near_side[1]
    near_sent[part:, :] = near_side[3]
    far_0[...] = far_side[0]
    far_1[...] = far_side[1]
    far_sent[:part, :] = far_side[2]
    far_sent[part:, :] = far_side[3]


def text_pull_kernel(place, *refs):
    *features, t0, t1, x_a, w_a2, w_a3, gy_2, gy_3, pick_a, pick_b = refs
    half = t0.shape[0]
    gy_2[...] = dot_tn(w_a2[...], x_a[...])
    gy_3[...] = dot_tn(w_a3[...], x_a[...])
    pick = picker(place, pick_a.shape[0], t0.shape[1], (0,))
    pick_a[:, :half] = dot_nt(pick, t0[...]).astype(BF16)
    pick_a[:, half:] = dot_nt(pick, t1[...]).astype(BF16)
    pick_b[...] = dot_nt(pick, rows_of(features)).astype(BF16)


def far_weights(core, x, y_a, y_2, y_3, w_a, w_2, w_3, d_a, d_2, d_3):
    half = x.shape[0]
    middle = half // 2
    d_a[...] = dot_nt(x, y_a[...])
    d_2[...] = dot_nt(x, y_2[...])
    weight_rows(d_a, w_a)
    d_3[...] = dot_nt(x, y_3[...])
    weight_rows(d_2, w_2, core * middle, 0, middle)
    weight_rows(d_2, w_2, None, middle, half)
    weight_rows(d_3, w_3, None, 0, middle)
    weight_rows(d_3, w_3, core * middle, middle, half)


def block_kernel(i2, image_head, y_a, y_2, y_3, x_first, x_second, w_a, w_2, w_3, p_b, x_b, d_a, d_2, d_3):
    middle = x_first.shape[0]
    p_b[...] = dot_nn(i2[...], image_head[...])
    unit_rows(p_b, x_b)
    x_first[...] = x_b[:middle, :]
    x_second[...] = x_b[middle:, :]
    far_weights(0, x_b[...], y_a, y_2, y_3, w_a, w_2, w_3, d_a, d_2, d_3)


def own_pull_kernel(x_first, x_second, w_a, w_2, w_3, gy_a_in, gy_2_in, gy_3_in, gy_a, gy_2, gy_3):
    x = rows_of((x_first, x_second))
    gy_a[...] = gy_a_in[...] + dot_tn(w_a[...], x)
    gy_2[...] = gy_2_in[...] + dot_tn(w_2[...], x)
    gy_3[...] = gy_3_in[...] + dot_tn(w_3[...], x)


def last_kernel(
    x_first, x_second, y_a, y_2, y_3, q_a, q_2, q_3, gy_a_in, gy_2_in, gy_3_in, pick_a, pick_b,
    h0, h1, h2, h3, dq_a, gy_a, gy_2, gy_3, dq_b, near_head, w_a, w_2, w_3, d_a, d_2, d_3,
):
    half = q_2.shape[0]
    x = rows_of((x_first, x_second))
    far_weights(1, x, y_a, y_2, y_3, w_a, w_2, w_3, d_a, d_2, d_3)
    gy_a[...] = gy_a_in[...] + dot_tn(w_a[...], x)
    gy_2[...] = gy_2_in[...] + dot_tn(w_2[...], x)
    back_rows(q_a, gy_a, dq_a)
    gy_3[...] = gy_3_in[...] + dot_tn(w_3[...], x)
    near_head[...] = dot_nn(pick_a[...], dq_a[...])
    back_rows(q_2, gy_2, dq_b, 0)
    back_rows(q_3, gy_3, dq_b, half)
    split_head(near_head[...] + dot_nn(pick_b[...], dq_b[...]), (h0, h1, h2, h3))


def grad_kernel(back, head, out):
    out[...] = dot_nt(back[: out.shape[0], :], head[...])


def place_kernel(place, *refs):
    *pieces, out = refs
    part = pieces[0].shape[0]
    for k, piece in enumerate(pieces):
        first = pl.multiple_of((place[1] ^ k) * part, part)
        out[pl.ds(first, part), :] = piece[...].astype(F32)


def call(kernel, outs, scratch, args, mib, place=None, macs=0, keep=True, far=()):
    far = [pltpu.with_memory_space_constraint(a, pltpu.HBM) for a in far]
    args = [pltpu.with_memory_space_constraint(a, pltpu.VMEM) for a in args] + far
    specs = [pl.BlockSpec(memory_space=pltpu.VMEM)] * (len(args) - len(far))
    specs += [pl.BlockSpec(memory_space=pltpu.HBM)] * len(far)
    if place is not None:
        args, specs = [place, *args], [pl.BlockSpec(memory_space=pltpu.SMEM), *specs]
    shape = pltpu.VMEM if keep else jax.ShapeDtypeStruct
    return pl.pallas_call(
        kernel,
        out_shape=[shape(s, t) for s, t in outs],
        in_specs=specs,
        out_specs=[pl.BlockSpec(memory_space=pltpu.VMEM)] * len(outs),
        scratch_shapes=[pltpu.VMEM(s, t) for s, t in scratch]
        + [pltpu.SemaphoreType.DMA((len(far),))] * bool(far),
        compiler_params=pltpu.CompilerParams(vmem_limit_bytes=mib * 1024 * 1024),
        cost_estimate=pl.CostEstimate(flops=2 * macs, bytes_accessed=0, transcendentals=0),
    )(*args)


def swap(array, axis, size, mask):
    return lax.ppermute(array, axis, [(i, i ^ mask) for i in range(size)])


def after(value, other):
    return lax.optimization_barrier((value, other))[0]


def per_device(n_loop, n_cuts, image_features, text_features, image_head, text_head):
    half, width = image_features.shape
    near = 2 * half
    rows_out = width // n_loop
    part = rows_out // QUAD
    loop = functools.partial(swap, axis="loop", size=n_loop)
    cuts = functools.partial(swap, axis="cuts", size=n_cuts)
    macs = half * width * width

    def both(rows, order, count):
        rows = after(rows, order)
        return [rows] + [loop(piece, mask=1) for piece in jnp.split(rows, count)]

    def add(own, others):
        return sum((other.astype(F32) for other in others), own.astype(F32)).astype(BF16)

    def spread(total):
        return [total] + [cuts(total, mask=k) for k in range(1, QUAD)]

    t2 = [loop(rows, mask=2) for rows in jnp.split(text_features, 2)]
    i2 = loop(image_features, mask=2)
    place = jnp.stack([lax.axis_index("loop"), lax.axis_index("cuts") & (QUAD - 1)])
    place = place.astype(jnp.int32)
    t0, i0, place = lax.optimization_barrier((text_features, image_features, place))
    t1 = loop(t0, mask=1)
    i1 = loop(i0, mask=1)
    wide, wide_b = ((near, width), F32), ((near, width), BF16)
    tall, tall_b = ((half, width), F32), ((half, width), BF16)
    head_b = ((width, width), BF16)
    block_w, block_dots = ((half, near), BF16), ((half, near), F32)
    side_w, side_dots = ((near, half), BF16), ((near, half), F32)
    pick_one, pick_two = ((rows_out, near), BF16), ((2 * rows_out, near), BF16)
    q_a, y_a, p_a, x_a, w_aa, gx, t0, i0, text_head, image_head = call(
        near_kernel,
        [wide, wide_b, wide, wide_b, ((near, near), BF16), wide, tall_b, tall_b, head_b, head_b],
        [((near, near), F32)],
        (t1, i1),
        8,
        far=(t0, i0, text_head, image_head),
    )
    first = both(t2[0], w_aa, 2)
    q_2, y_2, w_a2, gx, gy_a, pick_i = call(
        text_kernel,
        [tall, tall_b, side_w, wide, wide, pick_two],
        [side_dots],
        (*first, i0, i1, text_head, gx, x_a, w_aa),
        8,
        place,
    )
    second = both(t2[1], gy_a, 2)
    part_b, parts_b = ((part, width), BF16), ((2 * part, width), BF16)
    q_3, y_3, w_a3, dp_a, near_0, near_2, near_sent, far_0, far_1, far_sent = call(
        image_kernel,
        [tall, tall_b, side_w, wide_b] + [part_b, part_b, parts_b] * 2,
        [side_dots, wide],
        (*second, text_head, p_a, x_a, gx, pick_i),
        8,
    )
    near_came, far_came = cuts(near_sent, mask=1), cuts(far_sent, mask=2)
    gy_2, gy_3, pick_a, pick_b = call(
        text_pull_kernel,
        [tall, tall, pick_one, pick_one],
        [],
        (*first, *second, t0, t1, after(x_a, dp_a), w_a2, w_a3),
        8,
        place,
    )
    middle_b, corner, corner_dots = ((half // 2, width), BF16), ((half, half), BF16), ((half, half), F32)
    *x_2, w_2a, w_22, w_23 = call(
        block_kernel,
        [middle_b, middle_b, block_w, corner, corner],
        [tall, tall_b, block_dots, corner_dots, corner_dots],
        (after(i2, gy_2), image_head, y_a, y_2, y_3),
        8,
    )
    x_3 = [loop(rows, mask=1) for rows in x_2]
    gy_a, gy_2, gy_3 = call(
        own_pull_kernel,
        [wide, tall, tall],
        [],
        (*x_2, w_2a, w_22, w_23, gy_a, gy_2, gy_3),
        8,
    )
    near_came, far_came = after(near_came, gy_a), after(far_came, gy_a)
    near_sent, far_sent = add(near_2, [near_came[part:]]), add(far_1, [far_came[part:]])
    near_last, far_last = cuts(near_sent, mask=2), cuts(far_sent, mask=1)
    x_3 = [after(rows, (gy_a, near_sent, far_sent)) for rows in x_3]
    *text_parts, dq_a = call(
        last_kernel,
        [((part, width), BF16)] * QUAD + [wide_b],
        [wide, tall, tall, wide_b, ((rows_out, width), F32), block_w, corner, corner]
        + [block_dots, corner_dots, corner_dots],
        (*x_3, y_a, y_2, y_3, q_a, q_2, q_3, gy_a, gy_2, gy_3, pick_a, pick_b),
        16,
    )
    text_others = [cuts(text_parts[k], mask=k) for k in range(1, QUAD)]
    far_sum = add(far_0, [far_came[:part], after(far_last, dq_a)])
    near_sum = add(near_0, [near_came[:part], after(near_last, dq_a)])
    image_sum = add(near_sum, [loop(far_sum, mask=2)])
    grads = [
        call(grad_kernel, [tall], [], (after(back, image_sum), head), 4, macs=2 * macs, keep=False)[0]
        for back, head in ((dp_a, image_head), (dq_a, text_head))
    ]
    text_sum = add(text_parts[0], [after(other, (image_sum, grads)) for other in text_others])
    image_sum = add(image_sum, [cuts(image_sum, mask=QUAD)])
    image_pieces = spread(image_sum)
    text_sum = add(text_sum, [after(cuts(text_sum, mask=QUAD), image_pieces[1])])
    image_out, text_out = (
        call(place_kernel, [((rows_out, width), F32)], [], pieces, 4, place, keep=False)[0]
        for pieces in (image_pieces, spread(text_sum))
    )
    return (*grads, image_out, text_out)


def solution(mesh):
    n_loop, n_cuts = mesh.shape["loop"], mesh.shape["cuts"]
    if n_loop == 4 and n_cuts == 2 * QUAD:
        body = functools.partial(per_device, n_loop, n_cuts)
    else:
        body = plain_device
    placed = (P(("cuts", "loop"), None), P(("cuts", "loop"), None), P(), P())
    return jax.shard_map(
        body,
        mesh=mesh,
        in_specs=placed,
        out_specs=(
            P(("cuts", "loop"), None),
            P(("cuts", "loop"), None),
            P("loop", None),
            P("loop", None),
        ),
        check_vma=False,
    )
```

```python
import functools

import jax
import jax.numpy as jnp
from jax import lax
from jax.experimental import pallas as pl
from jax.experimental.pallas import tpu as pltpu
from jax.sharding import PartitionSpec as P

SCORE_SCALE = 10.0
SCORE_BIAS = -2.5
EPSILON = 1e-06
QUAD = 4
STRIP = 16
LANES = 128
F32 = jnp.float32
BF16 = jnp.bfloat16


def normalize(features, weight_matrix):
    projected = jnp.dot(features, weight_matrix, preferred_element_type=jnp.float32)
    factor = lax.rsqrt(jnp.sum(projected * projected, axis=-1, keepdims=True) + EPSILON)
    return (projected * factor, factor)


def pair_weights(image_vectors, text_vectors, image_offset):
    pair_scores = SCORE_SCALE * dot_nt(image_vectors, text_vectors) + SCORE_BIAS
    row_ids = image_offset + lax.broadcasted_iota(jnp.int32, pair_scores.shape, 0)
    col_ids = lax.broadcasted_iota(jnp.int32, pair_scores.shape, 1)
    match_targets = jnp.where(row_ids == col_ids, 1.0, -1.0).astype(jnp.float32)
    return (SCORE_SCALE * -match_targets * jax.nn.sigmoid(-match_targets * pair_scores)).astype(
        jnp.bfloat16
    )


def norm_back(unit, factor, gradient):
    return (factor * (gradient - unit * jnp.sum(unit * gradient, axis=-1, keepdims=True))).astype(
        jnp.bfloat16
    )


def dot_nn(left, right):
    return lax.dot_general(left, right, (((1,), (0,)), ((), ())), preferred_element_type=F32)


def dot_nt(left, right):
    return lax.dot_general(left, right, (((1,), (1,)), ((), ())), preferred_element_type=F32)


def dot_tn(left, right):
    return lax.dot_general(left, right, (((0,), (0,)), ((), ())), preferred_element_type=F32)


def plain_device(image_features, text_features, image_head, text_head):
    row_count = image_features.shape[0]
    own_start = lax.axis_index("loop") * row_count
    image_unit, image_factor = normalize(image_features, image_head)
    text_unit, text_factor = normalize(text_features, text_head)
    image_vectors = image_unit.astype(jnp.bfloat16)
    text_vectors = text_unit.astype(jnp.bfloat16)
    arrived = lax.all_gather(text_vectors, "loop", axis=0, tiled=True)
    weights = pair_weights(image_vectors, arrived, own_start)
    summed = jnp.dot(weights, arrived, preferred_element_type=jnp.float32)
    text_attraction = lax.psum_scatter(
        dot_tn(weights, image_vectors).astype(jnp.bfloat16), "loop", scatter_dimension=0, tiled=True
    ).astype(jnp.float32)
    image_back = norm_back(image_unit, image_factor, summed)
    text_back = norm_back(text_unit, text_factor, text_attraction)
    heads = []
    for features, back in ((image_features, image_back), (text_features, text_back)):
        term = dot_tn(features, back).astype(jnp.bfloat16)
        part = lax.psum_scatter(term, "loop", scatter_dimension=0, tiled=True)
        heads.append(lax.psum(part, "cuts").astype(jnp.float32))
    return (dot_nt(image_back, image_head), dot_nt(text_back, text_head), heads[0], heads[1])


def factor_of(ref, rows):
    p = ref[rows, :]
    return lax.rsqrt(jnp.sum(p * p, axis=-1, keepdims=True) + EPSILON)


def unit_rows(projected_ref, vectors_ref):
    for first in range(0, projected_ref.shape[0], STRIP):
        rows = slice(first, first + STRIP)
        factor = factor_of(projected_ref, rows)
        vectors_ref[rows, :] = (projected_ref[rows, :] * factor).astype(BF16)


def back_rows(projected_ref, gradient_ref, back_ref, at=0):
    for first in range(0, projected_ref.shape[0], STRIP):
        rows = slice(first, first + STRIP)
        factor = factor_of(projected_ref, rows)
        along = jnp.sum(projected_ref[rows, :] * gradient_ref[rows, :], axis=-1, keepdims=True)
        along = factor * factor * factor * along
        back = factor * gradient_ref[rows, :] - along * projected_ref[rows, :]
        back_ref[at + first : at + first + STRIP, :] = back.astype(BF16)


def weight_rows(dots_ref, weights_ref, pairs_from=None, begin=0, end=None):
    half_scale = 0.5 * SCORE_SCALE
    for first in range(begin, dots_ref.shape[0] if end is None else end, STRIP):
        rows = slice(first, first + STRIP)
        score = jnp.tanh(half_scale * dots_ref[rows, :] + 0.5 * SCORE_BIAS)
        weights = half_scale + half_scale * score
        if pairs_from is None:
            weights_ref[rows, :] = weights.astype(BF16)
            continue
        pair = pairs_from + first - begin
        left = pair // LANES * LANES
        right = min(left + LANES, weights.shape[1])
        shape = (STRIP, right - left)
        column = lax.broadcasted_iota(jnp.int32, shape, 1)
        same = column == lax.broadcasted_iota(jnp.int32, shape, 0) + (pair - left)
        middle = weights[:, left:right] - jnp.where(same, SCORE_SCALE, 0.0)
        pieces = [weights[:, :left], middle, weights[:, right:]]
        weights = jnp.concatenate([p for p in pieces if p.shape[1]], axis=1)
        weights_ref[rows, :] = weights.astype(BF16)


def one_hot(first, rows, width):
    wanted = first + lax.broadcasted_iota(jnp.int32, (rows, width), 0)
    column = lax.broadcasted_iota(jnp.int32, (rows, width), 1)
    return jnp.where(wanted == column, 1.0, 0.0)


def picker(place_ref, rows, width, sides):
    part = rows // QUAD
    pieces = []
    for k in range(QUAD):
        for side in sides:
            first = (place_ref[0] ^ side) * rows + (place_ref[1] ^ k) * part
            pieces.append(one_hot(first, part, width))
    return jnp.concatenate(pieces, axis=0).astype(BF16)


def split_head(head, outs):
    part = head.shape[0] // QUAD
    for k, out in enumerate(outs):
        out[...] = head[k * part : (k + 1) * part, :].astype(BF16)


def near_kernel(
    t1, i1, t0_far, i0_far, text_head_far, image_head_far,
    q_a, y_a, p_a, x_a, w_aa, gx, t0, i0, text_head, image_head, dots, sems,
):
    half = t0.shape[0]
    copies = [
        pltpu.make_async_copy(source, target, sems.at[n])
        for n, (source, target) in enumerate(
            ((t0_far, t0), (text_head_far, text_head), (i0_far, i0), (image_head_far, image_head))
        )
    ]
    for copy in copies:
        copy.start()
    copies[0].wait()
    copies[1].wait()
    q_a[:half, :] = dot_nn(t0[...], text_head[...])
    q_a[half:, :] = dot_nn(t1[...], text_head[...])
    copies[2].wait()
    copies[3].wait()
    p_a[:half, :] = dot_nn(i0[...], image_head[...])
    unit_rows(q_a, y_a)
    p_a[half:, :] = dot_nn(i1[...], image_head[...])
    unit_rows(p_a, x_a)
    dots[...] = dot_nt(x_a[...], y_a[...])
    weight_rows(dots, w_aa, 0)
    gx[...] = dot_nn(w_aa[...], y_a[...])


def rows_of(refs):
    return jnp.concatenate([ref[...] for ref in refs], axis=0)


def text_kernel(place, *refs):
    *features, i0, i1, text_head, gx_in, x_a = refs[:-6]
    q_2, y_2, w_a2, gx, pick_i, dots = refs[-6:]
    half, width = i0.shape
    q_2[...] = dot_nn(rows_of(features), text_head[...])
    pick = picker(place, pick_i.shape[0] // 2, width, (0, 2))
    unit_rows(q_2, y_2)
    dots[...] = dot_nt(x_a[...], y_2[...])
    pick_i[:, :half] = dot_nt(pick, i0[...]).astype(BF16)
    pick_i[:, half:] = dot_nt(pick, i1[...]).astype(BF16)
    weight_rows(dots, w_a2)
    gx[...] = gx_in[...] + dot_nn(w_a2[...], y_2[...])


def image_kernel(*refs):
    *features, text_head, p_a, x_a, gx_in, pick_i, q_3, y_3, w_a3, dp_a = refs[:-8]
    near_0, near_2, near_sent, far_0, far_1, far_sent, dots, gx = refs[-8:]
    q_3[...] = dot_nn(rows_of(features), text_head[...])
    unit_rows(q_3, y_3)
    dots[...] = dot_nt(x_a[...], y_3[...])
    weight_rows(dots, w_a3)
    gx[...] = gx_in[...] + dot_nn(w_a3[...], y_3[...])
    back_rows(p_a, gx, dp_a)
    head = dot_nn(pick_i[...], dp_a[...]).astype(BF16)
    part = near_0.shape[0]
    near_side, far_side = (
        [head[first : first + part, :] for first in range(side * part, 2 * QUAD * part, 2 * part)]
        for side in range(2)
    )
    near_0[...] = near_side[0]
    near_2[...] = near_side[2]
    near_sent[:part, :] = near_side[1]
    near_sent[part:, :] = near_side[3]
    far_0[...] = far_side[0]
    far_1[...] = far_side[1]
    far_sent[:part, :] = far_side[2]
    far_sent[part:, :] = far_side[3]


def text_pull_kernel(place, *refs):
    *features, t0, t1, x_a, w_aa, w_a2, w_a3, gy_a, gy_2, gy_3, pick_a, pick_b = refs
    half = t0.shape[0]
    gy_a[...] = dot_tn(w_aa[...], x_a[...])
    gy_2[...] = dot_tn(w_a2[...], x_a[...])
    gy_3[...] = dot_tn(w_a3[...], x_a[...])
    pick = picker(place, pick_a.shape[0], t0.shape[1], (0,))
    pick_a[:, :half] = dot_nt(pick, t0[...]).astype(BF16)
    pick_a[:, half:] = dot_nt(pick, t1[...]).astype(BF16)
    pick_b[...] = dot_nt(pick, rows_of(features)).astype(BF16)


def far_weights(core, x, y_a, y_2, y_3, w_a, w_2, w_3, d_a, d_2, d_3):
    half = x.shape[0]
    middle = half // 2
    d_a[...] = dot_nt(x, y_a[...])
    d_2[...] = dot_nt(x, y_2[...])
    weight_rows(d_a, w_a)
    d_3[...] = dot_nt(x, y_3[...])
    weight_rows(d_2, w_2, core * middle, 0, middle)
    weight_rows(d_2, w_2, None, middle, half)
    weight_rows(d_3, w_3, None, 0, middle)
    weight_rows(d_3, w_3, core * middle, middle, half)


def block_kernel(i2, image_head, y_a, y_2, y_3, x_first, x_second, w_a, w_2, w_3, p_b, x_b, d_a, d_2, d_3):
    middle = x_first.shape[0]
    p_b[...] = dot_nn(i2[...], image_head[...])
    unit_rows(p_b, x_b)
    x_first[...] = x_b[:middle, :]
    x_second[...] = x_b[middle:, :]
    far_weights(0, x_b[...], y_a, y_2, y_3, w_a, w_2, w_3, d_a, d_2, d_3)


def own_pull_kernel(x_first, x_second, w_a, w_2, w_3, gy_a_in, gy_2_in, gy_3_in, gy_a, gy_2, gy_3):
    x = rows_of((x_first, x_second))
    gy_a[...] = gy_a_in[...] + dot_tn(w_a[...], x)
    gy_2[...] = gy_2_in[...] + dot_tn(w_2[...], x)
    gy_3[...] = gy_3_in[...] + dot_tn(w_3[...], x)


def last_kernel(
    x_first, x_second, y_a, y_2, y_3, q_a, q_2, q_3, gy_a_in, gy_2_in, gy_3_in, pick_a, pick_b,
    h0, h1, h2, h3, dq_a, gy_a, gy_2, gy_3, dq_b, near_head, w_a, w_2, w_3, d_a, d_2, d_3,
):
    half = q_2.shape[0]
    x = rows_of((x_first, x_second))
    far_weights(1, x, y_a, y_2, y_3, w_a, w_2, w_3, d_a, d_2, d_3)
    gy_a[...] = gy_a_in[...] + dot_tn(w_a[...], x)
    gy_2[...] = gy_2_in[...] + dot_tn(w_2[...], x)
    back_rows(q_a, gy_a, dq_a)
    gy_3[...] = gy_3_in[...] + dot_tn(w_3[...], x)
    near_head[...] = dot_nn(pick_a[...], dq_a[...])
    back_rows(q_2, gy_2, dq_b, 0)
    back_rows(q_3, gy_3, dq_b, half)
    split_head(near_head[...] + dot_nn(pick_b[...], dq_b[...]), (h0, h1, h2, h3))


def grad_kernel(back, head, out):
    out[...] = dot_nt(back[: out.shape[0], :], head[...])


def place_kernel(place, *refs):
    *pieces, out = refs
    part = pieces[0].shape[0]
    for k, piece in enumerate(pieces):
        first = pl.multiple_of((place[1] ^ k) * part, part)
        out[pl.ds(first, part), :] = piece[...].astype(F32)


def call(kernel, outs, scratch, args, mib, place=None, macs=0, keep=True, far=()):
    far = [pltpu.with_memory_space_constraint(a, pltpu.HBM) for a in far]
    args = [pltpu.with_memory_space_constraint(a, pltpu.VMEM) for a in args] + far
    specs = [pl.BlockSpec(memory_space=pltpu.VMEM)] * (len(args) - len(far))
    specs += [pl.BlockSpec(memory_space=pltpu.HBM)] * len(far)
    if place is not None:
        args, specs = [place, *args], [pl.BlockSpec(memory_space=pltpu.SMEM), *specs]
    shape = pltpu.VMEM if keep else jax.ShapeDtypeStruct
    return pl.pallas_call(
        kernel,
        out_shape=[shape(s, t) for s, t in outs],
        in_specs=specs,
        out_specs=[pl.BlockSpec(memory_space=pltpu.VMEM)] * len(outs),
        scratch_shapes=[pltpu.VMEM(s, t) for s, t in scratch]
        + [pltpu.SemaphoreType.DMA((len(far),))] * bool(far),
        compiler_params=pltpu.CompilerParams(vmem_limit_bytes=mib * 1024 * 1024),
        cost_estimate=pl.CostEstimate(flops=2 * macs, bytes_accessed=0, transcendentals=0),
    )(*args)


def swap(array, axis, size, mask):
    return lax.ppermute(array, axis, [(i, i ^ mask) for i in range(size)])


def after(value, other):
    return lax.optimization_barrier((value, other))[0]


def per_device(n_loop, n_cuts, image_features, text_features, image_head, text_head):
    half, width = image_features.shape
    near = 2 * half
    rows_out = width // n_loop
    part = rows_out // QUAD
    loop = functools.partial(swap, axis="loop", size=n_loop)
    cuts = functools.partial(swap, axis="cuts", size=n_cuts)
    macs = half * width * width

    def both(rows, order, count):
        rows = after(rows, order)
        return [rows] + [loop(piece, mask=1) for piece in jnp.split(rows, count)]

    def add(own, others):
        return sum((other.astype(F32) for other in others), own.astype(F32)).astype(BF16)

    def spread(total):
        return [total] + [cuts(total, mask=k) for k in range(1, QUAD)]

    t2 = [loop(rows, mask=2) for rows in jnp.split(text_features, 2)]
    i2 = loop(image_features, mask=2)
    place = jnp.stack([lax.axis_index("loop"), lax.axis_index("cuts") & (QUAD - 1)])
    place = place.astype(jnp.int32)
    t0, i0, place = lax.optimization_barrier((text_features, image_features, place))
    t1 = loop(t0, mask=1)
    i1 = loop(i0, mask=1)
    wide, wide_b = ((near, width), F32), ((near, width), BF16)
    tall, tall_b = ((half, width), F32), ((half, width), BF16)
    head_b = ((width, width), BF16)
    block_w, block_dots = ((half, near), BF16), ((half, near), F32)
    side_w, side_dots = ((near, half), BF16), ((near, half), F32)
    pick_one, pick_two = ((rows_out, near), BF16), ((2 * rows_out, near), BF16)
    q_a, y_a, p_a, x_a, w_aa, gx, t0, i0, text_head, image_head = call(
        near_kernel,
        [wide, wide_b, wide, wide_b, ((near, near), BF16), wide, tall_b, tall_b, head_b, head_b],
        [((near, near), F32)],
        (t1, i1),
        8,
        far=(t0, i0, text_head, image_head),
    )
    first = both(t2[0], w_aa, 2)
    q_2, y_2, w_a2, gx, pick_i = call(
        text_kernel,
        [tall, tall_b, side_w, wide, pick_two],
        [side_dots],
        (*first, i0, i1, text_head, gx, x_a),
        8,
        place,
    )
    second = both(t2[1], gx, 2)
    part_b, parts_b = ((part, width), BF16), ((2 * part, width), BF16)
    q_3, y_3, w_a3, dp_a, near_0, near_2, near_sent, far_0, far_1, far_sent = call(
        image_kernel,
        [tall, tall_b, side_w, wide_b] + [part_b, part_b, parts_b] * 2,
        [side_dots, wide],
        (*second, text_head, p_a, x_a, gx, pick_i),
        8,
    )
    near_came, far_came = cuts(near_sent, mask=1), cuts(far_sent, mask=2)
    gy_a, gy_2, gy_3, pick_a, pick_b = call(
        text_pull_kernel,
        [wide, tall, tall, pick_one, pick_one],
        [],
        (*first, *second, t0, t1, after(x_a, dp_a), w_aa, w_a2, w_a3),
        8,
        place,
    )
    middle_b, corner, corner_dots = ((half // 2, width), BF16), ((half, half), BF16), ((half, half), F32)
    *x_2, w_2a, w_22, w_23 = call(
        block_kernel,
        [middle_b, middle_b, block_w, corner, corner],
        [tall, tall_b, block_dots, corner_dots, corner_dots],
        (after(i2, gy_2), image_head, y_a, y_2, y_3),
        8,
    )
    x_3 = [loop(rows, mask=1) for rows in x_2]
    gy_a, gy_2, gy_3 = call(
        own_pull_kernel,
        [wide, tall, tall],
        [],
        (*x_2, w_2a, w_22, w_23, gy_a, gy_2, gy_3),
        8,
    )
    near_came, far_came = after(near_came, gy_a), after(far_came, gy_a)
    near_sent, far_sent = add(near_2, [near_came[part:]]), add(far_1, [far_came[part:]])
    near_last, far_last = cuts(near_sent, mask=2), cuts(far_sent, mask=1)
    x_3 = [after(rows, (gy_a, near_sent, far_sent)) for rows in x_3]
    *text_parts, dq_a = call(
        last_kernel,
        [((part, width), BF16)] * QUAD + [wide_b],
        [wide, tall, tall, wide_b, ((rows_out, width), F32), block_w, corner, corner]
        + [block_dots, corner_dots, corner_dots],
        (*x_3, y_a, y_2, y_3, q_a, q_2, q_3, gy_a, gy_2, gy_3, pick_a, pick_b),
        16,
    )
    text_others = [cuts(text_parts[k], mask=k) for k in range(1, QUAD)]
    far_sum = add(far_0, [far_came[:part], after(far_last, dq_a)])
    near_sum = add(near_0, [near_came[:part], after(near_last, dq_a)])
    image_sum = add(near_sum, [loop(far_sum, mask=2)])
    grads = [
        call(grad_kernel, [tall], [], (after(back, image_sum), head), 4, macs=2 * macs, keep=False)[0]
        for back, head in ((dp_a, image_head), (dq_a, text_head))
    ]
    text_sum = add(text_parts[0], [after(other, (image_sum, grads)) for other in text_others])
    image_sum = add(image_sum, [cuts(image_sum, mask=QUAD)])
    image_pieces = spread(image_sum)
    text_sum = add(text_sum, [after(cuts(text_sum, mask=QUAD), image_pieces[1])])
    image_out, text_out = (
        call(place_kernel, [((rows_out, width), F32)], [], pieces, 4, place, keep=False)[0]
        for pieces in (image_pieces, spread(text_sum))
    )
    return (*grads, image_out, text_out)


def solution(mesh):
    n_loop, n_cuts = mesh.shape["loop"], mesh.shape["cuts"]
    if n_loop == 4 and n_cuts == 2 * QUAD:
        body = functools.partial(per_device, n_loop, n_cuts)
    else:
        body = plain_device
    placed = (P(("cuts", "loop"), None), P(("cuts", "loop"), None), P(), P())
    return jax.shard_map(
        body,
        mesh=mesh,
        in_specs=placed,
        out_specs=(
            P(("cuts", "loop"), None),
            P(("cuts", "loop"), None),
            P("loop", None),
            P("loop", None),
        ),
        check_vma=False,
    )
```
